32 devices in a mesh: grp: 2 (over y), hh: 4 (over z), per: 2 (over x), st: 2 (over core).
Axes of the slice: x: 2, y: 2, z: 4, core: 2. Of those that a mesh axis runs over, the one named last changes fastest.
Arguments:
- earnings: float32 [3072, 16], P(('hh', 'per')), may hold values from -5.4 to 5.4
- starts: int32 [3072], P(('hh', 'per')), may hold values from 0 to 12, as said below
- lengths: int32 [3072], P(('hh', 'per')), may hold values from 4 to 16
- block_count: int32 [8], P(('hh', 'per')), may hold values from 0 to 3, as said below
- trans_logits: bfloat16 [32, 256, 256], P(('grp', 'per', 'st')), parts along dimension 0, may hold values from -4 to 4
- init_logits: float32 [512], P('grp'), parts along dimension 0, may hold values from -4 to 4
- state_mean: float32 [512], P('grp'), parts along dimension 0, may hold values from -4 to 4
- log_sd: float32 [512], P('grp'), parts along dimension 0, may hold values from 0 to 1
Outputs:
- trans_grad: float32 [32, 256, 256], P(('grp', 'per'), 'hh', 'st'), parts along dimension 0
- mean_loglik: float32 [2], P('grp'), parts along dimension 0
The draws below stay inside these ranges and needn't reach their ends.
There are 2 independent parts, one for each index of `grp`. The reference program is written for one: setup_inputs(seed, part) draws one part's arguments, and reference() takes and returns one part's arrays. A program takes and returns all parts, laid end to end along the dimension named above; an argument that names none is the same for every part. Nothing has to cross between parts.
Inputs may be any that keep to these rules, and one draw needn't show every extreme that they name: starts[h] + lengths[h] <= 16. Exactly 1 device hold 3 blocks and as many hold 2; the counts sum to 8. Only the first block_count[d] blocks of device d's 3 slots hold households; the entries of the other slots are to be ignored.
All inputs are finite; a program needn't handle non-finite values.
Results may differ from the reference program's by a relative error of at most 0.00055.
Values may be sent and summed in bfloat16 or wider, within the bound.
No kernel may reach another device: no remote copies, remote signals or barrier semaphores. Data moves between devices by JAX's collectives and lax.ppermute only.
A program may use at most 64 MiB of HBM per device.

```python
import jax
import jax.numpy as jnp
from jax import lax

S = 256
NT = 16
HB = 128
CAP = 3
ND = 8


def draw_earnings(key, part):
    row_count = CAP * HB * ND
    slot_ids = jnp.arange(row_count, dtype=jnp.int32)
    device_ids = slot_ids // (CAP * HB)
    cycle_pos = slot_ids % (CAP * HB) % ND
    level_exp = (device_ids + cycle_pos).astype(jnp.float32) / ND
    row_scale = 0.3 * 3.0 ** level_exp
    base_draw = jnp.clip(jax.random.normal(key, (row_count, NT), jnp.float32), -2.0, 2.0)
    return base_draw * row_scale[:, None]


def household_times(key):
    row_count = CAP * HB * ND
    slot_ids = jnp.arange(row_count, dtype=jnp.int32)
    span_len = jax.random.randint(jax.random.fold_in(key, 101), (row_count,), 4, NT + 1)
    span_len = jnp.where(slot_ids == 0, NT, jnp.where(slot_ids == 1, 4, span_len))
    raw_bits = jax.random.randint(jax.random.fold_in(key, 202), (row_count,), 0, 1 << 20)
    begin_at = raw_bits % (NT - span_len + 1)
    begin_at = jnp.where(slot_ids == 1, NT - 4, begin_at)
    return (begin_at.astype(jnp.int32), span_len.astype(jnp.int32))


def draw_starts(key, part):
    return household_times(key)[0]


def draw_lengths(key, part):
    return household_times(key)[1]


def draw_block_count(key, part):
    eighth = ND // 8
    rank_ids = jnp.arange(ND, dtype=jnp.int32)
    count_table = jnp.where(rank_ids < eighth, CAP, jnp.where(rank_ids < CAP * eighth, 0, jnp.where(rank_ids < CAP * eighth + eighth, 2, jnp.where(rank_ids < CAP * eighth + 2 * eighth, 0, 1))))
    shuffle = jax.random.permutation(key, ND)
    return count_table[shuffle].astype(jnp.int32)


def block_levels(rng, shape, split, smallest, largest):
    def one(axis_at, blocks):
        steps = jax.random.uniform(jax.random.fold_in(jax.random.fold_in(rng, 6), axis_at), (blocks,), jnp.float32, smallest / len(split), largest / len(split))
        return jnp.repeat(jnp.exp(steps), shape[axis_at] // blocks).reshape((-1,) + (1,) * (len(shape) - axis_at - 1))

    level = one(*split[0])
    for cut in split[1:]:
        level = level * one(*cut)
    return level


def scatter_about(stream_key, extent, deviation, most, pieces=(), kind=jnp.bfloat16):
    factor_of = block_levels(stream_key, extent, pieces, -0.22, 0.18) if pieces else 1.0
    result = jax.random.normal(stream_key, extent, jnp.float32) * deviation * factor_of
    return jnp.minimum(jnp.maximum(result, -most), most).astype(kind)


def setup_inputs(seed: int = 0, part: int = 0) -> dict:
    streams_of = jax.random.split(jax.random.key(seed), 9)
    part_splits = jax.random.split(jax.random.fold_in(streams_of[8], part), 9)
    return {
        "earnings": draw_earnings(jax.random.fold_in(streams_of[8], 71), part),
        "starts": draw_starts(jax.random.fold_in(streams_of[8], 71), part),
        "lengths": draw_lengths(jax.random.fold_in(streams_of[8], 71), part),
        "block_count": draw_block_count(jax.random.fold_in(streams_of[8], 71), part),
        "trans_logits": scatter_about(part_splits[4], (NT, S, S), 1.0, 4.0, ((0, 4),)),
        "init_logits": scatter_about(part_splits[5], (S,), 1.0, 4.0, (), jnp.float32),
        "state_mean": jnp.clip(jax.random.uniform(part_splits[6], (S,), jnp.float32, -4.0, 4.0), -4.0, 4.0),
        "log_sd": jnp.clip(jax.random.uniform(part_splits[7], (S,), jnp.float32, 0.0, 1.0), 0.0, 1.0),
    }


top_precision = lax.Precision.HIGHEST


def emission(column, state_mean, log_sd):
    z_score = (column[:, None] - state_mean[None, :]) / jnp.exp(log_sd)[None, :]
    return jnp.exp(-0.5 * z_score * z_score - log_sd[None, :])


def reference(earnings, starts, lengths, block_count, trans_logits, init_logits, state_mean, log_sd):
    raised = jnp.exp(trans_logits.astype(jnp.float32))
    probs = raised / jnp.sum(raised, axis=2, keepdims=True)
    raised_first = jnp.exp(init_logits)
    first_probs = raised_first / jnp.sum(raised_first)
    num_states = first_probs.shape[0]
    block_total = ND * CAP
    block_alive = (jnp.arange(block_total, dtype=jnp.int32) % CAP) < jnp.repeat(block_count, CAP)
    earn_blocks = earnings.reshape(block_total, HB, NT)
    start_blocks = starts.reshape(block_total, HB)
    length_blocks = lengths.reshape(block_total, HB)
    period_ids = jnp.arange(NT, dtype=jnp.int32)

    def block_terms(earn_rows, begin_at, span_len):
        def forward(prev_alpha, inputs):
            matrix, column, step_now = inputs
            moved_mass = jnp.dot(prev_alpha, matrix, precision=top_precision, preferred_element_type=jnp.float32)
            joint_mass = jnp.where((step_now <= begin_at)[:, None], first_probs[None, :], moved_mass) * emission(column, state_mean, log_sd)
            seen_now = (step_now >= begin_at) & (step_now < begin_at + span_len)
            scale_now = jnp.where(seen_now, jnp.sum(joint_mass, axis=1), 1.0)
            new_alpha = jnp.where(seen_now[:, None], joint_mass / scale_now[:, None], prev_alpha)
            return new_alpha, (new_alpha, scale_now)

        start_alpha = jnp.broadcast_to(first_probs[None, :], (HB, num_states))
        columns = earn_rows.T
        _, (alphas, scales) = lax.scan(forward, start_alpha, (probs, columns, period_ids))

        def carry_of(back_now, column, scale_now, step_now):
            seen_now = (step_now >= begin_at) & (step_now < begin_at + span_len)
            return jnp.where(seen_now[:, None], emission(column, state_mean, log_sd) * back_now / scale_now[:, None], 0.0)

        def backward(carry_now, inputs):
            matrix, alpha_prev, column_prev, scale_prev, step_now = inputs
            moving = (step_now > begin_at) & (step_now < begin_at + span_len)
            weights = jnp.where(moving[:, None], alpha_prev, 0.0)
            grad_term = jnp.dot(weights.T, carry_now, precision=top_precision, preferred_element_type=jnp.float32)
            back_now = jnp.where(moving[:, None], jnp.dot(carry_now, matrix.T, precision=top_precision, preferred_element_type=jnp.float32), 1.0)
            return carry_of(back_now, column_prev, scale_prev, step_now - 1), grad_term

        last_carry = carry_of(jnp.ones((HB, num_states), jnp.float32), columns[NT - 1], scales[NT - 1], NT - 1)
        _, grad_terms = lax.scan(backward, last_carry, (probs[1:], alphas[:-1], columns[:-1], scales[:-1], period_ids[1:]), reverse=True)
        return grad_terms, jnp.sum(jnp.log(scales)), jnp.sum(span_len).astype(jnp.float32)

    def accumulate(totals, inputs):
        earn_rows, begin_at, span_len, alive_now = inputs

        def take_block(operands):
            counts, loglik, years = totals
            grad_terms, part_loglik, part_years = block_terms(operands[0], operands[1], operands[2])
            return counts.at[1:].add(grad_terms), loglik + part_loglik, years + part_years

        def skip_block(operands):
            return totals

        return lax.cond(alive_now, take_block, skip_block, (earn_rows, begin_at, span_len)), None

    zero_totals = (jnp.zeros((NT, num_states, num_states), jnp.float32), jnp.zeros((), jnp.float32), jnp.zeros((), jnp.float32))
    (counts, loglik, years), _ = lax.scan(accumulate, zero_totals, (earn_blocks, start_blocks, length_blocks, block_alive))
    weighted = probs * counts
    row_total = jnp.sum(weighted, axis=2, keepdims=True)
    factor = float(num_states * num_states * NT) / years
    trans_grad = factor * (weighted - probs * row_total)
    mean_loglik = jnp.reshape(loglik / years, (1,))
    return trans_grad, mean_loglik
```

```python
import functools

import jax
import jax.numpy as jnp
from jax import lax
from jax.experimental import pallas as pl
from jax.experimental.pallas import tpu as pltpu
from jax.sharding import PartitionSpec as P

HB = 128
LANES = 128
F32 = jnp.float32
BF16 = jnp.bfloat16
LOG2E = 1.4426950408889634
LN2 = 0.6931471805599453
VMEM_LIMIT = 40 * 1024 * 1024


def vmem():
    return pl.BlockSpec(memory_space=pltpu.VMEM)


def smem():
    return pl.BlockSpec(memory_space=pltpu.SMEM)


def params():
    return pltpu.CompilerParams(vmem_limit_bytes=VMEM_LIMIT)


def pack_kernel(count_ref, earn_ref, start_ref, len_ref, out_ref):
    periods, rows = earn_ref.shape
    live = lax.broadcasted_iota(jnp.int32, (1, rows), 1) < count_ref[0] * HB
    code = jnp.where(live, start_ref[...] * (2 * periods) + len_ref[...], -1)
    out_ref[:periods, :] = earn_ref[...]
    out_ref[periods:, :] = jnp.broadcast_to(code.astype(F32), (8, rows))


def prep_kernel(
    ids_ref, own_ref, other_ref, init_ref, mean_ref, sd_ref, first_mat, second_mat, row_probs, consts, scratch
):
    core, forward_first, row_begin = ids_ref[0], ids_ref[1], ids_ref[2]
    part, states, _ = own_ref.shape
    rows = row_probs.shape[1]

    def column(row):
        return jnp.broadcast_to(row, (LANES, states)).T

    raised = jnp.exp(init_ref[...])
    consts[0] = column(raised / jnp.sum(raised, axis=1, keepdims=True))
    consts[1] = column(mean_ref[...])
    consts[2] = column((-0.5 * LOG2E) * jnp.exp(-2.0 * sd_ref[...]))
    consts[3] = column(-LOG2E * sd_ref[...])

    def put(ref, at, value):
        high = value.astype(BF16)
        ref[at, :states, :] = high
        ref[at, states:, :] = (value - high.astype(F32)).astype(BF16)

    for source, ref in ((core, own_ref), (1 - core, other_ref)):

        @pl.loop(0, part)
        def _(i):
            at = source * part + i
            lifted = jnp.exp(ref[i].astype(F32))
            probs = lifted / jnp.sum(lifted, axis=1, keepdims=True)
            scratch[...] = probs
            row_probs[at] = scratch[pl.ds(pl.multiple_of(row_begin, rows), rows), :]
            turned = probs.T

            @pl.when(forward_first == 1)
            def _():
                put(first_mat, at, turned)
                put(second_mat, at, probs)

            @pl.when(forward_first == 0)
            def _():
                put(first_mat, at, probs)
                put(second_mat, at, turned)


def emission(sel_ref, consts, step_now, cols):
    gap = sel_ref[step_now, :1, cols] - consts[1]
    power = gap * gap * consts[2] + consts[3]
    top = jnp.max(power, axis=0, keepdims=True)
    return jnp.exp2(power - top), top


def spans(sel_ref, periods, cols):
    begin = sel_ref[periods, :1, cols]
    return begin, begin + sel_ref[periods + 1, :1, cols]


def run_forward(lead, mat, hist, sel_ref, consts, ab_ref, weights_ref, counts_ref, row_begin):
    steps, states, width = hist.shape
    periods = sel_ref.shape[0] - 3

    def body(k, carry):
        inverse, loglik = carry
        step_now = lead + k
        step_f = step_now.astype(F32)
        if counts_ref is None:
            hist[k] = ab_ref[...]
        else:
            rows = weights_ref.shape[0]
            own_alpha = ab_ref[pl.ds(pl.multiple_of(row_begin, rows), rows), :].astype(F32)
        product = jnp.dot(mat[k], ab_ref[...], preferred_element_type=F32)
        new_inverse, new_loglik = [], []
        for q in range(width // LANES):
            cols = slice(q * LANES, (q + 1) * LANES)
            begin, end = spans(sel_ref, periods, cols)
            moved = (product[:states, cols] + product[states:, cols]) * inverse[:, cols]
            if counts_ref is not None:
                total = jnp.sum(moved * hist[k, :, cols].astype(F32), axis=0, keepdims=True)
                moving = (step_f > begin) & (step_f < end)
                weight = jnp.where(moving, inverse[:, cols] / total, 0.0)
                weights_ref[:, cols] = (own_alpha[:, cols] * weight).astype(BF16)
            emit, top = emission(sel_ref, consts, step_now, cols)
            joint = jnp.where(step_f <= begin, consts[0], moved) * emit
            scale = jnp.sum(joint, axis=0, keepdims=True)
            seen = (step_f >= begin) & (step_f < end)
            new_loglik.append(loglik[:, cols] + jnp.where(seen, jnp.log(scale) + top * LN2, 0.0))
            new_inverse.append(1.0 / scale)
            ab_ref[:, cols] = joint.astype(BF16)
        if counts_ref is not None:
            counts_ref[k] += lax.dot_general(
                weights_ref[...], hist[k], (((1,), (1,)), ((), ())), preferred_element_type=F32
            )
        return jnp.concatenate(new_inverse, axis=1), jnp.concatenate(new_loglik, axis=1)

    inverse = 1.0 / jnp.sum(ab_ref[...].astype(F32), axis=0, keepdims=True)
    _, loglik = lax.fori_loop(0, steps, body, (inverse, jnp.zeros((1, width), F32)))
    return jnp.sum(loglik, axis=1, keepdims=True)


def run_backward(lead, mat, hist, sel_ref, consts, back_ref, ub_ref, weights_ref, counts_ref, row_begin):
    steps, states, width = hist.shape
    periods = sel_ref.shape[0] - 3

    def body(j, carry):
        k = steps - 1 - j
        step_now = lead + k
        step_f = step_now.astype(F32)
        shrink = []
        for q in range(width // LANES):
            cols = slice(q * LANES, (q + 1) * LANES)
            emit, _ = emission(sel_ref, consts, step_now, cols)
            carried = emit * back_ref[:, cols]
            shrink.append(1.0 / jnp.sum(carried, axis=0, keepdims=True))
            ub_ref[:, cols] = carried.astype(BF16)
        if counts_ref is None:
            hist[k] = ub_ref[...]
        product = jnp.dot(mat[k], ub_ref[...], preferred_element_type=F32)
        if counts_ref is not None:
            rows = weights_ref.shape[0]
            own_alpha = hist[k, pl.ds(pl.multiple_of(row_begin, rows), rows), :].astype(F32)
        for q in range(width // LANES):
            cols = slice(q * LANES, (q + 1) * LANES)
            begin, end = spans(sel_ref, periods, cols)
            moving = (step_f > begin) & (step_f < end)
            pulled = (product[:states, cols] + product[states:, cols]) * shrink[q]
            if counts_ref is not None:
                total = jnp.sum(pulled * hist[k, :, cols].astype(F32), axis=0, keepdims=True)
                weight = jnp.where(moving, shrink[q] / total, 0.0)
                weights_ref[:, cols] = (own_alpha[:, cols] * weight).astype(BF16)
            back_ref[:, cols] = jnp.where(moving, pulled, 1.0)
        if counts_ref is not None:
            counts_ref[k] += lax.dot_general(
                weights_ref[...], ub_ref[...], (((1,), (1,)), ((), ())), preferred_element_type=F32
            )
        return carry

    lax.fori_loop(0, steps, body, 0)


def first_kernel(direct, resume, group, chunks, *refs):
    refs = list(refs)
    ids_ref = refs.pop(0)
    gathered = [refs.pop(0) for _ in range(group)] if direct else [refs.pop(0)]
    mat, consts = refs.pop(0), refs.pop(0)
    state_in = refs.pop(0) if resume else None
    hist, state_out, sel_ref, ll_ref, ab_ref, back_ref = refs[:6]
    core, forward_first, lead, me, cores = ids_ref[0], ids_ref[1], ids_ref[3], ids_ref[4], ids_ref[5]
    chunk = pl.program_id(0) if chunks > 1 else 0
    steps, states, width = hist.shape
    periods = sel_ref.shape[0] - 3
    if direct:
        all_rows = refs[6]
        for r, ref in enumerate(gathered):
            all_rows[lax.rem(me + group - r, group)] = ref[...]
    else:
        all_rows = gathered[0]
    slots = all_rows.shape[2] // HB
    picks = width // HB
    base = 2.0 * periods
    pieces = (periods + 8) // 8

    def scan_source(d, carry):
        rank, years, picked = carry
        for slot in range(slots):
            cols = slice(slot * HB, (slot + 1) * HB)
            code = all_rows[d, periods:, cols]
            live = code >= 0.0
            begin = jnp.floor(code * (1.0 / base))
            years = years + jnp.where(live, code - begin * base, 0.0)
            block = [all_rows[d, 8 * p : 8 * p + 8, cols] for p in range(pieces)]
            fresh = []
            for q in range(picks):
                target = (chunk * picks + q) * cores + core
                hit = live & (rank == target)
                fresh.append([jnp.where(hit, new, old) for new, old in zip(block, picked[q])])
            picked = fresh
            rank = rank + live.astype(jnp.int32)
        return rank, years, picked

    zero = jnp.zeros((8, HB), F32)
    carry = (jnp.zeros((8, HB), jnp.int32), zero, [[zero] * pieces for _ in range(picks)])
    if group <= 8:
        for d in range(group):
            carry = scan_source(d, carry)
    else:
        carry = lax.fori_loop(0, group, scan_source, carry)
    _, years, picked = carry
    years = jnp.sum(years, axis=1, keepdims=True)
    for q in range(picks):
        cols = slice(q * HB, (q + 1) * HB)
        for p in range(pieces - 1):
            for i in range(8):
                sel_ref[8 * p + i, :, cols] = jnp.broadcast_to(picked[q][p][i : i + 1], (8, HB))
        begin = jnp.floor(picked[q][pieces - 1] * (1.0 / base))
        sel_ref[periods, :, cols] = begin
        sel_ref[periods + 1, :, cols] = picked[q][pieces - 1] - begin * base
        sel_ref[periods + 2, :, cols] = jnp.broadcast_to(years, (8, HB))

    @pl.when(chunk == 0)
    def _():
        ll_ref[...] = jnp.zeros_like(ll_ref)

    @pl.when(forward_first == 1)
    def _():
        if resume:
            ab_ref[...] = state_in[...]
        else:
            for q in range(width // LANES):
                ab_ref[:, q * LANES : (q + 1) * LANES] = consts[0].astype(BF16)
        loglik = run_forward(lead, mat, hist, sel_ref, consts, ab_ref, None, None, None)
        ll_ref[...] += jnp.broadcast_to(loglik, ll_ref.shape)
        state_out[...] = ab_ref[...]

    @pl.when(forward_first == 0)
    def _():
        if resume:
            back_ref[...] = state_in[...].astype(F32)
        else:
            back_ref[...] = jnp.ones_like(back_ref)
        run_backward(lead, mat, hist, sel_ref, consts, back_ref, ab_ref, None, None, None)
        state_out[...] = back_ref[...].astype(BF16)


def second_kernel(
    extend, chunks, ids_ref, sel_ref, mat, consts, hist, state_in, row_probs, ll_in, mine_ref, other_ref, ll_ref, *refs
):
    ab_ref, back_ref, weights_ref, counts_ref = refs[-4:]
    core, forward_first, row_begin, lead = ids_ref[0], ids_ref[1], ids_ref[2], ids_ref[3]
    chunk = pl.program_id(0) if chunks > 1 else 0
    steps, rows, half = mine_ref.shape
    states = hist.shape[1]
    periods = sel_ref.shape[0] - 3

    @pl.when(chunk == 0)
    def _():
        counts_ref[...] = jnp.zeros_like(counts_ref)
        ll_ref[...] = ll_in[...]

    @pl.when(forward_first == 0)
    def _():
        ab_ref[...] = state_in[...]
        loglik = run_forward(lead, mat, hist, sel_ref, consts, ab_ref, weights_ref, counts_ref, row_begin)
        ll_ref[...] += jnp.broadcast_to(loglik, ll_ref.shape)
        if extend:
            refs[0][...] = ab_ref[...]

    @pl.when(forward_first == 1)
    def _():
        back_ref[...] = state_in[...].astype(F32)
        run_backward(
            lead, mat, hist, sel_ref, consts, back_ref, ab_ref, weights_ref, counts_ref, row_begin
        )
        if extend:
            refs[0][...] = back_ref[...].astype(BF16)

    @pl.when(chunk == chunks - 1)
    def _():
        years = sel_ref[periods + 2, :1, :LANES]
        factor = float(states * states * periods) / years
        ll_ref[...] = ll_ref[...] / years
        for k in range(steps):
            probs = row_probs[k]
            weighted = probs * counts_ref[k]
            grad = weighted - probs * jnp.sum(weighted, axis=1, keepdims=True)
            for side in range(2):
                piece = grad[:, side * half : (side + 1) * half] * factor[:, :half]

                @pl.when(core == side)
                def _():
                    mine_ref[k] = piece

                @pl.when(core != side)
                def _():
                    other_ref[k] = piece


def per_device(
    earnings, starts, lengths, block_count, trans_logits, init_logits, state_mean, log_sd
):
    slot_rows, periods = earnings.shape
    states = init_logits.shape[0]
    group = lax.axis_size(("hh", "per"))
    sides = lax.axis_size("per")
    cores = lax.axis_size("st")
    part = trans_logits.shape[0]
    steps = part * cores
    rows = states // lax.axis_size("hh")
    half = states // cores
    households = group * HB // cores
    width = min(4 * HB, households)
    chunks = households // width
    direct = group <= 8
    me = lax.axis_index(("hh", "per"))
    side = lax.axis_index("per")
    core = lax.axis_index("st")
    forward_first = (2 * side < sides).astype(jnp.int32)
    ids = jnp.stack(
        [core, forward_first, lax.axis_index("hh") * rows, side * steps, me, jnp.int32(cores)]
    ).astype(jnp.int32)

    packed = pl.pallas_call(
        pack_kernel,
        out_shape=jax.ShapeDtypeStruct((periods + 8, slot_rows), F32),
        in_specs=[smem(), vmem(), vmem(), vmem()],
        out_specs=vmem(),
        name="pack",
    )(block_count, earnings.T, starts.reshape(1, slot_rows), lengths.reshape(1, slot_rows))
    swap = [(0, 1), (1, 0)]
    other_logits = lax.ppermute(trans_logits, "st", swap)
    if direct:
        gathered = [packed] + [
            lax.ppermute(packed, ("hh", "per"), [(i, (i + r) % group) for i in range(group)])
            for r in range(1, group)
        ]
    else:
        gathered = [lax.all_gather(packed, ("hh", "per"), axis=0)]

    shaped = jax.ShapeDtypeStruct
    first_mat, second_mat, row_probs, consts = pl.pallas_call(
        prep_kernel,
        out_shape=[
            shaped((steps, 2 * states, states), BF16),
            shaped((steps, 2 * states, states), BF16),
            shaped((steps, rows, states), F32),
            shaped((4, states, LANES), F32),
        ],
        in_specs=[smem()] + [vmem()] * 5,
        out_specs=[vmem()] * 4,
        scratch_shapes=[pltpu.VMEM((states, states), F32)],
        compiler_params=params(),
        name="prep",
    )(
        ids, trans_logits, other_logits,
        init_logits.reshape(1, states), state_mean.reshape(1, states), log_sd.reshape(1, states),
    )

    def whole(shape):
        if chunks == 1:
            return vmem()
        return pl.BlockSpec(shape, lambda g: (0,) * len(shape))

    def lanes(*lead):
        if chunks == 1:
            return vmem()
        return pl.BlockSpec(lead + (width,), lambda g: (0,) * len(lead) + (g,))

    hist_shape = shaped((steps, states, households), BF16)
    state_shape = shaped((states, households), BF16)
    sel_shape = shaped((periods + 3, 8, households), F32)
    ll_shape = shaped((8, LANES), F32)
    mat_spec = whole((steps, 2 * states, states))
    const_spec = whole((4, states, LANES))

    def first_pass(state_in):
        resume = state_in is not None
        scratch = [pltpu.VMEM((states, width), BF16), pltpu.VMEM((states, width), F32)]
        if direct:
            scratch.append(pltpu.VMEM((group, periods + 8, slot_rows), F32))
        return pl.pallas_call(
            functools.partial(first_kernel, direct, resume, group, chunks),
            grid=(chunks,) if chunks > 1 else (),
            out_shape=[hist_shape, state_shape, sel_shape, ll_shape],
            in_specs=[smem()]
            + [whole(x.shape) for x in gathered]
            + [mat_spec, const_spec]
            + ([lanes(states)] if resume else []),
            out_specs=[lanes(steps, states), lanes(states), lanes(periods + 3, 8), whole((8, LANES))],
            scratch_shapes=scratch,
            compiler_params=params(),
            name="first_pass",
        )(ids, *gathered, first_mat, consts, *([state_in] if resume else []))

    grad_shape = shaped((steps, rows, half), F32)

    def second_pass(state_in, hist, sel, loglik, extend):
        return pl.pallas_call(
            functools.partial(second_kernel, extend, chunks),
            grid=(chunks,) if chunks > 1 else (),
            out_shape=[grad_shape, grad_shape, ll_shape] + ([state_shape] if extend else []),
            in_specs=[
                smem(), lanes(periods + 3, 8), mat_spec, const_spec, lanes(steps, states), lanes(states),
                whole((steps, rows, states)), whole((8, LANES)),
            ],
            out_specs=[whole((steps, rows, half)), whole((steps, rows, half)), whole((8, LANES))]
            + ([lanes(states)] if extend else []),
            scratch_shapes=[
                pltpu.VMEM((states, width), BF16),
                pltpu.VMEM((states, width), F32),
                pltpu.VMEM((rows, width), BF16),
                pltpu.VMEM((steps, rows, states), F32),
            ],
            compiler_params=params(),
            name="second_pass",
        )(ids, sel, second_mat, consts, hist, state_in, row_probs, loglik)

    def hand_over(state, stage):
        moves = [(stage, stage + 1), (sides - 1 - stage, sides - 2 - stage)]
        return lax.ppermute(state, "per", moves)

    if sides == 2:
        hist, state, sel, loglik = first_pass(None)
        mine, other, loglik = second_pass(hand_over(state, 0), hist, sel, loglik, False)
    else:
        kept = [jnp.zeros(x.shape, x.dtype) for x in (hist_shape, state_shape, sel_shape, ll_shape)]
        done = [jnp.zeros(x.shape, x.dtype) for x in (grad_shape, grad_shape, ll_shape, state_shape)]
        state = None
        for stage in range(sides):
            active = (side == stage) | (side == sides - 1 - stage)
            if stage < sides // 2:
                kept = lax.cond(active, lambda x, kept: list(first_pass(x)), lambda x, kept: kept, state, kept)
                state = kept[1]
            else:
                done = lax.cond(
                    active,
                    lambda x, done: list(second_pass(x, kept[0], kept[2], kept[3], True)),
                    lambda x, done: done,
                    state,
                    done,
                )
                state = done[3]
            if stage < sides - 1:
                state = hand_over(state, stage)
        mine, other, loglik, _ = done
    received = lax.ppermute(other, "st", swap)
    trans_grad = mine + received
    if sides == 2:
        pairs = [(i, j) for i in range(sides) for j in range(cores)]
        total = loglik
        for flip in range(1, 4):
            moves = [(n, n ^ flip) for n in range(len(pairs))]
            total = total + lax.ppermute(loglik, ("per", "st"), moves)
    else:
        total = lax.psum(loglik, ("per", "st"))
    return (trans_grad, total[0, :1])


def solution(mesh):
    placed = (
        P(("hh", "per"), None),
        P(("hh", "per")),
        P(("hh", "per")),
        P(("hh", "per")),
        P(("grp", "per", "st"), None, None),
        P("grp"),
        P("grp"),
        P("grp"),
    )
    return jax.shard_map(
        per_device,
        mesh=mesh,
        in_specs=placed,
        out_specs=(P(("grp", "per"), "hh", "st"), P("grp")),
        check_vma=False,
    )
```

```python
import functools

import jax
import jax.numpy as jnp
from jax import lax
from jax.experimental import pallas as pl
from jax.experimental.pallas import tpu as pltpu
from jax.sharding import PartitionSpec as P

HB = 128
LANES = 128
HALF = HB // 2
SEEN = 16.0
F32 = jnp.float32
BF16 = jnp.bfloat16
LOG2E = 1.4426950408889634
LN2 = 0.6931471805599453
VMEM_LIMIT = 40 * 1024 * 1024
EXTRA = 16


def vmem():
    return pl.BlockSpec(memory_space=pltpu.VMEM)


def smem():
    return pl.BlockSpec(memory_space=pltpu.SMEM)


def anywhere():
    return pl.BlockSpec(memory_space=pl.ANY)


def params():
    return pltpu.CompilerParams(vmem_limit_bytes=VMEM_LIMIT)


def tiles(width):
    return [slice(q, q + LANES) for q in range(0, width, LANES)]


def pack_kernel(ids_ref, count_ref, earn_any, start_any, len_any, out_ref, earn_ref, start_ref, len_ref, sems):
    copies = [
        pltpu.make_async_copy(src, dst, sems.at[i])
        for i, (src, dst) in enumerate(((earn_any, earn_ref), (start_any, start_ref), (len_any, len_ref)))
    ]
    for copy in copies:
        copy.start()
    for copy in copies:
        copy.wait()
    periods, slot_rows = earn_ref.shape
    core = ids_ref[0]
    low_lane = lax.broadcasted_iota(jnp.int32, (periods // 2, HB), 1) < HALF
    time = lax.broadcasted_iota(jnp.int32, (periods, HB), 0)
    for slot in range(slot_rows // HB):
        cols = slice(slot * HB, (slot + 1) * HB)
        begin = start_ref[slot : slot + 1, :]
        seen = (time >= begin) & (time < begin + len_ref[slot : slot + 1, :])
        live = slot < count_ref[0]
        shift = jnp.where(live, jnp.where(seen, SEEN, 0.0), -SEEN)
        value = earn_ref[:, cols] + shift
        early, late = value[: periods // 2], value[periods // 2 :]
        turned = pltpu.roll(jnp.where(core == 0, late, early), HALF, 1)
        packed = jnp.where(low_lane, jnp.where(core == 0, early, turned), jnp.where(core == 0, turned, late))
        for to in range(out_ref.shape[0]):
            out_ref[to, :, cols] = packed


def prep_kernel(
    ids_ref, own_any, other_ref, init_any, mean_any, sd_any,
    first_mat, second_mat, row_probs, consts, scratch, own_ref, init_ref, mean_ref, sd_ref, sems,
):
    pairs = ((own_any, own_ref), (init_any, init_ref), (mean_any, mean_ref), (sd_any, sd_ref))
    copies = [pltpu.make_async_copy(src, dst, sems.at[i]) for i, (src, dst) in enumerate(pairs)]
    for copy in copies:
        copy.start()
    for copy in copies:
        copy.wait()
    core, forward_first, row_begin = ids_ref[0], ids_ref[1], ids_ref[2]
    part, states, _ = own_ref.shape
    rows = row_probs.shape[1]

    def column(row):
        return jnp.broadcast_to(row, (LANES, states)).T

    raised = jnp.exp(init_ref[...])
    start = raised / jnp.sum(raised, axis=1, keepdims=True)
    consts[0] = column(start)
    consts[1] = column(mean_ref[...])
    consts[2] = column((-0.5 * LOG2E) * jnp.exp(-2.0 * sd_ref[...]))
    consts[3] = column(-LOG2E * sd_ref[...])
    start_high = start.astype(BF16).astype(F32)
    row = lax.broadcasted_iota(jnp.int32, (EXTRA, states), 0)
    start_rows = jnp.where(row == 0, start_high, jnp.where(row == 1, start - start_high, 0.0)).astype(BF16)

    def put(ref, at, value):
        high = value.astype(BF16)
        ref[at, :states, :] = high
        ref[at, states : 2 * states, :] = (value - high.astype(F32)).astype(BF16)

    for source, ref in ((core, own_ref), (1 - core, other_ref)):

        @pl.loop(0, part)
        def _(i):
            at = source * part + i
            lifted = jnp.exp(ref[i].astype(F32))
            probs = lifted / jnp.sum(lifted, axis=1, keepdims=True)
            scratch[...] = probs
            row_probs[at] = scratch[pl.ds(pl.multiple_of(row_begin, rows), rows), :]
            turned = probs.T
            first_mat[at, 2 * states :, :] = start_rows

            @pl.when(forward_first == 1)
            def _():
                put(first_mat, at, turned)
                put(second_mat, at, probs)

            @pl.when(forward_first == 0)
            def _():
                put(first_mat, at, probs)
                put(second_mat, at, turned)


def emission(sel_ref, consts, step_now, cols):
    gap = sel_ref[0, step_now, :1, cols] - consts[1]
    power = gap * gap * consts[2] + consts[3]
    top = jnp.max(power, axis=0, keepdims=True)
    return jnp.exp2(power - top), top


def is_moving(sel_ref, step_now, cols):
    return sel_ref[1, step_now, :1, cols] > 0.5


def is_seen(sel_ref, step_now, cols):
    return sel_ref[2, step_now, :1, cols] > 0.5


def column_sum(x):
    return jnp.sum(x, axis=0, keepdims=True)


def own_rows(row_begin, rows):
    return pl.ds(pl.multiple_of(row_begin, rows), rows)


def outer_sum(weights_ref, carried):
    return lax.dot_general(weights_ref[...], carried, (((1,), (1,)), ((), ())), preferred_element_type=F32)


def run_forward(lead, mat, hist, sel_ref, consts, ab_ref, logs, second=None):
    steps, states, width = hist.shape
    cuts = tiles(width)
    inverse = [1.0 / column_sum(ab_ref[:, cols].astype(F32)) for cols in cuts]
    for k in range(steps):
        step_now = lead + k
        if second is None:
            hist[k] = ab_ref[...]
        else:
            weights_ref, counts_ref, row_begin = second
            own_alpha = ab_ref[own_rows(row_begin, weights_ref.shape[0]), :].astype(F32)
        product = jnp.dot(mat[k, : 2 * states, :], ab_ref[...], preferred_element_type=F32)
        for q, cols in enumerate(cuts):
            moved = (product[:states, cols] + product[states:, cols]) * inverse[q]
            moving = is_moving(sel_ref, step_now, cols)
            if second is not None:
                total = column_sum(moved * hist[k, :, cols].astype(F32))
                weight = jnp.where(moving, inverse[q] / total, 0.0)
                weights_ref[:, cols] = (own_alpha[:, cols] * weight).astype(BF16)
            emit, top = emission(sel_ref, consts, step_now, cols)
            joint = jnp.where(moving, moved, consts[0]) * emit
            scale = column_sum(joint)
            if second is None:
                seen = is_seen(sel_ref, step_now, cols)
                logs[q] = logs[q] + jnp.where(seen, jnp.log(scale) + top * LN2, 0.0)
            inverse[q] = 1.0 / scale
            ab_ref[:, cols] = joint.astype(BF16)
        if second is not None:
            counts_ref[k] += outer_sum(weights_ref, hist[k])
    return logs


def run_backward(lead, mat, hist, sel_ref, consts, back_ref, ub_ref, logs, second=None):
    steps, states, width = hist.shape
    cuts = tiles(width)
    for k in reversed(range(steps)):
        step_now = lead + k
        shrink = []
        for q, cols in enumerate(cuts):
            emit, top = emission(sel_ref, consts, step_now, cols)
            carried = emit * back_ref[:, cols]
            size = column_sum(carried)
            if second is None:
                seen = is_seen(sel_ref, step_now, cols)
                logs[q] = logs[q] + jnp.where(seen, jnp.log(size) + top * LN2, 0.0)
            shrink.append(1.0 / size)
            ub_ref[:, cols] = carried.astype(BF16)
        if second is None:
            hist[k] = ub_ref[...]
        else:
            weights_ref, counts_ref, row_begin = second
            own_alpha = hist[k, own_rows(row_begin, weights_ref.shape[0]), :].astype(F32)
        product = jnp.dot(mat[k], ub_ref[...], preferred_element_type=F32)
        for q, cols in enumerate(cuts):
            moving = is_moving(sel_ref, step_now, cols)
            pulled = (product[:states, cols] + product[states : 2 * states, cols]) * shrink[q]
            if second is None:
                seen = is_seen(sel_ref, step_now, cols)
                begun = column_sum(product[2 * states :, cols]) * shrink[q]
                rest = jnp.where(seen, begun, back_ref[:, cols])
            else:
                total = column_sum(pulled * hist[k, :, cols].astype(F32))
                weight = jnp.where(moving, shrink[q] / total, 0.0)
                weights_ref[:, cols] = (own_alpha[:, cols] * weight).astype(BF16)
                rest = 1.0
            back_ref[:, cols] = jnp.where(moving, pulled, rest)
        if second is not None:
            counts_ref[k] += outer_sum(weights_ref, ub_ref[...])
    return logs


def put_state(state_out, values, logs):
    states = state_out.shape[0] - EXTRA
    state_out[:states, :] = values
    for q, cols in enumerate(tiles(state_out.shape[1])):
        high = logs[q].astype(BF16).astype(F32)
        middle = (logs[q] - high).astype(BF16).astype(F32)
        row = lax.broadcasted_iota(jnp.int32, (EXTRA, LANES), 0)
        piece = jnp.where(
            row == 0, high, jnp.where(row == 1, middle, jnp.where(row == 2, logs[q] - high - middle, 0.0))
        )
        state_out[states:, cols] = piece.astype(BF16)


def state_logs(state_ref):
    states = state_ref.shape[0] - EXTRA
    return [column_sum(state_ref[states:, cols].astype(F32)) for cols in tiles(state_ref.shape[1])]


def first_kernel(resume, grids, part, ids_ref, rows_ref, mat, consts, *refs):
    state_in = refs[0] if resume else None
    hist, state_out, sel_ref, ab_ref, back_ref = refs[-5:]
    forward_first, lead = ids_ref[1], ids_ref[3]
    chunk = part * grids + (pl.program_id(0) if grids > 1 else 0)
    steps, states, width = hist.shape
    cuts = tiles(width)
    group, half_periods, slot_rows = rows_ref.shape
    tops = 2 * len(cuts)

    def scan_source(d, carry):
        rank, picked = carry
        for slot in range(slot_rows // HB):
            block = rows_ref[d, :, slot * HB : (slot + 1) * HB]
            live = block > -0.5 * SEEN
            picked = [jnp.where(live & (rank == chunk * tops + i), block, old) for i, old in enumerate(picked)]
            rank = rank + live.astype(jnp.int32)
        return rank, picked

    carry = (jnp.zeros((half_periods, HB), jnp.int32), [jnp.zeros((half_periods, HB), F32)] * tops)
    if group <= 8:
        for d in range(group):
            carry = scan_source(d, carry)
    else:
        carry = lax.fori_loop(0, group, scan_source, carry)
    low_lane = lax.broadcasted_iota(jnp.int32, (half_periods, HB), 1) < HALF
    for q, cols in enumerate(cuts):
        left, right = carry[1][2 * q], carry[1][2 * q + 1]
        before = jnp.zeros((1, HB), F32)
        for late in range(2):
            value = (
                jnp.where(low_lane, pltpu.roll(left, HALF, 1), right)
                if late
                else jnp.where(low_lane, left, pltpu.roll(right, HALF, 1))
            )
            seen = value > 0.5 * SEEN
            earn = jnp.where(seen, value - SEEN, value)
            seen = seen.astype(F32)
            for i in range(half_periods):
                at = late * half_periods + i
                now = seen[i : i + 1]
                sel_ref[0, at, :, cols] = jnp.broadcast_to(earn[i : i + 1], (8, HB))
                sel_ref[1, at, :, cols] = jnp.broadcast_to(now * before, (8, HB))
                sel_ref[2, at, :, cols] = jnp.broadcast_to(now, (8, HB))
                before = now
    zeros = [jnp.zeros((1, LANES), F32) for _ in cuts]

    @pl.when(forward_first == 1)
    def _():
        if resume:
            ab_ref[...] = state_in[:states, :]
        else:
            for cols in cuts:
                ab_ref[:, cols] = consts[0].astype(BF16)
        logs = state_logs(state_in) if resume else list(zeros)
        logs = run_forward(lead, mat, hist, sel_ref, consts, ab_ref, logs)
        put_state(state_out, ab_ref[...], logs)

    @pl.when(forward_first == 0)
    def _():
        if resume:
            back_ref[...] = state_in[:states, :].astype(F32)
        else:
            back_ref[...] = jnp.ones_like(back_ref)
        logs = state_logs(state_in) if resume else list(zeros)
        logs = run_backward(lead, mat, hist, sel_ref, consts, back_ref, ab_ref, logs)
        put_state(state_out, back_ref[...].astype(BF16), logs)


def second_kernel(resume, last, extend, grids, *refs):
    refs = list(refs)
    ids_ref, sel_ref, mat, consts, hist, own_state, state_in = (refs.pop(0) for _ in range(7))
    counts_in, sums_in = (refs.pop(0), refs.pop(0)) if resume else (None, None)
    row_probs = refs.pop(0) if last else None
    mine_ref, other_ref = (refs.pop(0), refs.pop(0)) if last else (None, None)
    counts_out, sums_out = (None, None) if last else (refs.pop(0), refs.pop(0))
    state_out = refs.pop(0) if extend else None
    ab_ref, back_ref, weights_ref = refs[:3]
    counts_ref, sums_ref = refs[3:] if last else (counts_out, sums_out)
    core, forward_first, row_begin, lead = ids_ref[0], ids_ref[1], ids_ref[2], ids_ref[3]
    chunk = pl.program_id(0) if grids > 1 else 0
    steps, states, width = hist.shape
    second = (weights_ref, counts_ref, row_begin)

    @pl.when(chunk == 0)
    def _():
        if resume:
            counts_ref[...] = counts_in[...]
            sums_ref[...] = sums_in[...]
        else:
            counts_ref[...] = jnp.zeros_like(counts_ref)
            sums_ref[...] = jnp.zeros_like(sums_ref)

    def add_sums(alpha_ref, other_state):
        total = jnp.zeros((1, LANES), F32)
        years = jnp.zeros((8, LANES), F32)
        for cols, here, there in zip(tiles(width), state_logs(alpha_ref), state_logs(other_state)):
            alpha = alpha_ref[:states, cols].astype(F32)
            meet = column_sum(alpha * other_state[:states, cols].astype(F32))
            total += here + there + jnp.log(meet / column_sum(alpha))
            years += jnp.sum(sel_ref[2, :, :, cols], axis=0)
        total = jnp.broadcast_to(jnp.sum(total, axis=1, keepdims=True), (1, LANES))
        years = jnp.broadcast_to(jnp.sum(years[:1], axis=1, keepdims=True), (1, LANES))
        row = lax.broadcasted_iota(jnp.int32, (8, LANES), 0)
        sums_ref[...] += jnp.where(row == 0, total, jnp.where(row == 1, years, 0.0))

    zeros = [jnp.zeros((1, LANES), F32) for _ in tiles(width)]

    @pl.when(forward_first == 0)
    def _():
        add_sums(state_in, own_state)
        ab_ref[...] = state_in[:states, :]
        run_forward(lead, mat, hist, sel_ref, consts, ab_ref, list(zeros), second)
        if extend:
            put_state(state_out, ab_ref[...], zeros)

    @pl.when(forward_first == 1)
    def _():
        add_sums(own_state, state_in)
        back_ref[...] = state_in[:states, :].astype(F32)
        run_backward(lead, mat, hist, sel_ref, consts, back_ref, ab_ref, list(zeros), second)
        if extend:
            put_state(state_out, back_ref[...].astype(BF16), zeros)

    if last:

        @pl.when(chunk == grids - 1)
        def _():
            rows = counts_ref.shape[1]
            for k in range(steps):
                probs = row_probs[k]
                weighted = probs * counts_ref[k]
                grad = weighted - probs * jnp.sum(weighted, axis=1, keepdims=True)
                for side in range(2):
                    piece = grad[:, side * LANES : (side + 1) * LANES]
                    at = slice(k * rows, (k + 1) * rows)

                    @pl.when(core == side)
                    def _():
                        mine_ref[at, :] = piece

                    @pl.when(core != side)
                    def _():
                        other_ref[at, :] = piece

            mine_ref[steps * rows :, :] = sums_ref[...]
            other_ref[steps * rows :, :] = sums_ref[...]


def finish_kernel(scale, mine_ref, other_ref, grad_ref, mean_ref):
    count = grad_ref.shape[0]
    total = mine_ref[count : count + 1, :] + other_ref[count : count + 1, :]
    years = mine_ref[count + 1 : count + 2, :] + other_ref[count + 1 : count + 2, :]
    grad_ref[...] = (mine_ref[:count, :] + other_ref[:count, :]) * (scale / years)
    mean_ref[0] = (total / years)[0, 0]


def per_device(
    earnings, starts, lengths, block_count, trans_logits, init_logits, state_mean, log_sd
):
    slot_rows, periods = earnings.shape
    states = init_logits.shape[0]
    group = lax.axis_size(("hh", "per"))
    sides = lax.axis_size("per")
    cores = lax.axis_size("st")
    part = trans_logits.shape[0]
    steps = part * cores
    rows = states // lax.axis_size("hh")
    households = group * HB // cores
    parts = 2 if households <= 4 * HB else 1
    share = households // parts
    width = min(2 * HB, share)
    grids = share // width
    side = lax.axis_index("per")
    core = lax.axis_index("st")
    forward_first = (2 * side < sides).astype(jnp.int32)
    ids = jnp.stack([core, forward_first, lax.axis_index("hh") * rows, side * steps]).astype(jnp.int32)
    shaped = jax.ShapeDtypeStruct
    dma = pltpu.SemaphoreType.DMA

    swap = [(0, 1), (1, 0)]
    other_logits = lax.ppermute(trans_logits, "st", swap)
    packed = pl.pallas_call(
        pack_kernel,
        out_shape=shaped((group, periods // 2, slot_rows), F32),
        in_specs=[smem(), smem(), anywhere(), anywhere(), anywhere()],
        out_specs=vmem(),
        scratch_shapes=[
            pltpu.VMEM((periods, slot_rows), F32),
            pltpu.VMEM((slot_rows // HB, HB), jnp.int32),
            pltpu.VMEM((slot_rows // HB, HB), jnp.int32),
            dma((3,)),
        ],
        name="pack",
    )(ids, block_count, earnings.T, starts.reshape(-1, HB), lengths.reshape(-1, HB))
    gathered = lax.all_to_all(packed, ("hh", "per"), split_axis=0, concat_axis=0, tiled=True)

    first_mat, second_mat, row_probs, consts = pl.pallas_call(
        prep_kernel,
        out_shape=[
            shaped((steps, 2 * states + EXTRA, states), BF16),
            shaped((steps, 2 * states, states), BF16),
            shaped((steps, rows, states), F32),
            shaped((4, states, LANES), F32),
        ],
        in_specs=[smem(), anywhere(), vmem(), anywhere(), anywhere(), anywhere()],
        out_specs=[vmem()] * 4,
        scratch_shapes=[
            pltpu.VMEM((states, states), F32),
            pltpu.VMEM(trans_logits.shape, BF16),
            pltpu.VMEM((1, states), F32),
            pltpu.VMEM((1, states), F32),
            pltpu.VMEM((1, states), F32),
            dma((4,)),
        ],
        compiler_params=params(),
        name="prep",
    )(
        ids, trans_logits, other_logits,
        init_logits.reshape(1, states), state_mean.reshape(1, states), log_sd.reshape(1, states),
    )

    def whole(*shape):
        if grids == 1:
            return vmem()
        return pl.BlockSpec(shape, lambda g: (0,) * len(shape))

    def lanes(*lead):
        if grids == 1:
            return vmem()
        return pl.BlockSpec(lead + (width,), lambda g: (0,) * len(lead) + (g,))

    grid = (grids,) if grids > 1 else ()
    hist_shape = shaped((steps, states, share), BF16)
    state_shape = shaped((states + EXTRA, share), BF16)
    sel_shape = shaped((3, periods, 8, share), F32)
    swap_shape = shaped((steps * rows + 8, LANES), F32)
    counts_shape = shaped((steps, rows, states), F32)
    sums_shape = shaped((8, LANES), F32)
    hist_spec, state_spec, sel_spec = lanes(steps, states), lanes(states + EXTRA), lanes(3, periods, 8)
    const_spec = whole(4, states, LANES)

    def first_pass(index, state_in):
        resume = state_in is not None
        return pl.pallas_call(
            functools.partial(first_kernel, resume, grids, index),
            grid=grid,
            out_shape=[hist_shape, state_shape, sel_shape],
            in_specs=[smem(), whole(*gathered.shape), whole(*first_mat.shape), const_spec]
            + [state_spec] * resume,
            out_specs=[hist_spec, state_spec, sel_spec],
            scratch_shapes=[pltpu.VMEM((states, width), BF16), pltpu.VMEM((states, width), F32)],
            compiler_params=params(),
            name="first_pass",
        )(ids, gathered, first_mat, consts, *([state_in] if resume else []))

    def second_pass(kept, state_in, sums_in, last, extend):
        hist, own_state, sel = kept
        resume = sums_in is not None
        scratch = [
            pltpu.VMEM((states, width), BF16),
            pltpu.VMEM((states, width), F32),
            pltpu.VMEM((rows, width), BF16),
        ]
        counts_spec, sums_spec = whole(*counts_shape.shape), whole(*sums_shape.shape)
        if last:
            out_shape = [swap_shape] * 2
            scratch += [pltpu.VMEM(counts_shape.shape, F32), pltpu.VMEM(sums_shape.shape, F32)]
        else:
            out_shape = [counts_shape, sums_shape]
        out_specs = [whole(*x.shape) for x in out_shape]
        if extend:
            out_shape, out_specs = out_shape + [state_shape], out_specs + [state_spec]
        return pl.pallas_call(
            functools.partial(second_kernel, resume, last, extend, grids),
            grid=grid,
            out_shape=out_shape,
            in_specs=[smem(), sel_spec, whole(*second_mat.shape), const_spec, hist_spec, state_spec, state_spec]
            + [counts_spec, sums_spec] * resume
            + [whole(*row_probs.shape)] * last,
            out_specs=out_specs,
            scratch_shapes=scratch,
            compiler_params=params(),
            name="second_pass",
        )(
            ids, sel, second_mat, consts, hist, own_state, state_in,
            *(sums_in if resume else []),
            *([row_probs] if last else []),
        )

    def hand_over(state, stage):
        moves = [(stage, stage + 1), (sides - 1 - stage, sides - 2 - stage)]
        return lax.ppermute(state, "per", moves)

    if sides == 2:
        kept = [first_pass(index, None) for index in range(parts)]
        arrived = [hand_over(each[1], 0) for each in kept]
        sums = None
        for index in range(parts):
            sums = second_pass(kept[index], arrived[index], sums, index == parts - 1, False)
        mine, other = sums
    else:
        kept = [jnp.zeros(x.shape, x.dtype) for x in (hist_shape, state_shape, sel_shape)]
        done = [jnp.zeros(x.shape, x.dtype) for x in (swap_shape, swap_shape, state_shape)]
        state = None
        for stage in range(sides):
            active = (side == stage) | (side == sides - 1 - stage)
            if stage < sides // 2:
                kept = lax.cond(
                    active, lambda x, kept: list(first_pass(0, x)), lambda x, kept: kept, state, kept
                )
                state = kept[1]
            else:
                done = lax.cond(
                    active,
                    lambda x, done: list(second_pass(kept, x, None, True, True)),
                    lambda x, done: done,
                    state,
                    done,
                )
                state = done[2]
            if stage < sides - 1:
                state = hand_over(state, stage)
        mine, other, _ = done
        total = jnp.where(side == sides // 2, mine[steps * rows], 0.0)
        total = lax.psum(total, "per")
        mine = mine.at[steps * rows].set(total)
        other = other.at[steps * rows].set(total)
    received = lax.ppermute(other, "st", swap)
    trans_grad, mean_loglik = pl.pallas_call(
        functools.partial(finish_kernel, float(states * states * periods)),
        out_shape=[shaped((steps * rows, LANES), F32), shaped((1,), F32)],
        in_specs=[vmem(), vmem()],
        out_specs=[vmem(), smem()],
        name="finish",
    )(mine, received)
    return (trans_grad.reshape(steps, rows, LANES), mean_loglik)


def solution(mesh):
    placed = (
        P(("hh", "per"), None),
        P(("hh", "per")),
        P(("hh", "per")),
        P(("hh", "per")),
        P(("grp", "per", "st"), None, None),
        P("grp"),
        P("grp"),
        P("grp"),
    )
    return jax.shard_map(
        per_device,
        mesh=mesh,
        in_specs=placed,
        out_specs=(P(("grp", "per"), "hh", "st"), P("grp")),
        check_vma=False,
    )
```

```python
import functools

import jax
import jax.numpy as jnp
from jax import lax
from jax.experimental import pallas as pl
from jax.experimental.pallas import tpu as pltpu
from jax.sharding import PartitionSpec as P

HB = 128
LANES = 128
HALF = HB // 2
SEEN = 16.0
F32 = jnp.float32
BF16 = jnp.bfloat16
LOG2E = 1.4426950408889634
LN2 = 0.6931471805599453
EXTRA = 16


def vmem():
    return pl.BlockSpec(memory_space=pltpu.VMEM)


def smem():
    return pl.BlockSpec(memory_space=pltpu.SMEM)


def hbm():
    return pl.BlockSpec(memory_space=pltpu.HBM)


def params(mebibytes):
    return pltpu.CompilerParams(vmem_limit_bytes=mebibytes * 1024 * 1024)


def core_index():
    return lax.axis_index("st")


def is_forward_first():
    return 2 * lax.axis_index("per") < lax.axis_size("per")


def tiles(width):
    return [slice(q, q + LANES) for q in range(0, width, LANES)]


def pack_kernel(count_ref, earn_any, start_any, len_any, out_ref, earn_ref, start_ref, len_ref, sems):
    copies = [
        pltpu.make_async_copy(src, dst, sems.at[i])
        for i, (src, dst) in enumerate(((earn_any, earn_ref), (start_any, start_ref), (len_any, len_ref)))
    ]
    for copy in copies:
        copy.start()
    for copy in copies:
        copy.wait()
    periods, slot_rows = earn_ref.shape
    core = core_index()
    low_lane = lax.broadcasted_iota(jnp.int32, (periods // 2, HB), 1) < HALF
    time = lax.broadcasted_iota(jnp.int32, (periods, HB), 0)
    for slot in range(slot_rows // HB):
        cols = slice(slot * HB, (slot + 1) * HB)
        begin = start_ref[slot : slot + 1, :]
        seen = (time >= begin) & (time < begin + len_ref[slot : slot + 1, :])
        live = slot < count_ref[0]
        shift = jnp.where(live, jnp.where(seen, SEEN, 0.0), -SEEN)
        value = earn_ref[:, cols] + shift
        early, late = value[: periods // 2], value[periods // 2 :]
        turned = pltpu.roll(jnp.where(core == 0, late, early), HALF, 1)
        packed = jnp.where(low_lane, jnp.where(core == 0, early, turned), jnp.where(core == 0, turned, late))
        for to in range(out_ref.shape[0]):
            out_ref[to, :, cols] = packed


def prep_kernel(
    own_any, other_ref, init_any, mean_any, sd_any,
    first_mat, second_mat, row_probs, consts, scratch, own_ref, init_ref, mean_ref, sd_ref, sems,
):
    pairs = ((own_any, own_ref), (init_any, init_ref), (mean_any, mean_ref), (sd_any, sd_ref))
    copies = [pltpu.make_async_copy(src, dst, sems.at[i]) for i, (src, dst) in enumerate(pairs)]
    for copy in copies:
        copy.start()
    for copy in copies:
        copy.wait()
    part, states, _ = own_ref.shape
    rows = row_probs.shape[1]
    core, forward_first, row_begin = core_index(), is_forward_first(), lax.axis_index("hh") * rows

    def column(row):
        return jnp.broadcast_to(row, (LANES, states)).T

    raised = jnp.exp(init_ref[...])
    start = raised / jnp.sum(raised, axis=1, keepdims=True)
    consts[0] = column(start)
    consts[1] = column(mean_ref[...])
    consts[2] = column((-0.5 * LOG2E) * jnp.exp(-2.0 * sd_ref[...]))
    consts[3] = column(-LOG2E * sd_ref[...])
    start_high = start.astype(BF16).astype(F32)
    row = lax.broadcasted_iota(jnp.int32, (EXTRA, states), 0)
    start_rows = jnp.where(row == 0, start_high, jnp.where(row == 1, start - start_high, 0.0)).astype(BF16)

    def put(ref, at, value):
        high = value.astype(BF16)
        ref[at, :states, :] = high
        ref[at, states : 2 * states, :] = (value - high.astype(F32)).astype(BF16)

    for source, ref in ((core, own_ref), (1 - core, other_ref)):

        @pl.loop(0, part)
        def _(i):
            at = source * part + i
            lifted = jnp.exp(ref[i].astype(F32))
            probs = lifted / jnp.sum(lifted, axis=1, keepdims=True)
            scratch[...] = probs
            row_probs[at] = scratch[pl.ds(pl.multiple_of(row_begin, rows), rows), :]
            turned = probs.T
            first_mat[at, 2 * states :, :] = start_rows

            @pl.when(forward_first)
            def _():
                put(first_mat, at, turned)
                put(second_mat, at, probs)

            @pl.when(jnp.logical_not(forward_first))
            def _():
                put(first_mat, at, probs)
                put(second_mat, at, turned)


def emission(sel_ref, consts, step_now, cols):
    gap = sel_ref[0, step_now, :1, cols] - consts[1]
    power = gap * gap * consts[2] + consts[3]
    top = jnp.max(power, axis=0, keepdims=True)
    return jnp.exp2(power - top), top


def is_moving(sel_ref, step_now, cols):
    return sel_ref[1, step_now, :1, cols] > 0.5


def is_seen(sel_ref, step_now, cols):
    return sel_ref[2, step_now, :1, cols] > 0.5


def column_sum(x):
    return jnp.sum(x, axis=0, keepdims=True)


def own_rows(row_begin, rows):
    return pl.ds(pl.multiple_of(row_begin, rows), rows)


def outer_sum(weights_ref, carried):
    return lax.dot_general(weights_ref[...], carried, (((1,), (1,)), ((), ())), preferred_element_type=F32)


def run_forward(lead, mat, hist, sel_ref, consts, ab_ref, logs, second=None):
    steps, states, width = hist.shape
    cuts = tiles(width)
    inverse = [1.0 / column_sum(ab_ref[:, cols].astype(F32)) for cols in cuts]
    for k in range(steps):
        step_now = lead + k
        if second is None:
            hist[k] = ab_ref[...]
        else:
            weights_ref, counts_ref, row_begin = second
            own_alpha = ab_ref[own_rows(row_begin, weights_ref.shape[0]), :].astype(F32)
        for q, cols in enumerate(cuts):
            product = jnp.dot(mat[k, : 2 * states, :], ab_ref[:, cols], preferred_element_type=F32)
            moved = (product[:states] + product[states:]) * inverse[q]
            moving = is_moving(sel_ref, step_now, cols)
            if second is not None:
                total = column_sum(moved * hist[k, :, cols].astype(F32))
                weight = jnp.where(moving, inverse[q] / total, 0.0)
                weights_ref[:, cols] = (own_alpha[:, cols] * weight).astype(BF16)
            emit, top = emission(sel_ref, consts, step_now, cols)
            joint = jnp.where(moving, moved, consts[0]) * emit
            scale = column_sum(joint)
            if second is None:
                seen = is_seen(sel_ref, step_now, cols)
                logs[q] = logs[q] + jnp.where(seen, jnp.log(scale) + top * LN2, 0.0)
            inverse[q] = 1.0 / scale
            ab_ref[:, cols] = joint.astype(BF16)
        if second is not None:
            counts_ref[k] += outer_sum(weights_ref, hist[k])
    return logs


def run_backward(lead, mat, hist, sel_ref, consts, back_ref, ub_ref, logs, second=None):
    steps, states, width = hist.shape
    cuts = tiles(width)
    for k in reversed(range(steps)):
        step_now = lead + k
        shrink = []
        for q, cols in enumerate(cuts):
            emit, top = emission(sel_ref, consts, step_now, cols)
            carried = emit * back_ref[:, cols]
            size = column_sum(carried)
            if second is None:
                seen = is_seen(sel_ref, step_now, cols)
                logs[q] = logs[q] + jnp.where(seen, jnp.log(size) + top * LN2, 0.0)
            shrink.append(1.0 / size)
            ub_ref[:, cols] = carried.astype(BF16)
        if second is None:
            hist[k] = ub_ref[...]
        else:
            weights_ref, counts_ref, row_begin = second
            own_alpha = hist[k, own_rows(row_begin, weights_ref.shape[0]), :].astype(F32)
        for q, cols in enumerate(cuts):
            product = jnp.dot(mat[k], ub_ref[:, cols], preferred_element_type=F32)
            moving = is_moving(sel_ref, step_now, cols)
            pulled = (product[:states] + product[states : 2 * states]) * shrink[q]
            if second is None:
                seen = is_seen(sel_ref, step_now, cols)
                begun = column_sum(product[2 * states :]) * shrink[q]
                rest = jnp.where(seen, begun, back_ref[:, cols])
            else:
                total = column_sum(pulled * hist[k, :, cols].astype(F32))
                weight = jnp.where(moving, shrink[q] / total, 0.0)
                weights_ref[:, cols] = (own_alpha[:, cols] * weight).astype(BF16)
                rest = 1.0
            back_ref[:, cols] = jnp.where(moving, pulled, rest)
        if second is not None:
            counts_ref[k] += outer_sum(weights_ref, ub_ref[...])
    return logs


def put_state(state_out, values, logs):
    states = state_out.shape[0] - EXTRA
    state_out[:states, :] = values
    for q, cols in enumerate(tiles(state_out.shape[1])):
        high = logs[q].astype(BF16).astype(F32)
        middle = (logs[q] - high).astype(BF16).astype(F32)
        row = lax.broadcasted_iota(jnp.int32, (EXTRA, LANES), 0)
        piece = jnp.where(
            row == 0, high, jnp.where(row == 1, middle, jnp.where(row == 2, logs[q] - high - middle, 0.0))
        )
        state_out[states:, cols] = piece.astype(BF16)


def state_logs(state_ref):
    states = state_ref.shape[0] - EXTRA
    return [column_sum(state_ref[states:, cols].astype(F32)) for cols in tiles(state_ref.shape[1])]


def first_kernel(resume, grids, part, rows_ref, mat, consts, *refs):
    state_in = refs[0] if resume else None
    hist, state_out, sel_ref, ab_ref, back_ref = refs[-5:]
    chunk = part * grids + (pl.program_id(0) if grids > 1 else 0)
    steps, states, width = hist.shape
    forward_first, lead = is_forward_first(), lax.axis_index("per") * steps
    cuts = tiles(width)
    group, half_periods, slot_rows = rows_ref.shape
    tops = 2 * len(cuts)

    def scan_source(d, carry):
        rank, picked = carry
        for slot in range(slot_rows // HB):
            block = rows_ref[d, :, slot * HB : (slot + 1) * HB]
            live = block > -0.5 * SEEN
            picked = [jnp.where(live & (rank == chunk * tops + i), block, old) for i, old in enumerate(picked)]
            rank = rank + live.astype(jnp.int32)
        return rank, picked

    carry = (jnp.zeros((half_periods, HB), jnp.int32), [jnp.zeros((half_periods, HB), F32)] * tops)
    if group <= 8:
        for d in range(group):
            carry = scan_source(d, carry)
    else:
        carry = lax.fori_loop(0, group, scan_source, carry)
    low_lane = lax.broadcasted_iota(jnp.int32, (half_periods, HB), 1) < HALF
    for q, cols in enumerate(cuts):
        left, right = carry[1][2 * q], carry[1][2 * q + 1]
        before = jnp.zeros((1, HB), F32)
        for late in range(2):
            value = (
                jnp.where(low_lane, pltpu.roll(left, HALF, 1), right)
                if late
                else jnp.where(low_lane, left, pltpu.roll(right, HALF, 1))
            )
            seen = value > 0.5 * SEEN
            earn = jnp.where(seen, value - SEEN, value)
            seen = seen.astype(F32)
            for i in range(half_periods):
                at = late * half_periods + i
                now = seen[i : i + 1]
                sel_ref[0, at, :, cols] = jnp.broadcast_to(earn[i : i + 1], (8, HB))
                sel_ref[1, at, :, cols] = jnp.broadcast_to(now * before, (8, HB))
                sel_ref[2, at, :, cols] = jnp.broadcast_to(now, (8, HB))
                before = now
    zeros = [jnp.zeros((1, LANES), F32) for _ in cuts]

    @pl.when(forward_first)
    def _():
        if resume:
            ab_ref[...] = state_in[:states, :]
        else:
            for cols in cuts:
                ab_ref[:, cols] = consts[0].astype(BF16)
        logs = state_logs(state_in) if resume else list(zeros)
        logs = run_forward(lead, mat, hist, sel_ref, consts, ab_ref, logs)
        put_state(state_out, ab_ref[...], logs)

    @pl.when(jnp.logical_not(forward_first))
    def _():
        if resume:
            back_ref[...] = state_in[:states, :].astype(F32)
        else:
            back_ref[...] = jnp.ones_like(back_ref)
        logs = state_logs(state_in) if resume else list(zeros)
        logs = run_backward(lead, mat, hist, sel_ref, consts, back_ref, ab_ref, logs)
        put_state(state_out, back_ref[...].astype(BF16), logs)


def second_kernel(resume, last, extend, grids, *refs):
    refs = list(refs)
    sel_ref, mat, consts, hist, own_state, state_in = (refs.pop(0) for _ in range(6))
    counts_in, sums_in = (refs.pop(0), refs.pop(0)) if resume else (None, None)
    row_probs = refs.pop(0) if last else None
    mine_ref, other_ref = (refs.pop(0), refs.pop(0)) if last else (None, None)
    counts_out, sums_out = (None, None) if last else (refs.pop(0), refs.pop(0))
    state_out = refs.pop(0) if extend else None
    ab_ref, back_ref, weights_ref = refs[:3]
    counts_ref, sums_ref = refs[3:] if last else (counts_out, sums_out)
    chunk = pl.program_id(0) if grids > 1 else 0
    steps, states, width = hist.shape
    core, forward_first = core_index(), is_forward_first()
    row_begin = lax.axis_index("hh") * counts_ref.shape[1]
    lead = lax.axis_index("per") * steps
    second = (weights_ref, counts_ref, row_begin)

    @pl.when(chunk == 0)
    def _():
        if resume:
            counts_ref[...] = counts_in[...]
            sums_ref[...] = sums_in[...]
        else:
            counts_ref[...] = jnp.zeros_like(counts_ref)
            sums_ref[...] = jnp.zeros_like(sums_ref)

    def add_sums(alpha_ref, other_state):
        total = jnp.zeros((1, LANES), F32)
        years = jnp.zeros((8, LANES), F32)
        for cols, here, there in zip(tiles(width), state_logs(alpha_ref), state_logs(other_state)):
            alpha = alpha_ref[:states, cols].astype(F32)
            meet = column_sum(alpha * other_state[:states, cols].astype(F32))
            total += here + there + jnp.log(meet / column_sum(alpha))
            years += jnp.sum(sel_ref[2, :, :, cols], axis=0)
        total = jnp.broadcast_to(jnp.sum(total, axis=1, keepdims=True), (1, LANES))
        years = jnp.broadcast_to(jnp.sum(years[:1], axis=1, keepdims=True), (1, LANES))
        row = lax.broadcasted_iota(jnp.int32, (8, LANES), 0)
        sums_ref[...] += jnp.where(row == 0, total, jnp.where(row == 1, years, 0.0))

    zeros = [jnp.zeros((1, LANES), F32) for _ in tiles(width)]

    @pl.when(jnp.logical_not(forward_first))
    def _():
        add_sums(state_in, own_state)
        ab_ref[...] = state_in[:states, :]
        run_forward(lead, mat, hist, sel_ref, consts, ab_ref, list(zeros), second)
        if extend:
            put_state(state_out, ab_ref[...], zeros)

    @pl.when(forward_first)
    def _():
        add_sums(own_state, state_in)
        back_ref[...] = state_in[:states, :].astype(F32)
        run_backward(lead, mat, hist, sel_ref, consts, back_ref, ab_ref, list(zeros), second)
        if extend:
            put_state(state_out, back_ref[...].astype(BF16), zeros)

    if last:

        @pl.when(chunk == grids - 1)
        def _():
            rows = counts_ref.shape[1]
            for k in range(steps):
                probs = row_probs[k]
                weighted = probs * counts_ref[k]
                grad = weighted - probs * jnp.sum(weighted, axis=1, keepdims=True)
                for side in range(2):
                    piece = grad[:, side * LANES : (side + 1) * LANES]
                    at = slice(k * rows, (k + 1) * rows)

                    @pl.when(core == side)
                    def _():
                        mine_ref[at, :] = piece

                    @pl.when(core != side)
                    def _():
                        other_ref[at, :] = piece

            mine_ref[steps * rows :, :] = sums_ref[...]
            other_ref[steps * rows :, :] = sums_ref[...]


def finish_kernel(scale, mine_ref, other_ref, grad_ref, mean_ref):
    count = grad_ref.shape[0]
    total = mine_ref[count : count + 1, :] + other_ref[count : count + 1, :]
    years = mine_ref[count + 1 : count + 2, :] + other_ref[count + 1 : count + 2, :]
    grad_ref[...] = (mine_ref[:count, :] + other_ref[:count, :]) * (scale / years)
    mean_ref[0] = (total / years)[0, 0]


def per_device(
    earnings, starts, lengths, block_count, trans_logits, init_logits, state_mean, log_sd
):
    slot_rows, periods = earnings.shape
    states = init_logits.shape[0]
    group = lax.axis_size(("hh", "per"))
    sides = lax.axis_size("per")
    cores = lax.axis_size("st")
    part = trans_logits.shape[0]
    steps = part * cores
    rows = states // lax.axis_size("hh")
    households = group * HB // cores
    parts = 2 if households <= 4 * HB else 1
    share = households // parts
    width = min(2 * HB, share)
    grids = share // width
    side = lax.axis_index("per")
    shaped = jax.ShapeDtypeStruct
    dma = pltpu.SemaphoreType.DMA

    swap = [(0, 1), (1, 0)]
    other_logits = lax.ppermute(trans_logits, "st", swap)
    packed = pl.pallas_call(
        pack_kernel,
        out_shape=shaped((group, periods // 2, slot_rows), F32),
        in_specs=[smem(), hbm(), hbm(), hbm()],
        out_specs=vmem(),
        scratch_shapes=[
            pltpu.VMEM((periods, slot_rows), F32),
            pltpu.VMEM((slot_rows // HB, HB), jnp.int32),
            pltpu.VMEM((slot_rows // HB, HB), jnp.int32),
            dma((3,)),
        ],
        compiler_params=params(4),
        name="pack",
    )(block_count, earnings.T, starts.reshape(-1, HB), lengths.reshape(-1, HB))
    gathered = lax.all_to_all(packed, ("hh", "per"), split_axis=0, concat_axis=0, tiled=True)

    first_mat, second_mat, row_probs, consts = pl.pallas_call(
        prep_kernel,
        out_shape=[
            shaped((steps, 2 * states + EXTRA, states), BF16),
            shaped((steps, 2 * states, states), BF16),
            shaped((steps, rows, states), F32),
            shaped((4, states, LANES), F32),
        ],
        in_specs=[hbm(), vmem(), hbm(), hbm(), hbm()],
        out_specs=[vmem()] * 4,
        scratch_shapes=[
            pltpu.VMEM((states, states), F32),
            pltpu.VMEM(trans_logits.shape, BF16),
            pltpu.VMEM((1, states), F32),
            pltpu.VMEM((1, states), F32),
            pltpu.VMEM((1, states), F32),
            dma((4,)),
        ],
        compiler_params=params(8),
        name="prep",
    )(
        trans_logits, other_logits,
        init_logits.reshape(1, states), state_mean.reshape(1, states), log_sd.reshape(1, states),
    )

    def whole(*shape):
        if grids == 1:
            return vmem()
        return pl.BlockSpec(shape, lambda g: (0,) * len(shape))

    def lanes(*lead):
        if grids == 1:
            return vmem()
        return pl.BlockSpec(lead + (width,), lambda g: (0,) * len(lead) + (g,))

    grid = (grids,) if grids > 1 else ()
    hist_shape = shaped((steps, states, share), BF16)
    state_shape = shaped((states + EXTRA, share), BF16)
    sel_shape = shaped((3, periods, 8, share), F32)
    swap_shape = shaped((steps * rows + 8, LANES), F32)
    counts_shape = shaped((steps, rows, states), F32)
    sums_shape = shaped((8, LANES), F32)
    hist_spec, state_spec, sel_spec = lanes(steps, states), lanes(states + EXTRA), lanes(3, periods, 8)
    const_spec = whole(4, states, LANES)

    def first_pass(index, state_in):
        resume = state_in is not None
        return pl.pallas_call(
            functools.partial(first_kernel, resume, grids, index),
            grid=grid,
            out_shape=[hist_shape, state_shape, sel_shape],
            in_specs=[whole(*gathered.shape), whole(*first_mat.shape), const_spec]
            + [state_spec] * resume,
            out_specs=[hist_spec, state_spec, sel_spec],
            scratch_shapes=[pltpu.VMEM((states, width), BF16), pltpu.VMEM((states, width), F32)],
            compiler_params=params(8 if grids == 1 else 32),
            name="first_pass",
        )(gathered, first_mat, consts, *([state_in] if resume else []))

    def second_pass(kept, state_in, sums_in, last, extend):
        hist, own_state, sel = kept
        resume = sums_in is not None
        scratch = [
            pltpu.VMEM((states, width), BF16),
            pltpu.VMEM((states, width), F32),
            pltpu.VMEM((rows, width), BF16),
        ]
        counts_spec, sums_spec = whole(*counts_shape.shape), whole(*sums_shape.shape)
        if last:
            out_shape = [swap_shape] * 2
            scratch += [pltpu.VMEM(counts_shape.shape, F32), pltpu.VMEM(sums_shape.shape, F32)]
        else:
            out_shape = [counts_shape, sums_shape]
        out_specs = [whole(*x.shape) for x in out_shape]
        if extend:
            out_shape, out_specs = out_shape + [state_shape], out_specs + [state_spec]
        return pl.pallas_call(
            functools.partial(second_kernel, resume, last, extend, grids),
            grid=grid,
            out_shape=out_shape,
            in_specs=[sel_spec, whole(*second_mat.shape), const_spec, hist_spec, state_spec, state_spec]
            + [counts_spec, sums_spec] * resume
            + [whole(*row_probs.shape)] * last,
            out_specs=out_specs,
            scratch_shapes=scratch,
            compiler_params=params(8 if grids == 1 else 32),
            name="second_pass",
        )(
            sel, second_mat, consts, hist, own_state, state_in,
            *(sums_in if resume else []),
            *([row_probs] if last else []),
        )

    def hand_over(state, stage):
        moves = [(stage, stage + 1), (sides - 1 - stage, sides - 2 - stage)]
        return lax.ppermute(state, "per", moves)

    if sides == 2:
        kept = [first_pass(index, None) for index in range(parts)]
        arrived = [hand_over(each[1], 0) for each in kept]
        sums = None
        for index in range(parts):
            sums = second_pass(kept[index], arrived[index], sums, index == parts - 1, False)
        mine, other = sums
    else:
        kept = [jnp.zeros(x.shape, x.dtype) for x in (hist_shape, state_shape, sel_shape)]
        done = [jnp.zeros(x.shape, x.dtype) for x in (swap_shape, swap_shape, state_shape)]
        state = None
        for stage in range(sides):
            active = (side == stage) | (side == sides - 1 - stage)
            if stage < sides // 2:
                kept = lax.cond(
                    active, lambda x, kept: list(first_pass(0, x)), lambda x, kept: kept, state, kept
                )
                state = kept[1]
            else:
                done = lax.cond(
                    active,
                    lambda x, done: list(second_pass(kept, x, None, True, True)),
                    lambda x, done: done,
                    state,
                    done,
                )
                state = done[2]
            if stage < sides - 1:
                state = hand_over(state, stage)
        mine, other, _ = done
        total = jnp.where(side == sides // 2, mine[steps * rows], 0.0)
        total = lax.psum(total, "per")
        mine = mine.at[steps * rows].set(total)
        other = other.at[steps * rows].set(total)
    received = lax.ppermute(other, "st", swap)
    trans_grad, mean_loglik = pl.pallas_call(
        functools.partial(finish_kernel, float(states * states * periods)),
        out_shape=[shaped((steps * rows, LANES), F32), shaped((1,), F32)],
        in_specs=[vmem(), vmem()],
        out_specs=[vmem(), smem()],
        compiler_params=params(4),
        name="finish",
    )(mine, received)
    return (trans_grad.reshape(steps, rows, LANES), mean_loglik)


def solution(mesh):
    placed = (
        P(("hh", "per"), None),
        P(("hh", "per")),
        P(("hh", "per")),
        P(("hh", "per")),
        P(("grp", "per", "st"), None, None),
        P("grp"),
        P("grp"),
        P("grp"),
    )
    return jax.shard_map(
        per_device,
        mesh=mesh,
        in_specs=placed,
        out_specs=(P(("grp", "per"), "hh", "st"), P("grp")),
        check_vma=False,
    )
```

```python
import functools

import jax
import jax.numpy as jnp
from jax import lax
from jax.experimental import pallas as pl
from jax.experimental.pallas import tpu as pltpu
from jax.sharding import PartitionSpec as P

HB = 128
LANES = 128
HALF = HB // 2
SEEN = 16.0
F32 = jnp.float32
BF16 = jnp.bfloat16
LOG2E = 1.4426950408889634
LN2 = 0.6931471805599453
EXTRA = 16


def vmem():
    return pl.BlockSpec(memory_space=pltpu.VMEM)


def smem():
    return pl.BlockSpec(memory_space=pltpu.SMEM)


def hbm():
    return pl.BlockSpec(memory_space=pltpu.HBM)


def params(mebibytes):
    return pltpu.CompilerParams(vmem_limit_bytes=mebibytes * 1024 * 1024)


def core_index():
    return lax.axis_index("st")


def is_forward_first():
    return 2 * lax.axis_index("per") < lax.axis_size("per")


def tiles(width):
    return [slice(q, q + LANES) for q in range(0, width, LANES)]


def fetch(pairs, sems):
    copies = [pltpu.make_async_copy(src, dst, sems.at[i]) for i, (src, dst) in enumerate(pairs)]
    for copy in copies:
        copy.start()
    for copy in copies:
        copy.wait()


def pack_kernel(
    count_any, earn_any, start_any, len_any, init_any, mean_any, sd_any, out_ref, vec_ref,
    count_ref, earn_ref, start_ref, len_ref, init_ref, mean_ref, sd_ref, sems,
):
    fetch(
        (
            (count_any, count_ref), (earn_any, earn_ref), (start_any, start_ref), (len_any, len_ref),
            (init_any, init_ref), (mean_any, mean_ref), (sd_any, sd_ref),
        ),
        sems,
    )
    periods, slot_rows = earn_ref.shape
    core = core_index()
    low_lane = lax.broadcasted_iota(jnp.int32, (periods // 2, HB), 1) < HALF
    time = lax.broadcasted_iota(jnp.int32, (periods, HB), 0)
    for slot in range(slot_rows // HB):
        cols = slice(slot * HB, (slot + 1) * HB)
        begin = start_ref[slot : slot + 1, :]
        seen = (time >= begin) & (time < begin + len_ref[slot : slot + 1, :])
        live = slot < count_ref[0]
        shift = jnp.where(live, jnp.where(seen, SEEN, 0.0), -SEEN)
        value = earn_ref[:, cols] + shift
        early, late = value[: periods // 2], value[periods // 2 :]
        turned = pltpu.roll(jnp.where(core == 0, late, early), HALF, 1)
        packed = jnp.where(low_lane, jnp.where(core == 0, early, turned), jnp.where(core == 0, turned, late))
        if len(out_ref.shape) == 2:
            out_ref[:, cols] = packed
        else:
            for to in range(out_ref.shape[0]):
                out_ref[to, :, cols] = packed
    raised = jnp.exp(init_ref[...])
    start = raised / jnp.sum(raised, axis=1, keepdims=True)
    row = lax.broadcasted_iota(jnp.int32, vec_ref.shape, 0)
    power = (-0.5 * LOG2E) * jnp.exp(-2.0 * sd_ref[...])
    vec_ref[...] = jnp.where(
        row == 0, start, jnp.where(row == 1, mean_ref[...], jnp.where(row == 2, power, -LOG2E * sd_ref[...]))
    )


def join_kernel(*refs):
    out_ref = refs[-1]
    here = lax.axis_index("hh")
    for r, ref in enumerate(refs[:-2]):
        out_ref[here ^ r] = ref[...]


def put(ref, at, value):
    states = value.shape[0]
    high = value.astype(BF16)
    ref[at, :states, :] = high
    ref[at, states : 2 * states, :] = (value - high.astype(F32)).astype(BF16)


def fill_periods(mat, row_probs, scratch, turned_pass, sources):
    for source, ref in sources:

        @pl.loop(0, ref.shape[0])
        def _(i):
            at = source * ref.shape[0] + i
            lifted = jnp.exp(ref[i].astype(F32))
            probs = lifted * (1.0 / jnp.sum(lifted, axis=1, keepdims=True))
            if row_probs is not None:
                rows = row_probs.shape[1]
                scratch[...] = probs
                row_probs[at] = scratch[own_rows(lax.axis_index("hh") * rows, rows), :]

            @pl.when(turned_pass)
            def _():
                put(mat, at, probs.T)

            @pl.when(jnp.logical_not(turned_pass))
            def _():
                put(mat, at, probs)


def prep_own_kernel(own_any, vec_any, mat, consts, own_ref, vec_ref, sems):
    fetch(((own_any, own_ref), (vec_any, vec_ref)), sems)
    states = own_ref.shape[1]
    for i in range(4):
        consts[i] = jnp.broadcast_to(vec_ref[i : i + 1, :], (LANES, states)).T
    start = vec_ref[:1, :]
    start_high = start.astype(BF16).astype(F32)
    row = lax.broadcasted_iota(jnp.int32, (EXTRA, states), 0)
    start_rows = jnp.where(row == 0, start_high, jnp.where(row == 1, start - start_high, 0.0)).astype(BF16)
    for k in range(mat.shape[0]):
        mat[k, 2 * states :, :] = start_rows
    fill_periods(mat, None, None, is_forward_first(), ((core_index(), own_ref),))


def prep_other_kernel(other_any, rows_any, mat_in, mat, other_ref, sems):
    fetch(((other_any, other_ref),), sems)
    fill_periods(mat, None, None, is_forward_first(), ((1 - core_index(), other_ref),))


def prep_second_kernel(own_any, other_any, state_any, mat, row_probs, scratch, own_ref, other_ref, sems):
    fetch(((own_any, own_ref), (other_any, other_ref)), sems)
    core = core_index()
    fill_periods(
        mat, row_probs, scratch, jnp.logical_not(is_forward_first()), ((core, own_ref), (1 - core, other_ref))
    )


def emission(sel_ref, consts, step_now, cols):
    gap = sel_ref[0, step_now, :1, cols] - consts[1]
    power = gap * gap * consts[2] + consts[3]
    top = jnp.max(power, axis=0, keepdims=True)
    return jnp.exp2(power - top), top


def is_moving(sel_ref, step_now, cols):
    return sel_ref[1, step_now, :1, cols] > 0.5


def is_seen(sel_ref, step_now, cols):
    return sel_ref[2, step_now, :1, cols] > 0.5


def column_sum(x):
    return jnp.sum(x, axis=0, keepdims=True)


def own_rows(row_begin, rows):
    return pl.ds(pl.multiple_of(row_begin, rows), rows)


def outer_sum(weights_ref, carried):
    return lax.dot_general(weights_ref[...], carried, (((1,), (1,)), ((), ())), preferred_element_type=F32)


def run_forward(lead, mat, hist, sel_ref, consts, ab_ref, logs, second=None):
    steps, states, width = hist.shape
    cuts = tiles(width)
    inverse = [1.0 / column_sum(ab_ref[:, cols].astype(F32)) for cols in cuts]
    for k in range(steps):
        step_now = lead + k
        if second is None:
            hist[k] = ab_ref[...]
        else:
            weights_ref, counts_ref, row_begin = second
            own_alpha = ab_ref[own_rows(row_begin, weights_ref.shape[0]), :].astype(F32)
        for q, cols in enumerate(cuts):
            product = jnp.dot(mat[k, : 2 * states, :], ab_ref[:, cols], preferred_element_type=F32)
            moved = (product[:states] + product[states:]) * inverse[q]
            moving = is_moving(sel_ref, step_now, cols)
            if second is not None:
                total = column_sum(moved * hist[k, :, cols].astype(F32))
                weight = jnp.where(moving, inverse[q] / total, 0.0)
                weights_ref[:, cols] = (own_alpha[:, cols] * weight).astype(BF16)
            emit, top = emission(sel_ref, consts, step_now, cols)
            joint = jnp.where(moving, moved, consts[0]) * emit
            scale = column_sum(joint)
            if second is None:
                seen = is_seen(sel_ref, step_now, cols)
                logs[q] = logs[q] + jnp.where(seen, jnp.log(scale) + top * LN2, 0.0)
            inverse[q] = 1.0 / scale
            ab_ref[:, cols] = joint.astype(BF16)
        if second is not None:
            counts_ref[k] += outer_sum(weights_ref, hist[k])
    return logs


def run_backward(lead, mat, hist, sel_ref, consts, back_ref, ub_ref, logs, second=None):
    steps, states, width = hist.shape
    cuts = tiles(width)
    for k in reversed(range(steps)):
        step_now = lead + k
        shrink = []
        for q, cols in enumerate(cuts):
            emit, top = emission(sel_ref, consts, step_now, cols)
            carried = emit * back_ref[:, cols]
            size = column_sum(carried)
            if second is None:
                seen = is_seen(sel_ref, step_now, cols)
                logs[q] = logs[q] + jnp.where(seen, jnp.log(size) + top * LN2, 0.0)
            shrink.append(1.0 / size)
            ub_ref[:, cols] = carried.astype(BF16)
        if second is None:
            hist[k] = ub_ref[...]
        else:
            weights_ref, counts_ref, row_begin = second
            own_alpha = hist[k, own_rows(row_begin, weights_ref.shape[0]), :].astype(F32)
        for q, cols in enumerate(cuts):
            product = jnp.dot(mat[k], ub_ref[:, cols], preferred_element_type=F32)
            moving = is_moving(sel_ref, step_now, cols)
            pulled = (product[:states] + product[states : 2 * states]) * shrink[q]
            if second is None:
                seen = is_seen(sel_ref, step_now, cols)
                begun = column_sum(product[2 * states :]) * shrink[q]
                rest = jnp.where(seen, begun, back_ref[:, cols])
            else:
                total = column_sum(pulled * hist[k, :, cols].astype(F32))
                weight = jnp.where(moving, shrink[q] / total, 0.0)
                weights_ref[:, cols] = (own_alpha[:, cols] * weight).astype(BF16)
                rest = 1.0
            back_ref[:, cols] = jnp.where(moving, pulled, rest)
        if second is not None:
            counts_ref[k] += outer_sum(weights_ref, ub_ref[...])
    return logs


def put_state(state_out, values, logs):
    states = state_out.shape[0] - EXTRA
    state_out[:states, :] = values
    for q, cols in enumerate(tiles(state_out.shape[1])):
        high = logs[q].astype(BF16).astype(F32)
        middle = (logs[q] - high).astype(BF16).astype(F32)
        row = lax.broadcasted_iota(jnp.int32, (EXTRA, LANES), 0)
        piece = jnp.where(
            row == 0, high, jnp.where(row == 1, middle, jnp.where(row == 2, logs[q] - high - middle, 0.0))
        )
        state_out[states:, cols] = piece.astype(BF16)


def state_logs(state_ref):
    states = state_ref.shape[0] - EXTRA
    return [column_sum(state_ref[states:, cols].astype(F32)) for cols in tiles(state_ref.shape[1])]


def first_kernel(resume, grids, part, near, *refs):
    refs = list(refs)
    rows_ref = refs.pop(0)
    rows_other = refs.pop(0) if near else None
    mat, consts = refs.pop(0), refs.pop(0)
    state_in = refs[0] if resume else None
    hist, state_out, sel_ref, ab_ref, back_ref = refs[-5:]
    chunk = part * grids + (pl.program_id(0) if grids > 1 else 0)
    steps, states, width = hist.shape
    forward_first, lead = is_forward_first(), lax.axis_index("per") * steps
    cuts = tiles(width)
    group, half_periods, slot_rows = rows_ref.shape
    tops = 2 * len(cuts)

    def scan_source(d, carry):
        rank, picked = carry
        for slot in range(slot_rows // HB):
            cols = slice(slot * HB, (slot + 1) * HB)
            if near:
                here = lax.axis_index("per") == d // group
                block = jnp.where(here, rows_ref[d % group, :, cols], rows_other[d % group, :, cols])
            else:
                block = rows_ref[d, :, cols]
            live = block > -0.5 * SEEN
            picked = [jnp.where(live & (rank == chunk * tops + i), block, old) for i, old in enumerate(picked)]
            rank = rank + live.astype(jnp.int32)
        return rank, picked

    carry = (jnp.zeros((half_periods, HB), jnp.int32), [jnp.zeros((half_periods, HB), F32)] * tops)
    if near:
        for d in range(2 * group):
            carry = scan_source(d, carry)
    else:
        carry = lax.fori_loop(0, group, scan_source, carry)
    low_lane = lax.broadcasted_iota(jnp.int32, (half_periods, HB), 1) < HALF
    for q, cols in enumerate(cuts):
        left, right = carry[1][2 * q], carry[1][2 * q + 1]
        before = jnp.zeros((1, HB), F32)
        for late in range(2):
            value = (
                jnp.where(low_lane, pltpu.roll(left, HALF, 1), right)
                if late
                else jnp.where(low_lane, left, pltpu.roll(right, HALF, 1))
            )
            seen = value > 0.5 * SEEN
            earn = jnp.where(seen, value - SEEN, value)
            seen = seen.astype(F32)
            for i in range(half_periods):
                at = late * half_periods + i
                now = seen[i : i + 1]
                sel_ref[0, at, :, cols] = jnp.broadcast_to(earn[i : i + 1], (8, HB))
                sel_ref[1, at, :, cols] = jnp.broadcast_to(now * before, (8, HB))
                sel_ref[2, at, :, cols] = jnp.broadcast_to(now, (8, HB))
                before = now
    zeros = [jnp.zeros((1, LANES), F32) for _ in cuts]

    @pl.when(forward_first)
    def _():
        if resume:
            ab_ref[...] = state_in[:states, :]
        else:
            for cols in cuts:
                ab_ref[:, cols] = consts[0].astype(BF16)
        logs = state_logs(state_in) if resume else list(zeros)
        logs = run_forward(lead, mat, hist, sel_ref, consts, ab_ref, logs)
        put_state(state_out, ab_ref[...], logs)

    @pl.when(jnp.logical_not(forward_first))
    def _():
        if resume:
            back_ref[...] = state_in[:states, :].astype(F32)
        else:
            back_ref[...] = jnp.ones_like(back_ref)
        logs = state_logs(state_in) if resume else list(zeros)
        logs = run_backward(lead, mat, hist, sel_ref, consts, back_ref, ab_ref, logs)
        put_state(state_out, back_ref[...].astype(BF16), logs)


def second_kernel(resume, last, extend, grids, *refs):
    refs = list(refs)
    sel_ref, mat, consts, hist, own_state, state_in = (refs.pop(0) for _ in range(6))
    counts_in, sums_in = (refs.pop(0), refs.pop(0)) if resume else (None, None)
    row_probs = refs.pop(0) if last else None
    mine_ref, other_ref = (refs.pop(0), refs.pop(0)) if last else (None, None)
    counts_out, sums_out = (None, None) if last else (refs.pop(0), refs.pop(0))
    state_out = refs.pop(0) if extend else None
    ab_ref, back_ref, weights_ref = refs[:3]
    counts_ref, sums_ref = refs[3:] if last else (counts_out, sums_out)
    chunk = pl.program_id(0) if grids > 1 else 0
    steps, states, width = hist.shape
    core, forward_first = core_index(), is_forward_first()
    row_begin = lax.axis_index("hh") * counts_ref.shape[1]
    lead = lax.axis_index("per") * steps
    second = (weights_ref, counts_ref, row_begin)

    @pl.when(chunk == 0)
    def _():
        if resume:
            counts_ref[...] = counts_in[...]
            sums_ref[...] = sums_in[...]
        else:
            counts_ref[...] = jnp.zeros_like(counts_ref)
            sums_ref[...] = jnp.zeros_like(sums_ref)

    def add_sums(alpha_ref, other_state):
        total = jnp.zeros((1, LANES), F32)
        years = jnp.zeros((8, LANES), F32)
        for cols, here, there in zip(tiles(width), state_logs(alpha_ref), state_logs(other_state)):
            alpha = alpha_ref[:states, cols].astype(F32)
            meet = column_sum(alpha * other_state[:states, cols].astype(F32))
            total += here + there + jnp.log(meet / column_sum(alpha))
            years += jnp.sum(sel_ref[2, :, :, cols], axis=0)
        total = jnp.broadcast_to(jnp.sum(total, axis=1, keepdims=True), (1, LANES))
        years = jnp.broadcast_to(jnp.sum(years[:1], axis=1, keepdims=True), (1, LANES))
        row = lax.broadcasted_iota(jnp.int32, (8, LANES), 0)
        sums_ref[...] += jnp.where(row == 0, total, jnp.where(row == 1, years, 0.0))

    zeros = [jnp.zeros((1, LANES), F32) for _ in tiles(width)]

    @pl.when(jnp.logical_not(forward_first))
    def _():
        add_sums(state_in, own_state)
        ab_ref[...] = state_in[:states, :]
        run_forward(lead, mat, hist, sel_ref, consts, ab_ref, list(zeros), second)
        if extend:
            put_state(state_out, ab_ref[...], zeros)

    @pl.when(forward_first)
    def _():
        add_sums(own_state, state_in)
        back_ref[...] = state_in[:states, :].astype(F32)
        run_backward(lead, mat, hist, sel_ref, consts, back_ref, ab_ref, list(zeros), second)
        if extend:
            put_state(state_out, back_ref[...].astype(BF16), zeros)

    if last:

        @pl.when(chunk == grids - 1)
        def _():
            rows = counts_ref.shape[1]
            for k in range(steps):
                probs = row_probs[k]
                weighted = probs * counts_ref[k]
                grad = weighted - probs * jnp.sum(weighted, axis=1, keepdims=True)
                for side in range(2):
                    piece = grad[:, side * LANES : (side + 1) * LANES]
                    at = slice(k * rows, (k + 1) * rows)

                    @pl.when(core == side)
                    def _():
                        mine_ref[at, :] = piece

                    @pl.when(core != side)
                    def _():
                        other_ref[at, :] = piece

            mine_ref[steps * rows :, :] = sums_ref[...]
            other_ref[steps * rows :, :] = sums_ref[...]


def finish_kernel(scale, mine_ref, other_ref, grad_ref, mean_ref):
    count = grad_ref.shape[0]
    total = mine_ref[count : count + 1, :] + other_ref[count : count + 1, :]
    years = mine_ref[count + 1 : count + 2, :] + other_ref[count + 1 : count + 2, :]
    grad_ref[...] = (mine_ref[:count, :] + other_ref[:count, :]) * (scale / years)
    mean_ref[0] = (total / years)[0, 0]


def per_device(
    earnings, starts, lengths, block_count, trans_logits, init_logits, state_mean, log_sd
):
    slot_rows, periods = earnings.shape
    states = init_logits.shape[0]
    group = lax.axis_size(("hh", "per"))
    sides = lax.axis_size("per")
    cores = lax.axis_size("st")
    part = trans_logits.shape[0]
    steps = part * cores
    rows = states // lax.axis_size("hh")
    households = group * HB // cores
    parts = 2 if households <= 4 * HB else 1
    share = households // parts
    width = min(2 * HB, share)
    grids = share // width
    side = lax.axis_index("per")
    shaped = jax.ShapeDtypeStruct
    dma = pltpu.SemaphoreType.DMA

    along = lax.axis_size("hh")
    near = sides == 2 and along <= 8 and along & (along - 1) == 0

    swap = [(0, 1), (1, 0)]
    other_logits = lax.ppermute(trans_logits, "st", swap)
    row_shape = (periods // 2, slot_rows)
    vec_row = pltpu.VMEM((1, states), F32)
    packed, vectors = pl.pallas_call(
        pack_kernel,
        out_shape=[shaped(row_shape if near else (group,) + row_shape, F32), shaped((8, states), F32)],
        in_specs=[hbm()] * 7,
        out_specs=[vmem()] * 2,
        scratch_shapes=[
            pltpu.SMEM((1,), jnp.int32),
            pltpu.VMEM((periods, slot_rows), F32),
            pltpu.VMEM((slot_rows // HB, HB), jnp.int32),
            pltpu.VMEM((slot_rows // HB, HB), jnp.int32),
            vec_row,
            vec_row,
            vec_row,
            dma((7,)),
        ],
        name="pack",
    )(
        block_count, earnings.T, starts.reshape(-1, HB), lengths.reshape(-1, HB),
        init_logits.reshape(1, states), state_mean.reshape(1, states), log_sd.reshape(1, states),
    )
    first_shape = shaped((steps, 2 * states + EXTRA, states), BF16)
    half_logits = pltpu.VMEM(trans_logits.shape, BF16)
    first_mat, consts = pl.pallas_call(
        prep_own_kernel,
        out_shape=[first_shape, shaped((4, states, LANES), F32)],
        in_specs=[hbm()] * 2,
        out_specs=[vmem()] * 2,
        scratch_shapes=[half_logits, pltpu.VMEM((8, states), F32), dma((2,))],
        compiler_params=params(4),
        name="prep_own",
    )(trans_logits, vectors)
    if near:
        pieces = [packed] + [
            lax.ppermute(packed, "hh", [(i, i ^ r) for i in range(along)]) for r in range(1, along)
        ]
        joined = pl.pallas_call(
            join_kernel,
            out_shape=shaped((along,) + row_shape, F32),
            in_specs=[vmem()] * along + [hbm()],
            out_specs=vmem(),
            compiler_params=params(2),
            name="join",
        )(*pieces, consts)
        gathered = [joined, lax.ppermute(joined, "per", swap)]
    else:
        gathered = [lax.all_to_all(packed, ("hh", "per"), split_axis=0, concat_axis=0, tiled=True)]
        joined = gathered[0]

    first_mat = pl.pallas_call(
        prep_other_kernel,
        out_shape=first_shape,
        in_specs=[hbm(), hbm(), vmem()],
        out_specs=vmem(),
        scratch_shapes=[half_logits, dma((1,))],
        input_output_aliases={2: 0},
        compiler_params=params(4),
        name="prep_other",
    )(other_logits, joined, first_mat)

    def prep_second(after):
        return pl.pallas_call(
            prep_second_kernel,
            out_shape=[shaped((steps, 2 * states, states), BF16), shaped((steps, rows, states), F32)],
            in_specs=[hbm()] * 3,
            out_specs=[vmem()] * 2,
            scratch_shapes=[pltpu.VMEM((states, states), F32), half_logits, half_logits, dma((2,))],
            compiler_params=params(4),
            name="prep_second",
        )(trans_logits, other_logits, after)

    def whole(*shape):
        if grids == 1:
            return vmem()
        return pl.BlockSpec(shape, lambda g: (0,) * len(shape))

    def lanes(*lead):
        if grids == 1:
            return vmem()
        return pl.BlockSpec(lead + (width,), lambda g: (0,) * len(lead) + (g,))

    grid = (grids,) if grids > 1 else ()
    hist_shape = shaped((steps, states, share), BF16)
    state_shape = shaped((states + EXTRA, share), BF16)
    sel_shape = shaped((3, periods, 8, share), F32)
    swap_shape = shaped((steps * rows + 8, LANES), F32)
    counts_shape = shaped((steps, rows, states), F32)
    sums_shape = shaped((8, LANES), F32)
    hist_spec, state_spec, sel_spec = lanes(steps, states), lanes(states + EXTRA), lanes(3, periods, 8)
    const_spec = whole(4, states, LANES)

    def first_pass(index, state_in):
        resume = state_in is not None
        return pl.pallas_call(
            functools.partial(first_kernel, resume, grids, index, near),
            grid=grid,
            out_shape=[hist_shape, state_shape, sel_shape],
            in_specs=[whole(*x.shape) for x in gathered + [first_mat]] + [const_spec]
            + [state_spec] * resume,
            out_specs=[hist_spec, state_spec, sel_spec],
            scratch_shapes=[pltpu.VMEM((states, width), BF16), pltpu.VMEM((states, width), F32)],
            compiler_params=params(8 if grids == 1 else 32),
            name="first_pass",
        )(*gathered, first_mat, consts, *([state_in] if resume else []))

    def second_pass(kept, state_in, sums_in, last, extend):
        hist, own_state, sel = kept
        resume = sums_in is not None
        scratch = [
            pltpu.VMEM((states, width), BF16),
            pltpu.VMEM((states, width), F32),
            pltpu.VMEM((rows, width), BF16),
        ]
        counts_spec, sums_spec = whole(*counts_shape.shape), whole(*sums_shape.shape)
        if last:
            out_shape = [swap_shape] * 2
            scratch += [pltpu.VMEM(counts_shape.shape, F32), pltpu.VMEM(sums_shape.shape, F32)]
        else:
            out_shape = [counts_shape, sums_shape]
        out_specs = [whole(*x.shape) for x in out_shape]
        if extend:
            out_shape, out_specs = out_shape + [state_shape], out_specs + [state_spec]
        return pl.pallas_call(
            functools.partial(second_kernel, resume, last, extend, grids),
            grid=grid,
            out_shape=out_shape,
            in_specs=[sel_spec, whole(*second_mat.shape), const_spec, hist_spec, state_spec, state_spec]
            + [counts_spec, sums_spec] * resume
            + [whole(*row_probs.shape)] * last,
            out_specs=out_specs,
            scratch_shapes=scratch,
            compiler_params=params(8 if grids == 1 else 32),
            name="second_pass",
        )(
            sel, second_mat, consts, hist, own_state, state_in,
            *(sums_in if resume else []),
            *([row_probs] if last else []),
        )

    def hand_over(state, stage):
        moves = [(stage, stage + 1), (sides - 1 - stage, sides - 2 - stage)]
        return lax.ppermute(state, "per", moves)

    if sides == 2:
        kept = [first_pass(index, None) for index in range(parts)]
        arrived = [hand_over(each[1], 0) for each in kept]
        second_mat, row_probs = prep_second(kept[-1][1])
        sums = None
        for index in range(parts):
            sums = second_pass(kept[index], arrived[index], sums, index == parts - 1, False)
        mine, other = sums
    else:
        kept = [jnp.zeros(x.shape, x.dtype) for x in (hist_shape, state_shape, sel_shape)]
        done = [jnp.zeros(x.shape, x.dtype) for x in (swap_shape, swap_shape, state_shape)]
        second_mat, row_probs = prep_second(joined)
        state = None
        for stage in range(sides):
            active = (side == stage) | (side == sides - 1 - stage)
            if stage < sides // 2:
                kept = lax.cond(
                    active, lambda x, kept: list(first_pass(0, x)), lambda x, kept: kept, state, kept
                )
                state = kept[1]
            else:
                done = lax.cond(
                    active,
                    lambda x, done: list(second_pass(kept, x, None, True, True)),
                    lambda x, done: done,
                    state,
                    done,
                )
                state = done[2]
            if stage < sides - 1:
                state = hand_over(state, stage)
        mine, other, _ = done
        total = jnp.where(side == sides // 2, mine[steps * rows], 0.0)
        total = lax.psum(total, "per")
        mine = mine.at[steps * rows].set(total)
        other = other.at[steps * rows].set(total)
    received = lax.ppermute(other, "st", swap)
    trans_grad, mean_loglik = pl.pallas_call(
        functools.partial(finish_kernel, float(states * states * periods)),
        out_shape=[shaped((steps * rows, LANES), F32), shaped((1,), F32)],
        in_specs=[vmem(), vmem()],
        out_specs=[vmem(), smem()],
        compiler_params=params(4),
        name="finish",
    )(mine, received)
    return (trans_grad.reshape(steps, rows, LANES), mean_loglik)


def solution(mesh):
    placed = (
        P(("hh", "per"), None),
        P(("hh", "per")),
        P(("hh", "per")),
        P(("hh", "per")),
        P(("grp", "per", "st"), None, None),
        P("grp"),
        P("grp"),
        P("grp"),
    )
    return jax.shard_map(
        per_device,
        mesh=mesh,
        in_specs=placed,
        out_specs=(P(("grp", "per"), "hh", "st"), P("grp")),
        check_vma=False,
    )
```

```python
import functools

import jax
import jax.numpy as jnp
from jax import lax
from jax.experimental import pallas as pl
from jax.experimental.pallas import tpu as pltpu
from jax.sharding import PartitionSpec as P

HB = 128
LANES = 128
HALF = HB // 2
SEEN = 16.0
F32 = jnp.float32
BF16 = jnp.bfloat16
LOG2E = 1.4426950408889634
LN2 = 0.6931471805599453
EXTRA = 16


def vmem():
    return pl.BlockSpec(memory_space=pltpu.VMEM)


def smem():
    return pl.BlockSpec(memory_space=pltpu.SMEM)


def hbm():
    return pl.BlockSpec(memory_space=pltpu.HBM)


def params(mebibytes):
    return pltpu.CompilerParams(vmem_limit_bytes=mebibytes * 1024 * 1024)


def core_index():
    return lax.axis_index("st")


def is_forward_first():
    return 2 * lax.axis_index("per") < lax.axis_size("per")


def tiles(width):
    return [slice(q, q + LANES) for q in range(0, width, LANES)]


def fetch(pairs, sems):
    copies = [pltpu.make_async_copy(src, dst, sems.at[i]) for i, (src, dst) in enumerate(pairs)]
    for copy in copies:
        copy.start()
    for copy in copies:
        copy.wait()


def pack_kernel(
    count_any, earn_any, start_any, len_any, init_any, mean_any, sd_any, out_ref, vec_ref,
    count_ref, earn_ref, start_ref, len_ref, init_ref, mean_ref, sd_ref, sems,
):
    fetch(
        (
            (count_any, count_ref), (earn_any, earn_ref), (start_any, start_ref), (len_any, len_ref),
            (init_any, init_ref), (mean_any, mean_ref), (sd_any, sd_ref),
        ),
        sems,
    )
    periods, slot_rows = earn_ref.shape
    core = core_index()
    low_lane = lax.broadcasted_iota(jnp.int32, (periods // 2, HB), 1) < HALF
    time = lax.broadcasted_iota(jnp.int32, (periods, HB), 0)
    for slot in range(slot_rows // HB):
        cols = slice(slot * HB, (slot + 1) * HB)
        begin = start_ref[slot : slot + 1, :]
        seen = (time >= begin) & (time < begin + len_ref[slot : slot + 1, :])
        live = slot < count_ref[0]
        shift = jnp.where(live, jnp.where(seen, SEEN, 0.0), -SEEN)
        value = earn_ref[:, cols] + shift
        early, late = value[: periods // 2], value[periods // 2 :]
        turned = pltpu.roll(jnp.where(core == 0, late, early), HALF, 1)
        packed = jnp.where(low_lane, jnp.where(core == 0, early, turned), jnp.where(core == 0, turned, late))
        if len(out_ref.shape) == 2:
            out_ref[:, cols] = packed
        else:
            for to in range(out_ref.shape[0]):
                out_ref[to, :, cols] = packed
    raised = jnp.exp(init_ref[...])
    start = raised / jnp.sum(raised, axis=1, keepdims=True)
    row = lax.broadcasted_iota(jnp.int32, vec_ref.shape, 0)
    power = (-0.5 * LOG2E) * jnp.exp(-2.0 * sd_ref[...])
    vec_ref[...] = jnp.where(
        row == 0, start, jnp.where(row == 1, mean_ref[...], jnp.where(row == 2, power, -LOG2E * sd_ref[...]))
    )


def join_kernel(bit, mine_ref, got_ref, after_any, out_ref):
    count = mine_ref.shape[0]
    upper = (lax.axis_index("hh") // bit) % 2
    out_ref[pl.ds(upper * count, count)] = mine_ref[...]
    out_ref[pl.ds((1 - upper) * count, count)] = got_ref[...]


def put(ref, at, value):
    states = value.shape[0]
    high = value.astype(BF16)
    ref[at, :states, :] = high
    ref[at, states : 2 * states, :] = (value - high.astype(F32)).astype(BF16)


def fill_periods(mat, row_probs, scratch, turned_pass, source, ref, periods, part):
    @pl.loop(periods[0], periods[1])
    def _(i):
        at = source * part + i
        lifted = jnp.exp(ref[i].astype(F32))
        probs = lifted * (1.0 / jnp.sum(lifted, axis=1, keepdims=True))
        if row_probs is not None:
            rows = row_probs.shape[1]
            scratch[...] = probs
            row_probs[at] = scratch[own_rows(lax.axis_index("hh") * rows, rows), :]

        @pl.when(turned_pass)
        def _():
            put(mat, at, probs.T)

        @pl.when(jnp.logical_not(turned_pass))
        def _():
            put(mat, at, probs)


def prep_own_kernel(periods, own_any, packed_any, mat, packed, own_ref, sems):
    fetch(((own_any, own_ref), (packed_any, packed)), sems)
    fill_periods(mat, None, None, is_forward_first(), core_index(), own_ref, periods, own_ref.shape[0])


def prep_rest_kernel(periods, own_any, vec_any, after_any, mat_in, mat, consts, own_ref, vec_ref, sems):
    fetch(((own_any, own_ref), (vec_any, vec_ref)), sems)
    states = own_ref.shape[1]
    for i in range(4):
        consts[i] = jnp.broadcast_to(vec_ref[i : i + 1, :], (LANES, states)).T
    start = vec_ref[:1, :]
    start_high = start.astype(BF16).astype(F32)
    row = lax.broadcasted_iota(jnp.int32, (EXTRA, states), 0)
    start_rows = jnp.where(row == 0, start_high, jnp.where(row == 1, start - start_high, 0.0)).astype(BF16)
    for k in range(mat.shape[0]):
        mat[k, 2 * states :, :] = start_rows
    fill_periods(mat, None, None, is_forward_first(), core_index(), own_ref, periods, own_ref.shape[0])


def prep_other_kernel(other_any, after_any, mat_in, mat, other_ref, sems):
    fetch(((other_any, other_ref),), sems)
    part = other_ref.shape[0]
    fill_periods(mat, None, None, is_forward_first(), 1 - core_index(), other_ref, (0, part), part)


def prep_second_kernel(own_any, other_any, after_any, mat, row_probs, scratch, own_ref, other_ref, sems):
    fetch(((own_any, own_ref), (other_any, other_ref)), sems)
    turned_pass, part = jnp.logical_not(is_forward_first()), own_ref.shape[0]
    for source, ref in ((core_index(), own_ref), (1 - core_index(), other_ref)):
        fill_periods(mat, row_probs, scratch, turned_pass, source, ref, (0, part), part)


def emission(sel_ref, consts, step_now, cols):
    gap = sel_ref[0, step_now, :1, cols] - consts[1]
    power = gap * gap * consts[2] + consts[3]
    top = jnp.max(power, axis=0, keepdims=True)
    return jnp.exp2(power - top), top


def is_moving(sel_ref, step_now, cols):
    return sel_ref[1, step_now, :1, cols] > 0.5


def is_seen(sel_ref, step_now, cols):
    return sel_ref[2, step_now, :1, cols] > 0.5


def column_sum(x):
    return jnp.sum(x, axis=0, keepdims=True)


def own_rows(row_begin, rows):
    return pl.ds(pl.multiple_of(row_begin, rows), rows)


def outer_sum(weights_ref, carried):
    return lax.dot_general(weights_ref[...], carried, (((1,), (1,)), ((), ())), preferred_element_type=F32)


def run_forward(lead, mat, hist, sel_ref, consts, ab_ref, logs, second=None):
    steps, states, width = hist.shape
    cuts = tiles(width)
    inverse = [1.0 / column_sum(ab_ref[:, cols].astype(F32)) for cols in cuts]
    for k in range(steps):
        step_now = lead + k
        if second is None:
            hist[k] = ab_ref[...]
        else:
            weights_ref, counts_ref, row_begin = second
            own_alpha = ab_ref[own_rows(row_begin, weights_ref.shape[0]), :].astype(F32)
        for q, cols in enumerate(cuts):
            product = jnp.dot(mat[k, : 2 * states, :], ab_ref[:, cols], preferred_element_type=F32)
            moved = (product[:states] + product[states:]) * inverse[q]
            moving = is_moving(sel_ref, step_now, cols)
            if second is not None:
                total = column_sum(moved * hist[k, :, cols].astype(F32))
                weight = jnp.where(moving, inverse[q] / total, 0.0)
                weights_ref[:, cols] = (own_alpha[:, cols] * weight).astype(BF16)
            emit, top = emission(sel_ref, consts, step_now, cols)
            joint = jnp.where(moving, moved, consts[0]) * emit
            scale = column_sum(joint)
            if second is None:
                seen = is_seen(sel_ref, step_now, cols)
                logs[q] = logs[q] + jnp.where(seen, jnp.log(scale) + top * LN2, 0.0)
            inverse[q] = 1.0 / scale
            ab_ref[:, cols] = joint.astype(BF16)
        if second is not None:
            counts_ref[k] += outer_sum(weights_ref, hist[k])
    return logs


def run_backward(lead, mat, hist, sel_ref, consts, back_ref, ub_ref, logs, second=None):
    steps, states, width = hist.shape
    cuts = tiles(width)
    for k in reversed(range(steps)):
        step_now = lead + k
        shrink = []
        for q, cols in enumerate(cuts):
            emit, top = emission(sel_ref, consts, step_now, cols)
            carried = emit * back_ref[:, cols]
            size = column_sum(carried)
            if second is None:
                seen = is_seen(sel_ref, step_now, cols)
                logs[q] = logs[q] + jnp.where(seen, jnp.log(size) + top * LN2, 0.0)
            shrink.append(1.0 / size)
            ub_ref[:, cols] = carried.astype(BF16)
        if second is None:
            hist[k] = ub_ref[...]
        else:
            weights_ref, counts_ref, row_begin = second
            own_alpha = hist[k, own_rows(row_begin, weights_ref.shape[0]), :].astype(F32)
        for q, cols in enumerate(cuts):
            product = jnp.dot(mat[k], ub_ref[:, cols], preferred_element_type=F32)
            moving = is_moving(sel_ref, step_now, cols)
            pulled = (product[:states] + product[states : 2 * states]) * shrink[q]
            if second is None:
                seen = is_seen(sel_ref, step_now, cols)
                begun = column_sum(product[2 * states :]) * shrink[q]
                rest = jnp.where(seen, begun, back_ref[:, cols])
            else:
                total = column_sum(pulled * hist[k, :, cols].astype(F32))
                weight = jnp.where(moving, shrink[q] / total, 0.0)
                weights_ref[:, cols] = (own_alpha[:, cols] * weight).astype(BF16)
                rest = 1.0
            back_ref[:, cols] = jnp.where(moving, pulled, rest)
        if second is not None:
            counts_ref[k] += outer_sum(weights_ref, ub_ref[...])
    return logs


def put_state(state_out, values, logs):
    states = state_out.shape[0] - EXTRA
    state_out[:states, :] = values
    for q, cols in enumerate(tiles(state_out.shape[1])):
        high = logs[q].astype(BF16).astype(F32)
        middle = (logs[q] - high).astype(BF16).astype(F32)
        row = lax.broadcasted_iota(jnp.int32, (EXTRA, LANES), 0)
        piece = jnp.where(
            row == 0, high, jnp.where(row == 1, middle, jnp.where(row == 2, logs[q] - high - middle, 0.0))
        )
        state_out[states:, cols] = piece.astype(BF16)


def state_logs(state_ref):
    states = state_ref.shape[0] - EXTRA
    return [column_sum(state_ref[states:, cols].astype(F32)) for cols in tiles(state_ref.shape[1])]


def first_kernel(resume, grids, part, near, *refs):
    refs = list(refs)
    rows_ref = refs.pop(0)
    rows_other = refs.pop(0) if near else None
    mat, consts = refs.pop(0), refs.pop(0)
    state_in = refs[0] if resume else None
    hist, state_out, sel_ref, ab_ref, back_ref = refs[-5:]
    chunk = part * grids + (pl.program_id(0) if grids > 1 else 0)
    steps, states, width = hist.shape
    forward_first, lead = is_forward_first(), lax.axis_index("per") * steps
    cuts = tiles(width)
    group, half_periods, slot_rows = rows_ref.shape
    tops = 2 * len(cuts)

    def scan_source(d, carry):
        rank, picked = carry
        for slot in range(slot_rows // HB):
            cols = slice(slot * HB, (slot + 1) * HB)
            if near:
                here = lax.axis_index("per") == d // group
                block = jnp.where(here, rows_ref[d % group, :, cols], rows_other[d % group, :, cols])
            else:
                block = rows_ref[d, :, cols]
            live = block > -0.5 * SEEN
            picked = [jnp.where(live & (rank == chunk * tops + i), block, old) for i, old in enumerate(picked)]
            rank = rank + live.astype(jnp.int32)
        return rank, picked

    carry = (jnp.zeros((half_periods, HB), jnp.int32), [jnp.zeros((half_periods, HB), F32)] * tops)
    if near:
        for d in range(2 * group):
            carry = scan_source(d, carry)
    else:
        carry = lax.fori_loop(0, group, scan_source, carry)
    low_lane = lax.broadcasted_iota(jnp.int32, (half_periods, HB), 1) < HALF
    for q, cols in enumerate(cuts):
        left, right = carry[1][2 * q], carry[1][2 * q + 1]
        before = jnp.zeros((1, HB), F32)
        for late in range(2):
            value = (
                jnp.where(low_lane, pltpu.roll(left, HALF, 1), right)
                if late
                else jnp.where(low_lane, left, pltpu.roll(right, HALF, 1))
            )
            seen = value > 0.5 * SEEN
            earn = jnp.where(seen, value - SEEN, value)
            seen = seen.astype(F32)
            for i in range(half_periods):
                at = late * half_periods + i
                now = seen[i : i + 1]
                sel_ref[0, at, :, cols] = jnp.broadcast_to(earn[i : i + 1], (8, HB))
                sel_ref[1, at, :, cols] = jnp.broadcast_to(now * before, (8, HB))
                sel_ref[2, at, :, cols] = jnp.broadcast_to(now, (8, HB))
                before = now
    zeros = [jnp.zeros((1, LANES), F32) for _ in cuts]

    @pl.when(forward_first)
    def _():
        if resume:
            ab_ref[...] = state_in[:states, :]
        else:
            for cols in cuts:
                ab_ref[:, cols] = consts[0].astype(BF16)
        logs = state_logs(state_in) if resume else list(zeros)
        logs = run_forward(lead, mat, hist, sel_ref, consts, ab_ref, logs)
        put_state(state_out, ab_ref[...], logs)

    @pl.when(jnp.logical_not(forward_first))
    def _():
        if resume:
            back_ref[...] = state_in[:states, :].astype(F32)
        else:
            back_ref[...] = jnp.ones_like(back_ref)
        logs = state_logs(state_in) if resume else list(zeros)
        logs = run_backward(lead, mat, hist, sel_ref, consts, back_ref, ab_ref, logs)
        put_state(state_out, back_ref[...].astype(BF16), logs)


def second_kernel(resume, last, extend, grids, *refs):
    refs = list(refs)
    sel_ref, mat, consts, hist, own_state, state_in = (refs.pop(0) for _ in range(6))
    counts_in, sums_in = (refs.pop(0), refs.pop(0)) if resume else (None, None)
    row_probs = refs.pop(0) if last else None
    mine_ref, other_ref = (refs.pop(0), refs.pop(0)) if last else (None, None)
    counts_out, sums_out = (None, None) if last else (refs.pop(0), refs.pop(0))
    state_out = refs.pop(0) if extend else None
    ab_ref, back_ref, weights_ref = refs[:3]
    counts_ref, sums_ref = refs[3:] if last else (counts_out, sums_out)
    chunk = pl.program_id(0) if grids > 1 else 0
    steps, states, width = hist.shape
    core, forward_first = core_index(), is_forward_first()
    row_begin = lax.axis_index("hh") * counts_ref.shape[1]
    lead = lax.axis_index("per") * steps
    second = (weights_ref, counts_ref, row_begin)

    @pl.when(chunk == 0)
    def _():
        if resume:
            counts_ref[...] = counts_in[...]
            sums_ref[...] = sums_in[...]
        else:
            counts_ref[...] = jnp.zeros_like(counts_ref)
            sums_ref[...] = jnp.zeros_like(sums_ref)

    def add_sums(alpha_ref, other_state):
        total = jnp.zeros((1, LANES), F32)
        years = jnp.zeros((8, LANES), F32)
        for cols, here, there in zip(tiles(width), state_logs(alpha_ref), state_logs(other_state)):
            alpha = alpha_ref[:states, cols].astype(F32)
            meet = column_sum(alpha * other_state[:states, cols].astype(F32))
            total += here + there + jnp.log(meet / column_sum(alpha))
            years += jnp.sum(sel_ref[2, :, :, cols], axis=0)
        total = jnp.broadcast_to(jnp.sum(total, axis=1, keepdims=True), (1, LANES))
        years = jnp.broadcast_to(jnp.sum(years[:1], axis=1, keepdims=True), (1, LANES))
        row = lax.broadcasted_iota(jnp.int32, (8, LANES), 0)
        sums_ref[...] += jnp.where(row == 0, total, jnp.where(row == 1, years, 0.0))

    zeros = [jnp.zeros((1, LANES), F32) for _ in tiles(width)]

    @pl.when(jnp.logical_not(forward_first))
    def _():
        add_sums(state_in, own_state)
        ab_ref[...] = state_in[:states, :]
        run_forward(lead, mat, hist, sel_ref, consts, ab_ref, list(zeros), second)
        if extend:
            put_state(state_out, ab_ref[...], zeros)

    @pl.when(forward_first)
    def _():
        add_sums(own_state, state_in)
        back_ref[...] = state_in[:states, :].astype(F32)
        run_backward(lead, mat, hist, sel_ref, consts, back_ref, ab_ref, list(zeros), second)
        if extend:
            put_state(state_out, back_ref[...].astype(BF16), zeros)

    if last:

        @pl.when(chunk == grids - 1)
        def _():
            rows = counts_ref.shape[1]
            for k in range(steps):
                probs = row_probs[k]
                weighted = probs * counts_ref[k]
                grad = weighted - probs * jnp.sum(weighted, axis=1, keepdims=True)
                for side in range(2):
                    piece = grad[:, side * LANES : (side + 1) * LANES]
                    at = slice(k * rows, (k + 1) * rows)

                    @pl.when(core == side)
                    def _():
                        mine_ref[at, :] = piece

                    @pl.when(core != side)
                    def _():
                        other_ref[at, :] = piece

            mine_ref[steps * rows :, :] = sums_ref[...]
            other_ref[steps * rows :, :] = sums_ref[...]


def finish_kernel(scale, mine_ref, other_ref, grad_ref, mean_ref):
    count = grad_ref.shape[0]
    total = mine_ref[count : count + 1, :] + other_ref[count : count + 1, :]
    years = mine_ref[count + 1 : count + 2, :] + other_ref[count + 1 : count + 2, :]
    grad_ref[...] = (mine_ref[:count, :] + other_ref[:count, :]) * (scale / years)
    mean_ref[0] = (total / years)[0, 0]


def per_device(
    earnings, starts, lengths, block_count, trans_logits, init_logits, state_mean, log_sd
):
    slot_rows, periods = earnings.shape
    states = init_logits.shape[0]
    group = lax.axis_size(("hh", "per"))
    sides = lax.axis_size("per")
    cores = lax.axis_size("st")
    part = trans_logits.shape[0]
    steps = part * cores
    rows = states // lax.axis_size("hh")
    households = group * HB // cores
    parts = 2 if households <= 4 * HB else 1
    share = households // parts
    width = min(2 * HB, share)
    grids = share // width
    side = lax.axis_index("per")
    shaped = jax.ShapeDtypeStruct
    dma = pltpu.SemaphoreType.DMA

    along = lax.axis_size("hh")
    near = sides == 2 and along <= 8 and along & (along - 1) == 0

    swap = [(0, 1), (1, 0)]
    other_logits = lax.ppermute(trans_logits, "st", swap)
    row_shape = (periods // 2, slot_rows)
    vec_row = pltpu.VMEM((1, states), F32)
    packed, vectors = pl.pallas_call(
        pack_kernel,
        out_shape=[shaped(row_shape if near else (group,) + row_shape, F32), shaped((8, states), F32)],
        in_specs=[hbm()] * 7,
        out_specs=[vmem()] * 2,
        scratch_shapes=[
            pltpu.SMEM((1,), jnp.int32),
            pltpu.VMEM((periods, slot_rows), F32),
            pltpu.VMEM((slot_rows // HB, HB), jnp.int32),
            pltpu.VMEM((slot_rows // HB, HB), jnp.int32),
            vec_row,
            vec_row,
            vec_row,
            dma((7,)),
        ],
        name="pack",
    )(
        block_count, earnings.T, starts.reshape(-1, HB), lengths.reshape(-1, HB),
        init_logits.reshape(1, states), state_mean.reshape(1, states), log_sd.reshape(1, states),
    )
    first_shape = shaped((steps, 2 * states + EXTRA, states), BF16)
    half_logits = pltpu.VMEM(trans_logits.shape, BF16)
    early = (part + 1) // 2
    first_mat, kept_rows = pl.pallas_call(
        functools.partial(prep_own_kernel, (0, early)),
        out_shape=[first_shape, shaped(packed.shape, F32)],
        in_specs=[hbm()] * 2,
        out_specs=[vmem()] * 2,
        scratch_shapes=[half_logits, dma((2,))],
        compiler_params=params(4),
        name="prep_own",
    )(trans_logits, packed)

    def prep_rest(mat, after):
        return pl.pallas_call(
            functools.partial(prep_rest_kernel, (early, part)),
            out_shape=[first_shape, shaped((4, states, LANES), F32)],
            in_specs=[hbm(), hbm(), hbm(), vmem()],
            out_specs=[vmem()] * 2,
            scratch_shapes=[half_logits, pltpu.VMEM((8, states), F32), dma((2,))],
            input_output_aliases={3: 0},
            compiler_params=params(4),
            name="prep_rest",
        )(trans_logits, vectors, after, mat)

    def prep_other(mat, after):
        return pl.pallas_call(
            prep_other_kernel,
            out_shape=first_shape,
            in_specs=[hbm(), hbm(), vmem()],
            out_specs=vmem(),
            scratch_shapes=[half_logits, dma((1,))],
            input_output_aliases={2: 0},
            compiler_params=params(4),
            name="prep_other",
        )(other_logits, after, mat)

    if near:
        rows_here, sent, consts = kept_rows[None], packed[None], None
        bit = along // 2
        while bit:
            got = lax.ppermute(sent, "hh", [(i, i ^ bit) for i in range(along)])
            if bit < along // 2 and consts is None:
                first_mat, consts = prep_rest(first_mat, rows_here)
            after = rows_here if consts is None else consts
            rows_here = pl.pallas_call(
                functools.partial(join_kernel, bit),
                out_shape=shaped((2 * rows_here.shape[0],) + row_shape, F32),
                in_specs=[vmem(), vmem(), hbm()],
                out_specs=vmem(),
                compiler_params=params(2),
                name="join",
            )(rows_here, got, after)
            sent = rows_here
            bit //= 2
        if consts is None:
            first_mat, consts = prep_rest(first_mat, rows_here)
        gathered = [rows_here, lax.ppermute(rows_here, "per", swap)]
    else:
        gathered = [lax.all_to_all(packed, ("hh", "per"), split_axis=0, concat_axis=0, tiled=True)]
        first_mat, consts = prep_rest(first_mat, gathered[0])
    first_mat = prep_other(first_mat, gathered[0])

    def prep_second(after):
        return pl.pallas_call(
            prep_second_kernel,
            out_shape=[shaped((steps, 2 * states, states), BF16), shaped((steps, rows, states), F32)],
            in_specs=[hbm()] * 3,
            out_specs=[vmem()] * 2,
            scratch_shapes=[pltpu.VMEM((states, states), F32), half_logits, half_logits, dma((2,))],
            compiler_params=params(4),
            name="prep_second",
        )(trans_logits, other_logits, after)

    def whole(*shape):
        if grids == 1:
            return vmem()
        return pl.BlockSpec(shape, lambda g: (0,) * len(shape))

    def lanes(*lead):
        if grids == 1:
            return vmem()
        return pl.BlockSpec(lead + (width,), lambda g: (0,) * len(lead) + (g,))

    grid = (grids,) if grids > 1 else ()
    hist_shape = shaped((steps, states, share), BF16)
    state_shape = shaped((states + EXTRA, share), BF16)
    sel_shape = shaped((3, periods, 8, share), F32)
    swap_shape = shaped((steps * rows + 8, LANES), F32)
    counts_shape = shaped((steps, rows, states), F32)
    sums_shape = shaped((8, LANES), F32)
    hist_spec, state_spec, sel_spec = lanes(steps, states), lanes(states + EXTRA), lanes(3, periods, 8)
    const_spec = whole(4, states, LANES)

    def first_pass(index, state_in):
        resume = state_in is not None
        return pl.pallas_call(
            functools.partial(first_kernel, resume, grids, index, near),
            grid=grid,
            out_shape=[hist_shape, state_shape, sel_shape],
            in_specs=[whole(*x.shape) for x in gathered + [first_mat]] + [const_spec]
            + [state_spec] * resume,
            out_specs=[hist_spec, state_spec, sel_spec],
            scratch_shapes=[pltpu.VMEM((states, width), BF16), pltpu.VMEM((states, width), F32)],
            compiler_params=params(8 if grids == 1 else 32),
            name="first_pass",
        )(*gathered, first_mat, consts, *([state_in] if resume else []))

    def second_pass(kept, state_in, sums_in, last, extend):
        hist, own_state, sel = kept
        resume = sums_in is not None
        scratch = [
            pltpu.VMEM((states, width), BF16),
            pltpu.VMEM((states, width), F32),
            pltpu.VMEM((rows, width), BF16),
        ]
        counts_spec, sums_spec = whole(*counts_shape.shape), whole(*sums_shape.shape)
        if last:
            out_shape = [swap_shape] * 2
            scratch += [pltpu.VMEM(counts_shape.shape, F32), pltpu.VMEM(sums_shape.shape, F32)]
        else:
            out_shape = [counts_shape, sums_shape]
        out_specs = [whole(*x.shape) for x in out_shape]
        if extend:
            out_shape, out_specs = out_shape + [state_shape], out_specs + [state_spec]
        return pl.pallas_call(
            functools.partial(second_kernel, resume, last, extend, grids),
            grid=grid,
            out_shape=out_shape,
            in_specs=[sel_spec, whole(*second_mat.shape), const_spec, hist_spec, state_spec, state_spec]
            + [counts_spec, sums_spec] * resume
            + [whole(*row_probs.shape)] * last,
            out_specs=out_specs,
            scratch_shapes=scratch,
            compiler_params=params(8 if grids == 1 else 32),
            name="second_pass",
        )(
            sel, second_mat, consts, hist, own_state, state_in,
            *(sums_in if resume else []),
            *([row_probs] if last else []),
        )

    def hand_over(state, stage):
        moves = [(stage, stage + 1), (sides - 1 - stage, sides - 2 - stage)]
        return lax.ppermute(state, "per", moves)

    if sides == 2:
        kept = [first_pass(index, None) for index in range(parts)]
        arrived = [hand_over(each[1], 0) for each in kept]
        second_mat, row_probs = prep_second(kept[-1][1])
        sums = None
        for index in range(parts):
            sums = second_pass(kept[index], arrived[index], sums, index == parts - 1, False)
        mine, other = sums
    else:
        kept = [jnp.zeros(x.shape, x.dtype) for x in (hist_shape, state_shape, sel_shape)]
        done = [jnp.zeros(x.shape, x.dtype) for x in (swap_shape, swap_shape, state_shape)]
        second_mat, row_probs = prep_second(gathered[0])
        state = None
        for stage in range(sides):
            active = (side == stage) | (side == sides - 1 - stage)
            if stage < sides // 2:
                kept = lax.cond(
                    active, lambda x, kept: list(first_pass(0, x)), lambda x, kept: kept, state, kept
                )
                state = kept[1]
            else:
                done = lax.cond(
                    active,
                    lambda x, done: list(second_pass(kept, x, None, True, True)),
                    lambda x, done: done,
                    state,
                    done,
                )
                state = done[2]
            if stage < sides - 1:
                state = hand_over(state, stage)
        mine, other, _ = done
        total = jnp.where(side == sides // 2, mine[steps * rows], 0.0)
        total = lax.psum(total, "per")
        mine = mine.at[steps * rows].set(total)
        other = other.at[steps * rows].set(total)
    received = lax.ppermute(other, "st", swap)
    trans_grad, mean_loglik = pl.pallas_call(
        functools.partial(finish_kernel, float(states * states * periods)),
        out_shape=[shaped((steps * rows, LANES), F32), shaped((1,), F32)],
        in_specs=[vmem(), vmem()],
        out_specs=[vmem(), smem()],
        compiler_params=params(4),
        name="finish",
    )(mine, received)
    return (trans_grad.reshape(steps, rows, LANES), mean_loglik)


def solution(mesh):
    placed = (
        P(("hh", "per"), None),
        P(("hh", "per")),
        P(("hh", "per")),
        P(("hh", "per")),
        P(("grp", "per", "st"), None, None),
        P("grp"),
        P("grp"),
        P("grp"),
    )
    return jax.shard_map(
        per_device,
        mesh=mesh,
        in_specs=placed,
        out_specs=(P(("grp", "per"), "hh", "st"), P("grp")),
        check_vma=False,
    )
```

```python
import functools

import jax
import jax.numpy as jnp
from jax import lax
from jax.experimental import pallas as pl
from jax.experimental.pallas import tpu as pltpu
from jax.sharding import PartitionSpec as P

HB = 128
LANES = 128
HALF = HB // 2
SEEN = 16.0
F32 = jnp.float32
BF16 = jnp.bfloat16
LOG2E = 1.4426950408889634
LN2 = 0.6931471805599453
EXTRA = 16


def vmem():
    return pl.BlockSpec(memory_space=pltpu.VMEM)


def smem():
    return pl.BlockSpec(memory_space=pltpu.SMEM)


def hbm():
    return pl.BlockSpec(memory_space=pltpu.HBM)


def params(mebibytes):
    return pltpu.CompilerParams(vmem_limit_bytes=mebibytes * 1024 * 1024)


def core_index():
    return lax.axis_index("st")


def is_forward_first():
    return 2 * lax.axis_index("per") < lax.axis_size("per")


def tiles(width):
    return [slice(q, q + LANES) for q in range(0, width, LANES)]


def fetch(pairs, sems):
    copies = [pltpu.make_async_copy(src, dst, sems.at[i]) for i, (src, dst) in enumerate(pairs)]
    for copy in copies:
        copy.start()
    for copy in copies:
        copy.wait()


def pack_kernel(
    count_any, earn_any, start_any, len_any, init_any, mean_any, sd_any, out_ref, vec_ref,
    count_ref, earn_ref, start_ref, len_ref, init_ref, mean_ref, sd_ref, sems,
):
    fetch(
        (
            (count_any, count_ref), (earn_any, earn_ref), (start_any, start_ref), (len_any, len_ref),
            (init_any, init_ref), (mean_any, mean_ref), (sd_any, sd_ref),
        ),
        sems,
    )
    periods, slot_rows = earn_ref.shape
    core = core_index()
    low_lane = lax.broadcasted_iota(jnp.int32, (periods // 2, HB), 1) < HALF
    time = lax.broadcasted_iota(jnp.int32, (periods, HB), 0)
    for slot in range(slot_rows // HB):
        cols = slice(slot * HB, (slot + 1) * HB)
        begin = start_ref[slot : slot + 1, :]
        seen = (time >= begin) & (time < begin + len_ref[slot : slot + 1, :])
        live = slot < count_ref[0]
        shift = jnp.where(live, jnp.where(seen, SEEN, 0.0), -SEEN)
        value = earn_ref[:, cols] + shift
        early, late = value[: periods // 2], value[periods // 2 :]
        turned = pltpu.roll(jnp.where(core == 0, late, early), HALF, 1)
        packed = jnp.where(low_lane, jnp.where(core == 0, early, turned), jnp.where(core == 0, turned, late))
        for to in range(out_ref.shape[0]):
            out_ref[to, :, cols] = packed
    raised = jnp.exp(init_ref[...])
    start = raised / jnp.sum(raised, axis=1, keepdims=True)
    row = lax.broadcasted_iota(jnp.int32, vec_ref.shape, 0)
    power = (-0.5 * LOG2E) * jnp.exp(-2.0 * sd_ref[...])
    vec_ref[...] = jnp.where(
        row == 0, start, jnp.where(row == 1, mean_ref[...], jnp.where(row == 2, power, -LOG2E * sd_ref[...]))
    )


def put(ref, at, value):
    states = value.shape[0]
    high = value.astype(BF16)
    ref[at, :states, :] = high
    ref[at, states : 2 * states, :] = (value - high.astype(F32)).astype(BF16)


def fill_periods(mat, row_probs, scratch, turned_pass, source, ref):
    @pl.loop(0, ref.shape[0])
    def _(i):
        at = source * ref.shape[0] + i
        lifted = jnp.exp(ref[i].astype(F32))
        probs = lifted * (1.0 / jnp.sum(lifted, axis=1, keepdims=True))
        if row_probs is not None:
            rows = row_probs.shape[1]
            scratch[...] = probs
            row_probs[at] = scratch[own_rows(lax.axis_index("hh") * rows, rows), :]

        @pl.when(turned_pass)
        def _():
            put(mat, at, probs.T)

        @pl.when(jnp.logical_not(turned_pass))
        def _():
            put(mat, at, probs)


def prep_first_kernel(own_any, other_any, vec_any, after_any, mat, consts, own_ref, other_ref, vec_ref, sems):
    fetch(((own_any, own_ref), (other_any, other_ref), (vec_any, vec_ref)), sems)
    part, states, _ = own_ref.shape
    for i in range(4):
        consts[i] = jnp.broadcast_to(vec_ref[i : i + 1, :], (LANES, states)).T
    start = vec_ref[:1, :]
    start_high = start.astype(BF16).astype(F32)
    row = lax.broadcasted_iota(jnp.int32, (EXTRA, states), 0)
    start_rows = jnp.where(row == 0, start_high, jnp.where(row == 1, start - start_high, 0.0)).astype(BF16)
    for k in range(mat.shape[0]):
        mat[k, 2 * states :, :] = start_rows
    for source, ref in ((core_index(), own_ref), (1 - core_index(), other_ref)):
        fill_periods(mat, None, None, is_forward_first(), source, ref)


def prep_second_kernel(own_any, other_any, after_any, mat, row_probs, scratch, own_ref, other_ref, sems):
    fetch(((own_any, own_ref), (other_any, other_ref)), sems)
    for source, ref in ((core_index(), own_ref), (1 - core_index(), other_ref)):
        fill_periods(mat, row_probs, scratch, jnp.logical_not(is_forward_first()), source, ref)


def emission(sel_ref, consts, step_now, cols):
    gap = sel_ref[0, step_now, :1, cols] - consts[1]
    power = gap * gap * consts[2] + consts[3]
    top = jnp.max(power, axis=0, keepdims=True)
    return jnp.exp2(power - top), top


def is_moving(sel_ref, step_now, cols):
    return sel_ref[1, step_now, :1, cols] > 0.5


def is_seen(sel_ref, step_now, cols):
    return sel_ref[2, step_now, :1, cols] > 0.5


def column_sum(x):
    return jnp.sum(x, axis=0, keepdims=True)


def own_rows(row_begin, rows):
    return pl.ds(pl.multiple_of(row_begin, rows), rows)


def outer_sum(weights_ref, carried):
    return lax.dot_general(weights_ref[...], carried, (((1,), (1,)), ((), ())), preferred_element_type=F32)


def run_forward(lead, mat, hist, sel_ref, consts, ab_ref, logs, second=None):
    steps, states, width = hist.shape
    cuts = tiles(width)
    inverse = [1.0 / column_sum(ab_ref[:, cols].astype(F32)) for cols in cuts]
    for k in range(steps):
        step_now = lead + k
        if second is None:
            hist[k] = ab_ref[...]
        else:
            weights_ref, counts_ref, row_begin = second
            own_alpha = ab_ref[own_rows(row_begin, weights_ref.shape[0]), :].astype(F32)
        for q, cols in enumerate(cuts):
            product = jnp.dot(mat[k, : 2 * states, :], ab_ref[:, cols], preferred_element_type=F32)
            moved = (product[:states] + product[states:]) * inverse[q]
            moving = is_moving(sel_ref, step_now, cols)
            if second is not None:
                total = column_sum(moved * hist[k, :, cols].astype(F32))
                weight = jnp.where(moving, inverse[q] / total, 0.0)
                weights_ref[:, cols] = (own_alpha[:, cols] * weight).astype(BF16)
            emit, top = emission(sel_ref, consts, step_now, cols)
            joint = jnp.where(moving, moved, consts[0]) * emit
            scale = column_sum(joint)
            if second is None:
                seen = is_seen(sel_ref, step_now, cols)
                logs[q] = logs[q] + jnp.where(seen, jnp.log(scale) + top * LN2, 0.0)
            inverse[q] = 1.0 / scale
            ab_ref[:, cols] = joint.astype(BF16)
        if second is not None:
            counts_ref[k] += outer_sum(weights_ref, hist[k])
    return logs


def run_backward(lead, mat, hist, sel_ref, consts, back_ref, ub_ref, logs, second=None):
    steps, states, width = hist.shape
    cuts = tiles(width)
    for k in reversed(range(steps)):
        step_now = lead + k
        shrink = []
        for q, cols in enumerate(cuts):
            emit, top = emission(sel_ref, consts, step_now, cols)
            carried = emit * back_ref[:, cols]
            size = column_sum(carried)
            if second is None:
                seen = is_seen(sel_ref, step_now, cols)
                logs[q] = logs[q] + jnp.where(seen, jnp.log(size) + top * LN2, 0.0)
            shrink.append(1.0 / size)
            ub_ref[:, cols] = carried.astype(BF16)
        if second is None:
            hist[k] = ub_ref[...]
        else:
            weights_ref, counts_ref, row_begin = second
            own_alpha = hist[k, own_rows(row_begin, weights_ref.shape[0]), :].astype(F32)
        for q, cols in enumerate(cuts):
            product = jnp.dot(mat[k], ub_ref[:, cols], preferred_element_type=F32)
            moving = is_moving(sel_ref, step_now, cols)
            pulled = (product[:states] + product[states : 2 * states]) * shrink[q]
            if second is None:
                seen = is_seen(sel_ref, step_now, cols)
                begun = column_sum(product[2 * states :]) * shrink[q]
                rest = jnp.where(seen, begun, back_ref[:, cols])
            else:
                total = column_sum(pulled * hist[k, :, cols].astype(F32))
                weight = jnp.where(moving, shrink[q] / total, 0.0)
                weights_ref[:, cols] = (own_alpha[:, cols] * weight).astype(BF16)
                rest = 1.0
            back_ref[:, cols] = jnp.where(moving, pulled, rest)
        if second is not None:
            counts_ref[k] += outer_sum(weights_ref, ub_ref[...])
    return logs


def put_state(state_out, values, logs):
    states = state_out.shape[0] - EXTRA
    state_out[:states, :] = values
    for q, cols in enumerate(tiles(state_out.shape[1])):
        high = logs[q].astype(BF16).astype(F32)
        middle = (logs[q] - high).astype(BF16).astype(F32)
        row = lax.broadcasted_iota(jnp.int32, (EXTRA, LANES), 0)
        piece = jnp.where(
            row == 0, high, jnp.where(row == 1, middle, jnp.where(row == 2, logs[q] - high - middle, 0.0))
        )
        state_out[states:, cols] = piece.astype(BF16)


def state_logs(state_ref):
    states = state_ref.shape[0] - EXTRA
    return [column_sum(state_ref[states:, cols].astype(F32)) for cols in tiles(state_ref.shape[1])]


def first_kernel(resume, grids, part, rows_ref, mat, consts, *refs):
    state_in = refs[0] if resume else None
    hist, state_out, sel_ref, ab_ref, back_ref = refs[-5:]
    chunk = part * grids + (pl.program_id(0) if grids > 1 else 0)
    steps, states, width = hist.shape
    forward_first, lead = is_forward_first(), lax.axis_index("per") * steps
    cuts = tiles(width)
    group, half_periods, slot_rows = rows_ref.shape
    tops = 2 * len(cuts)

    def scan_source(d, carry):
        rank, picked = carry
        for slot in range(slot_rows // HB):
            cols = slice(slot * HB, (slot + 1) * HB)
            block = rows_ref[d, :, cols]
            live = block > -0.5 * SEEN
            picked = [jnp.where(live & (rank == chunk * tops + i), block, old) for i, old in enumerate(picked)]
            rank = rank + live.astype(jnp.int32)
        return rank, picked

    carry = (jnp.zeros((half_periods, HB), jnp.int32), [jnp.zeros((half_periods, HB), F32)] * tops)
    if group <= 8:
        for d in range(group):
            carry = scan_source(d, carry)
    else:
        carry = lax.fori_loop(0, group, scan_source, carry)
    low_lane = lax.broadcasted_iota(jnp.int32, (half_periods, HB), 1) < HALF
    for q, cols in enumerate(cuts):
        left, right = carry[1][2 * q], carry[1][2 * q + 1]
        before = jnp.zeros((1, HB), F32)
        for late in range(2):
            value = (
                jnp.where(low_lane, pltpu.roll(left, HALF, 1), right)
                if late
                else jnp.where(low_lane, left, pltpu.roll(right, HALF, 1))
            )
            seen = value > 0.5 * SEEN
            earn = jnp.where(seen, value - SEEN, value)
            seen = seen.astype(F32)
            for i in range(half_periods):
                at = late * half_periods + i
                now = seen[i : i + 1]
                sel_ref[0, at, :, cols] = jnp.broadcast_to(earn[i : i + 1], (8, HB))
                sel_ref[1, at, :, cols] = jnp.broadcast_to(now * before, (8, HB))
                sel_ref[2, at, :, cols] = jnp.broadcast_to(now, (8, HB))
                before = now
    zeros = [jnp.zeros((1, LANES), F32) for _ in cuts]

    @pl.when(forward_first)
    def _():
        if resume:
            ab_ref[...] = state_in[:states, :]
        else:
            for cols in cuts:
                ab_ref[:, cols] = consts[0].astype(BF16)
        logs = state_logs(state_in) if resume else list(zeros)
        logs = run_forward(lead, mat, hist, sel_ref, consts, ab_ref, logs)
        put_state(state_out, ab_ref[...], logs)

    @pl.when(jnp.logical_not(forward_first))
    def _():
        if resume:
            back_ref[...] = state_in[:states, :].astype(F32)
        else:
            back_ref[...] = jnp.ones_like(back_ref)
        logs = state_logs(state_in) if resume else list(zeros)
        logs = run_backward(lead, mat, hist, sel_ref, consts, back_ref, ab_ref, logs)
        put_state(state_out, back_ref[...].astype(BF16), logs)


def second_kernel(resume, last, extend, grids, *refs):
    refs = list(refs)
    sel_ref, mat, consts, hist, own_state, state_in = (refs.pop(0) for _ in range(6))
    counts_in, sums_in = (refs.pop(0), refs.pop(0)) if resume else (None, None)
    row_probs = refs.pop(0) if last else None
    mine_ref, other_ref = (refs.pop(0), refs.pop(0)) if last else (None, None)
    counts_out, sums_out = (None, None) if last else (refs.pop(0), refs.pop(0))
    state_out = refs.pop(0) if extend else None
    ab_ref, back_ref, weights_ref = refs[:3]
    counts_ref, sums_ref = refs[3:] if last else (counts_out, sums_out)
    chunk = pl.program_id(0) if grids > 1 else 0
    steps, states, width = hist.shape
    core, forward_first = core_index(), is_forward_first()
    row_begin = lax.axis_index("hh") * counts_ref.shape[1]
    lead = lax.axis_index("per") * steps
    second = (weights_ref, counts_ref, row_begin)

    @pl.when(chunk == 0)
    def _():
        if resume:
            counts_ref[...] = counts_in[...]
            sums_ref[...] = sums_in[...]
        else:
            counts_ref[...] = jnp.zeros_like(counts_ref)
            sums_ref[...] = jnp.zeros_like(sums_ref)

    def add_sums(alpha_ref, other_state):
        total = jnp.zeros((1, LANES), F32)
        years = jnp.zeros((8, LANES), F32)
        for cols, here, there in zip(tiles(width), state_logs(alpha_ref), state_logs(other_state)):
            alpha = alpha_ref[:states, cols].astype(F32)
            meet = column_sum(alpha * other_state[:states, cols].astype(F32))
            total += here + there + jnp.log(meet / column_sum(alpha))
            years += jnp.sum(sel_ref[2, :, :, cols], axis=0)
        total = jnp.broadcast_to(jnp.sum(total, axis=1, keepdims=True), (1, LANES))
        years = jnp.broadcast_to(jnp.sum(years[:1], axis=1, keepdims=True), (1, LANES))
        row = lax.broadcasted_iota(jnp.int32, (8, LANES), 0)
        sums_ref[...] += jnp.where(row == 0, total, jnp.where(row == 1, years, 0.0))

    zeros = [jnp.zeros((1, LANES), F32) for _ in tiles(width)]

    @pl.when(jnp.logical_not(forward_first))
    def _():
        add_sums(state_in, own_state)
        ab_ref[...] = state_in[:states, :]
        run_forward(lead, mat, hist, sel_ref, consts, ab_ref, list(zeros), second)
        if extend:
            put_state(state_out, ab_ref[...], zeros)

    @pl.when(forward_first)
    def _():
        add_sums(own_state, state_in)
        back_ref[...] = state_in[:states, :].astype(F32)
        run_backward(lead, mat, hist, sel_ref, consts, back_ref, ab_ref, list(zeros), second)
        if extend:
            put_state(state_out, back_ref[...].astype(BF16), zeros)

    if last:

        @pl.when(chunk == grids - 1)
        def _():
            rows = counts_ref.shape[1]
            for k in range(steps):
                probs = row_probs[k]
                weighted = probs * counts_ref[k]
                grad = weighted - probs * jnp.sum(weighted, axis=1, keepdims=True)
                for side in range(2):
                    piece = grad[:, side * LANES : (side + 1) * LANES]
                    at = slice(k * rows, (k + 1) * rows)

                    @pl.when(core == side)
                    def _():
                        mine_ref[at, :] = piece

                    @pl.when(core != side)
                    def _():
                        other_ref[at, :] = piece

            mine_ref[steps * rows :, :] = sums_ref[...]
            other_ref[steps * rows :, :] = sums_ref[...]


def finish_kernel(scale, mine_ref, other_ref, grad_ref, mean_ref):
    count = grad_ref.shape[0]
    total = mine_ref[count : count + 1, :] + other_ref[count : count + 1, :]
    years = mine_ref[count + 1 : count + 2, :] + other_ref[count + 1 : count + 2, :]
    grad_ref[...] = (mine_ref[:count, :] + other_ref[:count, :]) * (scale / years)
    mean_ref[0] = (total / years)[0, 0]


def per_device(
    earnings, starts, lengths, block_count, trans_logits, init_logits, state_mean, log_sd
):
    slot_rows, periods = earnings.shape
    states = init_logits.shape[0]
    group = lax.axis_size(("hh", "per"))
    sides = lax.axis_size("per")
    cores = lax.axis_size("st")
    part = trans_logits.shape[0]
    steps = part * cores
    rows = states // lax.axis_size("hh")
    households = group * HB // cores
    parts = 2 if households <= 4 * HB else 1
    share = households // parts
    width = min(2 * HB, share)
    grids = share // width
    side = lax.axis_index("per")
    shaped = jax.ShapeDtypeStruct
    dma = pltpu.SemaphoreType.DMA

    swap = [(0, 1), (1, 0)]
    other_logits = lax.ppermute(trans_logits, "st", swap)
    vec_row = pltpu.VMEM((1, states), F32)
    packed, vectors = pl.pallas_call(
        pack_kernel,
        out_shape=[shaped((group, periods // 2, slot_rows), F32), shaped((8, states), F32)],
        in_specs=[hbm()] * 7,
        out_specs=[vmem()] * 2,
        scratch_shapes=[
            pltpu.SMEM((1,), jnp.int32),
            pltpu.VMEM((periods, slot_rows), F32),
            pltpu.VMEM((slot_rows // HB, HB), jnp.int32),
            pltpu.VMEM((slot_rows // HB, HB), jnp.int32),
            vec_row,
            vec_row,
            vec_row,
            dma((7,)),
        ],
        name="pack",
    )(
        block_count, earnings.T, starts.reshape(-1, HB), lengths.reshape(-1, HB),
        init_logits.reshape(1, states), state_mean.reshape(1, states), log_sd.reshape(1, states),
    )
    gathered = lax.all_to_all(packed, ("hh", "per"), split_axis=0, concat_axis=0, tiled=True)
    half_logits = pltpu.VMEM(trans_logits.shape, BF16)
    first_mat, consts = pl.pallas_call(
        prep_first_kernel,
        out_shape=[shaped((steps, 2 * states + EXTRA, states), BF16), shaped((4, states, LANES), F32)],
        in_specs=[hbm()] * 4,
        out_specs=[vmem()] * 2,
        scratch_shapes=[half_logits, half_logits, pltpu.VMEM((8, states), F32), dma((3,))],
        compiler_params=params(4),
        name="prep_first",
    )(trans_logits, other_logits, vectors, packed)

    def prep_second(after):
        return pl.pallas_call(
            prep_second_kernel,
            out_shape=[shaped((steps, 2 * states, states), BF16), shaped((steps, rows, states), F32)],
            in_specs=[hbm()] * 3,
            out_specs=[vmem()] * 2,
            scratch_shapes=[pltpu.VMEM((states, states), F32), half_logits, half_logits, dma((2,))],
            compiler_params=params(4),
            name="prep_second",
        )(trans_logits, other_logits, after)

    def whole(*shape):
        if grids == 1:
            return vmem()
        return pl.BlockSpec(shape, lambda g: (0,) * len(shape))

    def lanes(*lead):
        if grids == 1:
            return vmem()
        return pl.BlockSpec(lead + (width,), lambda g: (0,) * len(lead) + (g,))

    grid = (grids,) if grids > 1 else ()
    hist_shape = shaped((steps, states, share), BF16)
    state_shape = shaped((states + EXTRA, share), BF16)
    sel_shape = shaped((3, periods, 8, share), F32)
    swap_shape = shaped((steps * rows + 8, LANES), F32)
    counts_shape = shaped((steps, rows, states), F32)
    sums_shape = shaped((8, LANES), F32)
    hist_spec, state_spec, sel_spec = lanes(steps, states), lanes(states + EXTRA), lanes(3, periods, 8)
    const_spec = whole(4, states, LANES)

    def first_pass(index, state_in):
        resume = state_in is not None
        return pl.pallas_call(
            functools.partial(first_kernel, resume, grids, index),
            grid=grid,
            out_shape=[hist_shape, state_shape, sel_shape],
            in_specs=[whole(*gathered.shape), whole(*first_mat.shape), const_spec]
            + [state_spec] * resume,
            out_specs=[hist_spec, state_spec, sel_spec],
            scratch_shapes=[pltpu.VMEM((states, width), BF16), pltpu.VMEM((states, width), F32)],
            compiler_params=params(8 if grids == 1 else 32),
            name="first_pass",
        )(gathered, first_mat, consts, *([state_in] if resume else []))

    def second_pass(kept, state_in, sums_in, last, extend):
        hist, own_state, sel = kept
        resume = sums_in is not None
        scratch = [
            pltpu.VMEM((states, width), BF16),
            pltpu.VMEM((states, width), F32),
            pltpu.VMEM((rows, width), BF16),
        ]
        counts_spec, sums_spec = whole(*counts_shape.shape), whole(*sums_shape.shape)
        if last:
            out_shape = [swap_shape] * 2
            scratch += [pltpu.VMEM(counts_shape.shape, F32), pltpu.VMEM(sums_shape.shape, F32)]
        else:
            out_shape = [counts_shape, sums_shape]
        out_specs = [whole(*x.shape) for x in out_shape]
        if extend:
            out_shape, out_specs = out_shape + [state_shape], out_specs + [state_spec]
        return pl.pallas_call(
            functools.partial(second_kernel, resume, last, extend, grids),
            grid=grid,
            out_shape=out_shape,
            in_specs=[sel_spec, whole(*second_mat.shape), const_spec, hist_spec, state_spec, state_spec]
            + [counts_spec, sums_spec] * resume
            + [whole(*row_probs.shape)] * last,
            out_specs=out_specs,
            scratch_shapes=scratch,
            compiler_params=params(8 if grids == 1 else 32),
            name="second_pass",
        )(
            sel, second_mat, consts, hist, own_state, state_in,
            *(sums_in if resume else []),
            *([row_probs] if last else []),
        )

    def hand_over(state, stage):
        moves = [(stage, stage + 1), (sides - 1 - stage, sides - 2 - stage)]
        return lax.ppermute(state, "per", moves)

    if sides == 2:
        kept = [first_pass(index, None) for index in range(parts)]
        arrived = [hand_over(each[1], 0) for each in kept]
        second_mat, row_probs = prep_second(kept[-1][1])
        sums = None
        for index in range(parts):
            sums = second_pass(kept[index], arrived[index], sums, index == parts - 1, False)
        mine, other = sums
    else:
        kept = [jnp.zeros(x.shape, x.dtype) for x in (hist_shape, state_shape, sel_shape)]
        done = [jnp.zeros(x.shape, x.dtype) for x in (swap_shape, swap_shape, state_shape)]
        second_mat, row_probs = prep_second(gathered)
        state = None
        for stage in range(sides):
            active = (side == stage) | (side == sides - 1 - stage)
            if stage < sides // 2:
                kept = lax.cond(
                    active, lambda x, kept: list(first_pass(0, x)), lambda x, kept: kept, state, kept
                )
                state = kept[1]
            else:
                done = lax.cond(
                    active,
                    lambda x, done: list(second_pass(kept, x, None, True, True)),
                    lambda x, done: done,
                    state,
                    done,
                )
                state = done[2]
            if stage < sides - 1:
                state = hand_over(state, stage)
        mine, other, _ = done
        total = jnp.where(side == sides // 2, mine[steps * rows], 0.0)
        total = lax.psum(total, "per")
        mine = mine.at[steps * rows].set(total)
        other = other.at[steps * rows].set(total)
    received = lax.ppermute(other, "st", swap)
    trans_grad, mean_loglik = pl.pallas_call(
        functools.partial(finish_kernel, float(states * states * periods)),
        out_shape=[shaped((steps * rows, LANES), F32), shaped((1,), F32)],
        in_specs=[vmem(), vmem()],
        out_specs=[vmem(), smem()],
        compiler_params=params(4),
        name="finish",
    )(mine, received)
    return (trans_grad.reshape(steps, rows, LANES), mean_loglik)


def solution(mesh):
    placed = (
        P(("hh", "per"), None),
        P(("hh", "per")),
        P(("hh", "per")),
        P(("hh", "per")),
        P(("grp", "per", "st"), None, None),
        P("grp"),
        P("grp"),
        P("grp"),
    )
    return jax.shard_map(
        per_device,
        mesh=mesh,
        in_specs=placed,
        out_specs=(P(("grp", "per"), "hh", "st"), P("grp")),
        check_vma=False,
    )
```

```python
import functools

import jax
import jax.numpy as jnp
from jax import lax
from jax.experimental import pallas as pl
from jax.experimental.pallas import tpu as pltpu
from jax.sharding import PartitionSpec as P

HB = 128
LANES = 128
HALF = HB // 2
SEEN = 16.0
F32 = jnp.float32
BF16 = jnp.bfloat16
LOG2E = 1.4426950408889634
LN2 = 0.6931471805599453
EXTRA = 16
PACK = 16


def vmem():
    return pl.BlockSpec(memory_space=pltpu.VMEM)


def smem():
    return pl.BlockSpec(memory_space=pltpu.SMEM)


def hbm():
    return pl.BlockSpec(memory_space=pltpu.HBM)


def params(mebibytes):
    return pltpu.CompilerParams(vmem_limit_bytes=mebibytes * 1024 * 1024)


def core_index():
    return lax.axis_index("st")


def is_forward_first():
    return 2 * lax.axis_index("per") < lax.axis_size("per")


def tiles(width):
    return [slice(q, q + LANES) for q in range(0, width, LANES)]


def fetch(pairs, sems):
    copies = [pltpu.make_async_copy(src, dst, sems.at[i]) for i, (src, dst) in enumerate(pairs)]
    for copy in copies:
        copy.start()
    for copy in copies:
        copy.wait()


def pack_kernel(
    count_any, earn_any, start_any, len_any, init_any, mean_any, sd_any, out_ref, vec_ref,
    count_ref, earn_ref, start_ref, len_ref, init_ref, mean_ref, sd_ref, sems,
):
    fetch(
        (
            (count_any, count_ref), (earn_any, earn_ref), (start_any, start_ref), (len_any, len_ref),
            (init_any, init_ref), (mean_any, mean_ref), (sd_any, sd_ref),
        ),
        sems,
    )
    periods, slot_rows = earn_ref.shape
    core = core_index()
    low_lane = lax.broadcasted_iota(jnp.int32, (periods // 2, HB), 1) < HALF
    time = lax.broadcasted_iota(jnp.int32, (periods, HB), 0)
    for slot in range(slot_rows // HB):
        cols = slice(slot * HB, (slot + 1) * HB)
        begin = start_ref[slot : slot + 1, :]
        seen = (time >= begin) & (time < begin + len_ref[slot : slot + 1, :])
        live = slot < count_ref[0]
        shift = jnp.where(live, jnp.where(seen, SEEN, 0.0), -SEEN)
        value = earn_ref[:, cols] + shift
        early, late = value[: periods // 2], value[periods // 2 :]
        turned = pltpu.roll(jnp.where(core == 0, late, early), HALF, 1)
        packed = jnp.where(low_lane, jnp.where(core == 0, early, turned), jnp.where(core == 0, turned, late))
        for to in range(out_ref.shape[0]):
            out_ref[to, :, cols] = packed
    raised = jnp.exp(init_ref[...])
    start = raised / jnp.sum(raised, axis=1, keepdims=True)
    row = lax.broadcasted_iota(jnp.int32, vec_ref.shape, 0)
    power = (-0.5 * LOG2E) * jnp.exp(-2.0 * sd_ref[...])
    vec_ref[...] = jnp.where(
        row == 0, start, jnp.where(row == 1, mean_ref[...], jnp.where(row == 2, power, -LOG2E * sd_ref[...]))
    )


def put(ref, at, value):
    states = value.shape[0]
    high = value.astype(BF16)
    low = (value - high.astype(F32)).astype(BF16)
    ref[at, : states // PACK, :PACK, :] = high.reshape(states // PACK, PACK, states)
    ref[at, : states // PACK, PACK:, :] = low.reshape(states // PACK, PACK, states)


def both_halves(mat, state):
    blocks, rows, states = mat.shape
    product = jnp.dot(mat.reshape(blocks * rows, states), state, preferred_element_type=F32)
    product = product.reshape(blocks, rows, state.shape[1])
    main = product[: states // PACK]
    main = (main[:, :PACK] + main[:, PACK:]).reshape(states, state.shape[1])
    return main, product[states // PACK :]


def fill_periods(mat, row_probs, scratch, turned_pass, source, ref):
    @pl.loop(0, ref.shape[0])
    def _(i):
        at = source * ref.shape[0] + i
        lifted = jnp.exp(ref[i].astype(F32))
        probs = lifted * (1.0 / jnp.sum(lifted, axis=1, keepdims=True))
        if row_probs is not None:
            rows = row_probs.shape[1]
            scratch[...] = probs
            row_probs[at] = scratch[own_rows(lax.axis_index("hh") * rows, rows), :]

        @pl.when(turned_pass)
        def _():
            put(mat, at, probs.T)

        @pl.when(jnp.logical_not(turned_pass))
        def _():
            put(mat, at, probs)


def prep_first_kernel(own_any, other_any, vec_any, after_any, mat, consts, own_ref, other_ref, vec_ref, sems):
    fetch(((own_any, own_ref), (other_any, other_ref), (vec_any, vec_ref)), sems)
    part, states, _ = own_ref.shape
    for i in range(4):
        consts[i] = jnp.broadcast_to(vec_ref[i : i + 1, :], (LANES, states)).T
    start = vec_ref[:1, :]
    start_high = start.astype(BF16).astype(F32)
    row = lax.broadcasted_iota(jnp.int32, (2 * PACK, states), 0)
    start_rows = jnp.where(row == 0, start_high, jnp.where(row == 1, start - start_high, 0.0)).astype(BF16)
    for k in range(mat.shape[0]):
        mat[k, states // PACK] = start_rows
    for source, ref in ((core_index(), own_ref), (1 - core_index(), other_ref)):
        fill_periods(mat, None, None, is_forward_first(), source, ref)


def prep_second_kernel(own_any, other_any, after_any, mat, row_probs, scratch, own_ref, other_ref, sems):
    fetch(((own_any, own_ref), (other_any, other_ref)), sems)
    for source, ref in ((core_index(), own_ref), (1 - core_index(), other_ref)):
        fill_periods(mat, row_probs, scratch, jnp.logical_not(is_forward_first()), source, ref)


def emission(sel_ref, consts, step_now, cols):
    gap = sel_ref[0, step_now, :1, cols] - consts[1]
    power = gap * gap * consts[2] + consts[3]
    top = jnp.max(power, axis=0, keepdims=True)
    return jnp.exp2(power - top), top


def is_moving(sel_ref, step_now, cols):
    return sel_ref[1, step_now, :1, cols] > 0.5


def is_seen(sel_ref, step_now, cols):
    return sel_ref[2, step_now, :1, cols] > 0.5


def column_sum(x):
    return jnp.sum(x, axis=0, keepdims=True)


def own_rows(row_begin, rows):
    return pl.ds(pl.multiple_of(row_begin, rows), rows)


def outer_sum(weights_ref, carried):
    return lax.dot_general(weights_ref[...], carried, (((1,), (1,)), ((), ())), preferred_element_type=F32)


def run_forward(lead, mat, hist, sel_ref, consts, ab_ref, logs, second=None):
    steps, states, width = hist.shape
    cuts = tiles(width)
    inverse = [1.0 / column_sum(ab_ref[:, cols].astype(F32)) for cols in cuts]
    for k in range(steps):
        step_now = lead + k
        if second is None:
            hist[k] = ab_ref[...]
        else:
            weights_ref, counts_ref, row_begin = second
            own_alpha = ab_ref[own_rows(row_begin, weights_ref.shape[0]), :].astype(F32)
        for q, cols in enumerate(cuts):
            moved, _ = both_halves(mat[k, : states // PACK], ab_ref[:, cols])
            moved = moved * inverse[q]
            moving = is_moving(sel_ref, step_now, cols)
            if second is not None:
                total = column_sum(moved * hist[k, :, cols].astype(F32))
                weight = jnp.where(moving, inverse[q] / total, 0.0)
                weights_ref[:, cols] = (own_alpha[:, cols] * weight).astype(BF16)
            emit, top = emission(sel_ref, consts, step_now, cols)
            joint = jnp.where(moving, moved, consts[0]) * emit
            scale = column_sum(joint)
            if second is None:
                seen = is_seen(sel_ref, step_now, cols)
                logs[q] = logs[q] + jnp.where(seen, jnp.log(scale) + top * LN2, 0.0)
            inverse[q] = 1.0 / scale
            ab_ref[:, cols] = joint.astype(BF16)
        if second is not None:
            counts_ref[k] += outer_sum(weights_ref, hist[k])
    return logs


def run_backward(lead, mat, hist, sel_ref, consts, back_ref, ub_ref, logs, second=None):
    steps, states, width = hist.shape
    cuts = tiles(width)
    for k in reversed(range(steps)):
        step_now = lead + k
        shrink = []
        for q, cols in enumerate(cuts):
            emit, top = emission(sel_ref, consts, step_now, cols)
            carried = emit * back_ref[:, cols]
            size = column_sum(carried)
            if second is None:
                seen = is_seen(sel_ref, step_now, cols)
                logs[q] = logs[q] + jnp.where(seen, jnp.log(size) + top * LN2, 0.0)
            shrink.append(1.0 / size)
            ub_ref[:, cols] = carried.astype(BF16)
        if second is None:
            hist[k] = ub_ref[...]
        else:
            weights_ref, counts_ref, row_begin = second
            own_alpha = hist[k, own_rows(row_begin, weights_ref.shape[0]), :].astype(F32)
        for q, cols in enumerate(cuts):
            pulled, more = both_halves(mat[k], ub_ref[:, cols])
            moving = is_moving(sel_ref, step_now, cols)
            pulled = pulled * shrink[q]
            if second is None:
                seen = is_seen(sel_ref, step_now, cols)
                begun = column_sum(more[0]) * shrink[q]
                rest = jnp.where(seen, begun, back_ref[:, cols])
            else:
                total = column_sum(pulled * hist[k, :, cols].astype(F32))
                weight = jnp.where(moving, shrink[q] / total, 0.0)
                weights_ref[:, cols] = (own_alpha[:, cols] * weight).astype(BF16)
                rest = 1.0
            back_ref[:, cols] = jnp.where(moving, pulled, rest)
        if second is not None:
            counts_ref[k] += outer_sum(weights_ref, ub_ref[...])
    return logs


def put_state(state_out, values, logs):
    states = state_out.shape[0] - EXTRA
    state_out[:states, :] = values
    for q, cols in enumerate(tiles(state_out.shape[1])):
        high = logs[q].astype(BF16).astype(F32)
        middle = (logs[q] - high).astype(BF16).astype(F32)
        row = lax.broadcasted_iota(jnp.int32, (EXTRA, LANES), 0)
        piece = jnp.where(
            row == 0, high, jnp.where(row == 1, middle, jnp.where(row == 2, logs[q] - high - middle, 0.0))
        )
        state_out[states:, cols] = piece.astype(BF16)


def put_states(state_outs, values_ref, logs):
    share = values_ref.shape[1] // len(state_outs)
    for i, state_out in enumerate(state_outs):
        tile = i * share // LANES
        piece = values_ref[:, i * share : (i + 1) * share].astype(BF16)
        put_state(state_out, piece, logs[tile : tile + share // LANES])


def state_logs(state_ref):
    states = state_ref.shape[0] - EXTRA
    return [column_sum(state_ref[states:, cols].astype(F32)) for cols in tiles(state_ref.shape[1])]


def first_kernel(resume, grids, rows_ref, mat, consts, *refs):
    state_in = refs[0] if resume else None
    hist, sel_ref, *state_outs, ab_ref, back_ref = refs[1:] if resume else refs
    chunk = pl.program_id(0) if grids > 1 else 0
    steps, states, width = hist.shape
    forward_first, lead = is_forward_first(), lax.axis_index("per") * steps
    cuts = tiles(width)
    group, half_periods, slot_rows = rows_ref.shape
    tops = 2 * len(cuts)

    def scan_source(d, carry):
        rank, picked = carry
        for slot in range(slot_rows // HB):
            cols = slice(slot * HB, (slot + 1) * HB)
            block = rows_ref[d, :, cols]
            live = block > -0.5 * SEEN
            picked = [jnp.where(live & (rank == chunk * tops + i), block, old) for i, old in enumerate(picked)]
            rank = rank + live.astype(jnp.int32)
        return rank, picked

    carry = (jnp.zeros((half_periods, HB), jnp.int32), [jnp.zeros((half_periods, HB), F32)] * tops)
    if group <= 8:
        for d in range(group):
            carry = scan_source(d, carry)
    else:
        carry = lax.fori_loop(0, group, scan_source, carry)
    low_lane = lax.broadcasted_iota(jnp.int32, (half_periods, HB), 1) < HALF
    for q, cols in enumerate(cuts):
        left, right = carry[1][2 * q], carry[1][2 * q + 1]
        before = jnp.zeros((1, HB), F32)
        for late in range(2):
            value = (
                jnp.where(low_lane, pltpu.roll(left, HALF, 1), right)
                if late
                else jnp.where(low_lane, left, pltpu.roll(right, HALF, 1))
            )
            seen = value > 0.5 * SEEN
            earn = jnp.where(seen, value - SEEN, value)
            seen = seen.astype(F32)
            for i in range(half_periods):
                at = late * half_periods + i
                now = seen[i : i + 1]
                sel_ref[0, at, :, cols] = jnp.broadcast_to(earn[i : i + 1], (8, HB))
                sel_ref[1, at, :, cols] = jnp.broadcast_to(now * before, (8, HB))
                sel_ref[2, at, :, cols] = jnp.broadcast_to(now, (8, HB))
                before = now
    zeros = [jnp.zeros((1, LANES), F32) for _ in cuts]

    @pl.when(forward_first)
    def _():
        if resume:
            ab_ref[...] = state_in[:states, :]
        else:
            for cols in cuts:
                ab_ref[:, cols] = consts[0].astype(BF16)
        logs = state_logs(state_in) if resume else list(zeros)
        logs = run_forward(lead, mat, hist, sel_ref, consts, ab_ref, logs)
        put_states(state_outs, ab_ref, logs)

    @pl.when(jnp.logical_not(forward_first))
    def _():
        if resume:
            back_ref[...] = state_in[:states, :].astype(F32)
        else:
            back_ref[...] = jnp.ones_like(back_ref)
        logs = state_logs(state_in) if resume else list(zeros)
        logs = run_backward(lead, mat, hist, sel_ref, consts, back_ref, ab_ref, logs)
        put_states(state_outs, back_ref, logs)


def second_kernel(resume, last, extend, grids, begin, *refs):
    refs = list(refs)
    sel_ref, mat, consts, hist, own_state, state_in = (refs.pop(0) for _ in range(6))
    width = own_state.shape[1]
    sel_ref, hist = sel_ref.at[:, :, :, pl.ds(begin, width)], hist.at[:, :, pl.ds(begin, width)]
    counts_in, sums_in = (refs.pop(0), refs.pop(0)) if resume else (None, None)
    row_probs = refs.pop(0) if last else None
    mine_ref, other_ref = (refs.pop(0), refs.pop(0)) if last else (None, None)
    counts_out, sums_out = (None, None) if last else (refs.pop(0), refs.pop(0))
    state_out = refs.pop(0) if extend else None
    ab_ref, back_ref, weights_ref = refs[:3]
    counts_ref, sums_ref = refs[3:] if last else (counts_out, sums_out)
    chunk = pl.program_id(0) if grids > 1 else 0
    steps, states, width = hist.shape
    core, forward_first = core_index(), is_forward_first()
    row_begin = lax.axis_index("hh") * counts_ref.shape[1]
    lead = lax.axis_index("per") * steps
    second = (weights_ref, counts_ref, row_begin)

    @pl.when(chunk == 0)
    def _():
        if resume:
            counts_ref[...] = counts_in[...]
            sums_ref[...] = sums_in[...]
        else:
            counts_ref[...] = jnp.zeros_like(counts_ref)
            sums_ref[...] = jnp.zeros_like(sums_ref)

    def add_sums(alpha_ref, other_state):
        total = jnp.zeros((1, LANES), F32)
        years = jnp.zeros((8, LANES), F32)
        for cols, here, there in zip(tiles(width), state_logs(alpha_ref), state_logs(other_state)):
            alpha = alpha_ref[:states, cols].astype(F32)
            meet = column_sum(alpha * other_state[:states, cols].astype(F32))
            total += here + there + jnp.log(meet / column_sum(alpha))
            years += jnp.sum(sel_ref[2, :, :, cols], axis=0)
        total = jnp.broadcast_to(jnp.sum(total, axis=1, keepdims=True), (1, LANES))
        years = jnp.broadcast_to(jnp.sum(years[:1], axis=1, keepdims=True), (1, LANES))
        row = lax.broadcasted_iota(jnp.int32, (8, LANES), 0)
        sums_ref[...] += jnp.where(row == 0, total, jnp.where(row == 1, years, 0.0))

    zeros = [jnp.zeros((1, LANES), F32) for _ in tiles(width)]

    @pl.when(jnp.logical_not(forward_first))
    def _():
        add_sums(state_in, own_state)
        ab_ref[...] = state_in[:states, :]
        run_forward(lead, mat, hist, sel_ref, consts, ab_ref, list(zeros), second)
        if extend:
            put_state(state_out, ab_ref[...], zeros)

    @pl.when(forward_first)
    def _():
        add_sums(own_state, state_in)
        back_ref[...] = state_in[:states, :].astype(F32)
        run_backward(lead, mat, hist, sel_ref, consts, back_ref, ab_ref, list(zeros), second)
        if extend:
            put_state(state_out, back_ref[...].astype(BF16), zeros)

    if last:

        @pl.when(chunk == grids - 1)
        def _():
            rows = counts_ref.shape[1]
            for k in range(steps):
                probs = row_probs[k]
                weighted = probs * counts_ref[k]
                grad = weighted - probs * jnp.sum(weighted, axis=1, keepdims=True)
                for side in range(2):
                    piece = grad[:, side * LANES : (side + 1) * LANES]
                    at = slice(k * rows, (k + 1) * rows)

                    @pl.when(core == side)
                    def _():
                        mine_ref[at, :] = piece

                    @pl.when(core != side)
                    def _():
                        other_ref[at, :] = piece

            mine_ref[steps * rows :, :] = sums_ref[...]
            other_ref[steps * rows :, :] = sums_ref[...]


def finish_kernel(scale, mine_ref, other_ref, grad_ref, mean_ref):
    count = grad_ref.shape[0]
    total = mine_ref[count : count + 1, :] + other_ref[count : count + 1, :]
    years = mine_ref[count + 1 : count + 2, :] + other_ref[count + 1 : count + 2, :]
    grad_ref[...] = (mine_ref[:count, :] + other_ref[:count, :]) * (scale / years)
    mean_ref[0] = (total / years)[0, 0]


def per_device(
    earnings, starts, lengths, block_count, trans_logits, init_logits, state_mean, log_sd
):
    slot_rows, periods = earnings.shape
    states = init_logits.shape[0]
    group = lax.axis_size(("hh", "per"))
    sides = lax.axis_size("per")
    cores = lax.axis_size("st")
    part = trans_logits.shape[0]
    steps = part * cores
    rows = states // lax.axis_size("hh")
    households = group * HB // cores
    width = min(4 * HB, households)
    grids = households // width
    parts = 2 if sides == 2 and grids == 1 else 1
    share = households // parts
    side = lax.axis_index("per")
    shaped = jax.ShapeDtypeStruct
    dma = pltpu.SemaphoreType.DMA

    swap = [(0, 1), (1, 0)]
    other_logits = lax.ppermute(trans_logits, "st", swap)
    vec_row = pltpu.VMEM((1, states), F32)
    packed, vectors = pl.pallas_call(
        pack_kernel,
        out_shape=[shaped((group, periods // 2, slot_rows), F32), shaped((8, states), F32)],
        in_specs=[hbm()] * 7,
        out_specs=[vmem()] * 2,
        scratch_shapes=[
            pltpu.SMEM((1,), jnp.int32),
            pltpu.VMEM((periods, slot_rows), F32),
            pltpu.VMEM((slot_rows // HB, HB), jnp.int32),
            pltpu.VMEM((slot_rows // HB, HB), jnp.int32),
            vec_row,
            vec_row,
            vec_row,
            dma((7,)),
        ],
        name="pack",
    )(
        block_count, earnings.T, starts.reshape(-1, HB), lengths.reshape(-1, HB),
        init_logits.reshape(1, states), state_mean.reshape(1, states), log_sd.reshape(1, states),
    )
    gathered = lax.all_to_all(packed, ("hh", "per"), split_axis=0, concat_axis=0, tiled=True)
    half_logits = pltpu.VMEM(trans_logits.shape, BF16)
    first_mat, consts = pl.pallas_call(
        prep_first_kernel,
        out_shape=[shaped((steps, states // PACK + 1, 2 * PACK, states), BF16), shaped((4, states, LANES), F32)],
        in_specs=[hbm()] * 4,
        out_specs=[vmem()] * 2,
        scratch_shapes=[half_logits, half_logits, pltpu.VMEM((8, states), F32), dma((3,))],
        compiler_params=params(4),
        name="prep_first",
    )(trans_logits, other_logits, vectors, packed)

    def prep_second(after):
        return pl.pallas_call(
            prep_second_kernel,
            out_shape=[shaped((steps, states // PACK, 2 * PACK, states), BF16), shaped((steps, rows, states), F32)],
            in_specs=[hbm()] * 3,
            out_specs=[vmem()] * 2,
            scratch_shapes=[pltpu.VMEM((states, states), F32), half_logits, half_logits, dma((2,))],
            compiler_params=params(4),
            name="prep_second",
        )(trans_logits, other_logits, after)

    def whole(*shape):
        if grids == 1:
            return vmem()
        return pl.BlockSpec(shape, lambda g: (0,) * len(shape))

    def lanes(*lead):
        if grids == 1:
            return vmem()
        return pl.BlockSpec(lead + (width,), lambda g: (0,) * len(lead) + (g,))

    grid = (grids,) if grids > 1 else ()
    hist_shape = shaped((steps, states, households), BF16)
    state_shape = shaped((states + EXTRA, share), BF16)
    sel_shape = shaped((3, periods, 8, households), F32)
    swap_shape = shaped((steps * rows + 8, LANES), F32)
    counts_shape = shaped((steps, rows, states), F32)
    sums_shape = shaped((8, LANES), F32)
    hist_spec, state_spec, sel_spec = lanes(steps, states), lanes(states + EXTRA), lanes(3, periods, 8)
    const_spec = whole(4, states, LANES)

    def first_pass(state_in):
        resume = state_in is not None
        return pl.pallas_call(
            functools.partial(first_kernel, resume, grids),
            grid=grid,
            out_shape=[hist_shape, sel_shape] + [state_shape] * parts,
            in_specs=[whole(*gathered.shape), whole(*first_mat.shape), const_spec]
            + [state_spec] * resume,
            out_specs=[hist_spec, sel_spec] + [state_spec] * parts,
            scratch_shapes=[pltpu.VMEM((states, width), BF16), pltpu.VMEM((states, width), F32)],
            compiler_params=params(8 if grids == 1 else 32),
            name="first_pass",
        )(gathered, first_mat, consts, *([state_in] if resume else []))

    def second_pass(kept, index, state_in, sums_in, last, extend):
        hist, sel, own_state = kept[0], kept[1], kept[2 + index]
        resume = sums_in is not None
        span = width // parts
        scratch = [
            pltpu.VMEM((states, span), BF16),
            pltpu.VMEM((states, span), F32),
            pltpu.VMEM((rows, span), BF16),
        ]
        counts_spec, sums_spec = whole(*counts_shape.shape), whole(*sums_shape.shape)
        if last:
            out_shape = [swap_shape] * 2
            scratch += [pltpu.VMEM(counts_shape.shape, F32), pltpu.VMEM(sums_shape.shape, F32)]
        else:
            out_shape = [counts_shape, sums_shape]
        out_specs = [whole(*x.shape) for x in out_shape]
        if extend:
            out_shape, out_specs = out_shape + [state_shape], out_specs + [state_spec]
        return pl.pallas_call(
            functools.partial(second_kernel, resume, last, extend, grids, index * span),
            grid=grid,
            out_shape=out_shape,
            in_specs=[sel_spec, whole(*second_mat.shape), const_spec, hist_spec, state_spec, state_spec]
            + [counts_spec, sums_spec] * resume
            + [whole(*row_probs.shape)] * last,
            out_specs=out_specs,
            scratch_shapes=scratch,
            compiler_params=params(8 if grids == 1 else 32),
            name="second_pass",
        )(
            sel, second_mat, consts, hist, own_state, state_in,
            *(sums_in if resume else []),
            *([row_probs] if last else []),
        )

    def hand_over(state, stage):
        moves = [(stage, stage + 1), (sides - 1 - stage, sides - 2 - stage)]
        return lax.ppermute(state, "per", moves)

    if sides == 2:
        kept = first_pass(None)
        arrived = [hand_over(each, 0) for each in kept[2:]]
        second_mat, row_probs = prep_second(kept[2])
        sums = None
        for index in range(parts):
            sums = second_pass(kept, index, arrived[index], sums, index == parts - 1, False)
        mine, other = sums
    else:
        kept = [jnp.zeros(x.shape, x.dtype) for x in (hist_shape, sel_shape, state_shape)]
        done = [jnp.zeros(x.shape, x.dtype) for x in (swap_shape, swap_shape, state_shape)]
        second_mat, row_probs = prep_second(gathered)
        state = None
        for stage in range(sides):
            active = (side == stage) | (side == sides - 1 - stage)
            if stage < sides // 2:
                kept = lax.cond(
                    active, lambda x, kept: list(first_pass(x)), lambda x, kept: kept, state, kept
                )
                state = kept[2]
            else:
                done = lax.cond(
                    active,
                    lambda x, done: list(second_pass(kept, 0, x, None, True, True)),
                    lambda x, done: done,
                    state,
                    done,
                )
                state = done[2]
            if stage < sides - 1:
                state = hand_over(state, stage)
        mine, other, _ = done
        total = jnp.where(side == sides // 2, mine[steps * rows], 0.0)
        total = lax.psum(total, "per")
        mine = mine.at[steps * rows].set(total)
        other = other.at[steps * rows].set(total)
    received = lax.ppermute(other, "st", swap)
    trans_grad, mean_loglik = pl.pallas_call(
        functools.partial(finish_kernel, float(states * states * periods)),
        out_shape=[shaped((steps * rows, LANES), F32), shaped((1,), F32)],
        in_specs=[vmem(), vmem()],
        out_specs=[vmem(), smem()],
        compiler_params=params(4),
        name="finish",
    )(mine, received)
    return (trans_grad.reshape(steps, rows, LANES), mean_loglik)


def solution(mesh):
    placed = (
        P(("hh", "per"), None),
        P(("hh", "per")),
        P(("hh", "per")),
        P(("hh", "per")),
        P(("grp", "per", "st"), None, None),
        P("grp"),
        P("grp"),
        P("grp"),
    )
    return jax.shard_map(
        per_device,
        mesh=mesh,
        in_specs=placed,
        out_specs=(P(("grp", "per"), "hh", "st"), P("grp")),
        check_vma=False,
    )
```

```python
import functools

import jax
import jax.numpy as jnp
from jax import lax
from jax.experimental import pallas as pl
from jax.experimental.pallas import tpu as pltpu
from jax.sharding import PartitionSpec as P

HB = 128
LANES = 128
HALF = HB // 2
SEEN = 16.0
F32 = jnp.float32
BF16 = jnp.bfloat16
LOG2E = 1.4426950408889634
LN2 = 0.6931471805599453
EXTRA = 16


def vmem():
    return pl.BlockSpec(memory_space=pltpu.VMEM)


def smem():
    return pl.BlockSpec(memory_space=pltpu.SMEM)


def hbm():
    return pl.BlockSpec(memory_space=pltpu.HBM)


def in_hbm(*arrays):
    return [pltpu.with_memory_space_constraint(x, pltpu.HBM) for x in arrays]


def params(mebibytes):
    return pltpu.CompilerParams(vmem_limit_bytes=mebibytes * 1024 * 1024)


def core_index():
    return lax.axis_index("st")


def is_forward_first():
    return 2 * lax.axis_index("per") < lax.axis_size("per")


def tiles(width):
    return [slice(q, q + LANES) for q in range(0, width, LANES)]


def fetch(pairs, sems):
    copies = [pltpu.make_async_copy(src, dst, sems.at[i]) for i, (src, dst) in enumerate(pairs)]
    for copy in copies:
        copy.start()
    for copy in copies:
        copy.wait()


def pack_kernel(
    count_ref, earn_any, start_any, len_any, init_any, mean_any, sd_any, out_ref, vec_ref,
    earn_ref, start_ref, len_ref, init_ref, mean_ref, sd_ref, sems,
):
    fetch(
        (
            (earn_any, earn_ref), (start_any, start_ref), (len_any, len_ref),
            (init_any, init_ref), (mean_any, mean_ref), (sd_any, sd_ref),
        ),
        sems,
    )
    periods, slot_rows = earn_ref.shape
    core = core_index()
    low_lane = lax.broadcasted_iota(jnp.int32, (periods // 2, HB), 1) < HALF
    time = lax.broadcasted_iota(jnp.int32, (periods, HB), 0)
    for slot in range(slot_rows // HB):
        cols = slice(slot * HB, (slot + 1) * HB)
        begin = start_ref[slot : slot + 1, :]
        seen = (time >= begin) & (time < begin + len_ref[slot : slot + 1, :])
        live = slot < count_ref[0]
        shift = jnp.where(live, jnp.where(seen, SEEN, 0.0), -SEEN)
        value = earn_ref[:, cols] + shift
        early, late = value[: periods // 2], value[periods // 2 :]
        turned = pltpu.roll(jnp.where(core == 0, late, early), HALF, 1)
        packed = jnp.where(low_lane, jnp.where(core == 0, early, turned), jnp.where(core == 0, turned, late))
        for to in range(out_ref.shape[0]):
            out_ref[to, :, cols] = packed
    raised = jnp.exp(init_ref[...])
    start = raised / jnp.sum(raised, axis=1, keepdims=True)
    row = lax.broadcasted_iota(jnp.int32, vec_ref.shape, 0)
    power = (-0.5 * LOG2E) * jnp.exp(-2.0 * sd_ref[...])
    vec_ref[...] = jnp.where(
        row == 0, start, jnp.where(row == 1, mean_ref[...], jnp.where(row == 2, power, -LOG2E * sd_ref[...]))
    )


def put(ref, at, value):
    states = value.shape[0]
    high = value.astype(BF16)
    ref[at, :states, :] = high
    ref[at, states : 2 * states, :] = (value - high.astype(F32)).astype(BF16)


def prep_kernel(
    own_any, other_ref, vec_ref, first_mat, second_mat, row_probs, consts, scratch, own_ref, sem
):
    copy = pltpu.make_async_copy(own_any, own_ref, sem)
    copy.start()
    part, states, _ = own_ref.shape
    rows = row_probs.shape[1]
    for i in range(4):
        consts[i] = jnp.broadcast_to(vec_ref[i : i + 1, :], (LANES, states)).T
    start = vec_ref[:1, :]
    start_high = start.astype(BF16).astype(F32)
    row = lax.broadcasted_iota(jnp.int32, (EXTRA, states), 0)
    start_rows = jnp.where(row == 0, start_high, jnp.where(row == 1, start - start_high, 0.0)).astype(BF16)
    for k in range(first_mat.shape[0]):
        first_mat[k, 2 * states :, :] = start_rows
    for source, ref in ((1 - core_index(), other_ref), (core_index(), own_ref)):
        if ref is own_ref:
            copy.wait()

        @pl.loop(0, part)
        def _(i):
            at = source * part + i
            lifted = jnp.exp(ref[i].astype(F32))
            probs = lifted * (1.0 / jnp.sum(lifted, axis=1, keepdims=True))
            scratch[...] = probs
            row_probs[at] = scratch[own_rows(lax.axis_index("hh") * rows, rows), :]

            @pl.when(is_forward_first())
            def _():
                put(first_mat, at, probs.T)
                put(second_mat, at, probs)

            @pl.when(jnp.logical_not(is_forward_first()))
            def _():
                put(first_mat, at, probs)
                put(second_mat, at, probs.T)


def emission(sel_ref, consts, step_now, cols):
    gap = sel_ref[0, step_now, :1, cols] - consts[1]
    power = gap * gap * consts[2] + consts[3]
    top = jnp.max(power, axis=0, keepdims=True)
    return jnp.exp2(power - top), top


def is_moving(sel_ref, step_now, cols):
    return sel_ref[1, step_now, :1, cols] > 0.5


def is_seen(sel_ref, step_now, cols):
    return sel_ref[2, step_now, :1, cols] > 0.5


def column_sum(x):
    return jnp.sum(x, axis=0, keepdims=True)


def own_rows(row_begin, rows):
    return pl.ds(pl.multiple_of(row_begin, rows), rows)


def outer_sum(weights_ref, carried):
    return lax.dot_general(weights_ref[...], carried, (((1,), (1,)), ((), ())), preferred_element_type=F32)


def run_forward(lead, mat, hist, sel_ref, consts, ab_ref, logs, second=None):
    steps, states, width = hist.shape
    cuts = tiles(width)
    inverse = [1.0 / column_sum(ab_ref[:, cols].astype(F32)) for cols in cuts]
    for k in range(steps):
        step_now = lead + k
        if second is None:
            hist[k] = ab_ref[...]
        else:
            weights_ref, counts_ref, row_begin = second
            own_alpha = ab_ref[own_rows(row_begin, weights_ref.shape[0]), :].astype(F32)
        for q, cols in enumerate(cuts):
            product = jnp.dot(mat[k, : 2 * states, :], ab_ref[:, cols], preferred_element_type=F32)
            moved = (product[:states] + product[states:]) * inverse[q]
            moving = is_moving(sel_ref, step_now, cols)
            if second is not None:
                total = column_sum(moved * hist[k, :, cols].astype(F32))
                weight = jnp.where(moving, inverse[q] / total, 0.0)
                weights_ref[:, cols] = (own_alpha[:, cols] * weight).astype(BF16)
            emit, top = emission(sel_ref, consts, step_now, cols)
            joint = jnp.where(moving, moved, consts[0]) * emit
            scale = column_sum(joint)
            if second is None:
                seen = is_seen(sel_ref, step_now, cols)
                logs[q] = logs[q] + jnp.where(seen, jnp.log(scale) + top * LN2, 0.0)
            inverse[q] = 1.0 / scale
            ab_ref[:, cols] = joint.astype(BF16)
        if second is not None:
            counts_ref[k] += outer_sum(weights_ref, hist[k])
    return logs


def run_backward(lead, mat, hist, sel_ref, consts, back_ref, ub_ref, logs, second=None):
    steps, states, width = hist.shape
    cuts = tiles(width)
    for k in reversed(range(steps)):
        step_now = lead + k
        shrink = []
        for q, cols in enumerate(cuts):
            emit, top = emission(sel_ref, consts, step_now, cols)
            carried = emit * back_ref[:, cols]
            size = column_sum(carried)
            if second is None:
                seen = is_seen(sel_ref, step_now, cols)
                logs[q] = logs[q] + jnp.where(seen, jnp.log(size) + top * LN2, 0.0)
            shrink.append(1.0 / size)
            ub_ref[:, cols] = carried.astype(BF16)
        if second is None:
            hist[k] = ub_ref[...]
        else:
            weights_ref, counts_ref, row_begin = second
            own_alpha = hist[k, own_rows(row_begin, weights_ref.shape[0]), :].astype(F32)
        for q, cols in enumerate(cuts):
            product = jnp.dot(mat[k], ub_ref[:, cols], preferred_element_type=F32)
            moving = is_moving(sel_ref, step_now, cols)
            pulled = (product[:states] + product[states : 2 * states]) * shrink[q]
            if second is None:
                seen = is_seen(sel_ref, step_now, cols)
                begun = column_sum(product[2 * states :]) * shrink[q]
                rest = jnp.where(seen, begun, back_ref[:, cols])
            else:
                total = column_sum(pulled * hist[k, :, cols].astype(F32))
                weight = jnp.where(moving, shrink[q] / total, 0.0)
                weights_ref[:, cols] = (own_alpha[:, cols] * weight).astype(BF16)
                rest = 1.0
            back_ref[:, cols] = jnp.where(moving, pulled, rest)
        if second is not None:
            counts_ref[k] += outer_sum(weights_ref, ub_ref[...])
    return logs


def put_state(state_out, values, logs):
    states = state_out.shape[0] - EXTRA
    state_out[:states, :] = values
    for q, cols in enumerate(tiles(state_out.shape[1])):
        high = logs[q].astype(BF16).astype(F32)
        middle = (logs[q] - high).astype(BF16).astype(F32)
        row = lax.broadcasted_iota(jnp.int32, (EXTRA, LANES), 0)
        piece = jnp.where(
            row == 0, high, jnp.where(row == 1, middle, jnp.where(row == 2, logs[q] - high - middle, 0.0))
        )
        state_out[states:, cols] = piece.astype(BF16)


def state_logs(state_ref):
    states = state_ref.shape[0] - EXTRA
    return [column_sum(state_ref[states:, cols].astype(F32)) for cols in tiles(state_ref.shape[1])]


def first_kernel(resume, grids, part, rows_ref, mat, consts, *refs):
    state_in = refs[0] if resume else None
    hist, state_out, sel_ref, ab_ref, back_ref = refs[-5:]
    chunk = part * grids + (pl.program_id(0) if grids > 1 else 0)
    steps, states, width = hist.shape
    forward_first, lead = is_forward_first(), lax.axis_index("per") * steps
    cuts = tiles(width)
    group, half_periods, slot_rows = rows_ref.shape
    tops = 2 * len(cuts)

    def scan_source(d, carry):
        rank, picked = carry
        for slot in range(slot_rows // HB):
            cols = slice(slot * HB, (slot + 1) * HB)
            block = rows_ref[d, :, cols]
            live = block > -0.5 * SEEN
            picked = [jnp.where(live & (rank == chunk * tops + i), block, old) for i, old in enumerate(picked)]
            rank = rank + live.astype(jnp.int32)
        return rank, picked

    carry = (jnp.zeros((half_periods, HB), jnp.int32), [jnp.zeros((half_periods, HB), F32)] * tops)
    if group <= 8:
        for d in range(group):
            carry = scan_source(d, carry)
    else:
        carry = lax.fori_loop(0, group, scan_source, carry)
    low_lane = lax.broadcasted_iota(jnp.int32, (half_periods, HB), 1) < HALF
    for q, cols in enumerate(cuts):
        left, right = carry[1][2 * q], carry[1][2 * q + 1]
        before = jnp.zeros((1, HB), F32)
        for late in range(2):
            value = (
                jnp.where(low_lane, pltpu.roll(left, HALF, 1), right)
                if late
                else jnp.where(low_lane, left, pltpu.roll(right, HALF, 1))
            )
            seen = value > 0.5 * SEEN
            earn = jnp.where(seen, value - SEEN, value)
            seen = seen.astype(F32)
            for i in range(half_periods):
                at = late * half_periods + i
                now = seen[i : i + 1]
                sel_ref[0, at, :, cols] = jnp.broadcast_to(earn[i : i + 1], (8, HB))
                sel_ref[1, at, :, cols] = jnp.broadcast_to(now * before, (8, HB))
                sel_ref[2, at, :, cols] = jnp.broadcast_to(now, (8, HB))
                before = now
    zeros = [jnp.zeros((1, LANES), F32) for _ in cuts]

    @pl.when(forward_first)
    def _():
        if resume:
            ab_ref[...] = state_in[:states, :]
        else:
            for cols in cuts:
                ab_ref[:, cols] = consts[0].astype(BF16)
        logs = state_logs(state_in) if resume else list(zeros)
        logs = run_forward(lead, mat, hist, sel_ref, consts, ab_ref, logs)
        put_state(state_out, ab_ref[...], logs)

    @pl.when(jnp.logical_not(forward_first))
    def _():
        if resume:
            back_ref[...] = state_in[:states, :].astype(F32)
        else:
            back_ref[...] = jnp.ones_like(back_ref)
        logs = state_logs(state_in) if resume else list(zeros)
        logs = run_backward(lead, mat, hist, sel_ref, consts, back_ref, ab_ref, logs)
        put_state(state_out, back_ref[...].astype(BF16), logs)


def second_kernel(resume, last, extend, grids, *refs):
    refs = list(refs)
    sel_ref, mat, consts, hist, own_state, state_in = (refs.pop(0) for _ in range(6))
    counts_in, sums_in = (refs.pop(0), refs.pop(0)) if resume else (None, None)
    row_probs = refs.pop(0) if last else None
    mine_ref, other_ref = (refs.pop(0), refs.pop(0)) if last else (None, None)
    counts_out, sums_out = (None, None) if last else (refs.pop(0), refs.pop(0))
    state_out = refs.pop(0) if extend else None
    ab_ref, back_ref, weights_ref = refs[:3]
    counts_ref, sums_ref = refs[3:] if last else (counts_out, sums_out)
    chunk = pl.program_id(0) if grids > 1 else 0
    steps, states, width = hist.shape
    core, forward_first = core_index(), is_forward_first()
    row_begin = lax.axis_index("hh") * counts_ref.shape[1]
    lead = lax.axis_index("per") * steps
    second = (weights_ref, counts_ref, row_begin)

    @pl.when(chunk == 0)
    def _():
        if resume:
            counts_ref[...] = counts_in[...]
            sums_ref[...] = sums_in[...]
        else:
            counts_ref[...] = jnp.zeros_like(counts_ref)
            sums_ref[...] = jnp.zeros_like(sums_ref)

    def add_sums(alpha_ref, other_state):
        total = jnp.zeros((1, LANES), F32)
        years = jnp.zeros((8, LANES), F32)
        for cols, here, there in zip(tiles(width), state_logs(alpha_ref), state_logs(other_state)):
            alpha = alpha_ref[:states, cols].astype(F32)
            meet = column_sum(alpha * other_state[:states, cols].astype(F32))
            total += here + there + jnp.log(meet / column_sum(alpha))
            years += jnp.sum(sel_ref[2, :, :, cols], axis=0)
        total = jnp.broadcast_to(jnp.sum(total, axis=1, keepdims=True), (1, LANES))
        years = jnp.broadcast_to(jnp.sum(years[:1], axis=1, keepdims=True), (1, LANES))
        row = lax.broadcasted_iota(jnp.int32, (8, LANES), 0)
        sums_ref[...] += jnp.where(row == 0, total, jnp.where(row == 1, years, 0.0))

    zeros = [jnp.zeros((1, LANES), F32) for _ in tiles(width)]

    @pl.when(jnp.logical_not(forward_first))
    def _():
        add_sums(state_in, own_state)
        ab_ref[...] = state_in[:states, :]
        run_forward(lead, mat, hist, sel_ref, consts, ab_ref, list(zeros), second)
        if extend:
            put_state(state_out, ab_ref[...], zeros)

    @pl.when(forward_first)
    def _():
        add_sums(own_state, state_in)
        back_ref[...] = state_in[:states, :].astype(F32)
        run_backward(lead, mat, hist, sel_ref, consts, back_ref, ab_ref, list(zeros), second)
        if extend:
            put_state(state_out, back_ref[...].astype(BF16), zeros)

    if last:

        @pl.when(chunk == grids - 1)
        def _():
            rows = counts_ref.shape[1]
            for k in range(steps):
                probs = row_probs[k]
                weighted = probs * counts_ref[k]
                grad = weighted - probs * jnp.sum(weighted, axis=1, keepdims=True)
                for side in range(2):
                    piece = grad[:, side * LANES : (side + 1) * LANES]
                    at = slice(k * rows, (k + 1) * rows)

                    @pl.when(core == side)
                    def _():
                        mine_ref[at, :] = piece

                    @pl.when(core != side)
                    def _():
                        other_ref[at, :] = piece

            mine_ref[steps * rows :, :] = sums_ref[...]
            other_ref[steps * rows :, :] = sums_ref[...]


def finish_kernel(scale, mine_ref, other_ref, grad_ref, mean_ref):
    count = grad_ref.shape[0]
    total = mine_ref[count : count + 1, :] + other_ref[count : count + 1, :]
    years = mine_ref[count + 1 : count + 2, :] + other_ref[count + 1 : count + 2, :]
    grad_ref[...] = (mine_ref[:count, :] + other_ref[:count, :]) * (scale / years)
    mean_ref[0] = (total / years)[0, 0]


def per_device(
    earnings, starts, lengths, block_count, trans_logits, init_logits, state_mean, log_sd
):
    slot_rows, periods = earnings.shape
    states = init_logits.shape[0]
    group = lax.axis_size(("hh", "per"))
    sides = lax.axis_size("per")
    cores = lax.axis_size("st")
    part = trans_logits.shape[0]
    steps = part * cores
    rows = states // lax.axis_size("hh")
    households = group * HB // cores
    parts = 2 if households <= 4 * HB else 1
    share = households // parts
    width = min(2 * HB, share)
    grids = share // width
    side = lax.axis_index("per")
    shaped = jax.ShapeDtypeStruct
    dma = pltpu.SemaphoreType.DMA

    swap = [(0, 1), (1, 0)]
    other_logits = lax.ppermute(trans_logits, "st", swap)
    vec_row = pltpu.VMEM((1, states), F32)
    packed, vectors = pl.pallas_call(
        pack_kernel,
        out_shape=[shaped((group, periods // 2, slot_rows), F32), shaped((8, states), F32)],
        in_specs=[smem()] + [hbm()] * 6,
        out_specs=[vmem()] * 2,
        scratch_shapes=[
            pltpu.VMEM((periods, slot_rows), F32),
            pltpu.VMEM((slot_rows // HB, HB), jnp.int32),
            pltpu.VMEM((slot_rows // HB, HB), jnp.int32),
            vec_row,
            vec_row,
            vec_row,
            dma((6,)),
        ],
        compiler_params=params(2),
        name="pack",
    )(
        block_count,
        *in_hbm(
            earnings.T, starts.reshape(-1, HB), lengths.reshape(-1, HB),
            init_logits.reshape(1, states), state_mean.reshape(1, states), log_sd.reshape(1, states),
        ),
    )
    gathered = lax.all_to_all(packed, ("hh", "per"), split_axis=0, concat_axis=0, tiled=True)
    first_mat, second_mat, row_probs, consts = pl.pallas_call(
        prep_kernel,
        out_shape=[
            pltpu.VMEM((steps, 2 * states + EXTRA, states), BF16),
            pltpu.VMEM((steps, 2 * states, states), BF16),
            pltpu.VMEM((steps, rows, states), F32),
            pltpu.VMEM((4, states, LANES), F32),
        ],
        in_specs=[hbm(), vmem(), vmem()],
        out_specs=[vmem()] * 4,
        scratch_shapes=[pltpu.VMEM((states, states), F32), pltpu.VMEM(trans_logits.shape, BF16), dma],
        compiler_params=params(4),
        name="prep",
    )(*in_hbm(trans_logits), pltpu.with_memory_space_constraint(other_logits, pltpu.VMEM), vectors)

    def whole(*shape):
        if grids == 1:
            return vmem()
        return pl.BlockSpec(shape, lambda g: (0,) * len(shape))

    def lanes(*lead):
        if grids == 1:
            return vmem()
        return pl.BlockSpec(lead + (width,), lambda g: (0,) * len(lead) + (g,))

    grid = (grids,) if grids > 1 else ()
    hist_shape = shaped((steps, states, share), BF16)
    state_shape = shaped((states + EXTRA, share), BF16)
    sel_shape = shaped((3, periods, 8, share), F32)
    swap_shape = shaped((steps * rows + 8, LANES), F32)
    counts_shape = shaped((steps, rows, states), F32)
    sums_shape = shaped((8, LANES), F32)
    hist_spec, state_spec, sel_spec = lanes(steps, states), lanes(states + EXTRA), lanes(3, periods, 8)
    const_spec = whole(4, states, LANES)

    def first_pass(index, state_in):
        resume = state_in is not None
        return pl.pallas_call(
            functools.partial(first_kernel, resume, grids, index),
            grid=grid,
            out_shape=[hist_shape, state_shape, sel_shape],
            in_specs=[whole(*gathered.shape), whole(*first_mat.shape), const_spec]
            + [state_spec] * resume,
            out_specs=[hist_spec, state_spec, sel_spec],
            scratch_shapes=[pltpu.VMEM((states, width), BF16), pltpu.VMEM((states, width), F32)],
            compiler_params=params(8 if grids == 1 else 32),
            name="first_pass",
        )(gathered, first_mat, consts, *([state_in] if resume else []))

    def second_pass(kept, state_in, sums_in, last, extend):
        hist, own_state, sel = kept
        resume = sums_in is not None
        scratch = [
            pltpu.VMEM((states, width), BF16),
            pltpu.VMEM((states, width), F32),
            pltpu.VMEM((rows, width), BF16),
        ]
        counts_spec, sums_spec = whole(*counts_shape.shape), whole(*sums_shape.shape)
        if last:
            out_shape = [swap_shape] * 2
            scratch += [pltpu.VMEM(counts_shape.shape, F32), pltpu.VMEM(sums_shape.shape, F32)]
        else:
            out_shape = [counts_shape, sums_shape]
        out_specs = [whole(*x.shape) for x in out_shape]
        if extend:
            out_shape, out_specs = out_shape + [state_shape], out_specs + [state_spec]
        return pl.pallas_call(
            functools.partial(second_kernel, resume, last, extend, grids),
            grid=grid,
            out_shape=out_shape,
            in_specs=[sel_spec, whole(*second_mat.shape), const_spec, hist_spec, state_spec, state_spec]
            + [counts_spec, sums_spec] * resume
            + [whole(*row_probs.shape)] * last,
            out_specs=out_specs,
            scratch_shapes=scratch,
            compiler_params=params(8 if grids == 1 else 32),
            name="second_pass",
        )(
            sel, second_mat, consts, hist, own_state, state_in,
            *(sums_in if resume else []),
            *([row_probs] if last else []),
        )

    def hand_over(state, stage):
        moves = [(stage, stage + 1), (sides - 1 - stage, sides - 2 - stage)]
        return lax.ppermute(state, "per", moves)

    if sides == 2:
        kept = [first_pass(index, None) for index in range(parts)]
        arrived = [hand_over(each[1], 0) for each in kept]
        sums = None
        for index in range(parts):
            sums = second_pass(kept[index], arrived[index], sums, index == parts - 1, False)
        mine, other = sums
    else:
        kept = [jnp.zeros(x.shape, x.dtype) for x in (hist_shape, state_shape, sel_shape)]
        done = [jnp.zeros(x.shape, x.dtype) for x in (swap_shape, swap_shape, state_shape)]
        state = None
        for stage in range(sides):
            active = (side == stage) | (side == sides - 1 - stage)
            if stage < sides // 2:
                kept = lax.cond(
                    active, lambda x, kept: list(first_pass(0, x)), lambda x, kept: kept, state, kept
                )
                state = kept[1]
            else:
                done = lax.cond(
                    active,
                    lambda x, done: list(second_pass(kept, x, None, True, True)),
                    lambda x, done: done,
                    state,
                    done,
                )
                state = done[2]
            if stage < sides - 1:
                state = hand_over(state, stage)
        mine, other, _ = done
        total = jnp.where(side == sides // 2, mine[steps * rows], 0.0)
        total = lax.psum(total, "per")
        mine = mine.at[steps * rows].set(total)
        other = other.at[steps * rows].set(total)
    received = lax.ppermute(other, "st", swap)
    trans_grad, mean_loglik = pl.pallas_call(
        functools.partial(finish_kernel, float(states * states * periods)),
        out_shape=[shaped((steps * rows, LANES), F32), shaped((1,), F32)],
        in_specs=[vmem(), vmem()],
        out_specs=[vmem(), smem()],
        compiler_params=params(4),
        name="finish",
    )(mine, received)
    return (trans_grad.reshape(steps, rows, LANES), mean_loglik)


def solution(mesh):
    placed = (
        P(("hh", "per"), None),
        P(("hh", "per")),
        P(("hh", "per")),
        P(("hh", "per")),
        P(("grp", "per", "st"), None, None),
        P("grp"),
        P("grp"),
        P("grp"),
    )
    return jax.shard_map(
        per_device,
        mesh=mesh,
        in_specs=placed,
        out_specs=(P(("grp", "per"), "hh", "st"), P("grp")),
        check_vma=False,
    )
```

```python
import functools

import jax
import jax.numpy as jnp
from jax import lax
from jax.experimental import pallas as pl
from jax.experimental.pallas import tpu as pltpu
from jax.sharding import PartitionSpec as P

HB = 128
LANES = 128
HALF = HB // 2
SEEN = 16.0
F32 = jnp.float32
BF16 = jnp.bfloat16
LOG2E = 1.4426950408889634
LN2 = 0.6931471805599453
EXTRA = 16


def vmem():
    return pl.BlockSpec(memory_space=pltpu.VMEM)


def smem():
    return pl.BlockSpec(memory_space=pltpu.SMEM)


def hbm():
    return pl.BlockSpec(memory_space=pltpu.HBM)


def in_hbm(*arrays):
    return [pltpu.with_memory_space_constraint(x, pltpu.HBM) for x in arrays]


def params(mebibytes):
    return pltpu.CompilerParams(vmem_limit_bytes=mebibytes * 1024 * 1024)


def core_index():
    return lax.axis_index("st")


def is_forward_first():
    return 2 * lax.axis_index("per") < lax.axis_size("per")


def tiles(width):
    return [slice(q, q + LANES) for q in range(0, width, LANES)]


def fetch(pairs, sems):
    copies = [pltpu.make_async_copy(src, dst, sems.at[i]) for i, (src, dst) in enumerate(pairs)]
    for copy in copies:
        copy.start()
    for copy in copies:
        copy.wait()


def pack_kernel(
    count_ref, earn_any, start_any, len_any, init_any, mean_any, sd_any, out_ref, vec_ref,
    earn_ref, start_ref, len_ref, init_ref, mean_ref, sd_ref, sems,
):
    fetch(
        (
            (earn_any, earn_ref), (start_any, start_ref), (len_any, len_ref),
            (init_any, init_ref), (mean_any, mean_ref), (sd_any, sd_ref),
        ),
        sems,
    )
    periods, slot_rows = earn_ref.shape
    core = core_index()
    low_lane = lax.broadcasted_iota(jnp.int32, (periods // 2, HB), 1) < HALF
    time = lax.broadcasted_iota(jnp.int32, (periods, HB), 0)
    for slot in range(slot_rows // HB):
        cols = slice(slot * HB, (slot + 1) * HB)
        begin = start_ref[slot : slot + 1, :]
        seen = (time >= begin) & (time < begin + len_ref[slot : slot + 1, :])
        live = slot < count_ref[0]
        shift = jnp.where(live, jnp.where(seen, SEEN, 0.0), -SEEN)
        value = earn_ref[:, cols] + shift
        early, late = value[: periods // 2], value[periods // 2 :]
        turned = pltpu.roll(jnp.where(core == 0, late, early), HALF, 1)
        packed = jnp.where(low_lane, jnp.where(core == 0, early, turned), jnp.where(core == 0, turned, late))
        for to in range(out_ref.shape[0]):
            out_ref[to, :, cols] = packed
    raised = jnp.exp(init_ref[...])
    start = raised / jnp.sum(raised, axis=1, keepdims=True)
    row = lax.broadcasted_iota(jnp.int32, vec_ref.shape, 0)
    power = (-0.5 * LOG2E) * jnp.exp(-2.0 * sd_ref[...])
    vec_ref[...] = jnp.where(
        row == 0, start, jnp.where(row == 1, mean_ref[...], jnp.where(row == 2, power, -LOG2E * sd_ref[...]))
    )


def put(ref, at, value):
    states = value.shape[0]
    high = value.astype(BF16)
    ref[at, :states, :states] = high
    ref[at, :states, states:] = (value - high.astype(F32)).astype(BF16)


def put_twice(ref, cols, value):
    states = value.shape[0]
    value = value.astype(BF16)
    ref[:states, cols] = value
    ref[states:, cols] = value


def prep_kernel(
    own_any, other_any, vec_ref, first_mat, second_any, row_probs, consts,
    second_mat, scratch, own_ref, other_ref, sems, out_sems,
):
    copies = [
        pltpu.make_async_copy(src, dst, sems.at[i])
        for i, (src, dst) in enumerate(((own_any, own_ref), (other_any, other_ref)))
    ]
    for copy in copies:
        copy.start()
    part, states, _ = own_ref.shape

    def leave(at):
        return pltpu.make_async_copy(second_mat.at[at], second_any.at[at], out_sems.at[at])

    rows = row_probs.shape[1]
    for i in range(4):
        consts[i] = jnp.broadcast_to(vec_ref[i : i + 1, :], (LANES, states)).T
    start = vec_ref[:1, :]
    start_high = start.astype(BF16).astype(F32)
    row = lax.broadcasted_iota(jnp.int32, (EXTRA, states), 0)
    for k in range(first_mat.shape[0]):
        first_mat[k, states:, :states] = jnp.where(row == 0, start_high, 0.0).astype(BF16)
        first_mat[k, states:, states:] = jnp.where(row == 0, start - start_high, 0.0).astype(BF16)
    for copy, source, ref in zip(copies, (core_index(), 1 - core_index()), (own_ref, other_ref)):
        copy.wait()

        @pl.loop(0, part)
        def _(i):
            at = source * part + i
            lifted = jnp.exp(ref[i].astype(F32))
            probs = lifted * (1.0 / jnp.sum(lifted, axis=1, keepdims=True))
            scratch[...] = probs
            row_probs[at] = scratch[own_rows(lax.axis_index("hh") * rows, rows), :]

            @pl.when(is_forward_first())
            def _():
                put(first_mat, at, probs.T)
                put(second_mat, at, probs)

            @pl.when(jnp.logical_not(is_forward_first()))
            def _():
                put(first_mat, at, probs)
                put(second_mat, at, probs.T)

            leave(at).start()

    for at in range(2 * part):
        leave(at).wait()


def emission(sel_ref, consts, step_now, cols):
    gap = sel_ref[0, step_now, :1, cols] - consts[1]
    power = gap * gap * consts[2] + consts[3]
    top = jnp.max(power, axis=0, keepdims=True)
    return jnp.exp2(power - top), top


def is_moving(sel_ref, step_now, cols):
    return sel_ref[1, step_now, :1, cols] > 0.5


def is_seen(sel_ref, step_now, cols):
    return sel_ref[2, step_now, :1, cols] > 0.5


def column_sum(x):
    return jnp.sum(x, axis=0, keepdims=True)


def own_rows(row_begin, rows):
    return pl.ds(pl.multiple_of(row_begin, rows), rows)


def outer_sum(weights_ref, carried):
    return lax.dot_general(weights_ref[...], carried, (((1,), (1,)), ((), ())), preferred_element_type=F32)


def run_forward(lead, mat, hist, sel_ref, consts, ab_ref, logs, second=None):
    steps, states, width = hist.shape
    cuts = tiles(width)
    inverse = [1.0 / column_sum(ab_ref[:states, cols].astype(F32)) for cols in cuts]
    for k in range(steps):
        step_now = lead + k
        if second is None:
            hist[k] = ab_ref[:states, :]
        else:
            weights_ref, row_begin, add_counts = second
            own_alpha = ab_ref[own_rows(row_begin, weights_ref.shape[0]), :].astype(F32)
        for q, cols in enumerate(cuts):
            moved = jnp.dot(mat[k, :states, :], ab_ref[:, cols], preferred_element_type=F32) * inverse[q]
            moving = is_moving(sel_ref, step_now, cols)
            if second is not None:
                total = column_sum(moved * hist[k, :, cols].astype(F32))
                weight = jnp.where(moving, inverse[q] / total, 0.0)
                weights_ref[:, cols] = (own_alpha[:, cols] * weight).astype(BF16)
            emit, top = emission(sel_ref, consts, step_now, cols)
            joint = jnp.where(moving, moved, consts[0]) * emit
            scale = column_sum(joint)
            if second is None:
                seen = is_seen(sel_ref, step_now, cols)
                logs[q] = logs[q] + jnp.where(seen, jnp.log(scale) + top * LN2, 0.0)
            inverse[q] = 1.0 / scale
            put_twice(ab_ref, cols, joint)
        if second is not None:
            add_counts(k, outer_sum(weights_ref, hist[k]))
    return logs


def run_backward(lead, mat, hist, sel_ref, consts, back_ref, ub_ref, logs, second=None):
    steps, states, width = hist.shape
    cuts = tiles(width)

    def step(k):
        step_now = lead + k
        shrink = []
        for q, cols in enumerate(cuts):
            emit, top = emission(sel_ref, consts, step_now, cols)
            carried = emit * back_ref[:, cols]
            size = column_sum(carried)
            if second is None:
                seen = is_seen(sel_ref, step_now, cols)
                logs[q] = logs[q] + jnp.where(seen, jnp.log(size) + top * LN2, 0.0)
            shrink.append(1.0 / size)
            put_twice(ub_ref, cols, carried)
        if second is None:
            hist[k] = ub_ref[:states, :]
        else:
            weights_ref, row_begin, add_counts = second
            own_alpha = hist[k, own_rows(row_begin, weights_ref.shape[0]), :].astype(F32)
        for q, cols in enumerate(cuts):
            product = jnp.dot(mat[k], ub_ref[:, cols], preferred_element_type=F32)
            moving = is_moving(sel_ref, step_now, cols)
            pulled = product[:states] * shrink[q]
            if second is None:
                seen = is_seen(sel_ref, step_now, cols)
                begun = product[states : states + 1] * shrink[q]
                rest = jnp.where(seen, begun, back_ref[:, cols])
            else:
                total = column_sum(pulled * hist[k, :, cols].astype(F32))
                weight = jnp.where(moving, shrink[q] / total, 0.0)
                weights_ref[:, cols] = (own_alpha[:, cols] * weight).astype(BF16)
                rest = 1.0
            back_ref[:, cols] = jnp.where(moving, pulled, rest)
        if second is not None:
            add_counts(k, outer_sum(weights_ref, ub_ref[:states, :]))

    for k in reversed(range(1, steps)):
        step(k)
    if second is None:
        step(0)
    else:
        pl.when(lead > 0)(lambda: step(0))
        pl.when(lead == 0)(lambda: second[2](0, jnp.zeros((second[0].shape[0], states), F32)))
    return logs


def put_state(state_out, values, logs):
    states = state_out.shape[0] - EXTRA
    state_out[:states, :] = values
    for q, cols in enumerate(tiles(state_out.shape[1])):
        high = logs[q].astype(BF16).astype(F32)
        middle = (logs[q] - high).astype(BF16).astype(F32)
        row = lax.broadcasted_iota(jnp.int32, (EXTRA, LANES), 0)
        piece = jnp.where(
            row == 0, high, jnp.where(row == 1, middle, jnp.where(row == 2, logs[q] - high - middle, 0.0))
        )
        state_out[states:, cols] = piece.astype(BF16)


def state_logs(state_ref):
    states = state_ref.shape[0] - EXTRA
    return [column_sum(state_ref[states:, cols].astype(F32)) for cols in tiles(state_ref.shape[1])]


def first_kernel(resume, grids, part, rows_ref, mat, consts, *refs):
    state_in = refs[0] if resume else None
    hist, state_out, sel_ref, ab_ref, back_ref = refs[-5:]
    chunk = part * grids + (pl.program_id(0) if grids > 1 else 0)
    steps, states, width = hist.shape
    forward_first, lead = is_forward_first(), lax.axis_index("per") * steps
    cuts = tiles(width)
    group, half_periods, slot_rows = rows_ref.shape
    tops = 2 * len(cuts)

    def scan_source(d, carry):
        rank, picked = carry
        for slot in range(slot_rows // HB):
            cols = slice(slot * HB, (slot + 1) * HB)
            block = rows_ref[d, :, cols]
            live = block > -0.5 * SEEN
            picked = [jnp.where(live & (rank == chunk * tops + i), block, old) for i, old in enumerate(picked)]
            rank = rank + live.astype(jnp.int32)
        return rank, picked

    carry = (jnp.zeros((half_periods, HB), jnp.int32), [jnp.zeros((half_periods, HB), F32)] * tops)
    if group <= 8:
        for d in range(group):
            carry = scan_source(d, carry)
    else:
        carry = lax.fori_loop(0, group, scan_source, carry)
    low_lane = lax.broadcasted_iota(jnp.int32, (half_periods, HB), 1) < HALF
    for q, cols in enumerate(cuts):
        left, right = carry[1][2 * q], carry[1][2 * q + 1]
        before = jnp.zeros((1, HB), F32)
        for late in range(2):
            value = (
                jnp.where(low_lane, pltpu.roll(left, HALF, 1), right)
                if late
                else jnp.where(low_lane, left, pltpu.roll(right, HALF, 1))
            )
            seen = value > 0.5 * SEEN
            earn = jnp.where(seen, value - SEEN, value)
            seen = seen.astype(F32)
            for i in range(half_periods):
                at = late * half_periods + i
                now = seen[i : i + 1]
                sel_ref[0, at, :, cols] = jnp.broadcast_to(earn[i : i + 1], (8, HB))
                sel_ref[1, at, :, cols] = jnp.broadcast_to(now * before, (8, HB))
                sel_ref[2, at, :, cols] = jnp.broadcast_to(now, (8, HB))
                before = now
    zeros = [jnp.zeros((1, LANES), F32) for _ in cuts]

    @pl.when(forward_first)
    def _():
        if resume:
            put_twice(ab_ref, slice(None), state_in[:states, :])
        else:
            for cols in cuts:
                put_twice(ab_ref, cols, consts[0])
        logs = state_logs(state_in) if resume else list(zeros)
        logs = run_forward(lead, mat, hist, sel_ref, consts, ab_ref, logs)
        put_state(state_out, ab_ref[:states, :], logs)

    @pl.when(jnp.logical_not(forward_first))
    def _():
        if resume:
            back_ref[...] = state_in[:states, :].astype(F32)
        else:
            back_ref[...] = jnp.ones_like(back_ref)
        logs = state_logs(state_in) if resume else list(zeros)
        logs = run_backward(lead, mat, hist, sel_ref, consts, back_ref, ab_ref, logs)
        put_state(state_out, back_ref[...].astype(BF16), logs)


def second_kernel(resume, last, extend, grids, *refs):
    refs = list(refs)
    sel_ref, mat, consts, hist, own_state, state_in = (refs.pop(0) for _ in range(6))
    counts_in, sums_in = (refs.pop(0), refs.pop(0)) if resume else (None, None)
    row_probs = refs.pop(0) if last else None
    mine_ref, other_ref = (refs.pop(0), refs.pop(0)) if last else (None, None)
    counts_out, sums_out = (None, None) if last else (refs.pop(0), refs.pop(0))
    state_out = refs.pop(0) if extend else None
    ab_ref, back_ref, weights_ref = refs[:3]
    counts_ref, sums_ref = refs[3:] if last else (counts_out, sums_out)
    chunk = pl.program_id(0) if grids > 1 else 0
    steps, states, width = hist.shape
    core, forward_first = core_index(), is_forward_first()
    row_begin = lax.axis_index("hh") * weights_ref.shape[0]
    lead = lax.axis_index("per") * steps
    rows = weights_ref.shape[0]

    def centre(k, counts):
        probs = row_probs[k]
        weighted = probs * counts
        grad = weighted - probs * jnp.sum(weighted, axis=1, keepdims=True)
        at = slice(k * rows, (k + 1) * rows)
        left, right = grad[:, :LANES], grad[:, LANES:]
        mine_ref[at, :] = jnp.where(core == 0, left, right)
        other_ref[at, :] = jnp.where(core == 0, right, left)

    def add_counts(k, counts):
        if grids > 1:
            counts_ref[k] += counts
            return
        if resume:
            counts = counts + counts_in[k]
        if last:
            centre(k, counts)
        else:
            counts_ref[k] = counts

    second = (weights_ref, row_begin, add_counts)

    @pl.when(chunk == 0)
    def _():
        if grids > 1:
            counts_ref[...] = jnp.zeros_like(counts_ref)
        sums_ref[...] = sums_in[...] if resume else jnp.zeros_like(sums_ref)

    def add_sums(alpha_ref, other_state):
        total = jnp.zeros((1, LANES), F32)
        years = jnp.zeros((8, LANES), F32)
        for cols, here, there in zip(tiles(width), state_logs(alpha_ref), state_logs(other_state)):
            alpha = alpha_ref[:states, cols].astype(F32)
            meet = column_sum(alpha * other_state[:states, cols].astype(F32))
            total += here + there + jnp.log(meet / column_sum(alpha))
            years += jnp.sum(sel_ref[2, :, :, cols], axis=0)
        total = jnp.broadcast_to(jnp.sum(total, axis=1, keepdims=True), (1, LANES))
        years = jnp.broadcast_to(jnp.sum(years[:1], axis=1, keepdims=True), (1, LANES))
        row = lax.broadcasted_iota(jnp.int32, (8, LANES), 0)
        sums_ref[...] += jnp.where(row == 0, total, jnp.where(row == 1, years, 0.0))

    zeros = [jnp.zeros((1, LANES), F32) for _ in tiles(width)]

    @pl.when(jnp.logical_not(forward_first))
    def _():
        add_sums(state_in, own_state)
        put_twice(ab_ref, slice(None), state_in[:states, :])
        run_forward(lead, mat, hist, sel_ref, consts, ab_ref, list(zeros), second)
        if extend:
            put_state(state_out, ab_ref[:states, :], zeros)

    @pl.when(forward_first)
    def _():
        add_sums(own_state, state_in)
        back_ref[...] = state_in[:states, :].astype(F32)
        run_backward(lead, mat, hist, sel_ref, consts, back_ref, ab_ref, list(zeros), second)
        if extend:
            put_state(state_out, back_ref[...].astype(BF16), zeros)

    if last:

        @pl.when(chunk == grids - 1)
        def _():
            if grids > 1:
                for k in range(steps):
                    centre(k, counts_ref[k])
            mine_ref[steps * rows :, :] = sums_ref[...]
            other_ref[steps * rows :, :] = sums_ref[...]


def finish_kernel(scale, mine_ref, other_ref, grad_ref, mean_ref):
    count = grad_ref.shape[0]
    total = mine_ref[count : count + 1, :] + other_ref[count : count + 1, :]
    years = mine_ref[count + 1 : count + 2, :] + other_ref[count + 1 : count + 2, :]
    grad_ref[...] = (mine_ref[:count, :] + other_ref[:count, :]) * (scale / years)
    mean_ref[0] = (total / years)[0, 0]


def per_device(
    earnings, starts, lengths, block_count, trans_logits, init_logits, state_mean, log_sd
):
    slot_rows, periods = earnings.shape
    states = init_logits.shape[0]
    group = lax.axis_size(("hh", "per"))
    sides = lax.axis_size("per")
    cores = lax.axis_size("st")
    part = trans_logits.shape[0]
    steps = part * cores
    rows = states // lax.axis_size("hh")
    households = group * HB // cores
    parts = 2 if households <= 4 * HB else 1
    share = households // parts
    width = min(2 * HB, share)
    grids = share // width
    side = lax.axis_index("per")
    shaped = jax.ShapeDtypeStruct
    dma = pltpu.SemaphoreType.DMA

    swap = [(0, 1), (1, 0)]
    other_logits = lax.ppermute(trans_logits, "st", swap)
    vec_row = pltpu.VMEM((1, states), F32)
    packed, vectors = pl.pallas_call(
        pack_kernel,
        out_shape=[shaped((group, periods // 2, slot_rows), F32), shaped((8, states), F32)],
        in_specs=[smem()] + [hbm()] * 6,
        out_specs=[vmem()] * 2,
        scratch_shapes=[
            pltpu.VMEM((periods, slot_rows), F32),
            pltpu.VMEM((slot_rows // HB, HB), jnp.int32),
            pltpu.VMEM((slot_rows // HB, HB), jnp.int32),
            vec_row,
            vec_row,
            vec_row,
            dma((6,)),
        ],
        compiler_params=params(2),
        name="pack",
    )(
        block_count,
        *in_hbm(
            earnings.T, starts.reshape(-1, HB), lengths.reshape(-1, HB),
            init_logits.reshape(1, states), state_mean.reshape(1, states), log_sd.reshape(1, states),
        ),
    )
    gathered = lax.all_to_all(packed, ("hh", "per"), split_axis=0, concat_axis=0, tiled=True)
    first_mat, second_mat, row_probs, consts = pl.pallas_call(
        prep_kernel,
        out_shape=[
            pltpu.VMEM((steps, states + EXTRA, 2 * states), BF16),
            pltpu.HBM((steps, states, 2 * states), BF16),
            pltpu.VMEM((steps, rows, states), F32),
            pltpu.VMEM((4, states, LANES), F32),
        ],
        in_specs=[hbm(), hbm(), vmem()],
        out_specs=[vmem(), hbm(), vmem(), vmem()],
        scratch_shapes=[
            pltpu.VMEM((steps, states, 2 * states), BF16),
            pltpu.VMEM((states, states), F32),
            pltpu.VMEM(trans_logits.shape, BF16),
            pltpu.VMEM(trans_logits.shape, BF16),
            dma((2,)),
            dma((steps,)),
        ],
        compiler_params=params(6),
        name="prep",
    )(*in_hbm(trans_logits, other_logits), vectors)

    def whole(*shape):
        if grids == 1:
            return vmem()
        return pl.BlockSpec(shape, lambda g: (0,) * len(shape))

    def lanes(*lead):
        if grids == 1:
            return vmem()
        return pl.BlockSpec(lead + (width,), lambda g: (0,) * len(lead) + (g,))

    grid = (grids,) if grids > 1 else ()
    hist_shape = shaped((steps, states, share), BF16)
    state_shape = shaped((states + EXTRA, share), BF16)
    sel_shape = shaped((3, periods, 8, share), F32)
    swap_shape = shaped((steps * rows + 8, LANES), F32)
    counts_shape = shaped((steps, rows, states), F32)
    sums_shape = shaped((8, LANES), F32)
    hist_spec, state_spec, sel_spec = lanes(steps, states), lanes(states + EXTRA), lanes(3, periods, 8)
    const_spec = whole(4, states, LANES)

    def first_pass(index, state_in):
        resume = state_in is not None
        return pl.pallas_call(
            functools.partial(first_kernel, resume, grids, index),
            grid=grid,
            out_shape=[hist_shape, state_shape, sel_shape],
            in_specs=[whole(*gathered.shape), whole(*first_mat.shape), const_spec]
            + [state_spec] * resume,
            out_specs=[hist_spec, state_spec, sel_spec],
            scratch_shapes=[pltpu.VMEM((2 * states, width), BF16), pltpu.VMEM((states, width), F32)],
            compiler_params=params(8 if grids == 1 else 32),
            name="first_pass",
        )(gathered, first_mat, consts, *([state_in] if resume else []))

    def second_pass(kept, state_in, sums_in, last, extend):
        hist, own_state, sel = kept
        resume = sums_in is not None
        scratch = [
            pltpu.VMEM((2 * states, width), BF16),
            pltpu.VMEM((states, width), F32),
            pltpu.VMEM((rows, width), BF16),
        ]
        counts_spec, sums_spec = whole(*counts_shape.shape), whole(*sums_shape.shape)
        if last:
            out_shape = [swap_shape] * 2
            scratch += [pltpu.VMEM(counts_shape.shape, F32), pltpu.VMEM(sums_shape.shape, F32)]
        else:
            out_shape = [counts_shape, sums_shape]
        out_specs = [whole(*x.shape) for x in out_shape]
        if extend:
            out_shape, out_specs = out_shape + [state_shape], out_specs + [state_spec]
        return pl.pallas_call(
            functools.partial(second_kernel, resume, last, extend, grids),
            grid=grid,
            out_shape=out_shape,
            in_specs=[sel_spec, whole(*second_mat.shape), const_spec, hist_spec, state_spec, state_spec]
            + [counts_spec, sums_spec] * resume
            + [whole(*row_probs.shape)] * last,
            out_specs=out_specs,
            scratch_shapes=scratch,
            compiler_params=params(8 if grids == 1 else 32),
            name="second_pass",
        )(
            sel, second_mat, consts, hist, own_state, state_in,
            *(sums_in if resume else []),
            *([row_probs] if last else []),
        )

    def hand_over(state, stage):
        moves = [(stage, stage + 1), (sides - 1 - stage, sides - 2 - stage)]
        return lax.ppermute(state, "per", moves)

    if sides == 2:
        kept = [first_pass(index, None) for index in range(parts)]
        arrived = [hand_over(each[1], 0) for each in kept]
        sums = None
        for index in range(parts):
            sums = second_pass(kept[index], arrived[index], sums, index == parts - 1, False)
        mine, other = sums
    else:
        kept = [jnp.zeros(x.shape, x.dtype) for x in (hist_shape, state_shape, sel_shape)]
        done = [jnp.zeros(x.shape, x.dtype) for x in (swap_shape, swap_shape, state_shape)]
        state = None
        for stage in range(sides):
            active = (side == stage) | (side == sides - 1 - stage)
            if stage < sides // 2:
                kept = lax.cond(
                    active, lambda x, kept: list(first_pass(0, x)), lambda x, kept: kept, state, kept
                )
                state = kept[1]
            else:
                done = lax.cond(
                    active,
                    lambda x, done: list(second_pass(kept, x, None, True, True)),
                    lambda x, done: done,
                    state,
                    done,
                )
                state = done[2]
            if stage < sides - 1:
                state = hand_over(state, stage)
        mine, other, _ = done
        total = jnp.where(side == sides // 2, mine[steps * rows], 0.0)
        total = lax.psum(total, "per")
        mine = mine.at[steps * rows].set(total)
        other = other.at[steps * rows].set(total)
    received = lax.ppermute(other, "st", swap)
    trans_grad, mean_loglik = pl.pallas_call(
        functools.partial(finish_kernel, float(states * states * periods)),
        out_shape=[shaped((steps * rows, LANES), F32), shaped((1,), F32)],
        in_specs=[vmem(), vmem()],
        out_specs=[vmem(), smem()],
        compiler_params=params(4),
        name="finish",
    )(mine, received)
    return (trans_grad.reshape(steps, rows, LANES), mean_loglik)


def solution(mesh):
    placed = (
        P(("hh", "per"), None),
        P(("hh", "per")),
        P(("hh", "per")),
        P(("hh", "per")),
        P(("grp", "per", "st"), None, None),
        P("grp"),
        P("grp"),
        P("grp"),
    )
    return jax.shard_map(
        per_device,
        mesh=mesh,
        in_specs=placed,
        out_specs=(P(("grp", "per"), "hh", "st"), P("grp")),
        check_vma=False,
    )
```

```python
import functools

import jax
import jax.numpy as jnp
from jax import lax
from jax.experimental import pallas as pl
from jax.experimental.pallas import tpu as pltpu
from jax.sharding import PartitionSpec as P

HB = 128
LANES = 128
HALF = HB // 2
SEEN = 16.0
F32 = jnp.float32
BF16 = jnp.bfloat16
LOG2E = 1.4426950408889634
LN2 = 0.6931471805599453
EXTRA = 16


def vmem():
    return pl.BlockSpec(memory_space=pltpu.VMEM)


def smem():
    return pl.BlockSpec(memory_space=pltpu.SMEM)


def hbm():
    return pl.BlockSpec(memory_space=pltpu.HBM)


def in_hbm(*arrays):
    return [pltpu.with_memory_space_constraint(x, pltpu.HBM) for x in arrays]


def params(mebibytes):
    return pltpu.CompilerParams(vmem_limit_bytes=mebibytes * 1024 * 1024)


def core_index():
    return lax.axis_index("st")


def is_forward_first():
    return 2 * lax.axis_index("per") < lax.axis_size("per")


def tiles(width):
    return [slice(q, q + LANES) for q in range(0, width, LANES)]


def fetch(pairs, sems):
    copies = [pltpu.make_async_copy(src, dst, sems.at[i]) for i, (src, dst) in enumerate(pairs)]
    for copy in copies:
        copy.start()
    for copy in copies:
        copy.wait()


def pack_kernel(
    count_ref, earn_any, start_any, len_any, init_any, mean_any, sd_any, own_any, out_ref, vec_ref, own_ref,
    earn_ref, start_ref, len_ref, init_ref, mean_ref, sd_ref, sems,
):
    fetch(
        (
            (earn_any, earn_ref), (start_any, start_ref), (len_any, len_ref),
            (init_any, init_ref), (mean_any, mean_ref), (sd_any, sd_ref), (own_any, own_ref),
        ),
        sems,
    )
    periods, slot_rows = earn_ref.shape
    core = core_index()
    low_lane = lax.broadcasted_iota(jnp.int32, (periods // 2, HB), 1) < HALF
    time = lax.broadcasted_iota(jnp.int32, (periods, HB), 0)
    for slot in range(slot_rows // HB):
        cols = slice(slot * HB, (slot + 1) * HB)
        begin = start_ref[slot : slot + 1, :]
        seen = (time >= begin) & (time < begin + len_ref[slot : slot + 1, :])
        live = slot < count_ref[0]
        shift = jnp.where(live, jnp.where(seen, SEEN, 0.0), -SEEN)
        value = earn_ref[:, cols] + shift
        early, late = value[: periods // 2], value[periods // 2 :]
        turned = pltpu.roll(jnp.where(core == 0, late, early), HALF, 1)
        packed = jnp.where(low_lane, jnp.where(core == 0, early, turned), jnp.where(core == 0, turned, late))
        for to in range(out_ref.shape[0]):
            out_ref[to, :, cols] = packed
    raised = jnp.exp(init_ref[...])
    start = raised / jnp.sum(raised, axis=1, keepdims=True)
    row = lax.broadcasted_iota(jnp.int32, vec_ref.shape, 0)
    power = (-0.5 * LOG2E) * jnp.exp(-2.0 * sd_ref[...])
    vec_ref[...] = jnp.where(
        row == 0, start, jnp.where(row == 1, mean_ref[...], jnp.where(row == 2, power, -LOG2E * sd_ref[...]))
    )


def put(ref, at, value):
    states = value.shape[0]
    high = value.astype(BF16)
    ref[at, :states, :states] = high
    ref[at, :states, states:] = (value - high.astype(F32)).astype(BF16)


def put_twice(ref, cols, value):
    states = value.shape[0]
    value = value.astype(BF16)
    ref[:states, cols] = value
    ref[states:, cols] = value


def prep_kernel(
    own_ref, other_any, vec_ref, first_mat, second_any, row_probs, consts,
    second_mat, scratch, other_ref, sem, out_sems,
):
    copy = pltpu.make_async_copy(other_any, other_ref, sem)
    copy.start()
    part, states, _ = own_ref.shape

    def leave(at):
        return pltpu.make_async_copy(second_mat.at[at], second_any.at[at], out_sems.at[at])

    rows = row_probs.shape[1]
    for i in range(4):
        consts[i] = jnp.broadcast_to(vec_ref[i : i + 1, :], (LANES, states)).T
    for source, ref in ((core_index(), own_ref), (1 - core_index(), other_ref)):
        if ref is other_ref:
            copy.wait()

        @pl.loop(0, part)
        def _(i):
            at = source * part + i
            lifted = jnp.exp(ref[i].astype(F32))
            probs = lifted * (1.0 / jnp.sum(lifted, axis=1, keepdims=True))
            scratch[...] = probs
            row_probs[at] = scratch[own_rows(lax.axis_index("hh") * rows, rows), :]

            @pl.when(is_forward_first())
            def _():
                put(first_mat, at, probs.T)
                put(second_mat, at, probs)

            @pl.when(jnp.logical_not(is_forward_first()))
            def _():
                put(first_mat, at, probs)
                put(second_mat, at, probs.T)

            leave(at).start()

    for at in range(2 * part):
        leave(at).wait()


def emission(sel_ref, consts, step_now, cols, less):
    gap = sel_ref[0, step_now, :1, cols] - consts[1]
    power = gap * gap * consts[2] + consts[3]
    top = jnp.max(power, axis=0, keepdims=True)
    return jnp.exp2(power - (top + less)), top


def is_moving(sel_ref, step_now, cols):
    return sel_ref[1, step_now, :1, cols] > 0.5


def is_seen(sel_ref, step_now, cols):
    return sel_ref[2, step_now, :1, cols] > 0.5


def column_sum(x):
    return jnp.sum(x, axis=0, keepdims=True)


def own_rows(row_begin, rows):
    return pl.ds(pl.multiple_of(row_begin, rows), rows)


def outer_sum(weights_ref, carried):
    return lax.dot_general(weights_ref[...], carried, (((1,), (1,)), ((), ())), preferred_element_type=F32)


def run_forward(lead, mat, hist, sel_ref, consts, ab_ref, logs, second=None):
    steps, states, width = hist.shape
    cuts = tiles(width)
    size = [jnp.log2(column_sum(ab_ref[:states, cols].astype(F32))) for cols in cuts]
    for k in range(steps):
        step_now = lead + k
        if second is None:
            hist[k] = ab_ref[:states, :]
        else:
            weights_ref, row_begin, add_counts = second
            own_alpha = ab_ref[own_rows(row_begin, weights_ref.shape[0]), :].astype(F32)
        for q, cols in enumerate(cuts):
            product = jnp.dot(mat[k], ab_ref[:, cols], preferred_element_type=F32)
            moving = is_moving(sel_ref, step_now, cols)
            if second is not None:
                total = column_sum(product * hist[k, :, cols].astype(F32))
                weight = jnp.where(moving, 1.0 / total, 0.0)
                weights_ref[:, cols] = (own_alpha[:, cols] * weight).astype(BF16)
            emit, top = emission(sel_ref, consts, step_now, cols, jnp.where(moving, size[q], 0.0))
            joint = jnp.where(moving, product, consts[0]) * emit
            put_twice(ab_ref, cols, joint)
            size[q] = jnp.log2(column_sum(joint))
            if second is None:
                seen = is_seen(sel_ref, step_now, cols)
                logs[q] = logs[q] + jnp.where(seen, size[q] + top, 0.0)
        if second is not None:
            add_counts(k, outer_sum(weights_ref, hist[k]))
    return logs


def run_backward(lead, mat, hist, sel_ref, consts, state, ub_ref, logs, leave, second=None):
    steps, states, width = hist.shape
    cuts = tiles(width)
    rest = [x[:1] for x in state]
    size = [jnp.zeros((1, LANES), F32) for _ in cuts]

    def step(k):
        step_now = lead + k
        grown = []
        for q, cols in enumerate(cuts):
            emit, top = emission(sel_ref, consts, step_now, cols, size[q])
            carried = emit * state[q]
            put_twice(ub_ref, cols, carried)
            whole = column_sum(carried)
            grown.append(whole)
            size[q] = jnp.log2(whole)
            if second is None:
                seen = is_seen(sel_ref, step_now, cols)
                logs[q] = logs[q] + jnp.where(seen, size[q] + top, 0.0)
                begun = column_sum(carried * consts[0]) / whole
                rest[q] = jnp.where(seen, begun, rest[q])
        if second is None:
            hist[k] = ub_ref[:states, :]
        else:
            weights_ref, row_begin, add_counts = second
            own_alpha = hist[k, own_rows(row_begin, weights_ref.shape[0]), :].astype(F32)
        for q, cols in enumerate(cuts):
            product = jnp.dot(mat[k], ub_ref[:, cols], preferred_element_type=F32)
            moving = is_moving(sel_ref, step_now, cols)
            if second is not None:
                total = column_sum(product * hist[k, :, cols].astype(F32))
                weight = jnp.where(moving, 1.0 / total, 0.0)
                weights_ref[:, cols] = (own_alpha[:, cols] * weight).astype(BF16)
            state[q] = jnp.where(moving, product, rest[q] * grown[q])
        if second is not None:
            add_counts(k, outer_sum(weights_ref, ub_ref[:states, :]))

    def left():
        return [x * jnp.exp2(-y) for x, y in zip(state, size)]

    for k in reversed(range(1, steps)):
        step(k)
    if second is None:
        step(0)
        leave(left())
        return

    @pl.when(lead > 0)
    def _():
        step(0)
        leave(left())

    @pl.when(lead == 0)
    def _():
        second[2](0, jnp.zeros((second[0].shape[0], states), F32))


def put_state(state_out, values, logs):
    states = state_out.shape[0] - EXTRA
    row = lax.broadcasted_iota(jnp.int32, (EXTRA, LANES), 0)
    for q, cols in enumerate(tiles(state_out.shape[1])):
        state_out[:states, cols] = values[q].astype(BF16)
        high = logs[q].astype(BF16).astype(F32)
        middle = (logs[q] - high).astype(BF16).astype(F32)
        piece = jnp.where(
            row == 0, high, jnp.where(row == 1, middle, jnp.where(row == 2, logs[q] - high - middle, 0.0))
        )
        state_out[states:, cols] = piece.astype(BF16)


def state_logs(state_ref):
    states = state_ref.shape[0] - EXTRA
    return [column_sum(state_ref[states:, cols].astype(F32)) for cols in tiles(state_ref.shape[1])]


def first_kernel(resume, grids, part, rows_ref, mat, consts, *refs):
    state_in = refs[0] if resume else None
    hist, state_out, sel_ref, ab_ref = refs[-4:]
    chunk = part * grids + (pl.program_id(0) if grids > 1 else 0)
    steps, states, width = hist.shape
    forward_first, lead = is_forward_first(), lax.axis_index("per") * steps
    cuts = tiles(width)
    group, half_periods, slot_rows = rows_ref.shape
    tops = 2 * len(cuts)

    def scan_source(d, carry):
        rank, picked = carry
        for slot in range(slot_rows // HB):
            cols = slice(slot * HB, (slot + 1) * HB)
            block = rows_ref[d, :, cols]
            live = block > -0.5 * SEEN
            picked = [jnp.where(live & (rank == chunk * tops + i), block, old) for i, old in enumerate(picked)]
            rank = rank + live.astype(jnp.int32)
        return rank, picked

    carry = (jnp.zeros((half_periods, HB), jnp.int32), [jnp.zeros((half_periods, HB), F32)] * tops)
    if group <= 8:
        for d in range(group):
            carry = scan_source(d, carry)
    else:
        carry = lax.fori_loop(0, group, scan_source, carry)
    low_lane = lax.broadcasted_iota(jnp.int32, (half_periods, HB), 1) < HALF
    for q, cols in enumerate(cuts):
        left, right = carry[1][2 * q], carry[1][2 * q + 1]
        before = jnp.zeros((1, HB), F32)
        for late in range(2):
            value = (
                jnp.where(low_lane, pltpu.roll(left, HALF, 1), right)
                if late
                else jnp.where(low_lane, left, pltpu.roll(right, HALF, 1))
            )
            seen = value > 0.5 * SEEN
            earn = jnp.where(seen, value - SEEN, value)
            seen = seen.astype(F32)
            for i in range(half_periods):
                at = late * half_periods + i
                now = seen[i : i + 1]
                sel_ref[0, at, :, cols] = jnp.broadcast_to(earn[i : i + 1], (8, HB))
                sel_ref[1, at, :, cols] = jnp.broadcast_to(now * before, (8, HB))
                sel_ref[2, at, :, cols] = jnp.broadcast_to(now, (8, HB))
                before = now
    zeros = [jnp.zeros((1, LANES), F32) for _ in cuts]

    @pl.when(forward_first)
    def _():
        if resume:
            put_twice(ab_ref, slice(None), state_in[:states, :])
        else:
            for cols in cuts:
                put_twice(ab_ref, cols, consts[0])
        logs = state_logs(state_in) if resume else list(zeros)
        run_forward(lead, mat, hist, sel_ref, consts, ab_ref, logs)
        put_state(state_out, [ab_ref[:states, cols] for cols in cuts], logs)

    @pl.when(jnp.logical_not(forward_first))
    def _():
        state = [
            state_in[:states, cols].astype(F32) if resume else jnp.ones((states, LANES), F32) for cols in cuts
        ]
        logs = state_logs(state_in) if resume else list(zeros)
        leave = lambda values: put_state(state_out, values, logs)
        run_backward(lead, mat, hist, sel_ref, consts, state, ab_ref, logs, leave)


def second_kernel(resume, last, extend, grids, *refs):
    refs = list(refs)
    sel_ref, mat, consts, hist, own_state, state_in = (refs.pop(0) for _ in range(6))
    counts_in, sums_in = (refs.pop(0), refs.pop(0)) if resume else (None, None)
    row_probs = refs.pop(0) if last else None
    mine_ref, other_ref = (refs.pop(0), refs.pop(0)) if last else (None, None)
    counts_out, sums_out = (None, None) if last else (refs.pop(0), refs.pop(0))
    state_out = refs.pop(0) if extend else None
    ab_ref, weights_ref = refs[:2]
    counts_ref, sums_ref = refs[2:] if last else (counts_out, sums_out)
    chunk = pl.program_id(0) if grids > 1 else 0
    steps, states, width = hist.shape
    core, forward_first = core_index(), is_forward_first()
    row_begin = lax.axis_index("hh") * weights_ref.shape[0]
    lead = lax.axis_index("per") * steps
    rows = weights_ref.shape[0]

    def centre(k, counts):
        probs = row_probs[k]
        weighted = probs * counts
        grad = weighted - probs * jnp.sum(weighted, axis=1, keepdims=True)
        at = slice(k * rows, (k + 1) * rows)
        left, right = grad[:, :LANES], grad[:, LANES:]
        mine_ref[at, :] = jnp.where(core == 0, left, right)
        other_ref[at, :] = jnp.where(core == 0, right, left)

    def add_counts(k, counts):
        if grids > 1:
            counts_ref[k] += counts
            return
        if resume:
            counts = counts + counts_in[k]
        if last:
            centre(k, counts)
        else:
            counts_ref[k] = counts

    second = (weights_ref, row_begin, add_counts)

    @pl.when(chunk == 0)
    def _():
        if grids > 1:
            counts_ref[...] = jnp.zeros_like(counts_ref)
        sums_ref[...] = sums_in[...] if resume else jnp.zeros_like(sums_ref)

    def add_sums(alpha_ref, other_state):
        total = jnp.zeros((1, LANES), F32)
        years = jnp.zeros((8, LANES), F32)
        for cols, here, there in zip(tiles(width), state_logs(alpha_ref), state_logs(other_state)):
            alpha = alpha_ref[:states, cols].astype(F32)
            meet = column_sum(alpha * other_state[:states, cols].astype(F32))
            total += (here + there + jnp.log2(meet / column_sum(alpha))) * LN2
            years += jnp.sum(sel_ref[2, :, :, cols], axis=0)
        total = jnp.broadcast_to(jnp.sum(total, axis=1, keepdims=True), (1, LANES))
        years = jnp.broadcast_to(jnp.sum(years[:1], axis=1, keepdims=True), (1, LANES))
        row = lax.broadcasted_iota(jnp.int32, (8, LANES), 0)
        sums_ref[...] += jnp.where(row == 0, total, jnp.where(row == 1, years, 0.0))

    zeros = [jnp.zeros((1, LANES), F32) for _ in tiles(width)]

    @pl.when(jnp.logical_not(forward_first))
    def _():
        add_sums(state_in, own_state)
        put_twice(ab_ref, slice(None), state_in[:states, :])
        run_forward(lead, mat, hist, sel_ref, consts, ab_ref, list(zeros), second)
        if extend:
            put_state(state_out, [ab_ref[:states, cols] for cols in tiles(width)], zeros)

    @pl.when(forward_first)
    def _():
        add_sums(own_state, state_in)
        state = [state_in[:states, cols].astype(F32) for cols in tiles(width)]
        leave = lambda values: put_state(state_out, values, zeros) if extend else None
        run_backward(lead, mat, hist, sel_ref, consts, state, ab_ref, list(zeros), leave, second)

    if last:

        @pl.when(chunk == grids - 1)
        def _():
            if grids > 1:
                for k in range(steps):
                    centre(k, counts_ref[k])
            mine_ref[steps * rows :, :] = sums_ref[...]
            other_ref[steps * rows :, :] = sums_ref[...]


def finish_kernel(scale, mine_ref, other_ref, grad_ref, mean_ref):
    count = grad_ref.shape[0]
    total = mine_ref[count : count + 1, :] + other_ref[count : count + 1, :]
    years = mine_ref[count + 1 : count + 2, :] + other_ref[count + 1 : count + 2, :]
    grad_ref[...] = (mine_ref[:count, :] + other_ref[:count, :]) * (scale / years)
    mean_ref[0] = (total / years)[0, 0]


def per_device(
    earnings, starts, lengths, block_count, trans_logits, init_logits, state_mean, log_sd
):
    slot_rows, periods = earnings.shape
    states = init_logits.shape[0]
    group = lax.axis_size(("hh", "per"))
    sides = lax.axis_size("per")
    cores = lax.axis_size("st")
    part = trans_logits.shape[0]
    steps = part * cores
    rows = states // lax.axis_size("hh")
    households = group * HB // cores
    parts = 2 if households <= 4 * HB else 1
    share = households // parts
    width = min(2 * HB, share)
    grids = share // width
    side = lax.axis_index("per")
    shaped = jax.ShapeDtypeStruct
    dma = pltpu.SemaphoreType.DMA

    swap = [(0, 1), (1, 0)]
    other_logits = lax.ppermute(trans_logits, "st", swap)
    vec_row = pltpu.VMEM((1, states), F32)
    packed, vectors, own_logits = pl.pallas_call(
        pack_kernel,
        out_shape=[
            shaped((group, periods // 2, slot_rows), F32),
            shaped((8, states), F32),
            pltpu.VMEM(trans_logits.shape, BF16),
        ],
        in_specs=[smem()] + [hbm()] * 7,
        out_specs=[vmem()] * 3,
        scratch_shapes=[
            pltpu.VMEM((periods, slot_rows), F32),
            pltpu.VMEM((slot_rows // HB, HB), jnp.int32),
            pltpu.VMEM((slot_rows // HB, HB), jnp.int32),
            vec_row,
            vec_row,
            vec_row,
            dma((7,)),
        ],
        compiler_params=params(2),
        name="pack",
    )(
        block_count,
        *in_hbm(
            earnings.T, starts.reshape(-1, HB), lengths.reshape(-1, HB),
            init_logits.reshape(1, states), state_mean.reshape(1, states), log_sd.reshape(1, states), trans_logits,
        ),
    )
    gathered = lax.all_to_all(packed, ("hh", "per"), split_axis=0, concat_axis=0, tiled=True)
    first_mat, second_mat, row_probs, consts = pl.pallas_call(
        prep_kernel,
        out_shape=[
            pltpu.VMEM((steps, states, 2 * states), BF16),
            pltpu.HBM((steps, states, 2 * states), BF16),
            pltpu.VMEM((steps, rows, states), F32),
            pltpu.VMEM((4, states, LANES), F32),
        ],
        in_specs=[vmem(), hbm(), vmem()],
        out_specs=[vmem(), hbm(), vmem(), vmem()],
        scratch_shapes=[
            pltpu.VMEM((steps, states, 2 * states), BF16),
            pltpu.VMEM((states, states), F32),
            pltpu.VMEM(trans_logits.shape, BF16),
            dma,
            dma((steps,)),
        ],
        compiler_params=params(6),
        name="prep",
    )(own_logits, *in_hbm(other_logits), vectors)

    def whole(*shape):
        if grids == 1:
            return vmem()
        return pl.BlockSpec(shape, lambda g: (0,) * len(shape))

    def lanes(*lead):
        if grids == 1:
            return vmem()
        return pl.BlockSpec(lead + (width,), lambda g: (0,) * len(lead) + (g,))

    grid = (grids,) if grids > 1 else ()
    hist_shape = shaped((steps, states, share), BF16)
    state_shape = shaped((states + EXTRA, share), BF16)
    sel_shape = shaped((3, periods, 8, share), F32)
    swap_shape = shaped((steps * rows + 8, LANES), F32)
    counts_shape = shaped((steps, rows, states), F32)
    sums_shape = shaped((8, LANES), F32)
    hist_spec, state_spec, sel_spec = lanes(steps, states), lanes(states + EXTRA), lanes(3, periods, 8)
    const_spec = whole(4, states, LANES)

    def first_pass(index, state_in):
        resume = state_in is not None
        return pl.pallas_call(
            functools.partial(first_kernel, resume, grids, index),
            grid=grid,
            out_shape=[hist_shape, state_shape, sel_shape],
            in_specs=[whole(*gathered.shape), whole(*first_mat.shape), const_spec]
            + [state_spec] * resume,
            out_specs=[hist_spec, state_spec, sel_spec],
            scratch_shapes=[pltpu.VMEM((2 * states, width), BF16)],
            compiler_params=params(8 if grids == 1 else 32),
            name="first_pass",
        )(gathered, first_mat, consts, *([state_in] if resume else []))

    def second_pass(kept, state_in, sums_in, last, extend):
        hist, own_state, sel = kept
        resume = sums_in is not None
        scratch = [
            pltpu.VMEM((2 * states, width), BF16),
            pltpu.VMEM((rows, width), BF16),
        ]
        counts_spec, sums_spec = whole(*counts_shape.shape), whole(*sums_shape.shape)
        if last:
            out_shape = [swap_shape] * 2
            scratch += [pltpu.VMEM(counts_shape.shape, F32), pltpu.VMEM(sums_shape.shape, F32)]
        else:
            out_shape = [counts_shape, sums_shape]
        out_specs = [whole(*x.shape) for x in out_shape]
        if extend:
            out_shape, out_specs = out_shape + [state_shape], out_specs + [state_spec]
        return pl.pallas_call(
            functools.partial(second_kernel, resume, last, extend, grids),
            grid=grid,
            out_shape=out_shape,
            in_specs=[sel_spec, whole(*second_mat.shape), const_spec, hist_spec, state_spec, state_spec]
            + [counts_spec, sums_spec] * resume
            + [whole(*row_probs.shape)] * last,
            out_specs=out_specs,
            scratch_shapes=scratch,
            compiler_params=params(8 if grids == 1 else 32),
            name="second_pass",
        )(
            sel, second_mat, consts, hist, own_state, state_in,
            *(sums_in if resume else []),
            *([row_probs] if last else []),
        )

    def hand_over(state, stage):
        moves = [(stage, stage + 1), (sides - 1 - stage, sides - 2 - stage)]
        return lax.ppermute(state, "per", moves)

    if sides == 2:
        kept = [first_pass(index, None) for index in range(parts)]
        arrived = [hand_over(each[1], 0) for each in kept]
        sums = None
        for index in range(parts):
            sums = second_pass(kept[index], arrived[index], sums, index == parts - 1, False)
        mine, other = sums
    else:
        kept = [jnp.zeros(x.shape, x.dtype) for x in (hist_shape, state_shape, sel_shape)]
        done = [jnp.zeros(x.shape, x.dtype) for x in (swap_shape, swap_shape, state_shape)]
        state = None
        for stage in range(sides):
            active = (side == stage) | (side == sides - 1 - stage)
            if stage < sides // 2:
                kept = lax.cond(
                    active, lambda x, kept: list(first_pass(0, x)), lambda x, kept: kept, state, kept
                )
                state = kept[1]
            else:
                done = lax.cond(
                    active,
                    lambda x, done: list(second_pass(kept, x, None, True, True)),
                    lambda x, done: done,
                    state,
                    done,
                )
                state = done[2]
            if stage < sides - 1:
                state = hand_over(state, stage)
        mine, other, _ = done
        total = jnp.where(side == sides // 2, mine[steps * rows], 0.0)
        total = lax.psum(total, "per")
        mine = mine.at[steps * rows].set(total)
        other = other.at[steps * rows].set(total)
    received = lax.ppermute(other, "st", swap)
    trans_grad, mean_loglik = pl.pallas_call(
        functools.partial(finish_kernel, float(states * states * periods)),
        out_shape=[shaped((steps * rows, LANES), F32), shaped((1,), F32)],
        in_specs=[vmem(), vmem()],
        out_specs=[vmem(), smem()],
        compiler_params=params(4),
        name="finish",
    )(mine, received)
    return (trans_grad.reshape(steps, rows, LANES), mean_loglik)


def solution(mesh):
    placed = (
        P(("hh", "per"), None),
        P(("hh", "per")),
        P(("hh", "per")),
        P(("hh", "per")),
        P(("grp", "per", "st"), None, None),
        P("grp"),
        P("grp"),
        P("grp"),
    )
    return jax.shard_map(
        per_device,
        mesh=mesh,
        in_specs=placed,
        out_specs=(P(("grp", "per"), "hh", "st"), P("grp")),
        check_vma=False,
    )
```

```python
import functools

import jax
import jax.numpy as jnp
from jax import lax
from jax.experimental import pallas as pl
from jax.experimental.pallas import tpu as pltpu
from jax.sharding import PartitionSpec as P

HB = 128
LANES = 128
HALF = HB // 2
SEEN = 16.0
F32 = jnp.float32
BF16 = jnp.bfloat16
LOG2E = 1.4426950408889634
LN2 = 0.6931471805599453
EXTRA = 16


def vmem():
    return pl.BlockSpec(memory_space=pltpu.VMEM)


def smem():
    return pl.BlockSpec(memory_space=pltpu.SMEM)


def hbm():
    return pl.BlockSpec(memory_space=pltpu.HBM)


def in_hbm(*arrays):
    return [pltpu.with_memory_space_constraint(x, pltpu.HBM) for x in arrays]


def params(mebibytes):
    return pltpu.CompilerParams(vmem_limit_bytes=mebibytes * 1024 * 1024)


def core_index():
    return lax.axis_index("st")


def is_forward_first():
    return 2 * lax.axis_index("per") < lax.axis_size("per")


def tiles(width):
    return [slice(q, q + LANES) for q in range(0, width, LANES)]


def fetch(pairs, sems):
    copies = [pltpu.make_async_copy(src, dst, sems.at[i]) for i, (src, dst) in enumerate(pairs)]
    for copy in copies:
        copy.start()
    for copy in copies:
        copy.wait()


def pack_kernel(
    count_ref, earn_any, start_any, len_any, init_any, mean_any, sd_any, out_ref, vec_ref,
    earn_ref, start_ref, len_ref, init_ref, mean_ref, sd_ref, sems,
):
    fetch(
        (
            (earn_any, earn_ref), (start_any, start_ref), (len_any, len_ref),
            (init_any, init_ref), (mean_any, mean_ref), (sd_any, sd_ref),
        ),
        sems,
    )
    periods, slot_rows = earn_ref.shape
    core = core_index()
    low_lane = lax.broadcasted_iota(jnp.int32, (periods // 2, HB), 1) < HALF
    time = lax.broadcasted_iota(jnp.int32, (periods, HB), 0)
    for slot in range(slot_rows // HB):
        cols = slice(slot * HB, (slot + 1) * HB)
        begin = start_ref[slot : slot + 1, :]
        seen = (time >= begin) & (time < begin + len_ref[slot : slot + 1, :])
        live = slot < count_ref[0]
        shift = jnp.where(live, jnp.where(seen, SEEN, 0.0), -SEEN)
        value = earn_ref[:, cols] + shift
        early, late = value[: periods // 2], value[periods // 2 :]
        turned = pltpu.roll(jnp.where(core == 0, late, early), HALF, 1)
        packed = jnp.where(low_lane, jnp.where(core == 0, early, turned), jnp.where(core == 0, turned, late))
        for to in range(out_ref.shape[0]):
            out_ref[to, :, cols] = packed
    raised = jnp.exp(init_ref[...])
    start = raised / jnp.sum(raised, axis=1, keepdims=True)
    row = lax.broadcasted_iota(jnp.int32, vec_ref.shape, 0)
    power = (-0.5 * LOG2E) * jnp.exp(-2.0 * sd_ref[...])
    vec_ref[...] = jnp.where(
        row == 0, start, jnp.where(row == 1, mean_ref[...], jnp.where(row == 2, power, -LOG2E * sd_ref[...]))
    )


def put(ref, at, value):
    states = value.shape[0]
    high = value.astype(BF16)
    ref[at, :states, :states] = high
    ref[at, :states, states:] = (value - high.astype(F32)).astype(BF16)


def put_twice(ref, cols, value):
    states = value.shape[0]
    value = value.astype(BF16)
    ref[:states, cols] = value
    ref[states:, cols] = value


def prep_kernel(
    own_any, other_any, vec_ref, first_mat, second_any, row_probs, consts,
    second_mat, scratch, own_ref, other_ref, sems, out_sems,
):
    copies = [
        pltpu.make_async_copy(src, dst, sems.at[i])
        for i, (src, dst) in enumerate(((own_any, own_ref), (other_any, other_ref)))
    ]
    for copy in copies:
        copy.start()
    part, states, _ = own_ref.shape

    def leave(at):
        return pltpu.make_async_copy(second_mat.at[at], second_any.at[at], out_sems.at[at])

    rows = row_probs.shape[1]
    for i in range(4):
        consts[i] = jnp.broadcast_to(vec_ref[i : i + 1, :], (LANES, states)).T
    for copy, source, ref in zip(copies, (core_index(), 1 - core_index()), (own_ref, other_ref)):
        copy.wait()

        @pl.loop(0, part)
        def _(i):
            at = source * part + i
            lifted = jnp.exp(ref[i].astype(F32))
            probs = lifted * (1.0 / jnp.sum(lifted, axis=1, keepdims=True))
            scratch[...] = probs
            row_probs[at] = scratch[own_rows(lax.axis_index("hh") * rows, rows), :]

            @pl.when(is_forward_first())
            def _():
                put(first_mat, at, probs.T)
                put(second_mat, at, probs)

            @pl.when(jnp.logical_not(is_forward_first()))
            def _():
                put(first_mat, at, probs)
                put(second_mat, at, probs.T)

            leave(at).start()

    for at in range(2 * part):
        leave(at).wait()


def emission(sel_ref, consts, step_now, cols, less):
    gap = sel_ref[0, step_now, :1, cols] - consts[1]
    power = gap * gap * consts[2] + consts[3]
    top = jnp.max(power, axis=0, keepdims=True)
    return jnp.exp2(power - (top if less is None else top + less)), top


def is_moving(sel_ref, step_now, cols):
    return sel_ref[1, step_now, :1, cols] > 0.5


def is_seen(sel_ref, step_now, cols):
    return sel_ref[2, step_now, :1, cols] > 0.5


def column_sum(x):
    return jnp.sum(x, axis=0, keepdims=True)


def own_rows(row_begin, rows):
    return pl.ds(pl.multiple_of(row_begin, rows), rows)


def outer_sum(weights_ref, carried):
    return lax.dot_general(weights_ref[...], carried, (((1,), (1,)), ((), ())), preferred_element_type=F32)


def run_forward(lead, mat, hist, sel_ref, consts, ab_ref, logs, second=None):
    steps, states, width = hist.shape
    cuts = tiles(width)
    inverse = [1.0 / column_sum(ab_ref[:states, cols].astype(F32)) for cols in cuts]
    for k in range(steps):
        step_now = lead + k
        if second is None:
            hist[k] = ab_ref[:states, :]
        else:
            weights_ref, row_begin, add_counts = second
            own_alpha = ab_ref[own_rows(row_begin, weights_ref.shape[0]), :].astype(F32)
        for q, cols in enumerate(cuts):
            moved = jnp.dot(mat[k], ab_ref[:, cols], preferred_element_type=F32) * inverse[q]
            moving = is_moving(sel_ref, step_now, cols)
            if second is not None:
                total = column_sum(moved * hist[k, :, cols].astype(F32))
                weight = jnp.where(moving, inverse[q] / total, 0.0)
                weights_ref[:, cols] = (own_alpha[:, cols] * weight).astype(BF16)
            emit, top = emission(sel_ref, consts, step_now, cols, None)
            joint = jnp.where(moving, moved, consts[0]) * emit
            scale = column_sum(joint)
            if second is None:
                seen = is_seen(sel_ref, step_now, cols)
                logs[q] = logs[q] + jnp.where(seen, jnp.log2(scale) + top, 0.0)
            inverse[q] = 1.0 / scale
            put_twice(ab_ref, cols, joint)
        if second is not None:
            add_counts(k, outer_sum(weights_ref, hist[k]))
    return logs


def run_backward(lead, mat, hist, sel_ref, consts, state, ub_ref, logs, leave, second=None):
    steps, states, width = hist.shape
    cuts = tiles(width)
    rest = [x[:1] for x in state]
    size = [jnp.zeros((1, LANES), F32) for _ in cuts]

    def step(k):
        step_now = lead + k
        grown = []
        for q, cols in enumerate(cuts):
            emit, top = emission(sel_ref, consts, step_now, cols, size[q])
            carried = emit * state[q]
            put_twice(ub_ref, cols, carried)
            whole = column_sum(carried)
            grown.append(whole)
            size[q] = jnp.log2(whole)
            if second is None:
                seen = is_seen(sel_ref, step_now, cols)
                logs[q] = logs[q] + jnp.where(seen, size[q] + top, 0.0)
                begun = column_sum(carried * consts[0]) / whole
                rest[q] = jnp.where(seen, begun, rest[q])
        if second is None:
            hist[k] = ub_ref[:states, :]
        else:
            weights_ref, row_begin, add_counts = second
            own_alpha = hist[k, own_rows(row_begin, weights_ref.shape[0]), :].astype(F32)
        for q, cols in enumerate(cuts):
            product = jnp.dot(mat[k], ub_ref[:, cols], preferred_element_type=F32)
            moving = is_moving(sel_ref, step_now, cols)
            if second is not None:
                total = column_sum(product * hist[k, :, cols].astype(F32))
                weight = jnp.where(moving, 1.0 / total, 0.0)
                weights_ref[:, cols] = (own_alpha[:, cols] * weight).astype(BF16)
            state[q] = jnp.where(moving, product, rest[q] * grown[q])
        if second is not None:
            add_counts(k, outer_sum(weights_ref, ub_ref[:states, :]))

    def left():
        return [x * jnp.exp2(-y) for x, y in zip(state, size)]

    for k in reversed(range(1, steps)):
        step(k)
    if second is None:
        step(0)
        leave(left())
        return

    @pl.when(lead > 0)
    def _():
        step(0)
        leave(left())

    @pl.when(lead == 0)
    def _():
        second[2](0, jnp.zeros((second[0].shape[0], states), F32))


def put_state(state_out, values, logs):
    states = state_out.shape[0] - EXTRA
    row = lax.broadcasted_iota(jnp.int32, (EXTRA, LANES), 0)
    for q, cols in enumerate(tiles(state_out.shape[1])):
        state_out[:states, cols] = values[q].astype(BF16)
        high = logs[q].astype(BF16).astype(F32)
        middle = (logs[q] - high).astype(BF16).astype(F32)
        piece = jnp.where(
            row == 0, high, jnp.where(row == 1, middle, jnp.where(row == 2, logs[q] - high - middle, 0.0))
        )
        state_out[states:, cols] = piece.astype(BF16)


def state_logs(state_ref):
    states = state_ref.shape[0] - EXTRA
    return [column_sum(state_ref[states:, cols].astype(F32)) for cols in tiles(state_ref.shape[1])]


def first_kernel(resume, grids, part, rows_ref, mat, consts, *refs):
    state_in = refs[0] if resume else None
    hist, state_out, sel_ref, ab_ref = refs[-4:]
    chunk = part * grids + (pl.program_id(0) if grids > 1 else 0)
    steps, states, width = hist.shape
    forward_first, lead = is_forward_first(), lax.axis_index("per") * steps
    cuts = tiles(width)
    group, half_periods, slot_rows = rows_ref.shape
    tops = 2 * len(cuts)

    def scan_source(d, carry):
        rank, picked = carry
        for slot in range(slot_rows // HB):
            cols = slice(slot * HB, (slot + 1) * HB)
            block = rows_ref[d, :, cols]
            live = block > -0.5 * SEEN
            picked = [jnp.where(live & (rank == chunk * tops + i), block, old) for i, old in enumerate(picked)]
            rank = rank + live.astype(jnp.int32)
        return rank, picked

    carry = (jnp.zeros((half_periods, HB), jnp.int32), [jnp.zeros((half_periods, HB), F32)] * tops)
    if group <= 8:
        for d in range(group):
            carry = scan_source(d, carry)
    else:
        carry = lax.fori_loop(0, group, scan_source, carry)
    low_lane = lax.broadcasted_iota(jnp.int32, (half_periods, HB), 1) < HALF
    for q, cols in enumerate(cuts):
        left, right = carry[1][2 * q], carry[1][2 * q + 1]
        before = jnp.zeros((1, HB), F32)
        for late in range(2):
            value = (
                jnp.where(low_lane, pltpu.roll(left, HALF, 1), right)
                if late
                else jnp.where(low_lane, left, pltpu.roll(right, HALF, 1))
            )
            seen = value > 0.5 * SEEN
            earn = jnp.where(seen, value - SEEN, value)
            seen = seen.astype(F32)
            for i in range(half_periods):
                at = late * half_periods + i
                now = seen[i : i + 1]
                sel_ref[0, at, :, cols] = jnp.broadcast_to(earn[i : i + 1], (8, HB))
                sel_ref[1, at, :, cols] = jnp.broadcast_to(now * before, (8, HB))
                sel_ref[2, at, :, cols] = jnp.broadcast_to(now, (8, HB))
                before = now
    zeros = [jnp.zeros((1, LANES), F32) for _ in cuts]

    @pl.when(forward_first)
    def _():
        if resume:
            put_twice(ab_ref, slice(None), state_in[:states, :])
        else:
            for cols in cuts:
                put_twice(ab_ref, cols, consts[0])
        logs = state_logs(state_in) if resume else list(zeros)
        run_forward(lead, mat, hist, sel_ref, consts, ab_ref, logs)
        put_state(state_out, [ab_ref[:states, cols] for cols in cuts], logs)

    @pl.when(jnp.logical_not(forward_first))
    def _():
        state = [
            state_in[:states, cols].astype(F32) if resume else jnp.ones((states, LANES), F32) for cols in cuts
        ]
        logs = state_logs(state_in) if resume else list(zeros)
        leave = lambda values: put_state(state_out, values, logs)
        run_backward(lead, mat, hist, sel_ref, consts, state, ab_ref, logs, leave)


def second_kernel(resume, last, extend, grids, *refs):
    refs = list(refs)
    sel_ref, mat, consts, hist, own_state, state_in = (refs.pop(0) for _ in range(6))
    counts_in, sums_in = (refs.pop(0), refs.pop(0)) if resume else (None, None)
    row_probs = refs.pop(0) if last else None
    mine_ref, other_ref = (refs.pop(0), refs.pop(0)) if last else (None, None)
    counts_out, sums_out = (None, None) if last else (refs.pop(0), refs.pop(0))
    state_out = refs.pop(0) if extend else None
    ab_ref, weights_ref = refs[:2]
    counts_ref, sums_ref = refs[2:] if last else (counts_out, sums_out)
    chunk = pl.program_id(0) if grids > 1 else 0
    steps, states, width = hist.shape
    core, forward_first = core_index(), is_forward_first()
    row_begin = lax.axis_index("hh") * weights_ref.shape[0]
    lead = lax.axis_index("per") * steps
    rows = weights_ref.shape[0]

    def centre(k, counts):
        probs = row_probs[k]
        weighted = probs * counts
        grad = weighted - probs * jnp.sum(weighted, axis=1, keepdims=True)
        at = slice(k * rows, (k + 1) * rows)
        left, right = grad[:, :LANES], grad[:, LANES:]
        mine_ref[at, :] = jnp.where(core == 0, left, right)
        other_ref[at, :] = jnp.where(core == 0, right, left)

    def add_counts(k, counts):
        if grids > 1:
            counts_ref[k] += counts
            return
        if resume:
            counts = counts + counts_in[k]
        if last:
            centre(k, counts)
        else:
            counts_ref[k] = counts

    second = (weights_ref, row_begin, add_counts)

    @pl.when(chunk == 0)
    def _():
        if grids > 1:
            counts_ref[...] = jnp.zeros_like(counts_ref)
        sums_ref[...] = sums_in[...] if resume else jnp.zeros_like(sums_ref)

    def add_sums(alpha_ref, other_state):
        total = jnp.zeros((1, LANES), F32)
        years = jnp.zeros((8, LANES), F32)
        for cols, here, there in zip(tiles(width), state_logs(alpha_ref), state_logs(other_state)):
            alpha = alpha_ref[:states, cols].astype(F32)
            meet = column_sum(alpha * other_state[:states, cols].astype(F32))
            total += (here + there + jnp.log2(meet / column_sum(alpha))) * LN2
            years += jnp.sum(sel_ref[2, :, :, cols], axis=0)
        total = jnp.broadcast_to(jnp.sum(total, axis=1, keepdims=True), (1, LANES))
        years = jnp.broadcast_to(jnp.sum(years[:1], axis=1, keepdims=True), (1, LANES))
        row = lax.broadcasted_iota(jnp.int32, (8, LANES), 0)
        sums_ref[...] += jnp.where(row == 0, total, jnp.where(row == 1, years, 0.0))

    zeros = [jnp.zeros((1, LANES), F32) for _ in tiles(width)]

    @pl.when(jnp.logical_not(forward_first))
    def _():
        add_sums(state_in, own_state)
        put_twice(ab_ref, slice(None), state_in[:states, :])
        run_forward(lead, mat, hist, sel_ref, consts, ab_ref, list(zeros), second)
        if extend:
            put_state(state_out, [ab_ref[:states, cols] for cols in tiles(width)], zeros)

    @pl.when(forward_first)
    def _():
        add_sums(own_state, state_in)
        state = [state_in[:states, cols].astype(F32) for cols in tiles(width)]
        leave = lambda values: put_state(state_out, values, zeros) if extend else None
        run_backward(lead, mat, hist, sel_ref, consts, state, ab_ref, list(zeros), leave, second)

    if last:

        @pl.when(chunk == grids - 1)
        def _():
            if grids > 1:
                for k in range(steps):
                    centre(k, counts_ref[k])
            mine_ref[steps * rows :, :] = sums_ref[...]
            other_ref[steps * rows :, :] = sums_ref[...]


def finish_kernel(scale, mine_ref, other_ref, grad_ref, mean_ref):
    count = grad_ref.shape[0]
    total = mine_ref[count : count + 1, :] + other_ref[count : count + 1, :]
    years = mine_ref[count + 1 : count + 2, :] + other_ref[count + 1 : count + 2, :]
    grad_ref[...] = (mine_ref[:count, :] + other_ref[:count, :]) * (scale / years)
    mean_ref[0] = (total / years)[0, 0]


def per_device(
    earnings, starts, lengths, block_count, trans_logits, init_logits, state_mean, log_sd
):
    slot_rows, periods = earnings.shape
    states = init_logits.shape[0]
    group = lax.axis_size(("hh", "per"))
    sides = lax.axis_size("per")
    cores = lax.axis_size("st")
    part = trans_logits.shape[0]
    steps = part * cores
    rows = states // lax.axis_size("hh")
    households = group * HB // cores
    parts = 2 if households <= 4 * HB else 1
    share = households // parts
    width = min(2 * HB, share)
    grids = share // width
    side = lax.axis_index("per")
    shaped = jax.ShapeDtypeStruct
    dma = pltpu.SemaphoreType.DMA

    swap = [(0, 1), (1, 0)]
    vec_row = pltpu.VMEM((1, states), F32)
    packed, vectors = pl.pallas_call(
        pack_kernel,
        out_shape=[
            shaped((group, periods // 2, slot_rows), F32),
            shaped((8, states), F32),
        ],
        in_specs=[smem()] + [hbm()] * 6,
        out_specs=[vmem()] * 2,
        scratch_shapes=[
            pltpu.VMEM((periods, slot_rows), F32),
            pltpu.VMEM((slot_rows // HB, HB), jnp.int32),
            pltpu.VMEM((slot_rows // HB, HB), jnp.int32),
            vec_row,
            vec_row,
            vec_row,
            dma((6,)),
        ],
        compiler_params=params(2),
        name="pack",
    )(
        block_count,
        *in_hbm(
            earnings.T, starts.reshape(-1, HB), lengths.reshape(-1, HB),
            init_logits.reshape(1, states), state_mean.reshape(1, states), log_sd.reshape(1, states),
        ),
    )
    packed, later_logits = lax.optimization_barrier((packed, trans_logits))
    other_logits = lax.ppermute(later_logits, "st", swap)
    gathered = lax.all_to_all(packed, ("hh", "per"), split_axis=0, concat_axis=0, tiled=True)
    first_mat, second_mat, row_probs, consts = pl.pallas_call(
        prep_kernel,
        out_shape=[
            pltpu.VMEM((steps, states, 2 * states), BF16),
            pltpu.HBM((steps, states, 2 * states), BF16),
            pltpu.VMEM((steps, rows, states), F32),
            pltpu.VMEM((4, states, LANES), F32),
        ],
        in_specs=[hbm(), hbm(), vmem()],
        out_specs=[vmem(), hbm(), vmem(), vmem()],
        scratch_shapes=[
            pltpu.VMEM((steps, states, 2 * states), BF16),
            pltpu.VMEM((states, states), F32),
            pltpu.VMEM(trans_logits.shape, BF16),
            pltpu.VMEM(trans_logits.shape, BF16),
            dma((2,)),
            dma((steps,)),
        ],
        compiler_params=params(6),
        name="prep",
    )(*in_hbm(trans_logits, other_logits), vectors)

    def whole(*shape):
        if grids == 1:
            return vmem()
        return pl.BlockSpec(shape, lambda g: (0,) * len(shape))

    def lanes(*lead):
        if grids == 1:
            return vmem()
        return pl.BlockSpec(lead + (width,), lambda g: (0,) * len(lead) + (g,))

    grid = (grids,) if grids > 1 else ()
    hist_shape = shaped((steps, states, share), BF16)
    state_shape = shaped((states + EXTRA, share), BF16)
    sel_shape = shaped((3, periods, 8, share), F32)
    swap_shape = shaped((steps * rows + 8, LANES), F32)
    counts_shape = shaped((steps, rows, states), F32)
    sums_shape = shaped((8, LANES), F32)
    hist_spec, state_spec, sel_spec = lanes(steps, states), lanes(states + EXTRA), lanes(3, periods, 8)
    const_spec = whole(4, states, LANES)

    def first_pass(index, state_in):
        resume = state_in is not None
        return pl.pallas_call(
            functools.partial(first_kernel, resume, grids, index),
            grid=grid,
            out_shape=[hist_shape, state_shape, sel_shape],
            in_specs=[whole(*gathered.shape), whole(*first_mat.shape), const_spec]
            + [state_spec] * resume,
            out_specs=[hist_spec, state_spec, sel_spec],
            scratch_shapes=[pltpu.VMEM((2 * states, width), BF16)],
            compiler_params=params(8 if grids == 1 else 32),
            name="first_pass",
        )(gathered, first_mat, consts, *([state_in] if resume else []))

    def second_pass(kept, state_in, sums_in, last, extend):
        hist, own_state, sel = kept
        resume = sums_in is not None
        scratch = [
            pltpu.VMEM((2 * states, width), BF16),
            pltpu.VMEM((rows, width), BF16),
        ]
        counts_spec, sums_spec = whole(*counts_shape.shape), whole(*sums_shape.shape)
        if last:
            out_shape = [swap_shape] * 2
            scratch += [pltpu.VMEM(counts_shape.shape, F32), pltpu.VMEM(sums_shape.shape, F32)]
        else:
            out_shape = [counts_shape, sums_shape]
        out_specs = [whole(*x.shape) for x in out_shape]
        if extend:
            out_shape, out_specs = out_shape + [state_shape], out_specs + [state_spec]
        return pl.pallas_call(
            functools.partial(second_kernel, resume, last, extend, grids),
            grid=grid,
            out_shape=out_shape,
            in_specs=[sel_spec, whole(*second_mat.shape), const_spec, hist_spec, state_spec, state_spec]
            + [counts_spec, sums_spec] * resume
            + [whole(*row_probs.shape)] * last,
            out_specs=out_specs,
            scratch_shapes=scratch,
            compiler_params=params(8 if grids == 1 else 32),
            name="second_pass",
        )(
            sel, second_mat, consts, hist, own_state, state_in,
            *(sums_in if resume else []),
            *([row_probs] if last else []),
        )

    def hand_over(state, stage):
        moves = [(stage, stage + 1), (sides - 1 - stage, sides - 2 - stage)]
        return lax.ppermute(state, "per", moves)

    if sides == 2:
        kept = [first_pass(index, None) for index in range(parts)]
        arrived = [hand_over(each[1], 0) for each in kept]
        sums = None
        for index in range(parts):
            sums = second_pass(kept[index], arrived[index], sums, index == parts - 1, False)
        mine, other = sums
    else:
        kept = [jnp.zeros(x.shape, x.dtype) for x in (hist_shape, state_shape, sel_shape)]
        done = [jnp.zeros(x.shape, x.dtype) for x in (swap_shape, swap_shape, state_shape)]
        state = None
        for stage in range(sides):
            active = (side == stage) | (side == sides - 1 - stage)
            if stage < sides // 2:
                kept = lax.cond(
                    active, lambda x, kept: list(first_pass(0, x)), lambda x, kept: kept, state, kept
                )
                state = kept[1]
            else:
                done = lax.cond(
                    active,
                    lambda x, done: list(second_pass(kept, x, None, True, True)),
                    lambda x, done: done,
                    state,
                    done,
                )
                state = done[2]
            if stage < sides - 1:
                state = hand_over(state, stage)
        mine, other, _ = done
        total = jnp.where(side == sides // 2, mine[steps * rows], 0.0)
        total = lax.psum(total, "per")
        mine = mine.at[steps * rows].set(total)
        other = other.at[steps * rows].set(total)
    received = lax.ppermute(other, "st", swap)
    trans_grad, mean_loglik = pl.pallas_call(
        functools.partial(finish_kernel, float(states * states * periods)),
        out_shape=[shaped((steps * rows, LANES), F32), shaped((1,), F32)],
        in_specs=[vmem(), vmem()],
        out_specs=[vmem(), smem()],
        compiler_params=params(4),
        name="finish",
    )(mine, received)
    return (trans_grad.reshape(steps, rows, LANES), mean_loglik)


def solution(mesh):
    placed = (
        P(("hh", "per"), None),
        P(("hh", "per")),
        P(("hh", "per")),
        P(("hh", "per")),
        P(("grp", "per", "st"), None, None),
        P("grp"),
        P("grp"),
        P("grp"),
    )
    return jax.shard_map(
        per_device,
        mesh=mesh,
        in_specs=placed,
        out_specs=(P(("grp", "per"), "hh", "st"), P("grp")),
        check_vma=False,
    )
```

```python
import functools

import jax
import jax.numpy as jnp
from jax import lax
from jax.experimental import pallas as pl
from jax.experimental.pallas import tpu as pltpu
from jax.sharding import PartitionSpec as P

HB = 128
LANES = 128
HALF = HB // 2
SEEN = 16.0
F32 = jnp.float32
BF16 = jnp.bfloat16
LOG2E = 1.4426950408889634
LN2 = 0.6931471805599453
EXTRA = 16


def vmem():
    return pl.BlockSpec(memory_space=pltpu.VMEM)


def smem():
    return pl.BlockSpec(memory_space=pltpu.SMEM)


def hbm():
    return pl.BlockSpec(memory_space=pltpu.HBM)


def in_hbm(*arrays):
    return [pltpu.with_memory_space_constraint(x, pltpu.HBM) for x in arrays]


def params(mebibytes):
    return pltpu.CompilerParams(vmem_limit_bytes=mebibytes * 1024 * 1024)


def core_index():
    return lax.axis_index("st")


def is_forward_first():
    return 2 * lax.axis_index("per") < lax.axis_size("per")


def tiles(width):
    return [slice(q, q + LANES) for q in range(0, width, LANES)]


def fetch(pairs, sems):
    copies = [pltpu.make_async_copy(src, dst, sems.at[i]) for i, (src, dst) in enumerate(pairs)]
    for copy in copies:
        copy.start()
    for copy in copies:
        copy.wait()


def pack_kernel(
    count_ref, earn_any, start_any, len_any, init_any, mean_any, sd_any, out_ref, vec_ref,
    earn_ref, start_ref, len_ref, init_ref, mean_ref, sd_ref, sems,
):
    fetch(
        (
            (earn_any, earn_ref), (start_any, start_ref), (len_any, len_ref),
            (init_any, init_ref), (mean_any, mean_ref), (sd_any, sd_ref),
        ),
        sems,
    )
    periods, slot_rows = earn_ref.shape
    core = core_index()
    low_lane = lax.broadcasted_iota(jnp.int32, (periods // 2, HB), 1) < HALF
    time = lax.broadcasted_iota(jnp.int32, (periods, HB), 0)
    for slot in range(slot_rows // HB):
        cols = slice(slot * HB, (slot + 1) * HB)
        begin = start_ref[slot : slot + 1, :]
        seen = (time >= begin) & (time < begin + len_ref[slot : slot + 1, :])
        live = slot < count_ref[0]
        shift = jnp.where(live, jnp.where(seen, SEEN, 0.0), -SEEN)
        value = earn_ref[:, cols] + shift
        early, late = value[: periods // 2], value[periods // 2 :]
        turned = pltpu.roll(jnp.where(core == 0, late, early), HALF, 1)
        packed = jnp.where(low_lane, jnp.where(core == 0, early, turned), jnp.where(core == 0, turned, late))
        for to in range(out_ref.shape[0]):
            out_ref[to, :, cols] = packed
    raised = jnp.exp(init_ref[...])
    start = raised / jnp.sum(raised, axis=1, keepdims=True)
    row = lax.broadcasted_iota(jnp.int32, vec_ref.shape, 0)
    power = (-0.5 * LOG2E) * jnp.exp(-2.0 * sd_ref[...])
    vec_ref[...] = jnp.where(
        row == 0, start, jnp.where(row == 1, mean_ref[...], jnp.where(row == 2, power, -LOG2E * sd_ref[...]))
    )


def put(ref, at, value):
    states = value.shape[0]
    high = value.astype(BF16)
    ref[at, :states, :states] = high
    ref[at, :states, states:] = (value - high.astype(F32)).astype(BF16)


def put_twice(ref, cols, value):
    states = value.shape[0]
    value = value.astype(BF16)
    ref[:states, cols] = value
    ref[states:, cols] = value


def prep_kernel(
    own_any, other_any, vec_ref, first_mat, second_any, row_probs, consts,
    second_mat, scratch, own_ref, other_ref, sems, out_sems,
):
    copies = [
        pltpu.make_async_copy(src, dst, sems.at[i])
        for i, (src, dst) in enumerate(((own_any, own_ref), (other_any, other_ref)))
    ]
    for copy in copies:
        copy.start()
    part, states, _ = own_ref.shape

    def leave(at):
        return pltpu.make_async_copy(second_mat.at[at], second_any.at[at], out_sems.at[at])

    rows = row_probs.shape[1]
    for i in range(4):
        consts[i] = jnp.broadcast_to(vec_ref[i : i + 1, :], (LANES, states)).T
    for copy, source, ref in zip(copies, (core_index(), 1 - core_index()), (own_ref, other_ref)):
        copy.wait()

        @pl.loop(0, part)
        def _(i):
            at = source * part + i
            lifted = jnp.exp(ref[i].astype(F32))
            probs = lifted * (1.0 / jnp.sum(lifted, axis=1, keepdims=True))
            scratch[...] = probs
            row_probs[at] = scratch[own_rows(lax.axis_index("hh") * rows, rows), :]

            @pl.when(is_forward_first())
            def _():
                put(first_mat, at, probs.T)
                put(second_mat, at, probs)

            @pl.when(jnp.logical_not(is_forward_first()))
            def _():
                put(first_mat, at, probs)
                put(second_mat, at, probs.T)

            leave(at).start()

    for at in range(2 * part):
        leave(at).wait()


def emission(sel_ref, consts, step_now, cols, less=None):
    gap = sel_ref[0, step_now, :1, cols] - consts[1]
    power = gap * gap * consts[2] + consts[3]
    return jnp.exp2(power if less is None else power - less)


def is_moving(sel_ref, step_now, cols):
    return sel_ref[1, step_now, :1, cols] > 0.5


def is_seen(sel_ref, step_now, cols):
    return sel_ref[2, step_now, :1, cols] > 0.5


def column_sum(x):
    return jnp.sum(x, axis=0, keepdims=True)


def own_rows(row_begin, rows):
    return pl.ds(pl.multiple_of(row_begin, rows), rows)


def outer_sum(weights_ref, carried):
    return lax.dot_general(weights_ref[...], carried, (((1,), (1,)), ((), ())), preferred_element_type=F32)


def run_forward(lead, mat, hist, sel_ref, consts, ab_ref, logs, second=None):
    steps, states, width = hist.shape
    cuts = tiles(width)
    inverse = [1.0 / column_sum(ab_ref[:states, cols].astype(F32)) for cols in cuts]
    for k in range(steps):
        step_now = lead + k
        if second is None:
            hist[k] = ab_ref[:states, :]
        else:
            weights_ref, row_begin, add_counts = second
            own_alpha = ab_ref[own_rows(row_begin, weights_ref.shape[0]), :].astype(F32)
        for q, cols in enumerate(cuts):
            moved = jnp.dot(mat[k], ab_ref[:, cols], preferred_element_type=F32) * inverse[q]
            moving = is_moving(sel_ref, step_now, cols)
            if second is not None:
                total = column_sum(moved * hist[k, :, cols].astype(F32))
                weight = jnp.where(moving, 1.0 / total, 0.0)
                weights_ref[:, cols] = (own_alpha[:, cols] * inverse[q] * weight).astype(BF16)
            emit = emission(sel_ref, consts, step_now, cols)
            joint = jnp.where(moving, moved, consts[0]) * emit
            scale = column_sum(joint)
            if second is None:
                seen = is_seen(sel_ref, step_now, cols)
                logs[q] = logs[q] + jnp.where(seen, jnp.log2(scale), 0.0)
            inverse[q] = 1.0 / scale
            put_twice(ab_ref, cols, joint)
        if second is not None:
            add_counts(k, outer_sum(weights_ref, hist[k]))
    return logs


def run_backward(lead, mat, hist, sel_ref, consts, state, ub_ref, logs, leave, second=None):
    steps, states, width = hist.shape
    cuts = tiles(width)
    rest = [x[:1] for x in state]
    size = [jnp.zeros((1, LANES), F32) for _ in cuts]

    def step(k):
        step_now = lead + k
        grown = []
        for q, cols in enumerate(cuts):
            emit = emission(sel_ref, consts, step_now, cols, size[q] if second is None else None)
            carried = emit * state[q]
            put_twice(ub_ref, cols, carried)
            whole = column_sum(carried)
            grown.append(whole)
            if second is None:
                size[q] = jnp.log2(whole)
                seen = is_seen(sel_ref, step_now, cols)
                logs[q] = logs[q] + jnp.where(seen, size[q], 0.0)
                begun = column_sum(carried * consts[0]) / whole
                rest[q] = jnp.where(seen, begun, rest[q])
        if second is None:
            hist[k] = ub_ref[:states, :]
        else:
            weights_ref, row_begin, add_counts = second
            own_alpha = hist[k, own_rows(row_begin, weights_ref.shape[0]), :].astype(F32)
        for q, cols in enumerate(cuts):
            product = jnp.dot(mat[k], ub_ref[:, cols], preferred_element_type=F32)
            moving = is_moving(sel_ref, step_now, cols)
            if second is None:
                state[q] = jnp.where(moving, product, rest[q] * grown[q])
            else:
                shrink = 1.0 / grown[q]
                product = product * shrink
                total = column_sum(product * hist[k, :, cols].astype(F32))
                weight = jnp.where(moving, 1.0 / total, 0.0)
                weights_ref[:, cols] = (own_alpha[:, cols] * weight * shrink).astype(BF16)
                state[q] = jnp.where(moving, product, rest[q])
        if second is not None:
            add_counts(k, outer_sum(weights_ref, ub_ref[:states, :]))

    def left():
        return [x * jnp.exp2(-y) for x, y in zip(state, size)]

    for k in reversed(range(1, steps)):
        step(k)
    if second is None:
        step(0)
        leave(left())
        return

    @pl.when(lead > 0)
    def _():
        step(0)
        leave(left())

    @pl.when(lead == 0)
    def _():
        second[2](0, jnp.zeros((second[0].shape[0], states), F32))


def put_state(state_out, values, logs):
    states = state_out.shape[0] - EXTRA
    row = lax.broadcasted_iota(jnp.int32, (EXTRA, LANES), 0)
    for q, cols in enumerate(tiles(state_out.shape[1])):
        state_out[:states, cols] = values[q].astype(BF16)
        high = logs[q].astype(BF16).astype(F32)
        middle = (logs[q] - high).astype(BF16).astype(F32)
        piece = jnp.where(
            row == 0, high, jnp.where(row == 1, middle, jnp.where(row == 2, logs[q] - high - middle, 0.0))
        )
        state_out[states:, cols] = piece.astype(BF16)


def state_logs(state_ref):
    states = state_ref.shape[0] - EXTRA
    return [column_sum(state_ref[states:, cols].astype(F32)) for cols in tiles(state_ref.shape[1])]


def first_kernel(resume, grids, part, rows_ref, mat, consts, *refs):
    state_in = refs[0] if resume else None
    hist, state_out, sel_ref, ab_ref = refs[-4:]
    chunk = part * grids + (pl.program_id(0) if grids > 1 else 0)
    steps, states, width = hist.shape
    forward_first, lead = is_forward_first(), lax.axis_index("per") * steps
    cuts = tiles(width)
    group, half_periods, slot_rows = rows_ref.shape
    tops = 2 * len(cuts)

    def scan_source(d, carry):
        rank, picked = carry
        for slot in range(slot_rows // HB):
            cols = slice(slot * HB, (slot + 1) * HB)
            block = rows_ref[d, :, cols]
            live = block > -0.5 * SEEN
            picked = [jnp.where(live & (rank == chunk * tops + i), block, old) for i, old in enumerate(picked)]
            rank = rank + live.astype(jnp.int32)
        return rank, picked

    carry = (jnp.zeros((half_periods, HB), jnp.int32), [jnp.zeros((half_periods, HB), F32)] * tops)
    if group <= 8:
        for d in range(group):
            carry = scan_source(d, carry)
    else:
        carry = lax.fori_loop(0, group, scan_source, carry)
    low_lane = lax.broadcasted_iota(jnp.int32, (half_periods, HB), 1) < HALF
    for q, cols in enumerate(cuts):
        left, right = carry[1][2 * q], carry[1][2 * q + 1]
        before = jnp.zeros((1, HB), F32)
        for late in range(2):
            value = (
                jnp.where(low_lane, pltpu.roll(left, HALF, 1), right)
                if late
                else jnp.where(low_lane, left, pltpu.roll(right, HALF, 1))
            )
            seen = value > 0.5 * SEEN
            earn = jnp.where(seen, value - SEEN, value)
            seen = seen.astype(F32)
            for i in range(half_periods):
                at = late * half_periods + i
                now = seen[i : i + 1]
                sel_ref[0, at, :, cols] = jnp.broadcast_to(earn[i : i + 1], (8, HB))
                sel_ref[1, at, :, cols] = jnp.broadcast_to(now * before, (8, HB))
                sel_ref[2, at, :, cols] = jnp.broadcast_to(now, (8, HB))
                before = now
    zeros = [jnp.zeros((1, LANES), F32) for _ in cuts]

    @pl.when(forward_first)
    def _():
        if resume:
            put_twice(ab_ref, slice(None), state_in[:states, :])
        else:
            for cols in cuts:
                put_twice(ab_ref, cols, consts[0])
        logs = state_logs(state_in) if resume else list(zeros)
        run_forward(lead, mat, hist, sel_ref, consts, ab_ref, logs)
        put_state(state_out, [ab_ref[:states, cols] for cols in cuts], logs)

    @pl.when(jnp.logical_not(forward_first))
    def _():
        state = [
            state_in[:states, cols].astype(F32) if resume else jnp.ones((states, LANES), F32) for cols in cuts
        ]
        logs = state_logs(state_in) if resume else list(zeros)
        leave = lambda values: put_state(state_out, values, logs)
        run_backward(lead, mat, hist, sel_ref, consts, state, ab_ref, logs, leave)


def second_kernel(resume, last, extend, grids, *refs):
    refs = list(refs)
    sel_ref, mat, consts, hist, own_state, state_in = (refs.pop(0) for _ in range(6))
    counts_in, sums_in = (refs.pop(0), refs.pop(0)) if resume else (None, None)
    row_probs = refs.pop(0) if last else None
    mine_ref, other_ref = (refs.pop(0), refs.pop(0)) if last else (None, None)
    counts_out, sums_out = (None, None) if last else (refs.pop(0), refs.pop(0))
    state_out = refs.pop(0) if extend else None
    ab_ref, weights_ref = refs[:2]
    counts_ref, sums_ref = refs[2:] if last else (counts_out, sums_out)
    chunk = pl.program_id(0) if grids > 1 else 0
    steps, states, width = hist.shape
    core, forward_first = core_index(), is_forward_first()
    row_begin = lax.axis_index("hh") * weights_ref.shape[0]
    lead = lax.axis_index("per") * steps
    rows = weights_ref.shape[0]

    def centre(k, counts):
        probs = row_probs[k]
        weighted = probs * counts
        grad = weighted - probs * jnp.sum(weighted, axis=1, keepdims=True)
        at = slice(k * rows, (k + 1) * rows)
        left, right = grad[:, :LANES], grad[:, LANES:]
        mine_ref[at, :] = jnp.where(core == 0, left, right)
        other_ref[at, :] = jnp.where(core == 0, right, left)

    def add_counts(k, counts):
        if grids > 1:
            counts_ref[k] += counts
            return
        if resume:
            counts = counts + counts_in[k]
        if last:
            centre(k, counts)
        else:
            counts_ref[k] = counts

    second = (weights_ref, row_begin, add_counts)

    @pl.when(chunk == 0)
    def _():
        if grids > 1:
            counts_ref[...] = jnp.zeros_like(counts_ref)
        sums_ref[...] = sums_in[...] if resume else jnp.zeros_like(sums_ref)

    def add_sums(alpha_ref, other_state):
        total = jnp.zeros((1, LANES), F32)
        years = jnp.zeros((8, LANES), F32)
        for cols, here, there in zip(tiles(width), state_logs(alpha_ref), state_logs(other_state)):
            alpha = alpha_ref[:states, cols].astype(F32)
            meet = column_sum(alpha * other_state[:states, cols].astype(F32))
            total += (here + there + jnp.log2(meet / column_sum(alpha))) * LN2
            years += jnp.sum(sel_ref[2, :, :, cols], axis=0)
        total = jnp.broadcast_to(jnp.sum(total, axis=1, keepdims=True), (1, LANES))
        years = jnp.broadcast_to(jnp.sum(years[:1], axis=1, keepdims=True), (1, LANES))
        row = lax.broadcasted_iota(jnp.int32, (8, LANES), 0)
        sums_ref[...] += jnp.where(row == 0, total, jnp.where(row == 1, years, 0.0))

    zeros = [jnp.zeros((1, LANES), F32) for _ in tiles(width)]

    @pl.when(jnp.logical_not(forward_first))
    def _():
        add_sums(state_in, own_state)
        put_twice(ab_ref, slice(None), state_in[:states, :])
        run_forward(lead, mat, hist, sel_ref, consts, ab_ref, list(zeros), second)
        if extend:
            put_state(state_out, [ab_ref[:states, cols] for cols in tiles(width)], zeros)

    @pl.when(forward_first)
    def _():
        add_sums(own_state, state_in)
        state = [state_in[:states, cols].astype(F32) for cols in tiles(width)]
        leave = lambda values: put_state(state_out, values, zeros) if extend else None
        run_backward(lead, mat, hist, sel_ref, consts, state, ab_ref, list(zeros), leave, second)

    if last:

        @pl.when(chunk == grids - 1)
        def _():
            if grids > 1:
                for k in range(steps):
                    centre(k, counts_ref[k])
            mine_ref[steps * rows :, :] = sums_ref[...]
            other_ref[steps * rows :, :] = sums_ref[...]


def finish_kernel(scale, mine_ref, other_ref, grad_ref, mean_ref):
    count = grad_ref.shape[0]
    total = mine_ref[count : count + 1, :] + other_ref[count : count + 1, :]
    years = mine_ref[count + 1 : count + 2, :] + other_ref[count + 1 : count + 2, :]
    grad_ref[...] = (mine_ref[:count, :] + other_ref[:count, :]) * (scale / years)
    mean_ref[0] = (total / years)[0, 0]


def per_device(
    earnings, starts, lengths, block_count, trans_logits, init_logits, state_mean, log_sd
):
    slot_rows, periods = earnings.shape
    states = init_logits.shape[0]
    group = lax.axis_size(("hh", "per"))
    sides = lax.axis_size("per")
    cores = lax.axis_size("st")
    part = trans_logits.shape[0]
    steps = part * cores
    rows = states // lax.axis_size("hh")
    households = group * HB // cores
    parts = 2 if households <= 4 * HB else 1
    share = households // parts
    width = min(2 * HB, share)
    grids = share // width
    side = lax.axis_index("per")
    shaped = jax.ShapeDtypeStruct
    dma = pltpu.SemaphoreType.DMA

    swap = [(0, 1), (1, 0)]
    vec_row = pltpu.VMEM((1, states), F32)
    packed, vectors = pl.pallas_call(
        pack_kernel,
        out_shape=[
            shaped((group, periods // 2, slot_rows), F32),
            shaped((8, states), F32),
        ],
        in_specs=[smem()] + [hbm()] * 6,
        out_specs=[vmem()] * 2,
        scratch_shapes=[
            pltpu.VMEM((periods, slot_rows), F32),
            pltpu.VMEM((slot_rows // HB, HB), jnp.int32),
            pltpu.VMEM((slot_rows // HB, HB), jnp.int32),
            vec_row,
            vec_row,
            vec_row,
            dma((6,)),
        ],
        compiler_params=params(2),
        name="pack",
    )(
        block_count,
        *in_hbm(
            earnings.T, starts.reshape(-1, HB), lengths.reshape(-1, HB),
            init_logits.reshape(1, states), state_mean.reshape(1, states), log_sd.reshape(1, states),
        ),
    )
    packed, later_logits = lax.optimization_barrier((packed, trans_logits))
    other_logits = lax.ppermute(later_logits, "st", swap)
    gathered = lax.all_to_all(packed, ("hh", "per"), split_axis=0, concat_axis=0, tiled=True)
    first_mat, second_mat, row_probs, consts = pl.pallas_call(
        prep_kernel,
        out_shape=[
            pltpu.VMEM((steps, states, 2 * states), BF16),
            pltpu.HBM((steps, states, 2 * states), BF16),
            pltpu.VMEM((steps, rows, states), F32),
            pltpu.VMEM((4, states, LANES), F32),
        ],
        in_specs=[hbm(), hbm(), vmem()],
        out_specs=[vmem(), hbm(), vmem(), vmem()],
        scratch_shapes=[
            pltpu.VMEM((steps, states, 2 * states), BF16),
            pltpu.VMEM((states, states), F32),
            pltpu.VMEM(trans_logits.shape, BF16),
            pltpu.VMEM(trans_logits.shape, BF16),
            dma((2,)),
            dma((steps,)),
        ],
        compiler_params=params(6),
        name="prep",
    )(*in_hbm(trans_logits, other_logits), vectors)

    def whole(*shape):
        if grids == 1:
            return vmem()
        return pl.BlockSpec(shape, lambda g: (0,) * len(shape))

    def lanes(*lead):
        if grids == 1:
            return vmem()
        return pl.BlockSpec(lead + (width,), lambda g: (0,) * len(lead) + (g,))

    grid = (grids,) if grids > 1 else ()
    hist_shape = shaped((steps, states, share), BF16)
    state_shape = shaped((states + EXTRA, share), BF16)
    sel_shape = shaped((3, periods, 8, share), F32)
    swap_shape = shaped((steps * rows + 8, LANES), F32)
    counts_shape = shaped((steps, rows, states), F32)
    sums_shape = shaped((8, LANES), F32)
    hist_spec, state_spec, sel_spec = lanes(steps, states), lanes(states + EXTRA), lanes(3, periods, 8)
    const_spec = whole(4, states, LANES)

    def first_pass(index, state_in):
        resume = state_in is not None
        return pl.pallas_call(
            functools.partial(first_kernel, resume, grids, index),
            grid=grid,
            out_shape=[hist_shape, state_shape, sel_shape],
            in_specs=[whole(*gathered.shape), whole(*first_mat.shape), const_spec]
            + [state_spec] * resume,
            out_specs=[hist_spec, state_spec, sel_spec],
            scratch_shapes=[pltpu.VMEM((2 * states, width), BF16)],
            compiler_params=params(8 if grids == 1 else 32),
            name="first_pass",
        )(gathered, first_mat, consts, *([state_in] if resume else []))

    def second_pass(kept, state_in, sums_in, last, extend):
        hist, own_state, sel = kept
        resume = sums_in is not None
        scratch = [
            pltpu.VMEM((2 * states, width), BF16),
            pltpu.VMEM((rows, width), BF16),
        ]
        counts_spec, sums_spec = whole(*counts_shape.shape), whole(*sums_shape.shape)
        if last:
            out_shape = [swap_shape] * 2
            scratch += [pltpu.VMEM(counts_shape.shape, F32), pltpu.VMEM(sums_shape.shape, F32)]
        else:
            out_shape = [counts_shape, sums_shape]
        out_specs = [whole(*x.shape) for x in out_shape]
        if extend:
            out_shape, out_specs = out_shape + [state_shape], out_specs + [state_spec]
        return pl.pallas_call(
            functools.partial(second_kernel, resume, last, extend, grids),
            grid=grid,
            out_shape=out_shape,
            in_specs=[sel_spec, whole(*second_mat.shape), const_spec, hist_spec, state_spec, state_spec]
            + [counts_spec, sums_spec] * resume
            + [whole(*row_probs.shape)] * last,
            out_specs=out_specs,
            scratch_shapes=scratch,
            compiler_params=params(8 if grids == 1 else 32),
            name="second_pass",
        )(
            sel, second_mat, consts, hist, own_state, state_in,
            *(sums_in if resume else []),
            *([row_probs] if last else []),
        )

    def hand_over(state, stage):
        moves = [(stage, stage + 1), (sides - 1 - stage, sides - 2 - stage)]
        return lax.ppermute(state, "per", moves)

    if sides == 2:
        kept = [first_pass(index, None) for index in range(parts)]
        arrived = [hand_over(each[1], 0) for each in kept]
        sums = None
        for index in range(parts):
            sums = second_pass(kept[index], arrived[index], sums, index == parts - 1, False)
        mine, other = sums
    else:
        kept = [jnp.zeros(x.shape, x.dtype) for x in (hist_shape, state_shape, sel_shape)]
        done = [jnp.zeros(x.shape, x.dtype) for x in (swap_shape, swap_shape, state_shape)]
        state = None
        for stage in range(sides):
            active = (side == stage) | (side == sides - 1 - stage)
            if stage < sides // 2:
                kept = lax.cond(
                    active, lambda x, kept: list(first_pass(0, x)), lambda x, kept: kept, state, kept
                )
                state = kept[1]
            else:
                done = lax.cond(
                    active,
                    lambda x, done: list(second_pass(kept, x, None, True, True)),
                    lambda x, done: done,
                    state,
                    done,
                )
                state = done[2]
            if stage < sides - 1:
                state = hand_over(state, stage)
        mine, other, _ = done
        total = jnp.where(side == sides // 2, mine[steps * rows], 0.0)
        total = lax.psum(total, "per")
        mine = mine.at[steps * rows].set(total)
        other = other.at[steps * rows].set(total)
    received = lax.ppermute(other, "st", swap)
    trans_grad, mean_loglik = pl.pallas_call(
        functools.partial(finish_kernel, float(states * states * periods)),
        out_shape=[shaped((steps * rows, LANES), F32), shaped((1,), F32)],
        in_specs=[vmem(), vmem()],
        out_specs=[vmem(), smem()],
        compiler_params=params(4),
        name="finish",
    )(mine, received)
    return (trans_grad.reshape(steps, rows, LANES), mean_loglik)


def solution(mesh):
    placed = (
        P(("hh", "per"), None),
        P(("hh", "per")),
        P(("hh", "per")),
        P(("hh", "per")),
        P(("grp", "per", "st"), None, None),
        P("grp"),
        P("grp"),
        P("grp"),
    )
    return jax.shard_map(
        per_device,
        mesh=mesh,
        in_specs=placed,
        out_specs=(P(("grp", "per"), "hh", "st"), P("grp")),
        check_vma=False,
    )
```

```python
import functools

import jax
import jax.numpy as jnp
from jax import lax
from jax.experimental import pallas as pl
from jax.experimental.pallas import tpu as pltpu
from jax.sharding import PartitionSpec as P

HB = 128
LANES = 128
HALF = HB // 2
SEEN = 16.0
F32 = jnp.float32
BF16 = jnp.bfloat16
LOG2E = 1.4426950408889634
LN2 = 0.6931471805599453
EXTRA = 16


def vmem():
    return pl.BlockSpec(memory_space=pltpu.VMEM)


def smem():
    return pl.BlockSpec(memory_space=pltpu.SMEM)


def hbm():
    return pl.BlockSpec(memory_space=pltpu.HBM)


def in_hbm(*arrays):
    return [pltpu.with_memory_space_constraint(x, pltpu.HBM) for x in arrays]


def params(mebibytes):
    return pltpu.CompilerParams(vmem_limit_bytes=mebibytes * 1024 * 1024)


def core_index():
    return lax.axis_index("st")


def is_forward_first():
    return 2 * lax.axis_index("per") < lax.axis_size("per")


def tiles(width):
    return [slice(q, q + LANES) for q in range(0, width, LANES)]


def fetch(pairs, sems):
    copies = [pltpu.make_async_copy(src, dst, sems.at[i]) for i, (src, dst) in enumerate(pairs)]
    for copy in copies:
        copy.start()
    for copy in copies:
        copy.wait()


def pack_kernel(
    count_ref, earn_any, start_any, len_any, init_any, mean_any, sd_any, out_ref, vec_ref,
    earn_ref, start_ref, len_ref, init_ref, mean_ref, sd_ref, sems,
):
    fetch(
        (
            (earn_any, earn_ref), (start_any, start_ref), (len_any, len_ref),
            (init_any, init_ref), (mean_any, mean_ref), (sd_any, sd_ref),
        ),
        sems,
    )
    periods, slot_rows = earn_ref.shape
    core = core_index()
    low_lane = lax.broadcasted_iota(jnp.int32, (periods // 2, HB), 1) < HALF
    time = lax.broadcasted_iota(jnp.int32, (periods, HB), 0)
    for slot in range(slot_rows // HB):
        cols = slice(slot * HB, (slot + 1) * HB)
        begin = start_ref[slot : slot + 1, :]
        seen = (time >= begin) & (time < begin + len_ref[slot : slot + 1, :])
        live = slot < count_ref[0]
        shift = jnp.where(live, jnp.where(seen, SEEN, 0.0), -SEEN)
        value = earn_ref[:, cols] + shift
        early, late = value[: periods // 2], value[periods // 2 :]
        turned = pltpu.roll(jnp.where(core == 0, late, early), HALF, 1)
        packed = jnp.where(low_lane, jnp.where(core == 0, early, turned), jnp.where(core == 0, turned, late))
        for to in range(out_ref.shape[0]):
            out_ref[to, :, cols] = packed
    raised = jnp.exp(init_ref[...])
    start = raised / jnp.sum(raised, axis=1, keepdims=True)
    row = lax.broadcasted_iota(jnp.int32, vec_ref.shape, 0)
    power = (-0.5 * LOG2E) * jnp.exp(-2.0 * sd_ref[...])
    vec_ref[...] = jnp.where(
        row == 0, start, jnp.where(row == 1, mean_ref[...], jnp.where(row == 2, power, -LOG2E * sd_ref[...]))
    )


def put(ref, at, value):
    states = value.shape[0]
    high = value.astype(BF16)
    ref[at, :states, :states] = high
    ref[at, :states, states:] = (value - high.astype(F32)).astype(BF16)


def both_halves(mat, state):
    states = mat.shape[0]
    high = jnp.dot(mat[:, :states], state, preferred_element_type=F32)
    return high + jnp.dot(mat[:, states:], state, preferred_element_type=F32)


def prep_kernel(
    own_any, other_any, vec_ref, first_mat, second_any, row_probs, consts,
    second_mat, scratch, own_ref, other_ref, sems, out_sems,
):
    copies = [
        pltpu.make_async_copy(src, dst, sems.at[i])
        for i, (src, dst) in enumerate(((own_any, own_ref), (other_any, other_ref)))
    ]
    for copy in copies:
        copy.start()
    part, states, _ = own_ref.shape

    def leave(at):
        return pltpu.make_async_copy(second_mat.at[at], second_any.at[at], out_sems.at[at])

    rows = row_probs.shape[1]
    for i in range(4):
        consts[i] = jnp.broadcast_to(vec_ref[i : i + 1, :], (LANES, states)).T
    for copy, source, ref in zip(copies, (core_index(), 1 - core_index()), (own_ref, other_ref)):
        copy.wait()

        @pl.loop(0, part)
        def _(i):
            at = source * part + i
            lifted = jnp.exp(ref[i].astype(F32))
            probs = lifted * (1.0 / jnp.sum(lifted, axis=1, keepdims=True))
            scratch[...] = probs
            row_probs[at] = scratch[own_rows(lax.axis_index("hh") * rows, rows), :]

            @pl.when(is_forward_first())
            def _():
                put(first_mat, at, probs.T)
                put(second_mat, at, probs)

            @pl.when(jnp.logical_not(is_forward_first()))
            def _():
                put(first_mat, at, probs)
                put(second_mat, at, probs.T)

            leave(at).start()

    for at in range(2 * part):
        leave(at).wait()


def emission(sel_ref, consts, step_now, cols, less=None):
    gap = sel_ref[0, step_now, :1, cols] - consts[1]
    power = gap * gap * consts[2] + consts[3]
    return jnp.exp2(power if less is None else power - less)


def is_moving(sel_ref, step_now, cols):
    return sel_ref[1, step_now, :1, cols] > 0.5


def is_seen(sel_ref, step_now, cols):
    return sel_ref[2, step_now, :1, cols] > 0.5


def column_sum(x):
    return jnp.sum(x, axis=0, keepdims=True)


def own_rows(row_begin, rows):
    return pl.ds(pl.multiple_of(row_begin, rows), rows)


def outer_sum(weights_ref, carried):
    return lax.dot_general(weights_ref[...], carried, (((1,), (1,)), ((), ())), preferred_element_type=F32)


def run_forward(lead, mat, hist, sel_ref, consts, ab_ref, logs, second=None):
    steps, states, width = hist.shape
    cuts = tiles(width)
    inverse = [1.0 / column_sum(ab_ref[:, cols].astype(F32)) for cols in cuts]
    for k in range(steps):
        step_now = lead + k
        if second is None:
            hist[k] = ab_ref[...]
        else:
            weights_ref, row_begin, add_counts = second
            own_alpha = ab_ref[own_rows(row_begin, weights_ref.shape[0]), :].astype(F32)
        for q, cols in enumerate(cuts):
            moved = both_halves(mat[k], ab_ref[:, cols]) * inverse[q]
            moving = is_moving(sel_ref, step_now, cols)
            if second is not None:
                total = column_sum(moved * hist[k, :, cols].astype(F32))
                weight = jnp.where(moving, 1.0 / total, 0.0)
                weights_ref[:, cols] = (own_alpha[:, cols] * inverse[q] * weight).astype(BF16)
            emit = emission(sel_ref, consts, step_now, cols)
            joint = jnp.where(moving, moved, consts[0]) * emit
            scale = column_sum(joint)
            if second is None:
                seen = is_seen(sel_ref, step_now, cols)
                logs[q] = logs[q] + jnp.where(seen, jnp.log2(scale), 0.0)
            inverse[q] = 1.0 / scale
            ab_ref[:, cols] = joint.astype(BF16)
        if second is not None:
            add_counts(k, outer_sum(weights_ref, hist[k]))
    return logs


def run_backward(lead, mat, hist, sel_ref, consts, state, ub_ref, logs, leave, second=None, between=None):
    steps, states, width = hist.shape
    cuts = tiles(width)
    rest = [x[:1] for x in state]
    size = [jnp.zeros((1, LANES), F32) for _ in cuts]

    def step(k):
        step_now = lead + k
        grown = []
        for q, cols in enumerate(cuts):
            emit = emission(sel_ref, consts, step_now, cols, size[q] if second is None else None)
            carried = emit * state[q]
            ub_ref[:, cols] = carried.astype(BF16)
            whole = column_sum(carried)
            grown.append(whole)
            if second is None:
                size[q] = jnp.log2(whole)
                seen = is_seen(sel_ref, step_now, cols)
                logs[q] = logs[q] + jnp.where(seen, size[q], 0.0)
                begun = column_sum(carried * consts[0]) / whole
                rest[q] = jnp.where(seen, begun, rest[q])
        if second is None:
            hist[k] = ub_ref[...]
        else:
            weights_ref, row_begin, add_counts = second
            own_alpha = hist[k, own_rows(row_begin, weights_ref.shape[0]), :].astype(F32)
        for q, cols in enumerate(cuts):
            product = both_halves(mat[k], ub_ref[:, cols])
            moving = is_moving(sel_ref, step_now, cols)
            if second is None:
                state[q] = jnp.where(moving, product, rest[q] * grown[q])
            else:
                shrink = 1.0 / grown[q]
                product = product * shrink
                total = column_sum(product * hist[k, :, cols].astype(F32))
                weight = jnp.where(moving, 1.0 / total, 0.0)
                weights_ref[:, cols] = (own_alpha[:, cols] * weight * shrink).astype(BF16)
                state[q] = jnp.where(moving, product, rest[q])
        if second is not None:
            add_counts(k, outer_sum(weights_ref, ub_ref[...]))

    def left():
        return [x * jnp.exp2(-y) for x, y in zip(state, size)]

    for k in reversed(range(1, steps)):
        step(k)
    if second is None:
        step(0)
        leave(left())
        return
    between()

    @pl.when(lead > 0)
    def _():
        step(0)
        leave(left())

    @pl.when(lead == 0)
    def _():
        second[2](0, jnp.zeros((second[0].shape[0], states), F32))


def put_state(state_out, values, logs):
    states = state_out.shape[0] - EXTRA
    row = lax.broadcasted_iota(jnp.int32, (EXTRA, LANES), 0)
    for q, cols in enumerate(tiles(state_out.shape[1])):
        state_out[:states, cols] = values[q].astype(BF16)
        high = logs[q].astype(BF16).astype(F32)
        middle = (logs[q] - high).astype(BF16).astype(F32)
        piece = jnp.where(
            row == 0, high, jnp.where(row == 1, middle, jnp.where(row == 2, logs[q] - high - middle, 0.0))
        )
        state_out[states:, cols] = piece.astype(BF16)


def state_logs(state_ref):
    states = state_ref.shape[0] - EXTRA
    return [column_sum(state_ref[states:, cols].astype(F32)) for cols in tiles(state_ref.shape[1])]


def first_kernel(resume, grids, part, rows_ref, mat, consts, *refs):
    state_in = refs[0] if resume else None
    hist, state_out, sel_ref, ab_ref = refs[-4:]
    chunk = part * grids + (pl.program_id(0) if grids > 1 else 0)
    steps, states, width = hist.shape
    forward_first, lead = is_forward_first(), lax.axis_index("per") * steps
    cuts = tiles(width)
    group, half_periods, slot_rows = rows_ref.shape
    tops = 2 * len(cuts)

    def scan_source(d, carry):
        rank, picked = carry
        for slot in range(slot_rows // HB):
            cols = slice(slot * HB, (slot + 1) * HB)
            block = rows_ref[d, :, cols]
            live = block > -0.5 * SEEN
            picked = [jnp.where(live & (rank == chunk * tops + i), block, old) for i, old in enumerate(picked)]
            rank = rank + live.astype(jnp.int32)
        return rank, picked

    carry = (jnp.zeros((half_periods, HB), jnp.int32), [jnp.zeros((half_periods, HB), F32)] * tops)
    if group <= 8:
        for d in range(group):
            carry = scan_source(d, carry)
    else:
        carry = lax.fori_loop(0, group, scan_source, carry)
    low_lane = lax.broadcasted_iota(jnp.int32, (half_periods, HB), 1) < HALF
    for q, cols in enumerate(cuts):
        left, right = carry[1][2 * q], carry[1][2 * q + 1]
        before = jnp.zeros((1, HB), F32)
        for late in range(2):
            value = (
                jnp.where(low_lane, pltpu.roll(left, HALF, 1), right)
                if late
                else jnp.where(low_lane, left, pltpu.roll(right, HALF, 1))
            )
            seen = value > 0.5 * SEEN
            earn = jnp.where(seen, value - SEEN, value)
            seen = seen.astype(F32)
            for i in range(half_periods):
                at = late * half_periods + i
                now = seen[i : i + 1]
                sel_ref[0, at, :, cols] = jnp.broadcast_to(earn[i : i + 1], (8, HB))
                sel_ref[1, at, :, cols] = jnp.broadcast_to(now * before, (8, HB))
                sel_ref[2, at, :, cols] = jnp.broadcast_to(now, (8, HB))
                before = now
    zeros = [jnp.zeros((1, LANES), F32) for _ in cuts]

    @pl.when(forward_first)
    def _():
        if resume:
            ab_ref[...] = state_in[:states, :]
        else:
            for cols in cuts:
                ab_ref[:, cols] = consts[0].astype(BF16)
        logs = state_logs(state_in) if resume else list(zeros)
        run_forward(lead, mat, hist, sel_ref, consts, ab_ref, logs)
        put_state(state_out, [ab_ref[:, cols] for cols in cuts], logs)

    @pl.when(jnp.logical_not(forward_first))
    def _():
        state = [
            state_in[:states, cols].astype(F32) if resume else jnp.ones((states, LANES), F32) for cols in cuts
        ]
        logs = state_logs(state_in) if resume else list(zeros)
        leave = lambda values: put_state(state_out, values, logs)
        run_backward(lead, mat, hist, sel_ref, consts, state, ab_ref, logs, leave)


def second_kernel(resume, last, extend, grids, *refs):
    refs = list(refs)
    sel_ref, mat, consts, hist, own_state, state_in = (refs.pop(0) for _ in range(6))
    counts_in, sums_in = (refs.pop(0), refs.pop(0)) if resume else (None, None)
    row_probs = refs.pop(0) if last else None
    mine_ref, other_ref = (refs.pop(0), refs.pop(0)) if last else (None, None)
    counts_out, sums_out = (None, None) if last else (refs.pop(0), refs.pop(0))
    state_out = refs.pop(0) if extend else None
    ab_ref, weights_ref = refs[:2]
    counts_ref, sums_ref = refs[2:] if last else (counts_out, sums_out)
    chunk = pl.program_id(0) if grids > 1 else 0
    steps, states, width = hist.shape
    core, forward_first = core_index(), is_forward_first()
    row_begin = lax.axis_index("hh") * weights_ref.shape[0]
    lead = lax.axis_index("per") * steps
    rows = weights_ref.shape[0]

    def centre(k, counts):
        probs = row_probs[k]
        weighted = probs * counts
        grad = weighted - probs * jnp.sum(weighted, axis=1, keepdims=True)
        at = slice(k * rows, (k + 1) * rows)
        left, right = grad[:, :LANES], grad[:, LANES:]
        mine_ref[at, :] = jnp.where(core == 0, left, right)
        other_ref[at, :] = jnp.where(core == 0, right, left)

    def add_counts(k, counts):
        if grids > 1:
            counts_ref[k] += counts
            return
        if resume:
            counts = counts + counts_in[k]
        if last:
            centre(k, counts)
        else:
            counts_ref[k] = counts

    second = (weights_ref, row_begin, add_counts)

    @pl.when(chunk == 0)
    def _():
        if grids > 1:
            counts_ref[...] = jnp.zeros_like(counts_ref)
        sums_ref[...] = sums_in[...] if resume else jnp.zeros_like(sums_ref)

    def add_sums(alpha_ref, other_state):
        total = jnp.zeros((1, LANES), F32)
        years = jnp.zeros((8, LANES), F32)
        for cols, here, there in zip(tiles(width), state_logs(alpha_ref), state_logs(other_state)):
            alpha = alpha_ref[:states, cols].astype(F32)
            meet = column_sum(alpha * other_state[:states, cols].astype(F32))
            total += (here + there + jnp.log2(meet / column_sum(alpha))) * LN2
            years += jnp.sum(sel_ref[2, :, :, cols], axis=0)
        total = jnp.broadcast_to(jnp.sum(total, axis=1, keepdims=True), (1, LANES))
        years = jnp.broadcast_to(jnp.sum(years[:1], axis=1, keepdims=True), (1, LANES))
        row = lax.broadcasted_iota(jnp.int32, (8, LANES), 0)
        sums_ref[...] += jnp.where(row == 0, total, jnp.where(row == 1, years, 0.0))

    zeros = [jnp.zeros((1, LANES), F32) for _ in tiles(width)]

    @pl.when(jnp.logical_not(forward_first))
    def _():
        ab_ref[...] = state_in[:states, :]
        run_forward(lead, mat, hist, sel_ref, consts, ab_ref, list(zeros), second)
        add_sums(state_in, own_state)
        if extend:
            put_state(state_out, [ab_ref[:, cols] for cols in tiles(width)], zeros)

    @pl.when(forward_first)
    def _():
        state = [state_in[:states, cols].astype(F32) for cols in tiles(width)]
        leave = lambda values: put_state(state_out, values, zeros) if extend else None
        run_backward(lead, mat, hist, sel_ref, consts, state, ab_ref, list(zeros), leave, second, lambda: add_sums(own_state, state_in))

    if last:

        @pl.when(chunk == grids - 1)
        def _():
            if grids > 1:
                for k in range(steps):
                    centre(k, counts_ref[k])
            mine_ref[steps * rows :, :] = sums_ref[...]
            other_ref[steps * rows :, :] = sums_ref[...]


def finish_kernel(scale, mine_ref, other_ref, grad_ref, mean_ref):
    count = grad_ref.shape[0]
    total = mine_ref[count : count + 1, :] + other_ref[count : count + 1, :]
    years = mine_ref[count + 1 : count + 2, :] + other_ref[count + 1 : count + 2, :]
    grad_ref[...] = (mine_ref[:count, :] + other_ref[:count, :]) * (scale / years)
    mean_ref[0] = (total / years)[0, 0]


def per_device(
    earnings, starts, lengths, block_count, trans_logits, init_logits, state_mean, log_sd
):
    slot_rows, periods = earnings.shape
    states = init_logits.shape[0]
    group = lax.axis_size(("hh", "per"))
    sides = lax.axis_size("per")
    cores = lax.axis_size("st")
    part = trans_logits.shape[0]
    steps = part * cores
    rows = states // lax.axis_size("hh")
    households = group * HB // cores
    parts = 2 if households <= 4 * HB else 1
    share = households // parts
    width = min(2 * HB, share)
    grids = share // width
    side = lax.axis_index("per")
    shaped = jax.ShapeDtypeStruct
    dma = pltpu.SemaphoreType.DMA

    swap = [(0, 1), (1, 0)]
    vec_row = pltpu.VMEM((1, states), F32)
    packed, vectors = pl.pallas_call(
        pack_kernel,
        out_shape=[
            pltpu.VMEM((group, periods // 2, slot_rows), F32),
            pltpu.VMEM((8, states), F32),
        ],
        in_specs=[smem()] + [hbm()] * 6,
        out_specs=[vmem()] * 2,
        scratch_shapes=[
            pltpu.VMEM((periods, slot_rows), F32),
            pltpu.VMEM((slot_rows // HB, HB), jnp.int32),
            pltpu.VMEM((slot_rows // HB, HB), jnp.int32),
            vec_row,
            vec_row,
            vec_row,
            dma((6,)),
        ],
        compiler_params=params(2),
        name="pack",
    )(
        block_count,
        *in_hbm(
            earnings.T, starts.reshape(-1, HB), lengths.reshape(-1, HB),
            init_logits.reshape(1, states), state_mean.reshape(1, states), log_sd.reshape(1, states),
        ),
    )
    packed, later_logits = lax.optimization_barrier((packed, trans_logits))
    other_logits = lax.ppermute(later_logits, "st", swap)
    gathered = lax.all_to_all(packed, ("hh", "per"), split_axis=0, concat_axis=0, tiled=True)
    first_mat, second_mat, row_probs, consts = pl.pallas_call(
        prep_kernel,
        out_shape=[
            pltpu.VMEM((steps, states, 2 * states), BF16),
            pltpu.HBM((steps, states, 2 * states), BF16),
            pltpu.VMEM((steps, rows, states), F32),
            pltpu.VMEM((4, states, LANES), F32),
        ],
        in_specs=[hbm(), hbm(), vmem()],
        out_specs=[vmem(), hbm(), vmem(), vmem()],
        scratch_shapes=[
            pltpu.VMEM((steps, states, 2 * states), BF16),
            pltpu.VMEM((states, states), F32),
            pltpu.VMEM(trans_logits.shape, BF16),
            pltpu.VMEM(trans_logits.shape, BF16),
            dma((2,)),
            dma((steps,)),
        ],
        compiler_params=params(6),
        name="prep",
    )(*in_hbm(trans_logits, other_logits), vectors)

    def whole(*shape):
        if grids == 1:
            return vmem()
        return pl.BlockSpec(shape, lambda g: (0,) * len(shape))

    def lanes(*lead):
        if grids == 1:
            return vmem()
        return pl.BlockSpec(lead + (width,), lambda g: (0,) * len(lead) + (g,))

    grid = (grids,) if grids > 1 else ()
    hist_shape = shaped((steps, states, share), BF16)
    state_shape = shaped((states + EXTRA, share), BF16)
    sel_shape = shaped((3, periods, 8, share), F32)
    swap_shape = shaped((steps * rows + 8, LANES), F32)
    counts_shape = shaped((steps, rows, states), F32)
    sums_shape = shaped((8, LANES), F32)
    hist_spec, state_spec, sel_spec = lanes(steps, states), lanes(states + EXTRA), lanes(3, periods, 8)
    const_spec = whole(4, states, LANES)

    def first_pass(index, state_in):
        resume = state_in is not None
        return pl.pallas_call(
            functools.partial(first_kernel, resume, grids, index),
            grid=grid,
            out_shape=[hist_shape, state_shape, sel_shape],
            in_specs=[whole(*gathered.shape), whole(*first_mat.shape), const_spec]
            + [state_spec] * resume,
            out_specs=[hist_spec, state_spec, sel_spec],
            scratch_shapes=[pltpu.VMEM((states, width), BF16)],
            compiler_params=params(8 if grids == 1 else 32),
            name="first_pass",
        )(gathered, first_mat, consts, *([state_in] if resume else []))

    def second_pass(kept, state_in, sums_in, last, extend):
        hist, own_state, sel = kept
        resume = sums_in is not None
        scratch = [
            pltpu.VMEM((states, width), BF16),
            pltpu.VMEM((rows, width), BF16),
        ]
        counts_spec, sums_spec = whole(*counts_shape.shape), whole(*sums_shape.shape)
        if last:
            out_shape = [swap_shape] * 2
            scratch += [pltpu.VMEM(counts_shape.shape, F32), pltpu.VMEM(sums_shape.shape, F32)]
        else:
            out_shape = [counts_shape, sums_shape]
        out_specs = [whole(*x.shape) for x in out_shape]
        if extend:
            out_shape, out_specs = out_shape + [state_shape], out_specs + [state_spec]
        return pl.pallas_call(
            functools.partial(second_kernel, resume, last, extend, grids),
            grid=grid,
            out_shape=out_shape,
            in_specs=[sel_spec, whole(*second_mat.shape), const_spec, hist_spec, state_spec, state_spec]
            + [counts_spec, sums_spec] * resume
            + [whole(*row_probs.shape)] * last,
            out_specs=out_specs,
            scratch_shapes=scratch,
            compiler_params=params(8 if grids == 1 else 32),
            name="second_pass",
        )(
            sel, second_mat, consts, hist, own_state, state_in,
            *(sums_in if resume else []),
            *([row_probs] if last else []),
        )

    def hand_over(state, stage):
        moves = [(stage, stage + 1), (sides - 1 - stage, sides - 2 - stage)]
        return lax.ppermute(state, "per", moves)

    if sides == 2:
        kept = [first_pass(index, None) for index in range(parts)]
        arrived = [hand_over(each[1], 0) for each in kept]
        sums = None
        for index in range(parts):
            sums = second_pass(kept[index], arrived[index], sums, index == parts - 1, False)
        mine, other = sums
    else:
        kept = [jnp.zeros(x.shape, x.dtype) for x in (hist_shape, state_shape, sel_shape)]
        done = [jnp.zeros(x.shape, x.dtype) for x in (swap_shape, swap_shape, state_shape)]
        state = None
        for stage in range(sides):
            active = (side == stage) | (side == sides - 1 - stage)
            if stage < sides // 2:
                kept = lax.cond(
                    active, lambda x, kept: list(first_pass(0, x)), lambda x, kept: kept, state, kept
                )
                state = kept[1]
            else:
                done = lax.cond(
                    active,
                    lambda x, done: list(second_pass(kept, x, None, True, True)),
                    lambda x, done: done,
                    state,
                    done,
                )
                state = done[2]
            if stage < sides - 1:
                state = hand_over(state, stage)
        mine, other, _ = done
        total = jnp.where(side == sides // 2, mine[steps * rows], 0.0)
        total = lax.psum(total, "per")
        mine = mine.at[steps * rows].set(total)
        other = other.at[steps * rows].set(total)
    received = lax.ppermute(other, "st", swap)
    trans_grad, mean_loglik = pl.pallas_call(
        functools.partial(finish_kernel, float(states * states * periods)),
        out_shape=[shaped((steps * rows, LANES), F32), shaped((1,), F32)],
        in_specs=[vmem(), vmem()],
        out_specs=[vmem(), smem()],
        compiler_params=params(4),
        name="finish",
    )(mine, received)
    return (trans_grad.reshape(steps, rows, LANES), mean_loglik)


def solution(mesh):
    placed = (
        P(("hh", "per"), None),
        P(("hh", "per")),
        P(("hh", "per")),
        P(("hh", "per")),
        P(("grp", "per", "st"), None, None),
        P("grp"),
        P("grp"),
        P("grp"),
    )
    return jax.shard_map(
        per_device,
        mesh=mesh,
        in_specs=placed,
        out_specs=(P(("grp", "per"), "hh", "st"), P("grp")),
        check_vma=False,
    )
```

```python
import functools

import jax
import jax.numpy as jnp
from jax import lax
from jax.experimental import pallas as pl
from jax.experimental.pallas import tpu as pltpu
from jax.sharding import PartitionSpec as P

HB = 128
LANES = 128
HALF = HB // 2
SEEN = 16.0
F32 = jnp.float32
BF16 = jnp.bfloat16
LOG2E = 1.4426950408889634
LN2 = 0.6931471805599453
EXTRA = 16


def vmem():
    return pl.BlockSpec(memory_space=pltpu.VMEM)


def smem():
    return pl.BlockSpec(memory_space=pltpu.SMEM)


def hbm():
    return pl.BlockSpec(memory_space=pltpu.HBM)


def in_hbm(*arrays):
    return [pltpu.with_memory_space_constraint(x, pltpu.HBM) for x in arrays]


def params(mebibytes):
    return pltpu.CompilerParams(vmem_limit_bytes=mebibytes * 1024 * 1024)


def core_index():
    return lax.axis_index("st")


def half_index():
    return (lax.axis_index("st") + lax.axis_index("per")) % 2


def is_forward_first():
    return 2 * lax.axis_index("per") < lax.axis_size("per")


def tiles(width):
    return [slice(q, q + LANES) for q in range(0, width, LANES)]


def fetch(pairs, sems):
    copies = [pltpu.make_async_copy(src, dst, sems.at[i]) for i, (src, dst) in enumerate(pairs)]
    for copy in copies:
        copy.start()
    for copy in copies:
        copy.wait()


def pack_kernel(
    count_ref, earn_any, start_any, len_any, init_any, mean_any, sd_any, out_ref, vec_ref,
    earn_ref, start_ref, len_ref, init_ref, mean_ref, sd_ref, sems,
):
    fetch(
        (
            (earn_any, earn_ref), (start_any, start_ref), (len_any, len_ref),
            (init_any, init_ref), (mean_any, mean_ref), (sd_any, sd_ref),
        ),
        sems,
    )
    periods, slot_rows = earn_ref.shape
    core = half_index()
    low_lane = lax.broadcasted_iota(jnp.int32, (periods // 2, HB), 1) < HALF
    time = lax.broadcasted_iota(jnp.int32, (periods, HB), 0)
    for slot in range(slot_rows // HB):
        cols = slice(slot * HB, (slot + 1) * HB)
        begin = start_ref[slot : slot + 1, :]
        seen = (time >= begin) & (time < begin + len_ref[slot : slot + 1, :])
        live = slot < count_ref[0]
        shift = jnp.where(live, jnp.where(seen, SEEN, 0.0), -SEEN)
        value = earn_ref[:, cols] + shift
        early, late = value[: periods // 2], value[periods // 2 :]
        turned = pltpu.roll(jnp.where(core == 0, late, early), HALF, 1)
        packed = jnp.where(low_lane, jnp.where(core == 0, early, turned), jnp.where(core == 0, turned, late))
        for to in range(out_ref.shape[0]):
            out_ref[to, :, cols] = packed
    raised = jnp.exp(init_ref[...])
    start = raised / jnp.sum(raised, axis=1, keepdims=True)
    row = lax.broadcasted_iota(jnp.int32, vec_ref.shape, 0)
    power = (-0.5 * LOG2E) * jnp.exp(-2.0 * sd_ref[...])
    vec_ref[...] = jnp.where(
        row == 0, start, jnp.where(row == 1, mean_ref[...], jnp.where(row == 2, power, -LOG2E * sd_ref[...]))
    )


def put(ref, at, value):
    states = value.shape[0]
    high = value.astype(BF16)
    ref[at, :states, :states] = high
    ref[at, :states, states:] = (value - high.astype(F32)).astype(BF16)


def both_halves(mat, state):
    states = mat.shape[0]
    high = jnp.dot(mat[:, :states], state, preferred_element_type=F32)
    return high + jnp.dot(mat[:, states:], state, preferred_element_type=F32)


def prep_kernel(
    own_any, other_any, vec_ref, first_mat, second_any, row_probs, consts,
    second_mat, scratch, own_ref, other_ref, sems, out_sems,
):
    copies = [
        pltpu.make_async_copy(src, dst, sems.at[i])
        for i, (src, dst) in enumerate(((own_any, own_ref), (other_any, other_ref)))
    ]
    for copy in copies:
        copy.start()
    part, states, _ = own_ref.shape

    def leave(at):
        return pltpu.make_async_copy(second_mat.at[at], second_any.at[at], out_sems.at[at])

    rows = row_probs.shape[1]
    for i in range(4):
        consts[i] = jnp.broadcast_to(vec_ref[i : i + 1, :], (LANES, states)).T
    for copy, source, ref in zip(copies, (core_index(), 1 - core_index()), (own_ref, other_ref)):
        copy.wait()

        @pl.loop(0, part)
        def _(i):
            at = source * part + i
            lifted = jnp.exp(ref[i].astype(F32))
            probs = lifted * (1.0 / jnp.sum(lifted, axis=1, keepdims=True))
            scratch[...] = probs
            row_probs[at] = scratch[own_rows(lax.axis_index("hh") * rows, rows), :]

            @pl.when(is_forward_first())
            def _():
                put(first_mat, at, probs.T)
                put(second_mat, at, probs)

            @pl.when(jnp.logical_not(is_forward_first()))
            def _():
                put(first_mat, at, probs)
                put(second_mat, at, probs.T)

            leave(at).start()

    for at in range(2 * part):
        leave(at).wait()


def emission(sel_ref, consts, step_now, cols, less=None):
    gap = sel_ref[0, step_now, :1, cols] - consts[1]
    power = gap * gap * consts[2] + consts[3]
    return jnp.exp2(power if less is None else power - less)


def is_moving(sel_ref, step_now, cols):
    return sel_ref[1, step_now, :1, cols] > 0.5


def is_seen(sel_ref, step_now, cols):
    return sel_ref[2, step_now, :1, cols] > 0.5


def column_sum(x):
    return jnp.sum(x, axis=0, keepdims=True)


def own_rows(row_begin, rows):
    return pl.ds(pl.multiple_of(row_begin, rows), rows)


def outer_sum(weights_ref, carried):
    return lax.dot_general(weights_ref[...], carried, (((1,), (1,)), ((), ())), preferred_element_type=F32)


def run_forward(lead, mat, hist, sel_ref, consts, ab_ref, logs, second=None):
    steps, states, width = hist.shape
    cuts = tiles(width)
    inverse = [1.0 / column_sum(ab_ref[:, cols].astype(F32)) for cols in cuts]
    for k in range(steps):
        step_now = lead + k
        if second is None:
            hist[k] = ab_ref[...]
        else:
            weights_ref, row_begin, add_counts = second
            own_alpha = ab_ref[own_rows(row_begin, weights_ref.shape[0]), :].astype(F32)
        for q, cols in enumerate(cuts):
            moved = both_halves(mat[k], ab_ref[:, cols]) * inverse[q]
            moving = is_moving(sel_ref, step_now, cols)
            if second is not None:
                total = column_sum(moved * hist[k, :, cols].astype(F32))
                weight = jnp.where(moving, 1.0 / total, 0.0)
                weights_ref[:, cols] = (own_alpha[:, cols] * inverse[q] * weight).astype(BF16)
            emit = emission(sel_ref, consts, step_now, cols)
            joint = jnp.where(moving, moved, consts[0]) * emit
            scale = column_sum(joint)
            if second is None:
                seen = is_seen(sel_ref, step_now, cols)
                logs[q] = logs[q] + jnp.where(seen, jnp.log2(scale), 0.0)
            inverse[q] = 1.0 / scale
            ab_ref[:, cols] = joint.astype(BF16)
        if second is not None:
            add_counts(k, outer_sum(weights_ref, hist[k]))
    return logs


def run_backward(lead, mat, hist, sel_ref, consts, state, ub_ref, logs, leave, second=None, between=None):
    steps, states, width = hist.shape
    cuts = tiles(width)
    rest = [x[:1] for x in state]
    size = [jnp.zeros((1, LANES), F32) for _ in cuts]

    def step(k):
        step_now = lead + k
        grown = []
        for q, cols in enumerate(cuts):
            emit = emission(sel_ref, consts, step_now, cols, size[q] if second is None else None)
            carried = emit * state[q]
            ub_ref[:, cols] = carried.astype(BF16)
            whole = column_sum(carried)
            grown.append(whole)
            if second is None:
                size[q] = jnp.log2(whole)
                seen = is_seen(sel_ref, step_now, cols)
                logs[q] = logs[q] + jnp.where(seen, size[q], 0.0)
                begun = column_sum(carried * consts[0]) / whole
                rest[q] = jnp.where(seen, begun, rest[q])
        if second is None:
            hist[k] = ub_ref[...]
        else:
            weights_ref, row_begin, add_counts = second
            own_alpha = hist[k, own_rows(row_begin, weights_ref.shape[0]), :].astype(F32)
        for q, cols in enumerate(cuts):
            product = both_halves(mat[k], ub_ref[:, cols])
            moving = is_moving(sel_ref, step_now, cols)
            if second is None:
                state[q] = jnp.where(moving, product, rest[q] * grown[q])
            else:
                shrink = 1.0 / grown[q]
                product = product * shrink
                total = column_sum(product * hist[k, :, cols].astype(F32))
                weight = jnp.where(moving, 1.0 / total, 0.0)
                weights_ref[:, cols] = (own_alpha[:, cols] * weight * shrink).astype(BF16)
                state[q] = jnp.where(moving, product, rest[q])
        if second is not None:
            add_counts(k, outer_sum(weights_ref, ub_ref[...]))

    def left():
        return [x * jnp.exp2(-y) for x, y in zip(state, size)]

    for k in reversed(range(1, steps)):
        step(k)
    if second is None:
        step(0)
        leave(left())
        return
    between()

    @pl.when(lead > 0)
    def _():
        step(0)
        leave(left())

    @pl.when(lead == 0)
    def _():
        second[2](0, jnp.zeros((second[0].shape[0], states), F32))


def put_state(state_out, values, logs):
    states = state_out.shape[0] - EXTRA
    row = lax.broadcasted_iota(jnp.int32, (EXTRA, LANES), 0)
    for q, cols in enumerate(tiles(state_out.shape[1])):
        state_out[:states, cols] = values[q].astype(BF16)
        high = logs[q].astype(BF16).astype(F32)
        middle = (logs[q] - high).astype(BF16).astype(F32)
        piece = jnp.where(
            row == 0, high, jnp.where(row == 1, middle, jnp.where(row == 2, logs[q] - high - middle, 0.0))
        )
        state_out[states:, cols] = piece.astype(BF16)


def state_logs(state_ref):
    states = state_ref.shape[0] - EXTRA
    return [column_sum(state_ref[states:, cols].astype(F32)) for cols in tiles(state_ref.shape[1])]


def first_kernel(resume, grids, part, rows_ref, mat, consts, *refs):
    state_in = refs[0] if resume else None
    hist, state_out, sel_ref, ab_ref = refs[-4:]
    chunk = part * grids + (pl.program_id(0) if grids > 1 else 0)
    steps, states, width = hist.shape
    forward_first, lead = is_forward_first(), lax.axis_index("per") * steps
    cuts = tiles(width)
    group, half_periods, slot_rows = rows_ref.shape
    tops = 2 * len(cuts)

    def scan_source(d, carry):
        rank, picked = carry
        for slot in range(slot_rows // HB):
            cols = slice(slot * HB, (slot + 1) * HB)
            block = rows_ref[d, :, cols]
            live = block > -0.5 * SEEN
            picked = [jnp.where(live & (rank == chunk * tops + i), block, old) for i, old in enumerate(picked)]
            rank = rank + live.astype(jnp.int32)
        return rank, picked

    carry = (jnp.zeros((half_periods, HB), jnp.int32), [jnp.zeros((half_periods, HB), F32)] * tops)
    if group <= 8:
        for d in range(group):
            carry = scan_source(d, carry)
    else:
        carry = lax.fori_loop(0, group, scan_source, carry)
    low_lane = lax.broadcasted_iota(jnp.int32, (half_periods, HB), 1) < HALF
    for q, cols in enumerate(cuts):
        left, right = carry[1][2 * q], carry[1][2 * q + 1]
        before = jnp.zeros((1, HB), F32)
        for late in range(2):
            value = (
                jnp.where(low_lane, pltpu.roll(left, HALF, 1), right)
                if late
                else jnp.where(low_lane, left, pltpu.roll(right, HALF, 1))
            )
            seen = value > 0.5 * SEEN
            earn = jnp.where(seen, value - SEEN, value)
            seen = seen.astype(F32)
            for i in range(half_periods):
                at = late * half_periods + i
                now = seen[i : i + 1]
                sel_ref[0, at, :, cols] = jnp.broadcast_to(earn[i : i + 1], (8, HB))
                sel_ref[1, at, :, cols] = jnp.broadcast_to(now * before, (8, HB))
                sel_ref[2, at, :, cols] = jnp.broadcast_to(now, (8, HB))
                before = now
    zeros = [jnp.zeros((1, LANES), F32) for _ in cuts]

    @pl.when(forward_first)
    def _():
        if resume:
            ab_ref[...] = state_in[:states, :]
        else:
            for cols in cuts:
                ab_ref[:, cols] = consts[0].astype(BF16)
        logs = state_logs(state_in) if resume else list(zeros)
        run_forward(lead, mat, hist, sel_ref, consts, ab_ref, logs)
        put_state(state_out, [ab_ref[:, cols] for cols in cuts], logs)

    @pl.when(jnp.logical_not(forward_first))
    def _():
        state = [
            state_in[:states, cols].astype(F32) if resume else jnp.ones((states, LANES), F32) for cols in cuts
        ]
        logs = state_logs(state_in) if resume else list(zeros)
        leave = lambda values: put_state(state_out, values, logs)
        run_backward(lead, mat, hist, sel_ref, consts, state, ab_ref, logs, leave)


def second_kernel(resume, last, extend, grids, *refs):
    refs = list(refs)
    sel_ref, mat, consts, hist, own_state, state_in = (refs.pop(0) for _ in range(6))
    counts_in, sums_in = (refs.pop(0), refs.pop(0)) if resume else (None, None)
    row_probs = refs.pop(0) if last else None
    mine_ref, other_ref = (refs.pop(0), refs.pop(0)) if last else (None, None)
    counts_out, sums_out = (None, None) if last else (refs.pop(0), refs.pop(0))
    state_out = refs.pop(0) if extend else None
    ab_ref, weights_ref = refs[:2]
    counts_ref, sums_ref = refs[2:] if last else (counts_out, sums_out)
    chunk = pl.program_id(0) if grids > 1 else 0
    steps, states, width = hist.shape
    core, forward_first = core_index(), is_forward_first()
    row_begin = lax.axis_index("hh") * weights_ref.shape[0]
    lead = lax.axis_index("per") * steps
    rows = weights_ref.shape[0]

    def centre(k, counts):
        probs = row_probs[k]
        weighted = probs * counts
        grad = weighted - probs * jnp.sum(weighted, axis=1, keepdims=True)
        at = slice(k * rows, (k + 1) * rows)
        left, right = grad[:, :LANES], grad[:, LANES:]
        mine_ref[at, :] = jnp.where(core == 0, left, right)
        other_ref[at, :] = jnp.where(core == 0, right, left)

    def add_counts(k, counts):
        if grids > 1:
            counts_ref[k] += counts
            return
        if resume:
            counts = counts + counts_in[k]
        if last:
            centre(k, counts)
        else:
            counts_ref[k] = counts

    second = (weights_ref, row_begin, add_counts)

    @pl.when(chunk == 0)
    def _():
        if grids > 1:
            counts_ref[...] = jnp.zeros_like(counts_ref)
        sums_ref[...] = sums_in[...] if resume else jnp.zeros_like(sums_ref)

    def add_sums(alpha_ref, other_state):
        total = jnp.zeros((1, LANES), F32)
        years = jnp.zeros((8, LANES), F32)
        for cols, here, there in zip(tiles(width), state_logs(alpha_ref), state_logs(other_state)):
            alpha = alpha_ref[:states, cols].astype(F32)
            meet = column_sum(alpha * other_state[:states, cols].astype(F32))
            total += (here + there + jnp.log2(meet / column_sum(alpha))) * LN2
            years += jnp.sum(sel_ref[2, :, :, cols], axis=0)
        total = jnp.broadcast_to(jnp.sum(total, axis=1, keepdims=True), (1, LANES))
        years = jnp.broadcast_to(jnp.sum(years[:1], axis=1, keepdims=True), (1, LANES))
        row = lax.broadcasted_iota(jnp.int32, (8, LANES), 0)
        sums_ref[...] += jnp.where(row == 0, total, jnp.where(row == 1, years, 0.0))

    zeros = [jnp.zeros((1, LANES), F32) for _ in tiles(width)]

    @pl.when(jnp.logical_not(forward_first))
    def _():
        ab_ref[...] = state_in[:states, :]
        run_forward(lead, mat, hist, sel_ref, consts, ab_ref, list(zeros), second)
        add_sums(state_in, own_state)
        if extend:
            put_state(state_out, [ab_ref[:, cols] for cols in tiles(width)], zeros)

    @pl.when(forward_first)
    def _():
        state = [state_in[:states, cols].astype(F32) for cols in tiles(width)]
        leave = lambda values: put_state(state_out, values, zeros) if extend else None
        run_backward(lead, mat, hist, sel_ref, consts, state, ab_ref, list(zeros), leave, second, lambda: add_sums(own_state, state_in))

    if last:

        @pl.when(chunk == grids - 1)
        def _():
            if grids > 1:
                for k in range(steps):
                    centre(k, counts_ref[k])
            mine_ref[steps * rows :, :] = sums_ref[...]
            other_ref[steps * rows :, :] = sums_ref[...]


def finish_kernel(scale, mine_ref, other_ref, grad_ref, mean_ref):
    count = grad_ref.shape[0]
    total = mine_ref[count : count + 1, :] + other_ref[count : count + 1, :]
    years = mine_ref[count + 1 : count + 2, :] + other_ref[count + 1 : count + 2, :]
    grad_ref[...] = (mine_ref[:count, :] + other_ref[:count, :]) * (scale / years)
    mean_ref[0] = (total / years)[0, 0]


def per_device(
    earnings, starts, lengths, block_count, trans_logits, init_logits, state_mean, log_sd
):
    slot_rows, periods = earnings.shape
    states = init_logits.shape[0]
    group = lax.axis_size(("hh", "per"))
    sides = lax.axis_size("per")
    cores = lax.axis_size("st")
    part = trans_logits.shape[0]
    steps = part * cores
    rows = states // lax.axis_size("hh")
    households = group * HB // cores
    parts = 2 if households <= 4 * HB else 1
    share = households // parts
    width = min(2 * HB, share)
    grids = share // width
    side = lax.axis_index("per")
    shaped = jax.ShapeDtypeStruct
    dma = pltpu.SemaphoreType.DMA

    swap = [(0, 1), (1, 0)]
    vec_row = pltpu.VMEM((1, states), F32)
    packed, vectors = pl.pallas_call(
        pack_kernel,
        out_shape=[
            pltpu.VMEM((group, periods // 2, slot_rows), F32),
            pltpu.VMEM((8, states), F32),
        ],
        in_specs=[smem()] + [hbm()] * 6,
        out_specs=[vmem()] * 2,
        scratch_shapes=[
            pltpu.VMEM((periods, slot_rows), F32),
            pltpu.VMEM((slot_rows // HB, HB), jnp.int32),
            pltpu.VMEM((slot_rows // HB, HB), jnp.int32),
            vec_row,
            vec_row,
            vec_row,
            dma((6,)),
        ],
        compiler_params=params(2),
        name="pack",
    )(
        block_count,
        *in_hbm(
            earnings.T, starts.reshape(-1, HB), lengths.reshape(-1, HB),
            init_logits.reshape(1, states), state_mean.reshape(1, states), log_sd.reshape(1, states),
        ),
    )
    packed, later_logits = lax.optimization_barrier((packed, trans_logits))
    other_logits = lax.ppermute(later_logits, "st", swap)
    places = [(z, x) for z in range(group // sides) for x in range(sides)]
    gathered = lax.all_to_all(
        packed,
        ("hh", "per", "st"),
        split_axis=0,
        concat_axis=0,
        axis_index_groups=[[(z * sides + x) * 2 + (half + x) % 2 for z, x in places] for half in range(2)],
        tiled=True,
    )
    first_mat, second_mat, row_probs, consts = pl.pallas_call(
        prep_kernel,
        out_shape=[
            pltpu.VMEM((steps, states, 2 * states), BF16),
            pltpu.HBM((steps, states, 2 * states), BF16),
            pltpu.VMEM((steps, rows, states), F32),
            pltpu.VMEM((4, states, LANES), F32),
        ],
        in_specs=[hbm(), hbm(), vmem()],
        out_specs=[vmem(), hbm(), vmem(), vmem()],
        scratch_shapes=[
            pltpu.VMEM((steps, states, 2 * states), BF16),
            pltpu.VMEM((states, states), F32),
            pltpu.VMEM(trans_logits.shape, BF16),
            pltpu.VMEM(trans_logits.shape, BF16),
            dma((2,)),
            dma((steps,)),
        ],
        compiler_params=params(6),
        name="prep",
    )(*in_hbm(trans_logits, other_logits), vectors)

    def whole(*shape):
        if grids == 1:
            return vmem()
        return pl.BlockSpec(shape, lambda g: (0,) * len(shape))

    def lanes(*lead):
        if grids == 1:
            return vmem()
        return pl.BlockSpec(lead + (width,), lambda g: (0,) * len(lead) + (g,))

    grid = (grids,) if grids > 1 else ()
    hist_shape = shaped((steps, states, share), BF16)
    state_shape = shaped((states + EXTRA, share), BF16)
    sel_shape = shaped((3, periods, 8, share), F32)
    swap_shape = shaped((steps * rows + 8, LANES), F32)
    counts_shape = shaped((steps, rows, states), F32)
    sums_shape = shaped((8, LANES), F32)
    hist_spec, state_spec, sel_spec = lanes(steps, states), lanes(states + EXTRA), lanes(3, periods, 8)
    const_spec = whole(4, states, LANES)

    def first_pass(index, state_in):
        resume = state_in is not None
        return pl.pallas_call(
            functools.partial(first_kernel, resume, grids, index),
            grid=grid,
            out_shape=[hist_shape, state_shape, sel_shape],
            in_specs=[whole(*gathered.shape), whole(*first_mat.shape), const_spec]
            + [state_spec] * resume,
            out_specs=[hist_spec, state_spec, sel_spec],
            scratch_shapes=[pltpu.VMEM((states, width), BF16)],
            compiler_params=params(8 if grids == 1 else 32),
            name="first_pass",
        )(gathered, first_mat, consts, *([state_in] if resume else []))

    def second_pass(kept, state_in, sums_in, last, extend):
        hist, own_state, sel = kept
        resume = sums_in is not None
        scratch = [
            pltpu.VMEM((states, width), BF16),
            pltpu.VMEM((rows, width), BF16),
        ]
        counts_spec, sums_spec = whole(*counts_shape.shape), whole(*sums_shape.shape)
        if last:
            out_shape = [swap_shape] * 2
            scratch += [pltpu.VMEM(counts_shape.shape, F32), pltpu.VMEM(sums_shape.shape, F32)]
        else:
            out_shape = [counts_shape, sums_shape]
        out_specs = [whole(*x.shape) for x in out_shape]
        if extend:
            out_shape, out_specs = out_shape + [state_shape], out_specs + [state_spec]
        return pl.pallas_call(
            functools.partial(second_kernel, resume, last, extend, grids),
            grid=grid,
            out_shape=out_shape,
            in_specs=[sel_spec, whole(*second_mat.shape), const_spec, hist_spec, state_spec, state_spec]
            + [counts_spec, sums_spec] * resume
            + [whole(*row_probs.shape)] * last,
            out_specs=out_specs,
            scratch_shapes=scratch,
            compiler_params=params(8 if grids == 1 else 32),
            name="second_pass",
        )(
            sel, second_mat, consts, hist, own_state, state_in,
            *(sums_in if resume else []),
            *([row_probs] if last else []),
        )

    def hand_over(state, stage):
        moves = [(stage, stage + 1), (sides - 1 - stage, sides - 2 - stage)]
        return lax.ppermute(state, ("per", "st"), [(2 * a + c, 2 * b + 1 - c) for a, b in moves for c in range(2)])

    if sides == 2:
        kept = [first_pass(index, None) for index in range(parts)]
        arrived = [hand_over(each[1], 0) for each in kept]
        sums = None
        for index in range(parts):
            sums = second_pass(kept[index], arrived[index], sums, index == parts - 1, False)
        mine, other = sums
    else:
        kept = [jnp.zeros(x.shape, x.dtype) for x in (hist_shape, state_shape, sel_shape)]
        done = [jnp.zeros(x.shape, x.dtype) for x in (swap_shape, swap_shape, state_shape)]
        state = None
        for stage in range(sides):
            active = (side == stage) | (side == sides - 1 - stage)
            if stage < sides // 2:
                kept = lax.cond(
                    active, lambda x, kept: list(first_pass(0, x)), lambda x, kept: kept, state, kept
                )
                state = kept[1]
            else:
                done = lax.cond(
                    active,
                    lambda x, done: list(second_pass(kept, x, None, True, True)),
                    lambda x, done: done,
                    state,
                    done,
                )
                state = done[2]
            if stage < sides - 1:
                state = hand_over(state, stage)
        mine, other, _ = done
        total = jnp.where(side == sides // 2, mine[steps * rows], 0.0)
        total = lax.psum(total, "per")
        mine = mine.at[steps * rows].set(total)
        other = other.at[steps * rows].set(total)
    received = lax.ppermute(other, "st", swap)
    trans_grad, mean_loglik = pl.pallas_call(
        functools.partial(finish_kernel, float(states * states * periods)),
        out_shape=[shaped((steps * rows, LANES), F32), shaped((1,), F32)],
        in_specs=[vmem(), vmem()],
        out_specs=[vmem(), smem()],
        compiler_params=params(4),
        name="finish",
    )(mine, received)
    return (trans_grad.reshape(steps, rows, LANES), mean_loglik)


def solution(mesh):
    placed = (
        P(("hh", "per"), None),
        P(("hh", "per")),
        P(("hh", "per")),
        P(("hh", "per")),
        P(("grp", "per", "st"), None, None),
        P("grp"),
        P("grp"),
        P("grp"),
    )
    return jax.shard_map(
        per_device,
        mesh=mesh,
        in_specs=placed,
        out_specs=(P(("grp", "per"), "hh", "st"), P("grp")),
        check_vma=False,
    )
```

```python
import functools

import jax
import jax.numpy as jnp
from jax import lax
from jax.experimental import pallas as pl
from jax.experimental.pallas import tpu as pltpu
from jax.sharding import PartitionSpec as P

HB = 128
LANES = 128
HALF = HB // 2
SEEN = 16.0
F32 = jnp.float32
BF16 = jnp.bfloat16
LOG2E = 1.4426950408889634
LN2 = 0.6931471805599453
EXTRA = 16


def vmem():
    return pl.BlockSpec(memory_space=pltpu.VMEM)


def smem():
    return pl.BlockSpec(memory_space=pltpu.SMEM)


def hbm():
    return pl.BlockSpec(memory_space=pltpu.HBM)


def in_hbm(*arrays):
    return [pltpu.with_memory_space_constraint(x, pltpu.HBM) for x in arrays]


def params(mebibytes):
    return pltpu.CompilerParams(vmem_limit_bytes=mebibytes * 1024 * 1024)


def core_index():
    return lax.axis_index("st")


def is_forward_first():
    return 2 * lax.axis_index("per") < lax.axis_size("per")


def tiles(width):
    return [slice(q, q + LANES) for q in range(0, width, LANES)]


def fetch(pairs, sems):
    copies = [pltpu.make_async_copy(src, dst, sems.at[i]) for i, (src, dst) in enumerate(pairs)]
    for copy in copies:
        copy.start()
    for copy in copies:
        copy.wait()


def pack_kernel(
    count_ref, earn_any, start_any, len_any, init_any, mean_any, sd_any, out_ref, vec_ref,
    earn_ref, start_ref, len_ref, init_ref, mean_ref, sd_ref, sems,
):
    fetch(
        (
            (earn_any, earn_ref), (start_any, start_ref), (len_any, len_ref),
            (init_any, init_ref), (mean_any, mean_ref), (sd_any, sd_ref),
        ),
        sems,
    )
    periods, slot_rows = earn_ref.shape
    core = core_index()
    low_lane = lax.broadcasted_iota(jnp.int32, (periods // 2, HB), 1) < HALF
    time = lax.broadcasted_iota(jnp.int32, (periods, HB), 0)
    for slot in range(slot_rows // HB):
        cols = slice(slot * HB, (slot + 1) * HB)
        begin = start_ref[slot : slot + 1, :]
        seen = (time >= begin) & (time < begin + len_ref[slot : slot + 1, :])
        live = slot < count_ref[0]
        shift = jnp.where(live, jnp.where(seen, SEEN, 0.0), -SEEN)
        value = earn_ref[:, cols] + shift
        early, late = value[: periods // 2], value[periods // 2 :]
        turned = pltpu.roll(jnp.where(core == 0, late, early), HALF, 1)
        packed = jnp.where(low_lane, jnp.where(core == 0, early, turned), jnp.where(core == 0, turned, late))
        for to in range(out_ref.shape[0]):
            out_ref[to, :, cols] = packed
    raised = jnp.exp(init_ref[...])
    start = raised / jnp.sum(raised, axis=1, keepdims=True)
    row = lax.broadcasted_iota(jnp.int32, vec_ref.shape, 0)
    power = (-0.5 * LOG2E) * jnp.exp(-2.0 * sd_ref[...])
    vec_ref[...] = jnp.where(
        row == 0, start, jnp.where(row == 1, mean_ref[...], jnp.where(row == 2, power, -LOG2E * sd_ref[...]))
    )


def put(ref, at, value):
    states = value.shape[0]
    high = value.astype(BF16)
    ref[at, :states, :states] = high
    ref[at, :states, states:] = (value - high.astype(F32)).astype(BF16)


def both_halves(mat, state):
    states = mat.shape[0]
    high = jnp.dot(mat[:, :states], state, preferred_element_type=F32)
    return high + jnp.dot(mat[:, states:], state, preferred_element_type=F32)


def prep_kernel(
    own_any, other_any, vec_ref, first_mat, second_any, row_probs, consts,
    second_mat, scratch, own_ref, other_ref, sems, out_sems,
):
    copies = [
        pltpu.make_async_copy(src, dst, sems.at[i])
        for i, (src, dst) in enumerate(((own_any, own_ref), (other_any, other_ref)))
    ]
    for copy in copies:
        copy.start()
    part, states, _ = own_ref.shape

    def leave(at):
        return pltpu.make_async_copy(second_mat.at[at], second_any.at[at], out_sems.at[at])

    rows = row_probs.shape[1]
    for i in range(4):
        consts[i] = jnp.broadcast_to(vec_ref[i : i + 1, :], (LANES, states)).T
    for copy, source, ref in zip(copies, (core_index(), 1 - core_index()), (own_ref, other_ref)):
        copy.wait()

        @pl.loop(0, part)
        def _(i):
            at = source * part + i
            lifted = jnp.exp(ref[i].astype(F32))
            probs = lifted * (1.0 / jnp.sum(lifted, axis=1, keepdims=True))
            scratch[...] = probs
            row_probs[at] = scratch[own_rows(lax.axis_index("hh") * rows, rows), :]

            @pl.when(is_forward_first())
            def _():
                put(first_mat, at, probs.T)
                put(second_mat, at, probs)

            @pl.when(jnp.logical_not(is_forward_first()))
            def _():
                put(first_mat, at, probs)
                put(second_mat, at, probs.T)

            leave(at).start()

    for at in range(2 * part):
        leave(at).wait()


def emission(sel_ref, consts, step_now, cols, less=None):
    gap = sel_ref[0, step_now, :1, cols] - consts[1]
    power = gap * gap * consts[2] + consts[3]
    return jnp.exp2(power if less is None else power - less)


def is_moving(sel_ref, step_now, cols):
    return sel_ref[1, step_now, :1, cols] > 0.5


def is_seen(sel_ref, step_now, cols):
    return sel_ref[2, step_now, :1, cols] > 0.5


def column_sum(x):
    return jnp.sum(x, axis=0, keepdims=True)


def own_rows(row_begin, rows):
    return pl.ds(pl.multiple_of(row_begin, rows), rows)


def outer_sum(weights_ref, carried):
    return lax.dot_general(weights_ref[...], carried, (((1,), (1,)), ((), ())), preferred_element_type=F32)


def run_forward(lead, mat, hist, sel_ref, consts, ab_ref, logs, second=None):
    steps, states, width = hist.shape
    cuts = tiles(width)
    inverse = [1.0 / column_sum(ab_ref[:, cols].astype(F32)) for cols in cuts]
    for k in range(steps):
        step_now = lead + k
        if second is None:
            hist[k] = ab_ref[...]
        else:
            weights_ref, row_begin, add_counts = second
            own_alpha = ab_ref[own_rows(row_begin, weights_ref.shape[0]), :].astype(F32)
        for q, cols in enumerate(cuts):
            moved = both_halves(mat[k], ab_ref[:, cols]) * inverse[q]
            moving = is_moving(sel_ref, step_now, cols)
            if second is not None:
                total = column_sum(moved * hist[k, :, cols].astype(F32))
                weight = jnp.where(moving, 1.0 / total, 0.0)
                weights_ref[:, cols] = (own_alpha[:, cols] * inverse[q] * weight).astype(BF16)
            emit = emission(sel_ref, consts, step_now, cols)
            joint = jnp.where(moving, moved, consts[0]) * emit
            scale = column_sum(joint)
            if second is None:
                seen = is_seen(sel_ref, step_now, cols)
                logs[q] = logs[q] + jnp.where(seen, jnp.log2(scale), 0.0)
            inverse[q] = 1.0 / scale
            ab_ref[:, cols] = joint.astype(BF16)
        if second is not None:
            add_counts(k, outer_sum(weights_ref, hist[k]))
    return logs


def run_backward(lead, mat, hist, sel_ref, consts, state, ub_ref, logs, leave, second=None, between=None):
    steps, states, width = hist.shape
    cuts = tiles(width)
    rest = [x[:1] for x in state]
    size = [jnp.zeros((1, LANES), F32) for _ in cuts]

    def step(k):
        step_now = lead + k
        grown = []
        for q, cols in enumerate(cuts):
            emit = emission(sel_ref, consts, step_now, cols, size[q] if second is None else None)
            carried = emit * state[q]
            ub_ref[:, cols] = carried.astype(BF16)
            whole = column_sum(carried)
            grown.append(whole)
            if second is None:
                size[q] = jnp.log2(whole)
                seen = is_seen(sel_ref, step_now, cols)
                logs[q] = logs[q] + jnp.where(seen, size[q], 0.0)
                begun = column_sum(carried * consts[0]) / whole
                rest[q] = jnp.where(seen, begun, rest[q])
        if second is None:
            hist[k] = ub_ref[...]
        else:
            weights_ref, row_begin, add_counts = second
            own_alpha = hist[k, own_rows(row_begin, weights_ref.shape[0]), :].astype(F32)
        for q, cols in enumerate(cuts):
            product = both_halves(mat[k], ub_ref[:, cols])
            moving = is_moving(sel_ref, step_now, cols)
            if second is None:
                state[q] = jnp.where(moving, product, rest[q] * grown[q])
            else:
                shrink = 1.0 / grown[q]
                product = product * shrink
                total = column_sum(product * hist[k, :, cols].astype(F32))
                weight = jnp.where(moving, 1.0 / total, 0.0)
                weights_ref[:, cols] = (own_alpha[:, cols] * weight * shrink).astype(BF16)
                state[q] = jnp.where(moving, product, rest[q])
        if second is not None:
            add_counts(k, outer_sum(weights_ref, ub_ref[...]))

    def left():
        return [x * jnp.exp2(-y) for x, y in zip(state, size)]

    for k in reversed(range(1, steps)):
        step(k)
    if second is None:
        step(0)
        leave(left())
        return
    between()

    @pl.when(lead > 0)
    def _():
        step(0)
        leave(left())

    @pl.when(lead == 0)
    def _():
        second[2](0, jnp.zeros((second[0].shape[0], states), F32))


def put_state(state_out, values, logs):
    states = state_out.shape[0] - EXTRA
    row = lax.broadcasted_iota(jnp.int32, (EXTRA, LANES), 0)
    for q, cols in enumerate(tiles(state_out.shape[1])):
        state_out[:states, cols] = values[q].astype(BF16)
        high = logs[q].astype(BF16).astype(F32)
        middle = (logs[q] - high).astype(BF16).astype(F32)
        piece = jnp.where(
            row == 0, high, jnp.where(row == 1, middle, jnp.where(row == 2, logs[q] - high - middle, 0.0))
        )
        state_out[states:, cols] = piece.astype(BF16)


def state_logs(state_ref):
    states = state_ref.shape[0] - EXTRA
    return [column_sum(state_ref[states:, cols].astype(F32)) for cols in tiles(state_ref.shape[1])]


def first_kernel(resume, grids, part, rows_ref, mat, consts, *refs):
    state_in = refs[0] if resume else None
    hist, state_out, sel_ref, ab_ref = refs[-4:]
    chunk = part * grids + (pl.program_id(0) if grids > 1 else 0)
    steps, states, width = hist.shape
    forward_first, lead = is_forward_first(), lax.axis_index("per") * steps
    cuts = tiles(width)
    group, half_periods, slot_rows = rows_ref.shape
    tops = 2 * len(cuts)

    def scan_source(d, carry):
        rank, picked = carry
        for slot in range(slot_rows // HB):
            cols = slice(slot * HB, (slot + 1) * HB)
            block = rows_ref[d, :, cols]
            live = block > -0.5 * SEEN
            picked = [jnp.where(live & (rank == chunk * tops + i), block, old) for i, old in enumerate(picked)]
            rank = rank + live.astype(jnp.int32)
        return rank, picked

    carry = (jnp.zeros((half_periods, HB), jnp.int32), [jnp.zeros((half_periods, HB), F32)] * tops)
    if group <= 8:
        for d in range(group):
            carry = scan_source(d, carry)
    else:
        carry = lax.fori_loop(0, group, scan_source, carry)
    low_lane = lax.broadcasted_iota(jnp.int32, (half_periods, HB), 1) < HALF
    for q, cols in enumerate(cuts):
        left, right = carry[1][2 * q], carry[1][2 * q + 1]
        before = jnp.zeros((1, HB), F32)
        for late in range(2):
            value = (
                jnp.where(low_lane, pltpu.roll(left, HALF, 1), right)
                if late
                else jnp.where(low_lane, left, pltpu.roll(right, HALF, 1))
            )
            seen = value > 0.5 * SEEN
            earn = jnp.where(seen, value - SEEN, value)
            seen = seen.astype(F32)
            for i in range(half_periods):
                at = late * half_periods + i
                now = seen[i : i + 1]
                sel_ref[0, at, :, cols] = jnp.broadcast_to(earn[i : i + 1], (8, HB))
                sel_ref[1, at, :, cols] = jnp.broadcast_to(now * before, (8, HB))
                sel_ref[2, at, :, cols] = jnp.broadcast_to(now, (8, HB))
                before = now
    zeros = [jnp.zeros((1, LANES), F32) for _ in cuts]

    @pl.when(forward_first)
    def _():
        if resume:
            ab_ref[...] = state_in[:states, :]
        else:
            for cols in cuts:
                ab_ref[:, cols] = consts[0].astype(BF16)
        logs = state_logs(state_in) if resume else list(zeros)
        run_forward(lead, mat, hist, sel_ref, consts, ab_ref, logs)
        put_state(state_out, [ab_ref[:, cols] for cols in cuts], logs)

    @pl.when(jnp.logical_not(forward_first))
    def _():
        state = [
            state_in[:states, cols].astype(F32) if resume else jnp.ones((states, LANES), F32) for cols in cuts
        ]
        logs = state_logs(state_in) if resume else list(zeros)
        leave = lambda values: put_state(state_out, values, logs)
        run_backward(lead, mat, hist, sel_ref, consts, state, ab_ref, logs, leave)


def second_kernel(resume, last, extend, grids, *refs):
    refs = list(refs)
    sel_ref, mat, consts, hist, own_state, state_in = (refs.pop(0) for _ in range(6))
    counts_in, sums_in = (refs.pop(0), refs.pop(0)) if resume else (None, None)
    row_probs = refs.pop(0) if last else None
    mine_ref, other_ref = (refs.pop(0), refs.pop(0)) if last else (None, None)
    counts_out, sums_out = (None, None) if last else (refs.pop(0), refs.pop(0))
    state_out = refs.pop(0) if extend else None
    ab_ref, weights_ref = refs[:2]
    counts_ref, sums_ref = refs[2:] if last else (counts_out, sums_out)
    chunk = pl.program_id(0) if grids > 1 else 0
    steps, states, width = hist.shape
    core, forward_first = core_index(), is_forward_first()
    row_begin = lax.axis_index("hh") * weights_ref.shape[0]
    lead = lax.axis_index("per") * steps
    rows = weights_ref.shape[0]

    def centre(k, counts):
        probs = row_probs[k]
        weighted = probs * counts
        grad = weighted - probs * jnp.sum(weighted, axis=1, keepdims=True)
        at = slice(k * rows, (k + 1) * rows)
        left, right = grad[:, :LANES], grad[:, LANES:]
        mine_ref[at, :] = jnp.where(core == 0, left, right)
        other_ref[at, :] = jnp.where(core == 0, right, left)

    def add_counts(k, counts):
        if grids > 1:
            counts_ref[k] += counts
            return
        if resume:
            counts = counts + counts_in[k]
        if last:
            centre(k, counts)
        else:
            counts_ref[k] = counts

    second = (weights_ref, row_begin, add_counts)

    @pl.when(chunk == 0)
    def _():
        if grids > 1:
            counts_ref[...] = jnp.zeros_like(counts_ref)
        sums_ref[...] = sums_in[...] if resume else jnp.zeros_like(sums_ref)

    def add_sums(alpha_ref, other_state):
        total = jnp.zeros((1, LANES), F32)
        years = jnp.zeros((8, LANES), F32)
        for cols, here, there in zip(tiles(width), state_logs(alpha_ref), state_logs(other_state)):
            alpha = alpha_ref[:states, cols].astype(F32)
            meet = column_sum(alpha * other_state[:states, cols].astype(F32))
            total += (here + there + jnp.log2(meet / column_sum(alpha))) * LN2
            years += jnp.sum(sel_ref[2, :, :, cols], axis=0)
        total = jnp.broadcast_to(jnp.sum(total, axis=1, keepdims=True), (1, LANES))
        years = jnp.broadcast_to(jnp.sum(years[:1], axis=1, keepdims=True), (1, LANES))
        row = lax.broadcasted_iota(jnp.int32, (8, LANES), 0)
        sums_ref[...] += jnp.where(row == 0, total, jnp.where(row == 1, years, 0.0))

    zeros = [jnp.zeros((1, LANES), F32) for _ in tiles(width)]

    @pl.when(jnp.logical_not(forward_first))
    def _():
        ab_ref[...] = state_in[:states, :]
        run_forward(lead, mat, hist, sel_ref, consts, ab_ref, list(zeros), second)
        add_sums(state_in, own_state)
        if extend:
            put_state(state_out, [ab_ref[:, cols] for cols in tiles(width)], zeros)

    @pl.when(forward_first)
    def _():
        state = [state_in[:states, cols].astype(F32) for cols in tiles(width)]
        leave = lambda values: put_state(state_out, values, zeros) if extend else None
        run_backward(lead, mat, hist, sel_ref, consts, state, ab_ref, list(zeros), leave, second, lambda: add_sums(own_state, state_in))

    if last:

        @pl.when(chunk == grids - 1)
        def _():
            if grids > 1:
                for k in range(steps):
                    centre(k, counts_ref[k])
            mine_ref[steps * rows :, :] = sums_ref[...]
            other_ref[steps * rows :, :] = sums_ref[...]


def finish_kernel(scale, mine_ref, other_ref, grad_ref, mean_ref):
    count = grad_ref.shape[0]
    total = mine_ref[count : count + 1, :] + other_ref[count : count + 1, :]
    years = mine_ref[count + 1 : count + 2, :] + other_ref[count + 1 : count + 2, :]
    grad_ref[...] = (mine_ref[:count, :] + other_ref[:count, :]) * (scale / years)
    mean_ref[0] = (total / years)[0, 0]


def per_device(
    earnings, starts, lengths, block_count, trans_logits, init_logits, state_mean, log_sd
):
    slot_rows, periods = earnings.shape
    states = init_logits.shape[0]
    group = lax.axis_size(("hh", "per"))
    sides = lax.axis_size("per")
    cores = lax.axis_size("st")
    part = trans_logits.shape[0]
    steps = part * cores
    rows = states // lax.axis_size("hh")
    households = group * HB // cores
    parts = 2 if households <= 4 * HB else 1
    share = households // parts
    width = min(2 * HB, share)
    grids = share // width
    side = lax.axis_index("per")
    shaped = jax.ShapeDtypeStruct
    dma = pltpu.SemaphoreType.DMA

    swap = [(0, 1), (1, 0)]
    vec_row = pltpu.VMEM((1, states), F32)
    packed, vectors = pl.pallas_call(
        pack_kernel,
        out_shape=[
            pltpu.VMEM((group, periods // 2, slot_rows), F32),
            pltpu.VMEM((8, states), F32),
        ],
        in_specs=[smem()] + [hbm()] * 6,
        out_specs=[vmem()] * 2,
        scratch_shapes=[
            pltpu.VMEM((periods, slot_rows), F32),
            pltpu.VMEM((slot_rows // HB, HB), jnp.int32),
            pltpu.VMEM((slot_rows // HB, HB), jnp.int32),
            vec_row,
            vec_row,
            vec_row,
            dma((6,)),
        ],
        compiler_params=params(2),
        name="pack",
    )(
        block_count,
        *in_hbm(
            earnings.T, starts.reshape(-1, HB), lengths.reshape(-1, HB),
            init_logits.reshape(1, states), state_mean.reshape(1, states), log_sd.reshape(1, states),
        ),
    )
    packed, later_logits = lax.optimization_barrier((packed, trans_logits))
    other_logits = lax.ppermute(later_logits, "st", swap)
    downward = [[n * cores + c for n in reversed(range(group))] for c in range(cores)]
    gathered = lax.all_to_all(
        packed, ("hh", "per", "st"), split_axis=0, concat_axis=0, axis_index_groups=downward, tiled=True
    )
    first_mat, second_mat, row_probs, consts = pl.pallas_call(
        prep_kernel,
        out_shape=[
            pltpu.VMEM((steps, states, 2 * states), BF16),
            pltpu.HBM((steps, states, 2 * states), BF16),
            pltpu.VMEM((steps, rows, states), F32),
            pltpu.VMEM((4, states, LANES), F32),
        ],
        in_specs=[hbm(), hbm(), vmem()],
        out_specs=[vmem(), hbm(), vmem(), vmem()],
        scratch_shapes=[
            pltpu.VMEM((steps, states, 2 * states), BF16),
            pltpu.VMEM((states, states), F32),
            pltpu.VMEM(trans_logits.shape, BF16),
            pltpu.VMEM(trans_logits.shape, BF16),
            dma((2,)),
            dma((steps,)),
        ],
        compiler_params=params(6),
        name="prep",
    )(*in_hbm(trans_logits, other_logits), vectors)

    def whole(*shape):
        if grids == 1:
            return vmem()
        return pl.BlockSpec(shape, lambda g: (0,) * len(shape))

    def lanes(*lead):
        if grids == 1:
            return vmem()
        return pl.BlockSpec(lead + (width,), lambda g: (0,) * len(lead) + (g,))

    grid = (grids,) if grids > 1 else ()
    hist_shape = shaped((steps, states, share), BF16)
    state_shape = shaped((states + EXTRA, share), BF16)
    sel_shape = shaped((3, periods, 8, share), F32)
    swap_shape = shaped((steps * rows + 8, LANES), F32)
    counts_shape = shaped((steps, rows, states), F32)
    sums_shape = shaped((8, LANES), F32)
    hist_spec, state_spec, sel_spec = lanes(steps, states), lanes(states + EXTRA), lanes(3, periods, 8)
    const_spec = whole(4, states, LANES)

    def first_pass(index, state_in):
        resume = state_in is not None
        return pl.pallas_call(
            functools.partial(first_kernel, resume, grids, index),
            grid=grid,
            out_shape=[hist_shape, state_shape, sel_shape],
            in_specs=[whole(*gathered.shape), whole(*first_mat.shape), const_spec]
            + [state_spec] * resume,
            out_specs=[hist_spec, state_spec, sel_spec],
            scratch_shapes=[pltpu.VMEM((states, width), BF16)],
            compiler_params=params(8 if grids == 1 else 32),
            name="first_pass",
        )(gathered, first_mat, consts, *([state_in] if resume else []))

    def second_pass(kept, state_in, sums_in, last, extend):
        hist, own_state, sel = kept
        resume = sums_in is not None
        scratch = [
            pltpu.VMEM((states, width), BF16),
            pltpu.VMEM((rows, width), BF16),
        ]
        counts_spec, sums_spec = whole(*counts_shape.shape), whole(*sums_shape.shape)
        if last:
            out_shape = [swap_shape] * 2
            scratch += [pltpu.VMEM(counts_shape.shape, F32), pltpu.VMEM(sums_shape.shape, F32)]
        else:
            out_shape = [counts_shape, sums_shape]
        out_specs = [whole(*x.shape) for x in out_shape]
        if extend:
            out_shape, out_specs = out_shape + [state_shape], out_specs + [state_spec]
        return pl.pallas_call(
            functools.partial(second_kernel, resume, last, extend, grids),
            grid=grid,
            out_shape=out_shape,
            in_specs=[sel_spec, whole(*second_mat.shape), const_spec, hist_spec, state_spec, state_spec]
            + [counts_spec, sums_spec] * resume
            + [whole(*row_probs.shape)] * last,
            out_specs=out_specs,
            scratch_shapes=scratch,
            compiler_params=params(8 if grids == 1 else 32),
            name="second_pass",
        )(
            sel, second_mat, consts, hist, own_state, state_in,
            *(sums_in if resume else []),
            *([row_probs] if last else []),
        )

    def hand_over(state, stage):
        moves = [(stage, stage + 1), (sides - 1 - stage, sides - 2 - stage)]
        return lax.ppermute(state, "per", moves)

    if sides == 2:
        kept = [first_pass(index, None) for index in range(parts)]
        arrived = [hand_over(each[1], 0) for each in kept]
        sums = None
        for index in range(parts):
            sums = second_pass(kept[index], arrived[index], sums, index == parts - 1, False)
        mine, other = sums
    else:
        kept = [jnp.zeros(x.shape, x.dtype) for x in (hist_shape, state_shape, sel_shape)]
        done = [jnp.zeros(x.shape, x.dtype) for x in (swap_shape, swap_shape, state_shape)]
        state = None
        for stage in range(sides):
            active = (side == stage) | (side == sides - 1 - stage)
            if stage < sides // 2:
                kept = lax.cond(
                    active, lambda x, kept: list(first_pass(0, x)), lambda x, kept: kept, state, kept
                )
                state = kept[1]
            else:
                done = lax.cond(
                    active,
                    lambda x, done: list(second_pass(kept, x, None, True, True)),
                    lambda x, done: done,
                    state,
                    done,
                )
                state = done[2]
            if stage < sides - 1:
                state = hand_over(state, stage)
        mine, other, _ = done
        total = jnp.where(side == sides // 2, mine[steps * rows], 0.0)
        total = lax.psum(total, "per")
        mine = mine.at[steps * rows].set(total)
        other = other.at[steps * rows].set(total)
    received = lax.ppermute(other, "st", swap)
    trans_grad, mean_loglik = pl.pallas_call(
        functools.partial(finish_kernel, float(states * states * periods)),
        out_shape=[shaped((steps * rows, LANES), F32), shaped((1,), F32)],
        in_specs=[vmem(), vmem()],
        out_specs=[vmem(), smem()],
        compiler_params=params(4),
        name="finish",
    )(mine, received)
    return (trans_grad.reshape(steps, rows, LANES), mean_loglik)


def solution(mesh):
    placed = (
        P(("hh", "per"), None),
        P(("hh", "per")),
        P(("hh", "per")),
        P(("hh", "per")),
        P(("grp", "per", "st"), None, None),
        P("grp"),
        P("grp"),
        P("grp"),
    )
    return jax.shard_map(
        per_device,
        mesh=mesh,
        in_specs=placed,
        out_specs=(P(("grp", "per"), "hh", "st"), P("grp")),
        check_vma=False,
    )
```

```python
import functools

import jax
import jax.numpy as jnp
from jax import lax
from jax.experimental import pallas as pl
from jax.experimental.pallas import tpu as pltpu
from jax.sharding import PartitionSpec as P

HB = 128
LANES = 128
HALF = HB // 2
SEEN = 16.0
F32 = jnp.float32
BF16 = jnp.bfloat16
LOG2E = 1.4426950408889634
LN2 = 0.6931471805599453
EXTRA = 16


def vmem():
    return pl.BlockSpec(memory_space=pltpu.VMEM)


def smem():
    return pl.BlockSpec(memory_space=pltpu.SMEM)


def hbm():
    return pl.BlockSpec(memory_space=pltpu.HBM)


def in_hbm(*arrays):
    return [pltpu.with_memory_space_constraint(x, pltpu.HBM) for x in arrays]


def params(mebibytes):
    return pltpu.CompilerParams(vmem_limit_bytes=mebibytes * 1024 * 1024)


def core_index():
    return lax.axis_index("st")


def is_forward_first():
    return 2 * lax.axis_index("per") < lax.axis_size("per")


def tiles(width):
    return [slice(q, q + LANES) for q in range(0, width, LANES)]


def fetch(pairs, sems):
    copies = [pltpu.make_async_copy(src, dst, sems.at[i]) for i, (src, dst) in enumerate(pairs)]
    for copy in copies:
        copy.start()
    for copy in copies:
        copy.wait()


def pack_kernel(
    count_ref, earn_any, start_any, len_any, init_any, mean_any, sd_any, out_ref, vec_ref,
    earn_ref, start_ref, len_ref, init_ref, mean_ref, sd_ref, sems,
):
    fetch(
        (
            (earn_any, earn_ref), (start_any, start_ref), (len_any, len_ref),
            (init_any, init_ref), (mean_any, mean_ref), (sd_any, sd_ref),
        ),
        sems,
    )
    periods, slot_rows = earn_ref.shape
    core = core_index()
    low_lane = lax.broadcasted_iota(jnp.int32, (periods // 2, HB), 1) < HALF
    time = lax.broadcasted_iota(jnp.int32, (periods, HB), 0)
    for slot in range(slot_rows // HB):
        cols = slice(slot * HB, (slot + 1) * HB)
        begin = start_ref[slot : slot + 1, :]
        seen = (time >= begin) & (time < begin + len_ref[slot : slot + 1, :])
        live = slot < count_ref[0]
        shift = jnp.where(live, jnp.where(seen, SEEN, 0.0), -SEEN)
        value = earn_ref[:, cols] + shift
        early, late = value[: periods // 2], value[periods // 2 :]
        turned = pltpu.roll(jnp.where(core == 0, late, early), HALF, 1)
        packed = jnp.where(low_lane, jnp.where(core == 0, early, turned), jnp.where(core == 0, turned, late))
        for to in range(out_ref.shape[0]):
            out_ref[to, :, cols] = packed
    raised = jnp.exp(init_ref[...])
    start = raised / jnp.sum(raised, axis=1, keepdims=True)
    row = lax.broadcasted_iota(jnp.int32, vec_ref.shape, 0)
    power = (-0.5 * LOG2E) * jnp.exp(-2.0 * sd_ref[...])
    vec_ref[...] = jnp.where(
        row == 0, start, jnp.where(row == 1, mean_ref[...], jnp.where(row == 2, power, -LOG2E * sd_ref[...]))
    )


def put(ref, at, value):
    states = value.shape[0]
    high = value.astype(BF16)
    ref[at, :states, :states] = high
    ref[at, :states, states:] = (value - high.astype(F32)).astype(BF16)


def both_halves(mat, state):
    states = mat.shape[0]
    high = jnp.dot(mat[:, :states], state, preferred_element_type=F32)
    return high + jnp.dot(mat[:, states:], state, preferred_element_type=F32)


def fill_periods(mat, row_probs, scratch, turned_pass, source, ref):
    @pl.loop(0, ref.shape[0])
    def _(i):
        at = source * ref.shape[0] + i
        lifted = jnp.exp(ref[i].astype(F32))
        probs = lifted * (1.0 / jnp.sum(lifted, axis=1, keepdims=True))
        if row_probs is not None:
            rows = row_probs.shape[1]
            scratch[...] = probs
            row_probs[at] = scratch[own_rows(lax.axis_index("hh") * rows, rows), :]

        @pl.when(turned_pass)
        def _():
            put(mat, at, probs.T)

        @pl.when(jnp.logical_not(turned_pass))
        def _():
            put(mat, at, probs)


def prep_first_kernel(own_any, other_any, vec_ref, mat, consts, own_ref, other_ref, sems):
    copies = [
        pltpu.make_async_copy(src, dst, sems.at[i])
        for i, (src, dst) in enumerate(((own_any, own_ref), (other_any, other_ref)))
    ]
    for copy in copies:
        copy.start()
    for i in range(4):
        consts[i] = jnp.broadcast_to(vec_ref[i : i + 1, :], (LANES, own_ref.shape[1])).T
    for copy, source, ref in zip(copies, (core_index(), 1 - core_index()), (own_ref, other_ref)):
        copy.wait()
        fill_periods(mat, None, None, is_forward_first(), source, ref)


def prep_second_kernel(own_ref, other_ref, after_any, mat, row_probs, scratch):
    for source, ref in ((core_index(), own_ref), (1 - core_index(), other_ref)):
        fill_periods(mat, row_probs, scratch, jnp.logical_not(is_forward_first()), source, ref)


def emission(sel_ref, consts, step_now, cols, less=None):
    gap = sel_ref[0, step_now, :1, cols] - consts[1]
    power = gap * gap * consts[2] + consts[3]
    return jnp.exp2(power if less is None else power - less)


def is_moving(sel_ref, step_now, cols):
    return sel_ref[1, step_now, :1, cols] > 0.5


def is_seen(sel_ref, step_now, cols):
    return sel_ref[2, step_now, :1, cols] > 0.5


def column_sum(x):
    return jnp.sum(x, axis=0, keepdims=True)


def own_rows(row_begin, rows):
    return pl.ds(pl.multiple_of(row_begin, rows), rows)


def outer_sum(weights_ref, carried):
    return lax.dot_general(weights_ref[...], carried, (((1,), (1,)), ((), ())), preferred_element_type=F32)


def run_forward(lead, mat, hist, sel_ref, consts, ab_ref, logs, second=None):
    steps, states, width = hist.shape
    cuts = tiles(width)
    inverse = [1.0 / column_sum(ab_ref[:, cols].astype(F32)) for cols in cuts]
    for k in range(steps):
        step_now = lead + k
        if second is None:
            hist[k] = ab_ref[...]
        else:
            weights_ref, row_begin, add_counts = second
            own_alpha = ab_ref[own_rows(row_begin, weights_ref.shape[0]), :].astype(F32)
        for q, cols in enumerate(cuts):
            moved = both_halves(mat[k], ab_ref[:, cols]) * inverse[q]
            moving = is_moving(sel_ref, step_now, cols)
            if second is not None:
                total = column_sum(moved * hist[k, :, cols].astype(F32))
                weight = jnp.where(moving, 1.0 / total, 0.0)
                weights_ref[:, cols] = (own_alpha[:, cols] * inverse[q] * weight).astype(BF16)
            emit = emission(sel_ref, consts, step_now, cols)
            joint = jnp.where(moving, moved, consts[0]) * emit
            scale = column_sum(joint)
            if second is None:
                seen = is_seen(sel_ref, step_now, cols)
                logs[q] = logs[q] + jnp.where(seen, jnp.log2(scale), 0.0)
            inverse[q] = 1.0 / scale
            ab_ref[:, cols] = joint.astype(BF16)
        if second is not None:
            add_counts(k, outer_sum(weights_ref, hist[k]))
    return logs


def run_backward(lead, mat, hist, sel_ref, consts, state, ub_ref, logs, leave, second=None, between=None):
    steps, states, width = hist.shape
    cuts = tiles(width)
    rest = [x[:1] for x in state]
    size = [jnp.zeros((1, LANES), F32) for _ in cuts]

    def step(k):
        step_now = lead + k
        grown = []
        for q, cols in enumerate(cuts):
            emit = emission(sel_ref, consts, step_now, cols, size[q] if second is None else None)
            carried = emit * state[q]
            ub_ref[:, cols] = carried.astype(BF16)
            whole = column_sum(carried)
            grown.append(whole)
            if second is None:
                size[q] = jnp.log2(whole)
                seen = is_seen(sel_ref, step_now, cols)
                logs[q] = logs[q] + jnp.where(seen, size[q], 0.0)
                begun = column_sum(carried * consts[0]) / whole
                rest[q] = jnp.where(seen, begun, rest[q])
        if second is None:
            hist[k] = ub_ref[...]
        else:
            weights_ref, row_begin, add_counts = second
            own_alpha = hist[k, own_rows(row_begin, weights_ref.shape[0]), :].astype(F32)
        for q, cols in enumerate(cuts):
            product = both_halves(mat[k], ub_ref[:, cols])
            moving = is_moving(sel_ref, step_now, cols)
            if second is None:
                state[q] = jnp.where(moving, product, rest[q] * grown[q])
            else:
                shrink = 1.0 / grown[q]
                product = product * shrink
                total = column_sum(product * hist[k, :, cols].astype(F32))
                weight = jnp.where(moving, 1.0 / total, 0.0)
                weights_ref[:, cols] = (own_alpha[:, cols] * weight * shrink).astype(BF16)
                state[q] = jnp.where(moving, product, rest[q])
        if second is not None:
            add_counts(k, outer_sum(weights_ref, ub_ref[...]))

    def left():
        return [x * jnp.exp2(-y) for x, y in zip(state, size)]

    for k in reversed(range(1, steps)):
        step(k)
    if second is None:
        step(0)
        leave(left())
        return
    between()

    @pl.when(lead > 0)
    def _():
        step(0)
        leave(left())

    @pl.when(lead == 0)
    def _():
        second[2](0, jnp.zeros((second[0].shape[0], states), F32))


def put_state(state_out, values, logs):
    states = state_out.shape[0] - EXTRA
    row = lax.broadcasted_iota(jnp.int32, (EXTRA, LANES), 0)
    for q, cols in enumerate(tiles(state_out.shape[1])):
        state_out[:states, cols] = values[q].astype(BF16)
        high = logs[q].astype(BF16).astype(F32)
        middle = (logs[q] - high).astype(BF16).astype(F32)
        piece = jnp.where(
            row == 0, high, jnp.where(row == 1, middle, jnp.where(row == 2, logs[q] - high - middle, 0.0))
        )
        state_out[states:, cols] = piece.astype(BF16)


def state_logs(state_ref):
    states = state_ref.shape[0] - EXTRA
    return [column_sum(state_ref[states:, cols].astype(F32)) for cols in tiles(state_ref.shape[1])]


def first_kernel(resume, grids, part, rows_ref, mat, consts, *refs):
    state_in = refs[0] if resume else None
    hist, state_out, sel_ref, ab_ref = refs[-4:]
    chunk = part * grids + (pl.program_id(0) if grids > 1 else 0)
    steps, states, width = hist.shape
    forward_first, lead = is_forward_first(), lax.axis_index("per") * steps
    cuts = tiles(width)
    group, half_periods, slot_rows = rows_ref.shape
    tops = 2 * len(cuts)

    def scan_source(d, carry):
        rank, picked = carry
        for slot in range(slot_rows // HB):
            cols = slice(slot * HB, (slot + 1) * HB)
            block = rows_ref[d, :, cols]
            live = block > -0.5 * SEEN
            picked = [jnp.where(live & (rank == chunk * tops + i), block, old) for i, old in enumerate(picked)]
            rank = rank + live.astype(jnp.int32)
        return rank, picked

    carry = (jnp.zeros((half_periods, HB), jnp.int32), [jnp.zeros((half_periods, HB), F32)] * tops)
    if group <= 8:
        for d in range(group):
            carry = scan_source(d, carry)
    else:
        carry = lax.fori_loop(0, group, scan_source, carry)
    low_lane = lax.broadcasted_iota(jnp.int32, (half_periods, HB), 1) < HALF
    for q, cols in enumerate(cuts):
        left, right = carry[1][2 * q], carry[1][2 * q + 1]
        before = jnp.zeros((1, HB), F32)
        for late in range(2):
            value = (
                jnp.where(low_lane, pltpu.roll(left, HALF, 1), right)
                if late
                else jnp.where(low_lane, left, pltpu.roll(right, HALF, 1))
            )
            seen = value > 0.5 * SEEN
            earn = jnp.where(seen, value - SEEN, value)
            seen = seen.astype(F32)
            for i in range(half_periods):
                at = late * half_periods + i
                now = seen[i : i + 1]
                sel_ref[0, at, :, cols] = jnp.broadcast_to(earn[i : i + 1], (8, HB))
                sel_ref[1, at, :, cols] = jnp.broadcast_to(now * before, (8, HB))
                sel_ref[2, at, :, cols] = jnp.broadcast_to(now, (8, HB))
                before = now
    zeros = [jnp.zeros((1, LANES), F32) for _ in cuts]

    @pl.when(forward_first)
    def _():
        if resume:
            ab_ref[...] = state_in[:states, :]
        else:
            for cols in cuts:
                ab_ref[:, cols] = consts[0].astype(BF16)
        logs = state_logs(state_in) if resume else list(zeros)
        run_forward(lead, mat, hist, sel_ref, consts, ab_ref, logs)
        put_state(state_out, [ab_ref[:, cols] for cols in cuts], logs)

    @pl.when(jnp.logical_not(forward_first))
    def _():
        state = [
            state_in[:states, cols].astype(F32) if resume else jnp.ones((states, LANES), F32) for cols in cuts
        ]
        logs = state_logs(state_in) if resume else list(zeros)
        leave = lambda values: put_state(state_out, values, logs)
        run_backward(lead, mat, hist, sel_ref, consts, state, ab_ref, logs, leave)


def second_kernel(resume, last, extend, grids, *refs):
    refs = list(refs)
    sel_ref, mat, consts, hist, own_state, state_in = (refs.pop(0) for _ in range(6))
    counts_in, sums_in = (refs.pop(0), refs.pop(0)) if resume else (None, None)
    row_probs = refs.pop(0) if last else None
    mine_ref, other_ref = (refs.pop(0), refs.pop(0)) if last else (None, None)
    counts_out, sums_out = (None, None) if last else (refs.pop(0), refs.pop(0))
    state_out = refs.pop(0) if extend else None
    ab_ref, weights_ref = refs[:2]
    counts_ref, sums_ref = refs[2:] if last else (counts_out, sums_out)
    chunk = pl.program_id(0) if grids > 1 else 0
    steps, states, width = hist.shape
    core, forward_first = core_index(), is_forward_first()
    row_begin = lax.axis_index("hh") * weights_ref.shape[0]
    lead = lax.axis_index("per") * steps
    rows = weights_ref.shape[0]

    def centre(k, counts):
        probs = row_probs[k]
        weighted = probs * counts
        grad = weighted - probs * jnp.sum(weighted, axis=1, keepdims=True)
        at = slice(k * rows, (k + 1) * rows)
        left, right = grad[:, :LANES], grad[:, LANES:]
        mine_ref[at, :] = jnp.where(core == 0, left, right)
        other_ref[at, :] = jnp.where(core == 0, right, left)

    def add_counts(k, counts):
        if grids > 1:
            counts_ref[k] += counts
            return
        if resume:
            counts = counts + counts_in[k]
        if last:
            centre(k, counts)
        else:
            counts_ref[k] = counts

    second = (weights_ref, row_begin, add_counts)

    @pl.when(chunk == 0)
    def _():
        if grids > 1:
            counts_ref[...] = jnp.zeros_like(counts_ref)
        sums_ref[...] = sums_in[...] if resume else jnp.zeros_like(sums_ref)

    def add_sums(alpha_ref, other_state):
        total = jnp.zeros((1, LANES), F32)
        years = jnp.zeros((8, LANES), F32)
        for cols, here, there in zip(tiles(width), state_logs(alpha_ref), state_logs(other_state)):
            alpha = alpha_ref[:states, cols].astype(F32)
            meet = column_sum(alpha * other_state[:states, cols].astype(F32))
            total += (here + there + jnp.log2(meet / column_sum(alpha))) * LN2
            years += jnp.sum(sel_ref[2, :, :, cols], axis=0)
        total = jnp.broadcast_to(jnp.sum(total, axis=1, keepdims=True), (1, LANES))
        years = jnp.broadcast_to(jnp.sum(years[:1], axis=1, keepdims=True), (1, LANES))
        row = lax.broadcasted_iota(jnp.int32, (8, LANES), 0)
        sums_ref[...] += jnp.where(row == 0, total, jnp.where(row == 1, years, 0.0))

    zeros = [jnp.zeros((1, LANES), F32) for _ in tiles(width)]

    @pl.when(jnp.logical_not(forward_first))
    def _():
        ab_ref[...] = state_in[:states, :]
        run_forward(lead, mat, hist, sel_ref, consts, ab_ref, list(zeros), second)
        add_sums(state_in, own_state)
        if extend:
            put_state(state_out, [ab_ref[:, cols] for cols in tiles(width)], zeros)

    @pl.when(forward_first)
    def _():
        state = [state_in[:states, cols].astype(F32) for cols in tiles(width)]
        leave = lambda values: put_state(state_out, values, zeros) if extend else None
        run_backward(lead, mat, hist, sel_ref, consts, state, ab_ref, list(zeros), leave, second, lambda: add_sums(own_state, state_in))

    if last:

        @pl.when(chunk == grids - 1)
        def _():
            if grids > 1:
                for k in range(steps):
                    centre(k, counts_ref[k])
            mine_ref[steps * rows :, :] = sums_ref[...]
            other_ref[steps * rows :, :] = sums_ref[...]


def finish_kernel(scale, mine_ref, other_ref, grad_ref, mean_ref):
    count = grad_ref.shape[0]
    total = mine_ref[count : count + 1, :] + other_ref[count : count + 1, :]
    years = mine_ref[count + 1 : count + 2, :] + other_ref[count + 1 : count + 2, :]
    grad_ref[...] = (mine_ref[:count, :] + other_ref[:count, :]) * (scale / years)
    mean_ref[0] = (total / years)[0, 0]


def per_device(
    earnings, starts, lengths, block_count, trans_logits, init_logits, state_mean, log_sd
):
    slot_rows, periods = earnings.shape
    states = init_logits.shape[0]
    group = lax.axis_size(("hh", "per"))
    sides = lax.axis_size("per")
    cores = lax.axis_size("st")
    part = trans_logits.shape[0]
    steps = part * cores
    rows = states // lax.axis_size("hh")
    households = group * HB // cores
    parts = 2 if households <= 4 * HB else 1
    share = households // parts
    width = min(2 * HB, share)
    grids = share // width
    side = lax.axis_index("per")
    shaped = jax.ShapeDtypeStruct
    dma = pltpu.SemaphoreType.DMA

    swap = [(0, 1), (1, 0)]
    vec_row = pltpu.VMEM((1, states), F32)
    packed, vectors = pl.pallas_call(
        pack_kernel,
        out_shape=[
            pltpu.VMEM((group, periods // 2, slot_rows), F32),
            pltpu.VMEM((8, states), F32),
        ],
        in_specs=[smem()] + [hbm()] * 6,
        out_specs=[vmem()] * 2,
        scratch_shapes=[
            pltpu.VMEM((periods, slot_rows), F32),
            pltpu.VMEM((slot_rows // HB, HB), jnp.int32),
            pltpu.VMEM((slot_rows // HB, HB), jnp.int32),
            vec_row,
            vec_row,
            vec_row,
            dma((6,)),
        ],
        compiler_params=params(2),
        name="pack",
    )(
        block_count,
        *in_hbm(
            earnings.T, starts.reshape(-1, HB), lengths.reshape(-1, HB),
            init_logits.reshape(1, states), state_mean.reshape(1, states), log_sd.reshape(1, states),
        ),
    )
    packed, later_logits = lax.optimization_barrier((packed, trans_logits))
    other_logits = lax.ppermute(later_logits, "st", swap)
    downward = [[n * cores + c for n in reversed(range(group))] for c in range(cores)]
    gathered = lax.all_to_all(
        packed, ("hh", "per", "st"), split_axis=0, concat_axis=0, axis_index_groups=downward, tiled=True
    )
    mat_shape = shaped((steps, states, 2 * states), BF16)
    first_mat, consts = pl.pallas_call(
        prep_first_kernel,
        out_shape=[pltpu.VMEM(mat_shape.shape, BF16), pltpu.VMEM((4, states, LANES), F32)],
        in_specs=[hbm(), hbm(), vmem()],
        out_specs=[vmem(), vmem()],
        scratch_shapes=[pltpu.VMEM(trans_logits.shape, BF16), pltpu.VMEM(trans_logits.shape, BF16), dma((2,))],
        compiler_params=params(4),
        name="prep_first",
    )(*in_hbm(trans_logits, other_logits), vectors)

    def prep_second(after):
        return pl.pallas_call(
            prep_second_kernel,
            out_shape=[mat_shape, shaped((steps, rows, states), F32)],
            in_specs=[vmem(), vmem(), hbm()],
            out_specs=[vmem(), vmem()],
            scratch_shapes=[pltpu.VMEM((states, states), F32)],
            compiler_params=params(4),
            name="prep_second",
        )(trans_logits, other_logits, after)

    def whole(*shape):
        if grids == 1:
            return vmem()
        return pl.BlockSpec(shape, lambda g: (0,) * len(shape))

    def lanes(*lead):
        if grids == 1:
            return vmem()
        return pl.BlockSpec(lead + (width,), lambda g: (0,) * len(lead) + (g,))

    grid = (grids,) if grids > 1 else ()
    hist_shape = shaped((steps, states, share), BF16)
    state_shape = shaped((states + EXTRA, share), BF16)
    sel_shape = shaped((3, periods, 8, share), F32)
    swap_shape = shaped((steps * rows + 8, LANES), F32)
    counts_shape = shaped((steps, rows, states), F32)
    sums_shape = shaped((8, LANES), F32)
    hist_spec, state_spec, sel_spec = lanes(steps, states), lanes(states + EXTRA), lanes(3, periods, 8)
    const_spec = whole(4, states, LANES)

    def first_pass(index, state_in):
        resume = state_in is not None
        return pl.pallas_call(
            functools.partial(first_kernel, resume, grids, index),
            grid=grid,
            out_shape=[hist_shape, state_shape, sel_shape],
            in_specs=[whole(*gathered.shape), whole(*first_mat.shape), const_spec]
            + [state_spec] * resume,
            out_specs=[hist_spec, state_spec, sel_spec],
            scratch_shapes=[pltpu.VMEM((states, width), BF16)],
            compiler_params=params(8 if grids == 1 else 32),
            name="first_pass",
        )(gathered, first_mat, consts, *([state_in] if resume else []))

    def second_pass(kept, state_in, sums_in, last, extend):
        hist, own_state, sel = kept
        resume = sums_in is not None
        scratch = [
            pltpu.VMEM((states, width), BF16),
            pltpu.VMEM((rows, width), BF16),
        ]
        counts_spec, sums_spec = whole(*counts_shape.shape), whole(*sums_shape.shape)
        if last:
            out_shape = [swap_shape] * 2
            scratch += [pltpu.VMEM(counts_shape.shape, F32), pltpu.VMEM(sums_shape.shape, F32)]
        else:
            out_shape = [counts_shape, sums_shape]
        out_specs = [whole(*x.shape) for x in out_shape]
        if extend:
            out_shape, out_specs = out_shape + [state_shape], out_specs + [state_spec]
        return pl.pallas_call(
            functools.partial(second_kernel, resume, last, extend, grids),
            grid=grid,
            out_shape=out_shape,
            in_specs=[sel_spec, whole(*second_mat.shape), const_spec, hist_spec, state_spec, state_spec]
            + [counts_spec, sums_spec] * resume
            + [whole(*row_probs.shape)] * last,
            out_specs=out_specs,
            scratch_shapes=scratch,
            compiler_params=params(8 if grids == 1 else 32),
            name="second_pass",
        )(
            sel, second_mat, consts, hist, own_state, state_in,
            *(sums_in if resume else []),
            *([row_probs] if last else []),
        )

    def hand_over(state, stage):
        moves = [(stage, stage + 1), (sides - 1 - stage, sides - 2 - stage)]
        return lax.ppermute(state, "per", moves)

    if sides == 2:
        kept = [first_pass(index, None) for index in range(parts)]
        arrived = [hand_over(each[1], 0) for each in kept]
        second_mat, row_probs = prep_second(kept[-1][1])
        sums = None
        for index in range(parts):
            sums = second_pass(kept[index], arrived[index], sums, index == parts - 1, False)
        mine, other = sums
    else:
        kept = [jnp.zeros(x.shape, x.dtype) for x in (hist_shape, state_shape, sel_shape)]
        done = [jnp.zeros(x.shape, x.dtype) for x in (swap_shape, swap_shape, state_shape)]
        state = None
        second_mat, row_probs = prep_second(gathered)
        for stage in range(sides):
            active = (side == stage) | (side == sides - 1 - stage)
            if stage < sides // 2:
                kept = lax.cond(
                    active, lambda x, kept: list(first_pass(0, x)), lambda x, kept: kept, state, kept
                )
                state = kept[1]
            else:
                done = lax.cond(
                    active,
                    lambda x, done: list(second_pass(kept, x, None, True, True)),
                    lambda x, done: done,
                    state,
                    done,
                )
                state = done[2]
            if stage < sides - 1:
                state = hand_over(state, stage)
        mine, other, _ = done
        total = jnp.where(side == sides // 2, mine[steps * rows], 0.0)
        total = lax.psum(total, "per")
        mine = mine.at[steps * rows].set(total)
        other = other.at[steps * rows].set(total)
    received = lax.ppermute(other, "st", swap)
    trans_grad, mean_loglik = pl.pallas_call(
        functools.partial(finish_kernel, float(states * states * periods)),
        out_shape=[shaped((steps * rows, LANES), F32), shaped((1,), F32)],
        in_specs=[vmem(), vmem()],
        out_specs=[vmem(), smem()],
        compiler_params=params(4),
        name="finish",
    )(mine, received)
    return (trans_grad.reshape(steps, rows, LANES), mean_loglik)


def solution(mesh):
    placed = (
        P(("hh", "per"), None),
        P(("hh", "per")),
        P(("hh", "per")),
        P(("hh", "per")),
        P(("grp", "per", "st"), None, None),
        P("grp"),
        P("grp"),
        P("grp"),
    )
    return jax.shard_map(
        per_device,
        mesh=mesh,
        in_specs=placed,
        out_specs=(P(("grp", "per"), "hh", "st"), P("grp")),
        check_vma=False,
    )
```

```python
import functools

import jax
import jax.numpy as jnp
from jax import lax
from jax.experimental import pallas as pl
from jax.experimental.pallas import tpu as pltpu
from jax.sharding import PartitionSpec as P

HB = 128
LANES = 128
HALF = HB // 2
SEEN = 16.0
F32 = jnp.float32
BF16 = jnp.bfloat16
LOG2E = 1.4426950408889634
LN2 = 0.6931471805599453
EXTRA = 16


def vmem():
    return pl.BlockSpec(memory_space=pltpu.VMEM)


def smem():
    return pl.BlockSpec(memory_space=pltpu.SMEM)


def hbm():
    return pl.BlockSpec(memory_space=pltpu.HBM)


def in_hbm(*arrays):
    return [pltpu.with_memory_space_constraint(x, pltpu.HBM) for x in arrays]


def params(mebibytes):
    return pltpu.CompilerParams(vmem_limit_bytes=mebibytes * 1024 * 1024)


def core_index():
    return lax.axis_index("st")


def is_forward_first():
    return 2 * lax.axis_index("per") < lax.axis_size("per")


def tiles(width):
    return [slice(q, q + LANES) for q in range(0, width, LANES)]


def fetch(pairs, sems):
    copies = [pltpu.make_async_copy(src, dst, sems.at[i]) for i, (src, dst) in enumerate(pairs)]
    for copy in copies:
        copy.start()
    for copy in copies:
        copy.wait()


def pack_kernel(
    count_ref, earn_any, start_any, len_any, init_any, mean_any, sd_any, out_ref, vec_ref,
    earn_ref, start_ref, len_ref, init_ref, mean_ref, sd_ref, sems,
):
    fetch(
        (
            (earn_any, earn_ref), (start_any, start_ref), (len_any, len_ref),
            (init_any, init_ref), (mean_any, mean_ref), (sd_any, sd_ref),
        ),
        sems,
    )
    periods, slot_rows = earn_ref.shape
    core = core_index()
    low_lane = lax.broadcasted_iota(jnp.int32, (periods // 2, HB), 1) < HALF
    time = lax.broadcasted_iota(jnp.int32, (periods, HB), 0)
    for slot in range(slot_rows // HB):
        cols = slice(slot * HB, (slot + 1) * HB)
        begin = start_ref[slot : slot + 1, :]
        seen = (time >= begin) & (time < begin + len_ref[slot : slot + 1, :])
        live = slot < count_ref[0]
        shift = jnp.where(live, jnp.where(seen, SEEN, 0.0), -SEEN)
        value = earn_ref[:, cols] + shift
        early, late = value[: periods // 2], value[periods // 2 :]
        turned = pltpu.roll(jnp.where(core == 0, late, early), HALF, 1)
        packed = jnp.where(low_lane, jnp.where(core == 0, early, turned), jnp.where(core == 0, turned, late))
        for to in range(out_ref.shape[0]):
            out_ref[to, :, cols] = packed
    raised = jnp.exp(init_ref[...])
    start = raised / jnp.sum(raised, axis=1, keepdims=True)
    row = lax.broadcasted_iota(jnp.int32, vec_ref.shape, 0)
    power = (-0.5 * LOG2E) * jnp.exp(-2.0 * sd_ref[...])
    vec_ref[...] = jnp.where(
        row == 0, start, jnp.where(row == 1, mean_ref[...], jnp.where(row == 2, power, -LOG2E * sd_ref[...]))
    )


def put(ref, at, value):
    states = value.shape[0]
    high = value.astype(BF16)
    ref[at, :states, :states] = high
    ref[at, :states, states:] = (value - high.astype(F32)).astype(BF16)


def both_halves(mat, state):
    states = mat.shape[0]
    high = jnp.dot(mat[:, :states], state, preferred_element_type=F32)
    return high + jnp.dot(mat[:, states:], state, preferred_element_type=F32)


def fill_periods(mat, turned_pass, source, ref):
    @pl.loop(0, ref.shape[0])
    def _(i):
        at = source * ref.shape[0] + i

        @pl.when(turned_pass)
        def _():
            lifted = jnp.exp(ref[i].T.astype(F32))
            put(mat, at, lifted * (1.0 / jnp.sum(lifted, axis=0, keepdims=True)))

        @pl.when(jnp.logical_not(turned_pass))
        def _():
            lifted = jnp.exp(ref[i].astype(F32))
            put(mat, at, lifted * (1.0 / jnp.sum(lifted, axis=1, keepdims=True)))


def prep_own_kernel(own_any, vec_ref, mat, consts, own_ref, sem):
    copy = pltpu.make_async_copy(own_any, own_ref, sem)
    copy.start()
    for i in range(4):
        consts[i] = jnp.broadcast_to(vec_ref[i : i + 1, :], (LANES, own_ref.shape[1])).T
    copy.wait()
    fill_periods(mat, is_forward_first(), core_index(), own_ref)


def prep_other_kernel(other_ref, mat_in, mat):
    fill_periods(mat, is_forward_first(), 1 - core_index(), other_ref)


def prep_second_kernel(own_ref, other_ref, after_any, mat, row_probs):
    rows = row_probs.shape[1]
    here = own_rows(lax.axis_index("hh") * rows, rows)
    for source, ref in ((core_index(), own_ref), (1 - core_index(), other_ref)):
        for i in range(ref.shape[0]):
            lifted = jnp.exp(ref[i, here, :].astype(F32))
            row_probs[source * ref.shape[0] + i] = lifted * (1.0 / jnp.sum(lifted, axis=1, keepdims=True))
        fill_periods(mat, jnp.logical_not(is_forward_first()), source, ref)


def emission(sel_ref, consts, step_now, cols, less=None):
    gap = sel_ref[0, step_now, :1, cols] - consts[1]
    power = gap * gap * consts[2] + consts[3]
    return jnp.exp2(power if less is None else power - less)


def is_moving(sel_ref, step_now, cols):
    return sel_ref[1, step_now, :1, cols] > 0.5


def is_seen(sel_ref, step_now, cols):
    return sel_ref[2, step_now, :1, cols] > 0.5


def column_sum(x):
    return jnp.sum(x, axis=0, keepdims=True)


def own_rows(row_begin, rows):
    return pl.ds(pl.multiple_of(row_begin, rows), rows)


def outer_sum(weights_ref, carried):
    return lax.dot_general(weights_ref[...], carried, (((1,), (1,)), ((), ())), preferred_element_type=F32)


def run_forward(lead, mat, hist, sel_ref, consts, ab_ref, logs, second=None):
    steps, states, width = hist.shape
    cuts = tiles(width)
    inverse = [1.0 / column_sum(ab_ref[:, cols].astype(F32)) for cols in cuts]
    for k in range(steps):
        step_now = lead + k
        if second is None:
            hist[k] = ab_ref[...]
        else:
            weights_ref, row_begin, add_counts = second
            own_alpha = ab_ref[own_rows(row_begin, weights_ref.shape[0]), :].astype(F32)
        for q, cols in enumerate(cuts):
            moved = both_halves(mat[k], ab_ref[:, cols]) * inverse[q]
            moving = is_moving(sel_ref, step_now, cols)
            if second is not None:
                total = column_sum(moved * hist[k, :, cols].astype(F32))
                weight = jnp.where(moving, 1.0 / total, 0.0)
                weights_ref[:, cols] = (own_alpha[:, cols] * inverse[q] * weight).astype(BF16)
            emit = emission(sel_ref, consts, step_now, cols)
            joint = jnp.where(moving, moved, consts[0]) * emit
            scale = column_sum(joint)
            if second is None:
                seen = is_seen(sel_ref, step_now, cols)
                logs[q] = logs[q] + jnp.where(seen, jnp.log2(scale), 0.0)
            inverse[q] = 1.0 / scale
            ab_ref[:, cols] = joint.astype(BF16)
        if second is not None:
            add_counts(k, outer_sum(weights_ref, hist[k]))
    return logs


def run_backward(lead, mat, hist, sel_ref, consts, state, ub_ref, logs, leave, second=None, between=None):
    steps, states, width = hist.shape
    cuts = tiles(width)
    rest = [x[:1] for x in state]
    size = [jnp.zeros((1, LANES), F32) for _ in cuts]

    def step(k):
        step_now = lead + k
        grown = []
        for q, cols in enumerate(cuts):
            emit = emission(sel_ref, consts, step_now, cols, size[q] if second is None else None)
            carried = emit * state[q]
            ub_ref[:, cols] = carried.astype(BF16)
            whole = column_sum(carried)
            grown.append(whole)
            if second is None:
                size[q] = jnp.log2(whole)
                seen = is_seen(sel_ref, step_now, cols)
                logs[q] = logs[q] + jnp.where(seen, size[q], 0.0)
                begun = column_sum(carried * consts[0]) / whole
                rest[q] = jnp.where(seen, begun, rest[q])
        if second is None:
            hist[k] = ub_ref[...]
        else:
            weights_ref, row_begin, add_counts = second
            own_alpha = hist[k, own_rows(row_begin, weights_ref.shape[0]), :].astype(F32)
        for q, cols in enumerate(cuts):
            product = both_halves(mat[k], ub_ref[:, cols])
            moving = is_moving(sel_ref, step_now, cols)
            if second is None:
                state[q] = jnp.where(moving, product, rest[q] * grown[q])
            else:
                shrink = 1.0 / grown[q]
                product = product * shrink
                total = column_sum(product * hist[k, :, cols].astype(F32))
                weight = jnp.where(moving, 1.0 / total, 0.0)
                weights_ref[:, cols] = (own_alpha[:, cols] * weight * shrink).astype(BF16)
                state[q] = jnp.where(moving, product, rest[q])
        if second is not None:
            add_counts(k, outer_sum(weights_ref, ub_ref[...]))

    def left():
        return [x * jnp.exp2(-y) for x, y in zip(state, size)]

    for k in reversed(range(1, steps)):
        step(k)
    if second is None:
        step(0)
        leave(left())
        return
    between()

    @pl.when(lead > 0)
    def _():
        step(0)
        leave(left())

    @pl.when(lead == 0)
    def _():
        second[2](0, jnp.zeros((second[0].shape[0], states), F32))


def put_state(state_out, values, logs):
    states = state_out.shape[0] - EXTRA
    row = lax.broadcasted_iota(jnp.int32, (EXTRA, LANES), 0)
    for q, cols in enumerate(tiles(state_out.shape[1])):
        state_out[:states, cols] = values[q].astype(BF16)
        high = logs[q].astype(BF16).astype(F32)
        middle = (logs[q] - high).astype(BF16).astype(F32)
        piece = jnp.where(
            row == 0, high, jnp.where(row == 1, middle, jnp.where(row == 2, logs[q] - high - middle, 0.0))
        )
        state_out[states:, cols] = piece.astype(BF16)


def state_logs(state_ref):
    states = state_ref.shape[0] - EXTRA
    return [column_sum(state_ref[states:, cols].astype(F32)) for cols in tiles(state_ref.shape[1])]


def first_kernel(resume, grids, part, rows_ref, mat, consts, *refs):
    state_in = refs[0] if resume else None
    hist, state_out, sel_ref, ab_ref = refs[-4:]
    chunk = part * grids + (pl.program_id(0) if grids > 1 else 0)
    steps, states, width = hist.shape
    forward_first, lead = is_forward_first(), lax.axis_index("per") * steps
    cuts = tiles(width)
    group, half_periods, slot_rows = rows_ref.shape
    tops = 2 * len(cuts)

    def scan_source(d, carry):
        rank, picked = carry
        for slot in range(slot_rows // HB):
            cols = slice(slot * HB, (slot + 1) * HB)
            block = rows_ref[d, :, cols]
            live = block > -0.5 * SEEN
            picked = [jnp.where(live & (rank == chunk * tops + i), block, old) for i, old in enumerate(picked)]
            rank = rank + live.astype(jnp.int32)
        return rank, picked

    carry = (jnp.zeros((half_periods, HB), jnp.int32), [jnp.zeros((half_periods, HB), F32)] * tops)
    if group <= 8:
        for d in range(group):
            carry = scan_source(d, carry)
    else:
        carry = lax.fori_loop(0, group, scan_source, carry)
    low_lane = lax.broadcasted_iota(jnp.int32, (half_periods, HB), 1) < HALF
    for q, cols in enumerate(cuts):
        left, right = carry[1][2 * q], carry[1][2 * q + 1]
        before = jnp.zeros((1, HB), F32)
        for late in range(2):
            value = (
                jnp.where(low_lane, pltpu.roll(left, HALF, 1), right)
                if late
                else jnp.where(low_lane, left, pltpu.roll(right, HALF, 1))
            )
            seen = value > 0.5 * SEEN
            earn = jnp.where(seen, value - SEEN, value)
            seen = seen.astype(F32)
            for i in range(half_periods):
                at = late * half_periods + i
                now = seen[i : i + 1]
                sel_ref[0, at, :, cols] = jnp.broadcast_to(earn[i : i + 1], (8, HB))
                sel_ref[1, at, :, cols] = jnp.broadcast_to(now * before, (8, HB))
                sel_ref[2, at, :, cols] = jnp.broadcast_to(now, (8, HB))
                before = now
    zeros = [jnp.zeros((1, LANES), F32) for _ in cuts]

    @pl.when(forward_first)
    def _():
        if resume:
            ab_ref[...] = state_in[:states, :]
        else:
            for cols in cuts:
                ab_ref[:, cols] = consts[0].astype(BF16)
        logs = state_logs(state_in) if resume else list(zeros)
        run_forward(lead, mat, hist, sel_ref, consts, ab_ref, logs)
        put_state(state_out, [ab_ref[:, cols] for cols in cuts], logs)

    @pl.when(jnp.logical_not(forward_first))
    def _():
        state = [
            state_in[:states, cols].astype(F32) if resume else jnp.ones((states, LANES), F32) for cols in cuts
        ]
        logs = state_logs(state_in) if resume else list(zeros)
        leave = lambda values: put_state(state_out, values, logs)
        run_backward(lead, mat, hist, sel_ref, consts, state, ab_ref, logs, leave)


def second_kernel(resume, last, extend, grids, *refs):
    refs = list(refs)
    sel_ref, mat, consts, hist, own_state, state_in = (refs.pop(0) for _ in range(6))
    counts_in, sums_in = (refs.pop(0), refs.pop(0)) if resume else (None, None)
    row_probs = refs.pop(0) if last else None
    mine_ref, other_ref = (refs.pop(0), refs.pop(0)) if last else (None, None)
    counts_out, sums_out = (None, None) if last else (refs.pop(0), refs.pop(0))
    state_out = refs.pop(0) if extend else None
    ab_ref, weights_ref = refs[:2]
    counts_ref, sums_ref = refs[2:] if last else (counts_out, sums_out)
    chunk = pl.program_id(0) if grids > 1 else 0
    steps, states, width = hist.shape
    core, forward_first = core_index(), is_forward_first()
    row_begin = lax.axis_index("hh") * weights_ref.shape[0]
    lead = lax.axis_index("per") * steps
    rows = weights_ref.shape[0]

    def centre(k, counts):
        probs = row_probs[k]
        weighted = probs * counts
        grad = weighted - probs * jnp.sum(weighted, axis=1, keepdims=True)
        at = slice(k * rows, (k + 1) * rows)
        left, right = grad[:, :LANES], grad[:, LANES:]
        mine_ref[at, :] = jnp.where(core == 0, left, right)
        other_ref[at, :] = jnp.where(core == 0, right, left)

    def add_counts(k, counts):
        if grids > 1:
            counts_ref[k] += counts
            return
        if resume:
            counts = counts + counts_in[k]
        if last:
            centre(k, counts)
        else:
            counts_ref[k] = counts

    second = (weights_ref, row_begin, add_counts)

    @pl.when(chunk == 0)
    def _():
        if grids > 1:
            counts_ref[...] = jnp.zeros_like(counts_ref)
        sums_ref[...] = sums_in[...] if resume else jnp.zeros_like(sums_ref)

    def add_sums(alpha_ref, other_state):
        total = jnp.zeros((1, LANES), F32)
        years = jnp.zeros((8, LANES), F32)
        for cols, here, there in zip(tiles(width), state_logs(alpha_ref), state_logs(other_state)):
            alpha = alpha_ref[:states, cols].astype(F32)
            meet = column_sum(alpha * other_state[:states, cols].astype(F32))
            total += (here + there + jnp.log2(meet / column_sum(alpha))) * LN2
            years += jnp.sum(sel_ref[2, :, :, cols], axis=0)
        total = jnp.broadcast_to(jnp.sum(total, axis=1, keepdims=True), (1, LANES))
        years = jnp.broadcast_to(jnp.sum(years[:1], axis=1, keepdims=True), (1, LANES))
        row = lax.broadcasted_iota(jnp.int32, (8, LANES), 0)
        sums_ref[...] += jnp.where(row == 0, total, jnp.where(row == 1, years, 0.0))

    zeros = [jnp.zeros((1, LANES), F32) for _ in tiles(width)]

    @pl.when(jnp.logical_not(forward_first))
    def _():
        ab_ref[...] = state_in[:states, :]
        run_forward(lead, mat, hist, sel_ref, consts, ab_ref, list(zeros), second)
        add_sums(state_in, own_state)
        if extend:
            put_state(state_out, [ab_ref[:, cols] for cols in tiles(width)], zeros)

    @pl.when(forward_first)
    def _():
        state = [state_in[:states, cols].astype(F32) for cols in tiles(width)]
        leave = lambda values: put_state(state_out, values, zeros) if extend else None
        run_backward(lead, mat, hist, sel_ref, consts, state, ab_ref, list(zeros), leave, second, lambda: add_sums(own_state, state_in))

    if last:

        @pl.when(chunk == grids - 1)
        def _():
            if grids > 1:
                for k in range(steps):
                    centre(k, counts_ref[k])
            mine_ref[steps * rows :, :] = sums_ref[...]
            other_ref[steps * rows :, :] = sums_ref[...]


def finish_kernel(scale, mine_ref, other_ref, grad_ref, mean_ref):
    count = grad_ref.shape[0]
    total = mine_ref[count : count + 1, :] + other_ref[count : count + 1, :]
    years = mine_ref[count + 1 : count + 2, :] + other_ref[count + 1 : count + 2, :]
    grad_ref[...] = (mine_ref[:count, :] + other_ref[:count, :]) * (scale / years)
    mean_ref[0] = (total / years)[0, 0]


def per_device(
    earnings, starts, lengths, block_count, trans_logits, init_logits, state_mean, log_sd
):
    slot_rows, periods = earnings.shape
    states = init_logits.shape[0]
    group = lax.axis_size(("hh", "per"))
    sides = lax.axis_size("per")
    cores = lax.axis_size("st")
    part = trans_logits.shape[0]
    steps = part * cores
    rows = states // lax.axis_size("hh")
    households = group * HB // cores
    parts = 2 if households <= 4 * HB else 1
    share = households // parts
    width = min(2 * HB, share)
    grids = share // width
    side = lax.axis_index("per")
    shaped = jax.ShapeDtypeStruct
    dma = pltpu.SemaphoreType.DMA

    swap = [(0, 1), (1, 0)]
    vec_row = pltpu.VMEM((1, states), F32)
    packed, vectors = pl.pallas_call(
        pack_kernel,
        out_shape=[
            pltpu.VMEM((group, periods // 2, slot_rows), F32),
            pltpu.VMEM((8, states), F32),
        ],
        in_specs=[smem()] + [hbm()] * 6,
        out_specs=[vmem()] * 2,
        scratch_shapes=[
            pltpu.VMEM((periods, slot_rows), F32),
            pltpu.VMEM((slot_rows // HB, HB), jnp.int32),
            pltpu.VMEM((slot_rows // HB, HB), jnp.int32),
            vec_row,
            vec_row,
            vec_row,
            dma((6,)),
        ],
        compiler_params=params(2),
        name="pack",
    )(
        block_count,
        *in_hbm(
            earnings.T, starts.reshape(-1, HB), lengths.reshape(-1, HB),
            init_logits.reshape(1, states), state_mean.reshape(1, states), log_sd.reshape(1, states),
        ),
    )
    packed, later_logits = lax.optimization_barrier((packed, trans_logits))
    other_logits = lax.ppermute(later_logits, "st", swap)
    along = group // sides
    centre = along // 2
    outward = sorted(range(along), key=lambda z: (abs(z - centre), -z))
    listed = [z * sides + x for z in outward for x in reversed(range(sides))]
    gathered = lax.all_to_all(
        packed, ("hh", "per", "st"), split_axis=0, concat_axis=0,
        axis_index_groups=[[n * cores + c for n in listed] for c in range(cores)], tiled=True,
    )
    mat_shape = shaped((steps, states, 2 * states), BF16)
    first_mat, consts = pl.pallas_call(
        prep_own_kernel,
        out_shape=[pltpu.VMEM(mat_shape.shape, BF16), pltpu.VMEM((4, states, LANES), F32)],
        in_specs=[hbm(), vmem()],
        out_specs=[vmem(), vmem()],
        scratch_shapes=[pltpu.VMEM(trans_logits.shape, BF16), dma],
        compiler_params=params(4),
        name="prep_own",
    )(*in_hbm(trans_logits), vectors)
    first_mat = pl.pallas_call(
        prep_other_kernel,
        out_shape=pltpu.VMEM(mat_shape.shape, BF16),
        in_specs=[vmem(), vmem()],
        out_specs=vmem(),
        input_output_aliases={1: 0},
        compiler_params=params(4),
        name="prep_other",
    )(other_logits, first_mat)

    def prep_second(after):
        return pl.pallas_call(
            prep_second_kernel,
            out_shape=[mat_shape, shaped((steps, rows, states), F32)],
            in_specs=[vmem(), vmem(), hbm()],
            out_specs=[vmem(), vmem()],
            compiler_params=params(4),
            name="prep_second",
        )(trans_logits, other_logits, after)

    def whole(*shape):
        if grids == 1:
            return vmem()
        return pl.BlockSpec(shape, lambda g: (0,) * len(shape))

    def lanes(*lead):
        if grids == 1:
            return vmem()
        return pl.BlockSpec(lead + (width,), lambda g: (0,) * len(lead) + (g,))

    grid = (grids,) if grids > 1 else ()
    hist_shape = shaped((steps, states, share), BF16)
    state_shape = shaped((states + EXTRA, share), BF16)
    sel_shape = shaped((3, periods, 8, share), F32)
    swap_shape = shaped((steps * rows + 8, LANES), F32)
    counts_shape = shaped((steps, rows, states), F32)
    sums_shape = shaped((8, LANES), F32)
    hist_spec, state_spec, sel_spec = lanes(steps, states), lanes(states + EXTRA), lanes(3, periods, 8)
    const_spec = whole(4, states, LANES)

    def first_pass(index, state_in):
        resume = state_in is not None
        return pl.pallas_call(
            functools.partial(first_kernel, resume, grids, index),
            grid=grid,
            out_shape=[hist_shape, state_shape, sel_shape],
            in_specs=[whole(*gathered.shape), whole(*first_mat.shape), const_spec]
            + [state_spec] * resume,
            out_specs=[hist_spec, state_spec, sel_spec],
            scratch_shapes=[pltpu.VMEM((states, width), BF16)],
            compiler_params=params(8 if grids == 1 else 32),
            name="first_pass",
        )(gathered, first_mat, consts, *([state_in] if resume else []))

    def second_pass(kept, state_in, sums_in, last, extend):
        hist, own_state, sel = kept
        resume = sums_in is not None
        scratch = [
            pltpu.VMEM((states, width), BF16),
            pltpu.VMEM((rows, width), BF16),
        ]
        counts_spec, sums_spec = whole(*counts_shape.shape), whole(*sums_shape.shape)
        if last:
            out_shape = [swap_shape] * 2
            scratch += [pltpu.VMEM(counts_shape.shape, F32), pltpu.VMEM(sums_shape.shape, F32)]
        else:
            out_shape = [counts_shape, sums_shape]
        out_specs = [whole(*x.shape) for x in out_shape]
        if extend:
            out_shape, out_specs = out_shape + [state_shape], out_specs + [state_spec]
        return pl.pallas_call(
            functools.partial(second_kernel, resume, last, extend, grids),
            grid=grid,
            out_shape=out_shape,
            in_specs=[sel_spec, whole(*second_mat.shape), const_spec, hist_spec, state_spec, state_spec]
            + [counts_spec, sums_spec] * resume
            + [whole(*row_probs.shape)] * last,
            out_specs=out_specs,
            scratch_shapes=scratch,
            compiler_params=params(8 if grids == 1 else 32),
            name="second_pass",
        )(
            sel, second_mat, consts, hist, own_state, state_in,
            *(sums_in if resume else []),
            *([row_probs] if last else []),
        )

    def hand_over(state, stage):
        moves = [(stage, stage + 1), (sides - 1 - stage, sides - 2 - stage)]
        return lax.ppermute(state, "per", moves)

    if sides == 2:
        kept = [first_pass(index, None) for index in range(parts)]
        arrived = [hand_over(each[1], 0) for each in kept]
        second_mat, row_probs = prep_second(kept[-1][1])
        sums = None
        for index in range(parts):
            sums = second_pass(kept[index], arrived[index], sums, index == parts - 1, False)
        mine, other = sums
    else:
        kept = [jnp.zeros(x.shape, x.dtype) for x in (hist_shape, state_shape, sel_shape)]
        done = [jnp.zeros(x.shape, x.dtype) for x in (swap_shape, swap_shape, state_shape)]
        state = None
        second_mat, row_probs = prep_second(gathered)
        for stage in range(sides):
            active = (side == stage) | (side == sides - 1 - stage)
            if stage < sides // 2:
                kept = lax.cond(
                    active, lambda x, kept: list(first_pass(0, x)), lambda x, kept: kept, state, kept
                )
                state = kept[1]
            else:
                done = lax.cond(
                    active,
                    lambda x, done: list(second_pass(kept, x, None, True, True)),
                    lambda x, done: done,
                    state,
                    done,
                )
                state = done[2]
            if stage < sides - 1:
                state = hand_over(state, stage)
        mine, other, _ = done
        total = jnp.where(side == sides // 2, mine[steps * rows], 0.0)
        total = lax.psum(total, "per")
        mine = mine.at[steps * rows].set(total)
        other = other.at[steps * rows].set(total)
    received = lax.ppermute(other, "st", swap)
    trans_grad, mean_loglik = pl.pallas_call(
        functools.partial(finish_kernel, float(states * states * periods)),
        out_shape=[shaped((steps * rows, LANES), F32), shaped((1,), F32)],
        in_specs=[vmem(), vmem()],
        out_specs=[vmem(), smem()],
        compiler_params=params(4),
        name="finish",
    )(mine, received)
    return (trans_grad.reshape(steps, rows, LANES), mean_loglik)


def solution(mesh):
    placed = (
        P(("hh", "per"), None),
        P(("hh", "per")),
        P(("hh", "per")),
        P(("hh", "per")),
        P(("grp", "per", "st"), None, None),
        P("grp"),
        P("grp"),
        P("grp"),
    )
    return jax.shard_map(
        per_device,
        mesh=mesh,
        in_specs=placed,
        out_specs=(P(("grp", "per"), "hh", "st"), P("grp")),
        check_vma=False,
    )
```

```python
import functools

import jax
import jax.numpy as jnp
from jax import lax
from jax.experimental import pallas as pl
from jax.experimental.pallas import tpu as pltpu
from jax.sharding import PartitionSpec as P

HB = 128
LANES = 128
HALF = HB // 2
SEEN = 16.0
F32 = jnp.float32
BF16 = jnp.bfloat16
LOG2E = 1.4426950408889634
LN2 = 0.6931471805599453
EXTRA = 16


def vmem():
    return pl.BlockSpec(memory_space=pltpu.VMEM)


def smem():
    return pl.BlockSpec(memory_space=pltpu.SMEM)


def hbm():
    return pl.BlockSpec(memory_space=pltpu.HBM)


def in_hbm(*arrays):
    return [pltpu.with_memory_space_constraint(x, pltpu.HBM) for x in arrays]


def params(mebibytes):
    return pltpu.CompilerParams(vmem_limit_bytes=mebibytes * 1024 * 1024)


def core_index():
    return lax.axis_index("st")


def is_forward_first():
    return 2 * lax.axis_index("per") < lax.axis_size("per")


def tiles(width):
    return [slice(q, q + LANES) for q in range(0, width, LANES)]


def fetch(pairs, sems):
    copies = [pltpu.make_async_copy(src, dst, sems.at[i]) for i, (src, dst) in enumerate(pairs)]
    for copy in copies:
        copy.start()
    for copy in copies:
        copy.wait()


def pack_kernel(count_ref, earn_any, start_any, len_any, out_ref, earn_ref, start_ref, len_ref, sems):
    fetch(((earn_any, earn_ref), (start_any, start_ref), (len_any, len_ref)), sems)
    periods, slot_rows = earn_ref.shape
    core = core_index()
    low_lane = lax.broadcasted_iota(jnp.int32, (periods // 2, HB), 1) < HALF
    time = lax.broadcasted_iota(jnp.int32, (periods, HB), 0)
    for slot in range(slot_rows // HB):
        cols = slice(slot * HB, (slot + 1) * HB)
        begin = start_ref[slot : slot + 1, :]
        seen = (time >= begin) & (time < begin + len_ref[slot : slot + 1, :])
        live = slot < count_ref[0]
        shift = jnp.where(live, jnp.where(seen, SEEN, 0.0), -SEEN)
        value = earn_ref[:, cols] + shift
        early, late = value[: periods // 2], value[periods // 2 :]
        turned = pltpu.roll(jnp.where(core == 0, late, early), HALF, 1)
        packed = jnp.where(low_lane, jnp.where(core == 0, early, turned), jnp.where(core == 0, turned, late))
        for to in range(out_ref.shape[0]):
            out_ref[to, :, cols] = packed


def put(ref, at, value):
    states = value.shape[0]
    high = value.astype(BF16)
    ref[at, :states, :states] = high
    ref[at, :states, states:] = (value - high.astype(F32)).astype(BF16)


def both_halves(mat, state):
    states = mat.shape[0]
    high = jnp.dot(mat[:, :states], state, preferred_element_type=F32)
    return high + jnp.dot(mat[:, states:], state, preferred_element_type=F32)


def fill_periods(mat, turned_pass, source, ref):
    @pl.loop(0, ref.shape[0])
    def _(i):
        at = source * ref.shape[0] + i

        @pl.when(turned_pass)
        def _():
            lifted = jnp.exp(ref[i].T.astype(F32))
            put(mat, at, lifted * (1.0 / jnp.sum(lifted, axis=0, keepdims=True)))

        @pl.when(jnp.logical_not(turned_pass))
        def _():
            lifted = jnp.exp(ref[i].astype(F32))
            put(mat, at, lifted * (1.0 / jnp.sum(lifted, axis=1, keepdims=True)))


def prep_own_kernel(
    own_any, init_any, mean_any, sd_any, mat, consts, own_ref, init_ref, mean_ref, sd_ref, sem, sems
):
    copy = pltpu.make_async_copy(own_any, own_ref, sem)
    copy.start()
    fetch(((init_any, init_ref), (mean_any, mean_ref), (sd_any, sd_ref)), sems)
    raised = jnp.exp(init_ref[...])
    rows = (
        raised / jnp.sum(raised, axis=1, keepdims=True),
        mean_ref[...],
        (-0.5 * LOG2E) * jnp.exp(-2.0 * sd_ref[...]),
        -LOG2E * sd_ref[...],
    )
    for i, row in enumerate(rows):
        consts[i] = jnp.broadcast_to(row, (LANES, own_ref.shape[1])).T
    copy.wait()
    fill_periods(mat, is_forward_first(), core_index(), own_ref)


def prep_other_kernel(other_ref, mat_in, mat):
    fill_periods(mat, is_forward_first(), 1 - core_index(), other_ref)


def prep_second_kernel(own_ref, other_ref, after_any, mat, row_probs):
    rows = row_probs.shape[1]
    here = own_rows(lax.axis_index("hh") * rows, rows)
    for source, ref in ((core_index(), own_ref), (1 - core_index(), other_ref)):
        for i in range(ref.shape[0]):
            lifted = jnp.exp(ref[i, here, :].astype(F32))
            row_probs[source * ref.shape[0] + i] = lifted * (1.0 / jnp.sum(lifted, axis=1, keepdims=True))
        fill_periods(mat, jnp.logical_not(is_forward_first()), source, ref)


def emission(sel_ref, consts, step_now, cols, less=None):
    gap = sel_ref[0, step_now, :1, cols] - consts[1]
    power = gap * gap * consts[2] + consts[3]
    return jnp.exp2(power if less is None else power - less)


def is_moving(sel_ref, step_now, cols):
    return sel_ref[1, step_now, :1, cols] > 0.5


def is_seen(sel_ref, step_now, cols):
    return sel_ref[2, step_now, :1, cols] > 0.5


def column_sum(x):
    return jnp.sum(x, axis=0, keepdims=True)


def own_rows(row_begin, rows):
    return pl.ds(pl.multiple_of(row_begin, rows), rows)


def outer_sum(weights_ref, carried):
    return lax.dot_general(weights_ref[...], carried, (((1,), (1,)), ((), ())), preferred_element_type=F32)


def run_forward(lead, mat, hist, sel_ref, consts, ab_ref, logs, second=None, fresh=False):
    steps, states, width = hist.shape
    cuts = tiles(width)
    inverse = [1.0 / column_sum(ab_ref[:, cols].astype(F32)) for cols in cuts]
    for k in range(steps):
        step_now = lead + k
        if second is None:
            hist[k] = ab_ref[...]
        else:
            weights_ref, row_begin, add_counts = second
            own_alpha = ab_ref[own_rows(row_begin, weights_ref.shape[0]), :].astype(F32)
        for q, cols in enumerate(cuts):
            begins = fresh and k == 0
            if not begins:
                moved = both_halves(mat[k], ab_ref[:, cols]) * inverse[q]
                moving = is_moving(sel_ref, step_now, cols)
            if second is not None:
                total = column_sum(moved * hist[k, :, cols].astype(F32))
                weight = jnp.where(moving, 1.0 / total, 0.0)
                weights_ref[:, cols] = (own_alpha[:, cols] * inverse[q] * weight).astype(BF16)
            emit = emission(sel_ref, consts, step_now, cols)
            joint = (consts[0] if begins else jnp.where(moving, moved, consts[0])) * emit
            scale = column_sum(joint)
            if second is None:
                seen = is_seen(sel_ref, step_now, cols)
                logs[q] = logs[q] + jnp.where(seen, jnp.log2(scale), 0.0)
            inverse[q] = 1.0 / scale
            ab_ref[:, cols] = joint.astype(BF16)
        if second is not None:
            add_counts(k, outer_sum(weights_ref, hist[k]))
    return logs


def run_backward(lead, mat, hist, sel_ref, consts, state, ub_ref, logs, leave, second=None, between=None):
    steps, states, width = hist.shape
    cuts = tiles(width)
    rest = [x[:1] for x in state]
    size = [jnp.zeros((1, LANES), F32) for _ in cuts]

    def step(k):
        step_now = lead + k
        grown = []
        for q, cols in enumerate(cuts):
            emit = emission(sel_ref, consts, step_now, cols, size[q] if second is None else None)
            carried = emit * state[q]
            ub_ref[:, cols] = carried.astype(BF16)
            whole = column_sum(carried)
            grown.append(whole)
            if second is None:
                size[q] = jnp.log2(whole)
                seen = is_seen(sel_ref, step_now, cols)
                logs[q] = logs[q] + jnp.where(seen, size[q], 0.0)
                begun = column_sum(carried * consts[0]) / whole
                rest[q] = jnp.where(seen, begun, rest[q])
        if second is None:
            hist[k] = ub_ref[...]
        else:
            weights_ref, row_begin, add_counts = second
            own_alpha = hist[k, own_rows(row_begin, weights_ref.shape[0]), :].astype(F32)
        for q, cols in enumerate(cuts):
            product = both_halves(mat[k], ub_ref[:, cols])
            moving = is_moving(sel_ref, step_now, cols)
            if second is None:
                state[q] = jnp.where(moving, product, rest[q] * grown[q])
            else:
                shrink = 1.0 / grown[q]
                product = product * shrink
                total = column_sum(product * hist[k, :, cols].astype(F32))
                weight = jnp.where(moving, 1.0 / total, 0.0)
                weights_ref[:, cols] = (own_alpha[:, cols] * weight * shrink).astype(BF16)
                state[q] = jnp.where(moving, product, rest[q])
        if second is not None:
            add_counts(k, outer_sum(weights_ref, ub_ref[...]))

    def left():
        return [x * jnp.exp2(-y) for x, y in zip(state, size)]

    for k in reversed(range(1, steps)):
        step(k)
    if second is None:
        step(0)
        leave(left())
        return
    between()

    @pl.when(lead > 0)
    def _():
        step(0)
        leave(left())

    @pl.when(lead == 0)
    def _():
        second[2](0, jnp.zeros((second[0].shape[0], states), F32))


def put_state(state_out, values, logs):
    states = state_out.shape[0] - EXTRA
    row = lax.broadcasted_iota(jnp.int32, (EXTRA, LANES), 0)
    for q, cols in enumerate(tiles(state_out.shape[1])):
        state_out[:states, cols] = values[q].astype(BF16)
        high = logs[q].astype(BF16).astype(F32)
        middle = (logs[q] - high).astype(BF16).astype(F32)
        piece = jnp.where(
            row == 0, high, jnp.where(row == 1, middle, jnp.where(row == 2, logs[q] - high - middle, 0.0))
        )
        state_out[states:, cols] = piece.astype(BF16)


def state_logs(state_ref):
    states = state_ref.shape[0] - EXTRA
    return [column_sum(state_ref[states:, cols].astype(F32)) for cols in tiles(state_ref.shape[1])]


def first_kernel(resume, grids, part, rows_ref, mat, consts, *refs):
    state_in = refs[0] if resume else None
    hist, state_out, sel_ref, ab_ref = refs[-4:]
    chunk = part * grids + (pl.program_id(0) if grids > 1 else 0)
    steps, states, width = hist.shape
    forward_first, lead = is_forward_first(), lax.axis_index("per") * steps
    cuts = tiles(width)
    group, half_periods, slot_rows = rows_ref.shape
    tops = 2 * len(cuts)

    def scan_source(d, carry):
        rank, picked = carry
        for slot in range(slot_rows // HB):
            cols = slice(slot * HB, (slot + 1) * HB)
            block = rows_ref[d, :, cols]
            live = block > -0.5 * SEEN
            picked = [jnp.where(live & (rank == chunk * tops + i), block, old) for i, old in enumerate(picked)]
            rank = rank + live.astype(jnp.int32)
        return rank, picked

    carry = (jnp.zeros((half_periods, HB), jnp.int32), [jnp.zeros((half_periods, HB), F32)] * tops)
    if group <= 8:
        for d in range(group):
            carry = scan_source(d, carry)
    else:
        carry = lax.fori_loop(0, group, scan_source, carry)
    low_lane = lax.broadcasted_iota(jnp.int32, (half_periods, HB), 1) < HALF
    for q, cols in enumerate(cuts):
        left, right = carry[1][2 * q], carry[1][2 * q + 1]
        before = jnp.zeros((1, HB), F32)
        for late in range(2):
            value = (
                jnp.where(low_lane, pltpu.roll(left, HALF, 1), right)
                if late
                else jnp.where(low_lane, left, pltpu.roll(right, HALF, 1))
            )
            seen = value > 0.5 * SEEN
            earn = jnp.where(seen, value - SEEN, value)
            seen = seen.astype(F32)
            for i in range(half_periods):
                at = late * half_periods + i
                now = seen[i : i + 1]
                sel_ref[0, at, :, cols] = jnp.broadcast_to(earn[i : i + 1], (8, HB))
                sel_ref[1, at, :, cols] = jnp.broadcast_to(now * before, (8, HB))
                sel_ref[2, at, :, cols] = jnp.broadcast_to(now, (8, HB))
                before = now
    zeros = [jnp.zeros((1, LANES), F32) for _ in cuts]

    @pl.when(forward_first)
    def _():
        if resume:
            ab_ref[...] = state_in[:states, :]
        else:
            for cols in cuts:
                ab_ref[:, cols] = consts[0].astype(BF16)
        logs = state_logs(state_in) if resume else list(zeros)
        fresh = lax.axis_size("per") == 2
        run_forward(lead, mat, hist, sel_ref, consts, ab_ref, logs, fresh=fresh)
        put_state(state_out, [ab_ref[:, cols] for cols in cuts], logs)

    @pl.when(jnp.logical_not(forward_first))
    def _():
        state = [
            state_in[:states, cols].astype(F32) if resume else jnp.ones((states, LANES), F32) for cols in cuts
        ]
        logs = state_logs(state_in) if resume else list(zeros)
        leave = lambda values: put_state(state_out, values, logs)
        run_backward(lead, mat, hist, sel_ref, consts, state, ab_ref, logs, leave)


def second_kernel(resume, last, extend, grids, *refs):
    refs = list(refs)
    sel_ref, mat, consts, hist, own_state, state_in = (refs.pop(0) for _ in range(6))
    counts_in, sums_in = (refs.pop(0), refs.pop(0)) if resume else (None, None)
    row_probs = refs.pop(0) if last else None
    mine_ref, other_ref = (refs.pop(0), refs.pop(0)) if last else (None, None)
    counts_out, sums_out = (None, None) if last else (refs.pop(0), refs.pop(0))
    state_out = refs.pop(0) if extend else None
    ab_ref, weights_ref = refs[:2]
    counts_ref, sums_ref = refs[2:] if last else (counts_out, sums_out)
    chunk = pl.program_id(0) if grids > 1 else 0
    steps, states, width = hist.shape
    core, forward_first = core_index(), is_forward_first()
    row_begin = lax.axis_index("hh") * weights_ref.shape[0]
    lead = lax.axis_index("per") * steps
    rows = weights_ref.shape[0]

    def centre(k, counts):
        probs = row_probs[k]
        weighted = probs * counts
        grad = weighted - probs * jnp.sum(weighted, axis=1, keepdims=True)
        at = slice(k * rows, (k + 1) * rows)
        left, right = grad[:, :LANES], grad[:, LANES:]
        mine_ref[at, :] = jnp.where(core == 0, left, right)
        other_ref[at, :] = jnp.where(core == 0, right, left)

    def add_counts(k, counts):
        if grids > 1:
            counts_ref[k] += counts
            return
        if resume:
            counts = counts + counts_in[k]
        if last:
            centre(k, counts)
        else:
            counts_ref[k] = counts

    second = (weights_ref, row_begin, add_counts)

    @pl.when(chunk == 0)
    def _():
        if grids > 1:
            counts_ref[...] = jnp.zeros_like(counts_ref)
        sums_ref[...] = sums_in[...] if resume else jnp.zeros_like(sums_ref)

    def add_sums(alpha_ref, other_state):
        total = jnp.zeros((1, LANES), F32)
        years = jnp.zeros((8, LANES), F32)
        for cols, here, there in zip(tiles(width), state_logs(alpha_ref), state_logs(other_state)):
            alpha = alpha_ref[:states, cols].astype(F32)
            meet = column_sum(alpha * other_state[:states, cols].astype(F32))
            total += (here + there + jnp.log2(meet / column_sum(alpha))) * LN2
            years += jnp.sum(sel_ref[2, :, :, cols], axis=0)
        total = jnp.broadcast_to(jnp.sum(total, axis=1, keepdims=True), (1, LANES))
        years = jnp.broadcast_to(jnp.sum(years[:1], axis=1, keepdims=True), (1, LANES))
        row = lax.broadcasted_iota(jnp.int32, (8, LANES), 0)
        sums_ref[...] += jnp.where(row == 0, total, jnp.where(row == 1, years, 0.0))

    zeros = [jnp.zeros((1, LANES), F32) for _ in tiles(width)]

    @pl.when(jnp.logical_not(forward_first))
    def _():
        ab_ref[...] = state_in[:states, :]
        run_forward(lead, mat, hist, sel_ref, consts, ab_ref, list(zeros), second)
        add_sums(state_in, own_state)
        if extend:
            put_state(state_out, [ab_ref[:, cols] for cols in tiles(width)], zeros)

    @pl.when(forward_first)
    def _():
        state = [state_in[:states, cols].astype(F32) for cols in tiles(width)]
        leave = lambda values: put_state(state_out, values, zeros) if extend else None
        run_backward(lead, mat, hist, sel_ref, consts, state, ab_ref, list(zeros), leave, second, lambda: add_sums(own_state, state_in))

    if last:

        @pl.when(chunk == grids - 1)
        def _():
            if grids > 1:
                for k in range(steps):
                    centre(k, counts_ref[k])
            mine_ref[steps * rows :, :] = sums_ref[...]
            other_ref[steps * rows :, :] = sums_ref[...]


def finish_kernel(scale, mine_ref, other_ref, grad_ref, mean_ref):
    count = grad_ref.shape[0]
    total = mine_ref[count : count + 1, :] + other_ref[count : count + 1, :]
    years = mine_ref[count + 1 : count + 2, :] + other_ref[count + 1 : count + 2, :]
    grad_ref[...] = (mine_ref[:count, :] + other_ref[:count, :]) * (scale / years)
    mean_ref[0] = (total / years)[0, 0]


def per_device(
    earnings, starts, lengths, block_count, trans_logits, init_logits, state_mean, log_sd
):
    slot_rows, periods = earnings.shape
    states = init_logits.shape[0]
    group = lax.axis_size(("hh", "per"))
    sides = lax.axis_size("per")
    cores = lax.axis_size("st")
    part = trans_logits.shape[0]
    steps = part * cores
    rows = states // lax.axis_size("hh")
    households = group * HB // cores
    parts = 2 if households <= 4 * HB else 1
    share = households // parts
    width = min(2 * HB, share)
    grids = share // width
    side = lax.axis_index("per")
    shaped = jax.ShapeDtypeStruct
    dma = pltpu.SemaphoreType.DMA

    swap = [(0, 1), (1, 0)]
    vec_row = pltpu.VMEM((1, states), F32)
    slots = pltpu.VMEM((slot_rows // HB, HB), jnp.int32)
    packed = pl.pallas_call(
        pack_kernel,
        out_shape=pltpu.VMEM((group, periods // 2, slot_rows), F32),
        in_specs=[smem()] + [hbm()] * 3,
        out_specs=vmem(),
        scratch_shapes=[pltpu.VMEM((periods, slot_rows), F32), slots, slots, dma((3,))],
        compiler_params=params(2),
        name="pack",
    )(block_count, *in_hbm(earnings.T, starts.reshape(-1, HB), lengths.reshape(-1, HB)))
    packed, later_logits = lax.optimization_barrier((packed, trans_logits))
    other_logits = lax.ppermute(later_logits, "st", swap)
    along = group // sides
    centre = along // 2
    outward = sorted(range(along), key=lambda z: (abs(z - centre), -z))
    listed = [z * sides + x for z in outward for x in reversed(range(sides))]
    gathered = lax.all_to_all(
        packed, ("hh", "per", "st"), split_axis=0, concat_axis=0,
        axis_index_groups=[[n * cores + c for n in listed] for c in range(cores)], tiled=True,
    )
    mat_shape = shaped((steps, states, 2 * states), BF16)
    first_mat, consts = pl.pallas_call(
        prep_own_kernel,
        out_shape=[pltpu.VMEM(mat_shape.shape, BF16), pltpu.VMEM((4, states, LANES), F32)],
        in_specs=[hbm()] * 4,
        out_specs=[vmem(), vmem()],
        scratch_shapes=[pltpu.VMEM(trans_logits.shape, BF16), vec_row, vec_row, vec_row, dma, dma((3,))],
        compiler_params=params(4),
        name="prep_own",
    )(
        *in_hbm(
            trans_logits,
            init_logits.reshape(1, states), state_mean.reshape(1, states), log_sd.reshape(1, states),
        )
    )
    first_mat = pl.pallas_call(
        prep_other_kernel,
        out_shape=pltpu.VMEM(mat_shape.shape, BF16),
        in_specs=[vmem(), vmem()],
        out_specs=vmem(),
        input_output_aliases={1: 0},
        compiler_params=params(4),
        name="prep_other",
    )(other_logits, first_mat)

    def prep_second(after):
        return pl.pallas_call(
            prep_second_kernel,
            out_shape=[mat_shape, shaped((steps, rows, states), F32)],
            in_specs=[vmem(), vmem(), hbm()],
            out_specs=[vmem(), vmem()],
            compiler_params=params(4),
            name="prep_second",
        )(trans_logits, other_logits, after)

    def whole(*shape):
        if grids == 1:
            return vmem()
        return pl.BlockSpec(shape, lambda g: (0,) * len(shape))

    def lanes(*lead):
        if grids == 1:
            return vmem()
        return pl.BlockSpec(lead + (width,), lambda g: (0,) * len(lead) + (g,))

    grid = (grids,) if grids > 1 else ()
    hist_shape = shaped((steps, states, share), BF16)
    state_shape = shaped((states + EXTRA, share), BF16)
    sel_shape = shaped((3, periods, 8, share), F32)
    swap_shape = shaped((steps * rows + 8, LANES), F32)
    counts_shape = shaped((steps, rows, states), F32)
    sums_shape = shaped((8, LANES), F32)
    hist_spec, state_spec, sel_spec = lanes(steps, states), lanes(states + EXTRA), lanes(3, periods, 8)
    const_spec = whole(4, states, LANES)

    def first_pass(index, state_in):
        resume = state_in is not None
        return pl.pallas_call(
            functools.partial(first_kernel, resume, grids, index),
            grid=grid,
            out_shape=[hist_shape, state_shape, sel_shape],
            in_specs=[whole(*gathered.shape), whole(*first_mat.shape), const_spec]
            + [state_spec] * resume,
            out_specs=[hist_spec, state_spec, sel_spec],
            scratch_shapes=[pltpu.VMEM((states, width), BF16)],
            compiler_params=params(8 if grids == 1 else 32),
            name="first_pass",
        )(gathered, first_mat, consts, *([state_in] if resume else []))

    def second_pass(kept, state_in, sums_in, last, extend):
        hist, own_state, sel = kept
        resume = sums_in is not None
        scratch = [
            pltpu.VMEM((states, width), BF16),
            pltpu.VMEM((rows, width), BF16),
        ]
        counts_spec, sums_spec = whole(*counts_shape.shape), whole(*sums_shape.shape)
        if last:
            out_shape = [swap_shape] * 2
            scratch += [pltpu.VMEM(counts_shape.shape, F32), pltpu.VMEM(sums_shape.shape, F32)]
        else:
            out_shape = [counts_shape, sums_shape]
        out_specs = [whole(*x.shape) for x in out_shape]
        if extend:
            out_shape, out_specs = out_shape + [state_shape], out_specs + [state_spec]
        return pl.pallas_call(
            functools.partial(second_kernel, resume, last, extend, grids),
            grid=grid,
            out_shape=out_shape,
            in_specs=[sel_spec, whole(*second_mat.shape), const_spec, hist_spec, state_spec, state_spec]
            + [counts_spec, sums_spec] * resume
            + [whole(*row_probs.shape)] * last,
            out_specs=out_specs,
            scratch_shapes=scratch,
            compiler_params=params(8 if grids == 1 else 32),
            name="second_pass",
        )(
            sel, second_mat, consts, hist, own_state, state_in,
            *(sums_in if resume else []),
            *([row_probs] if last else []),
        )

    def hand_over(state, stage):
        moves = [(stage, stage + 1), (sides - 1 - stage, sides - 2 - stage)]
        return lax.ppermute(state, "per", moves)

    if sides == 2:
        kept = [first_pass(index, None) for index in range(parts)]
        arrived = [hand_over(each[1], 0) for each in kept]
        second_mat, row_probs = prep_second(kept[-1][1])
        sums = None
        for index in range(parts):
            sums = second_pass(kept[index], arrived[index], sums, index == parts - 1, False)
        mine, other = sums
    else:
        kept = [jnp.zeros(x.shape, x.dtype) for x in (hist_shape, state_shape, sel_shape)]
        done = [jnp.zeros(x.shape, x.dtype) for x in (swap_shape, swap_shape, state_shape)]
        state = None
        second_mat, row_probs = prep_second(gathered)
        for stage in range(sides):
            active = (side == stage) | (side == sides - 1 - stage)
            if stage < sides // 2:
                kept = lax.cond(
                    active, lambda x, kept: list(first_pass(0, x)), lambda x, kept: kept, state, kept
                )
                state = kept[1]
            else:
                done = lax.cond(
                    active,
                    lambda x, done: list(second_pass(kept, x, None, True, True)),
                    lambda x, done: done,
                    state,
                    done,
                )
                state = done[2]
            if stage < sides - 1:
                state = hand_over(state, stage)
        mine, other, _ = done
        total = jnp.where(side == sides // 2, mine[steps * rows], 0.0)
        total = lax.psum(total, "per")
        mine = mine.at[steps * rows].set(total)
        other = other.at[steps * rows].set(total)
    received = lax.ppermute(other, "st", swap)
    trans_grad, mean_loglik = pl.pallas_call(
        functools.partial(finish_kernel, float(states * states * periods)),
        out_shape=[shaped((steps * rows, LANES), F32), shaped((1,), F32)],
        in_specs=[vmem(), vmem()],
        out_specs=[vmem(), smem()],
        compiler_params=params(4),
        name="finish",
    )(mine, received)
    return (trans_grad.reshape(steps, rows, LANES), mean_loglik)


def solution(mesh):
    placed = (
        P(("hh", "per"), None),
        P(("hh", "per")),
        P(("hh", "per")),
        P(("hh", "per")),
        P(("grp", "per", "st"), None, None),
        P("grp"),
        P("grp"),
        P("grp"),
    )
    return jax.shard_map(
        per_device,
        mesh=mesh,
        in_specs=placed,
        out_specs=(P(("grp", "per"), "hh", "st"), P("grp")),
        check_vma=False,
    )
```

```python
import functools

import jax
import jax.numpy as jnp
from jax import lax
from jax.experimental import pallas as pl
from jax.experimental.pallas import tpu as pltpu
from jax.sharding import PartitionSpec as P

HB = 128
LANES = 128
HALF = HB // 2
SEEN = 16.0
F32 = jnp.float32
BF16 = jnp.bfloat16
LOG2E = 1.4426950408889634
LN2 = 0.6931471805599453
EXTRA = 16


def vmem():
    return pl.BlockSpec(memory_space=pltpu.VMEM)


def smem():
    return pl.BlockSpec(memory_space=pltpu.SMEM)


def hbm():
    return pl.BlockSpec(memory_space=pltpu.HBM)


def in_hbm(*arrays):
    return [pltpu.with_memory_space_constraint(x, pltpu.HBM) for x in arrays]


def params(mebibytes):
    return pltpu.CompilerParams(vmem_limit_bytes=mebibytes * 1024 * 1024)


def core_index():
    return lax.axis_index("st")


def is_forward_first():
    return 2 * lax.axis_index("per") < lax.axis_size("per")


def tiles(width):
    return [slice(q, q + LANES) for q in range(0, width, LANES)]


def fetch(pairs, sems):
    copies = [pltpu.make_async_copy(src, dst, sems.at[i]) for i, (src, dst) in enumerate(pairs)]
    for copy in copies:
        copy.start()
    for copy in copies:
        copy.wait()


def pack_kernel(count_ref, earn_any, start_any, len_any, out_ref, earn_ref, start_ref, len_ref, sems):
    fetch(((earn_any, earn_ref), (start_any, start_ref), (len_any, len_ref)), sems)
    periods, slot_rows = earn_ref.shape
    core = core_index()
    low_lane = lax.broadcasted_iota(jnp.int32, (periods // 2, HB), 1) < HALF
    time = lax.broadcasted_iota(jnp.int32, (periods, HB), 0)
    for slot in range(slot_rows // HB):
        cols = slice(slot * HB, (slot + 1) * HB)
        begin = start_ref[slot : slot + 1, :]
        seen = (time >= begin) & (time < begin + len_ref[slot : slot + 1, :])
        live = slot < count_ref[0]
        shift = jnp.where(live, jnp.where(seen, SEEN, 0.0), -SEEN)
        value = earn_ref[:, cols] + shift
        early, late = value[: periods // 2], value[periods // 2 :]
        turned = pltpu.roll(jnp.where(core == 0, late, early), HALF, 1)
        packed = jnp.where(low_lane, jnp.where(core == 0, early, turned), jnp.where(core == 0, turned, late))
        for to in range(out_ref.shape[0]):
            out_ref[to, :, cols] = packed


def put(ref, at, value):
    states = value.shape[0]
    high = value.astype(BF16)
    ref[at, :states, :states] = high
    ref[at, :states, states:] = (value - high.astype(F32)).astype(BF16)


def both_halves(mat, state):
    states = mat.shape[0]
    high = jnp.dot(mat[:, :states], state, preferred_element_type=F32)
    return high + jnp.dot(mat[:, states:], state, preferred_element_type=F32)


def fill_periods(mat, turned_pass, source, ref):
    @pl.loop(0, ref.shape[0])
    def _(i):
        at = source * ref.shape[0] + i

        @pl.when(turned_pass)
        def _():
            lifted = jnp.exp(ref[i].T.astype(F32))
            put(mat, at, lifted * (1.0 / jnp.sum(lifted, axis=0, keepdims=True)))

        @pl.when(jnp.logical_not(turned_pass))
        def _():
            lifted = jnp.exp(ref[i].astype(F32))
            put(mat, at, lifted * (1.0 / jnp.sum(lifted, axis=1, keepdims=True)))


def prep_own_kernel(
    own_any, init_any, mean_any, sd_any, mat, consts, own_ref, init_ref, mean_ref, sd_ref, sem, sems
):
    copy = pltpu.make_async_copy(own_any, own_ref, sem)
    copy.start()
    fetch(((init_any, init_ref), (mean_any, mean_ref), (sd_any, sd_ref)), sems)
    raised = jnp.exp(init_ref[...])
    rows = (
        raised / jnp.sum(raised, axis=1, keepdims=True),
        mean_ref[...],
        (-0.5 * LOG2E) * jnp.exp(-2.0 * sd_ref[...]),
        -LOG2E * sd_ref[...],
    )
    for i, row in enumerate(rows):
        consts[i] = jnp.broadcast_to(row, (LANES, own_ref.shape[1])).T
    copy.wait()
    fill_periods(mat, is_forward_first(), core_index(), own_ref)


def prep_other_kernel(other_ref, mat_in, mat):
    fill_periods(mat, is_forward_first(), 1 - core_index(), other_ref)


def prep_second_kernel(own_ref, other_ref, after_any, mat, row_probs):
    rows = row_probs.shape[2]
    here = own_rows(lax.axis_index("hh") * rows, rows)
    for source, ref in ((core_index(), own_ref), (1 - core_index(), other_ref)):
        for i in range(ref.shape[0]):
            lifted = jnp.exp(ref[i, here, :].astype(F32))
            row_probs[source * ref.shape[0] + i] = (lifted * (1.0 / jnp.sum(lifted, axis=1, keepdims=True))).T
        fill_periods(mat, jnp.logical_not(is_forward_first()), source, ref)


def emission(sel_ref, consts, step_now, cols, less=None):
    gap = sel_ref[0, step_now, :1, cols] - consts[1]
    power = gap * gap * consts[2] + consts[3]
    return jnp.exp2(power if less is None else power - less)


def is_moving(sel_ref, step_now, cols):
    return sel_ref[1, step_now, :1, cols] > 0.5


def is_seen(sel_ref, step_now, cols):
    return sel_ref[2, step_now, :1, cols] > 0.5


def column_sum(x):
    return jnp.sum(x, axis=0, keepdims=True)


def own_rows(row_begin, rows):
    return pl.ds(pl.multiple_of(row_begin, rows), rows)


def outer_sum(carried, weights_ref):
    return lax.dot_general(carried, weights_ref[...], (((1,), (1,)), ((), ())), preferred_element_type=F32)


def run_forward(lead, mat, hist, sel_ref, consts, ab_ref, logs, second=None, fresh=False):
    steps, states, width = hist.shape
    cuts = tiles(width)
    inverse = [1.0 / column_sum(ab_ref[:, cols].astype(F32)) for cols in cuts]
    for k in range(steps):
        step_now = lead + k
        if second is None:
            hist[k] = ab_ref[...]
        else:
            weights_ref, row_begin, add_counts = second
            own_alpha = ab_ref[own_rows(row_begin, weights_ref.shape[0]), :].astype(F32)
        for q, cols in enumerate(cuts):
            begins = fresh and k == 0
            if not begins:
                moved = both_halves(mat[k], ab_ref[:, cols]) * inverse[q]
                moving = is_moving(sel_ref, step_now, cols)
            if second is not None:
                total = column_sum(moved * hist[k, :, cols].astype(F32))
                weight = jnp.where(moving, 1.0 / total, 0.0)
                weights_ref[:, cols] = (own_alpha[:, cols] * inverse[q] * weight).astype(BF16)
            emit = emission(sel_ref, consts, step_now, cols)
            joint = (consts[0] if begins else jnp.where(moving, moved, consts[0])) * emit
            scale = column_sum(joint)
            if second is None:
                seen = is_seen(sel_ref, step_now, cols)
                logs[q] = logs[q] + jnp.where(seen, jnp.log2(scale), 0.0)
            inverse[q] = 1.0 / scale
            ab_ref[:, cols] = joint.astype(BF16)
        if second is not None:
            add_counts(k, outer_sum(hist[k], weights_ref))
    return logs


def run_backward(lead, mat, hist, sel_ref, consts, state, ub_ref, logs, leave, second=None, between=None):
    steps, states, width = hist.shape
    cuts = tiles(width)
    rest = [x[:1] for x in state]
    size = [jnp.zeros((1, LANES), F32) for _ in cuts]

    def step(k):
        step_now = lead + k
        grown = []
        for q, cols in enumerate(cuts):
            emit = emission(sel_ref, consts, step_now, cols, size[q] if second is None else None)
            carried = emit * state[q]
            ub_ref[:, cols] = carried.astype(BF16)
            whole = column_sum(carried)
            grown.append(whole)
            if second is None:
                size[q] = jnp.log2(whole)
                seen = is_seen(sel_ref, step_now, cols)
                logs[q] = logs[q] + jnp.where(seen, size[q], 0.0)
                begun = column_sum(carried * consts[0]) / whole
                rest[q] = jnp.where(seen, begun, rest[q])
        if second is None:
            hist[k] = ub_ref[...]
        else:
            weights_ref, row_begin, add_counts = second
            own_alpha = hist[k, own_rows(row_begin, weights_ref.shape[0]), :].astype(F32)
        for q, cols in enumerate(cuts):
            product = both_halves(mat[k], ub_ref[:, cols])
            moving = is_moving(sel_ref, step_now, cols)
            if second is None:
                state[q] = jnp.where(moving, product, rest[q] * grown[q])
            else:
                shrink = 1.0 / grown[q]
                product = product * shrink
                total = column_sum(product * hist[k, :, cols].astype(F32))
                weight = jnp.where(moving, 1.0 / total, 0.0)
                weights_ref[:, cols] = (own_alpha[:, cols] * weight * shrink).astype(BF16)
                state[q] = jnp.where(moving, product, rest[q])
        if second is not None:
            add_counts(k, outer_sum(ub_ref[...], weights_ref))

    def left():
        return [x * jnp.exp2(-y) for x, y in zip(state, size)]

    for k in reversed(range(1, steps)):
        step(k)
    if second is None:
        step(0)
        leave(left())
        return
    between()

    @pl.when(lead > 0)
    def _():
        step(0)
        leave(left())

    @pl.when(lead == 0)
    def _():
        second[2](0, jnp.zeros((states, second[0].shape[0]), F32))


def put_state(state_out, values, logs):
    states = state_out.shape[0] - EXTRA
    row = lax.broadcasted_iota(jnp.int32, (EXTRA, LANES), 0)
    for q, cols in enumerate(tiles(state_out.shape[1])):
        state_out[:states, cols] = values[q].astype(BF16)
        high = logs[q].astype(BF16).astype(F32)
        middle = (logs[q] - high).astype(BF16).astype(F32)
        piece = jnp.where(
            row == 0, high, jnp.where(row == 1, middle, jnp.where(row == 2, logs[q] - high - middle, 0.0))
        )
        state_out[states:, cols] = piece.astype(BF16)


def state_logs(state_ref):
    states = state_ref.shape[0] - EXTRA
    return [column_sum(state_ref[states:, cols].astype(F32)) for cols in tiles(state_ref.shape[1])]


def first_kernel(resume, grids, part, rows_ref, mat, consts, *refs):
    state_in = refs[0] if resume else None
    hist, state_out, sel_ref, ab_ref = refs[-4:]
    chunk = part * grids + (pl.program_id(0) if grids > 1 else 0)
    steps, states, width = hist.shape
    forward_first, lead = is_forward_first(), lax.axis_index("per") * steps
    cuts = tiles(width)
    group, half_periods, slot_rows = rows_ref.shape
    tops = 2 * len(cuts)

    def scan_source(d, carry):
        rank, picked = carry
        for slot in range(slot_rows // HB):
            cols = slice(slot * HB, (slot + 1) * HB)
            block = rows_ref[d, :, cols]
            live = block > -0.5 * SEEN
            picked = [jnp.where(live & (rank == chunk * tops + i), block, old) for i, old in enumerate(picked)]
            rank = rank + live.astype(jnp.int32)
        return rank, picked

    carry = (jnp.zeros((half_periods, HB), jnp.int32), [jnp.zeros((half_periods, HB), F32)] * tops)
    if group <= 8:
        for d in range(group):
            carry = scan_source(d, carry)
    else:
        carry = lax.fori_loop(0, group, scan_source, carry)
    low_lane = lax.broadcasted_iota(jnp.int32, (half_periods, HB), 1) < HALF
    for q, cols in enumerate(cuts):
        left, right = carry[1][2 * q], carry[1][2 * q + 1]
        before = jnp.zeros((1, HB), F32)
        for late in range(2):
            value = (
                jnp.where(low_lane, pltpu.roll(left, HALF, 1), right)
                if late
                else jnp.where(low_lane, left, pltpu.roll(right, HALF, 1))
            )
            seen = value > 0.5 * SEEN
            earn = jnp.where(seen, value - SEEN, value)
            seen = seen.astype(F32)
            for i in range(half_periods):
                at = late * half_periods + i
                now = seen[i : i + 1]
                sel_ref[0, at, :, cols] = jnp.broadcast_to(earn[i : i + 1], (8, HB))
                sel_ref[1, at, :, cols] = jnp.broadcast_to(now * before, (8, HB))
                sel_ref[2, at, :, cols] = jnp.broadcast_to(now, (8, HB))
                before = now
    zeros = [jnp.zeros((1, LANES), F32) for _ in cuts]

    @pl.when(forward_first)
    def _():
        if resume:
            ab_ref[...] = state_in[:states, :]
        else:
            for cols in cuts:
                ab_ref[:, cols] = consts[0].astype(BF16)
        logs = state_logs(state_in) if resume else list(zeros)
        fresh = lax.axis_size("per") == 2
        run_forward(lead, mat, hist, sel_ref, consts, ab_ref, logs, fresh=fresh)
        put_state(state_out, [ab_ref[:, cols] for cols in cuts], logs)

    @pl.when(jnp.logical_not(forward_first))
    def _():
        state = [
            state_in[:states, cols].astype(F32) if resume else jnp.ones((states, LANES), F32) for cols in cuts
        ]
        logs = state_logs(state_in) if resume else list(zeros)
        leave = lambda values: put_state(state_out, values, logs)
        run_backward(lead, mat, hist, sel_ref, consts, state, ab_ref, logs, leave)


def second_kernel(resume, last, extend, grids, *refs):
    refs = list(refs)
    sel_ref, mat, consts, hist, own_state, state_in = (refs.pop(0) for _ in range(6))
    counts_in, sums_in = (refs.pop(0), refs.pop(0)) if resume else (None, None)
    row_probs = refs.pop(0) if last else None
    mine_ref, other_ref = (refs.pop(0), refs.pop(0)) if last else (None, None)
    counts_out, sums_out = (None, None) if last else (refs.pop(0), refs.pop(0))
    state_out = refs.pop(0) if extend else None
    ab_ref, weights_ref = refs[:2]
    counts_ref, sums_ref = refs[2:] if last else (counts_out, sums_out)
    chunk = pl.program_id(0) if grids > 1 else 0
    steps, states, width = hist.shape
    core, forward_first = core_index(), is_forward_first()
    row_begin = lax.axis_index("hh") * weights_ref.shape[0]
    lead = lax.axis_index("per") * steps
    rows = weights_ref.shape[0]

    def centre(k, counts):
        probs = row_probs[k]
        weighted = probs * counts
        grad = weighted - probs * column_sum(weighted)
        half = states // 2
        beside = mine_ref.shape[1] // rows
        at = slice(k // beside * half, (k // beside + 1) * half)
        cols = slice(k % beside * rows, (k % beside + 1) * rows)
        mine_ref[at, cols] = jnp.where(core == 0, grad[:half], grad[half:])
        other_ref[at, cols] = jnp.where(core == 0, grad[half:], grad[:half])

    def add_counts(k, counts):
        if grids > 1:
            counts_ref[k] += counts
            return
        if resume:
            counts = counts + counts_in[k]
        if last:
            centre(k, counts)
        else:
            counts_ref[k] = counts

    second = (weights_ref, row_begin, add_counts)

    @pl.when(chunk == 0)
    def _():
        if grids > 1:
            counts_ref[...] = jnp.zeros_like(counts_ref)
        sums_ref[...] = sums_in[...] if resume else jnp.zeros_like(sums_ref)

    def add_sums(alpha_ref, other_state):
        total = jnp.zeros((1, LANES), F32)
        years = jnp.zeros((8, LANES), F32)
        for cols, here, there in zip(tiles(width), state_logs(alpha_ref), state_logs(other_state)):
            alpha = alpha_ref[:states, cols].astype(F32)
            meet = column_sum(alpha * other_state[:states, cols].astype(F32))
            total += (here + there + jnp.log2(meet / column_sum(alpha))) * LN2
            years += jnp.sum(sel_ref[2, :, :, cols], axis=0)
        total = jnp.broadcast_to(jnp.sum(total, axis=1, keepdims=True), (1, LANES))
        years = jnp.broadcast_to(jnp.sum(years[:1], axis=1, keepdims=True), (1, LANES))
        row = lax.broadcasted_iota(jnp.int32, (8, LANES), 0)
        sums_ref[...] += jnp.where(row == 0, total, jnp.where(row == 1, years, 0.0))

    zeros = [jnp.zeros((1, LANES), F32) for _ in tiles(width)]

    @pl.when(jnp.logical_not(forward_first))
    def _():
        ab_ref[...] = state_in[:states, :]
        run_forward(lead, mat, hist, sel_ref, consts, ab_ref, list(zeros), second)
        add_sums(state_in, own_state)
        if extend:
            put_state(state_out, [ab_ref[:, cols] for cols in tiles(width)], zeros)

    @pl.when(forward_first)
    def _():
        state = [state_in[:states, cols].astype(F32) for cols in tiles(width)]
        leave = lambda values: put_state(state_out, values, zeros) if extend else None
        run_backward(lead, mat, hist, sel_ref, consts, state, ab_ref, list(zeros), leave, second, lambda: add_sums(own_state, state_in))

    if last:

        @pl.when(chunk == grids - 1)
        def _():
            if grids > 1:
                for k in range(steps):
                    centre(k, counts_ref[k])
            tail = mine_ref.shape[0] - 8
            mine_ref[tail:, :] = sums_ref[:, : mine_ref.shape[1]]
            other_ref[tail:, :] = sums_ref[:, : mine_ref.shape[1]]


def finish_kernel(scale, mine_ref, other_ref, grad_ref, mean_ref):
    count, beside = mine_ref.shape
    count -= 8
    total = mine_ref[count : count + 1, :] + other_ref[count : count + 1, :]
    years = mine_ref[count + 1 : count + 2, :] + other_ref[count + 1 : count + 2, :]
    half = grad_ref.shape[1]
    for at in range(count // half):
        here = slice(at * half, (at + 1) * half)
        grad = (mine_ref[here, :] + other_ref[here, :]) * (scale / years)
        grad_ref[at * beside : (at + 1) * beside, :] = grad.T
    mean_ref[0] = (total / years)[0, 0]


def per_device(
    earnings, starts, lengths, block_count, trans_logits, init_logits, state_mean, log_sd
):
    slot_rows, periods = earnings.shape
    states = init_logits.shape[0]
    group = lax.axis_size(("hh", "per"))
    sides = lax.axis_size("per")
    cores = lax.axis_size("st")
    part = trans_logits.shape[0]
    steps = part * cores
    rows = states // lax.axis_size("hh")
    households = group * HB // cores
    parts = 2 if households <= 4 * HB else 1
    share = households // parts
    width = min(2 * HB, share)
    grids = share // width
    side = lax.axis_index("per")
    shaped = jax.ShapeDtypeStruct
    dma = pltpu.SemaphoreType.DMA

    swap = [(0, 1), (1, 0)]
    vec_row = pltpu.VMEM((1, states), F32)
    slots = pltpu.VMEM((slot_rows // HB, HB), jnp.int32)
    packed = pl.pallas_call(
        pack_kernel,
        out_shape=pltpu.VMEM((group, periods // 2, slot_rows), F32),
        in_specs=[smem()] + [hbm()] * 3,
        out_specs=vmem(),
        scratch_shapes=[pltpu.VMEM((periods, slot_rows), F32), slots, slots, dma((3,))],
        compiler_params=params(2),
        name="pack",
    )(block_count, *in_hbm(earnings.T, starts.reshape(-1, HB), lengths.reshape(-1, HB)))
    packed, later_logits = lax.optimization_barrier((packed, trans_logits))
    other_logits = lax.ppermute(later_logits, "st", swap)
    along = group // sides
    centre = along // 2
    outward = sorted(range(along), key=lambda z: (abs(z - centre), -z))
    listed = [z * sides + x for z in outward for x in reversed(range(sides))]
    gathered = lax.all_to_all(
        packed, ("hh", "per", "st"), split_axis=0, concat_axis=0,
        axis_index_groups=[[n * cores + c for n in listed] for c in range(cores)], tiled=True,
    )
    mat_shape = shaped((steps, states, 2 * states), BF16)
    first_mat, consts = pl.pallas_call(
        prep_own_kernel,
        out_shape=[pltpu.VMEM(mat_shape.shape, BF16), pltpu.VMEM((4, states, LANES), F32)],
        in_specs=[hbm()] * 4,
        out_specs=[vmem(), vmem()],
        scratch_shapes=[pltpu.VMEM(trans_logits.shape, BF16), vec_row, vec_row, vec_row, dma, dma((3,))],
        compiler_params=params(4),
        name="prep_own",
    )(
        *in_hbm(
            trans_logits,
            init_logits.reshape(1, states), state_mean.reshape(1, states), log_sd.reshape(1, states),
        )
    )
    first_mat = pl.pallas_call(
        prep_other_kernel,
        out_shape=pltpu.VMEM(mat_shape.shape, BF16),
        in_specs=[vmem(), vmem()],
        out_specs=vmem(),
        input_output_aliases={1: 0},
        compiler_params=params(4),
        name="prep_other",
    )(other_logits, first_mat)

    def prep_second(after):
        return pl.pallas_call(
            prep_second_kernel,
            out_shape=[mat_shape, shaped((steps, states, rows), F32)],
            in_specs=[vmem(), vmem(), hbm()],
            out_specs=[vmem(), vmem()],
            compiler_params=params(4),
            name="prep_second",
        )(trans_logits, other_logits, after)

    def whole(*shape):
        if grids == 1:
            return vmem()
        return pl.BlockSpec(shape, lambda g: (0,) * len(shape))

    def lanes(*lead):
        if grids == 1:
            return vmem()
        return pl.BlockSpec(lead + (width,), lambda g: (0,) * len(lead) + (g,))

    grid = (grids,) if grids > 1 else ()
    hist_shape = shaped((steps, states, share), BF16)
    state_shape = shaped((states + EXTRA, share), BF16)
    sel_shape = shaped((3, periods, 8, share), F32)
    beside = min(LANES, steps * rows)
    swap_shape = shaped((steps * rows // beside * (states // cores) + 8, beside), F32)
    counts_shape = shaped((steps, states, rows), F32)
    sums_shape = shaped((8, LANES), F32)
    hist_spec, state_spec, sel_spec = lanes(steps, states), lanes(states + EXTRA), lanes(3, periods, 8)
    const_spec = whole(4, states, LANES)

    def first_pass(index, state_in):
        resume = state_in is not None
        return pl.pallas_call(
            functools.partial(first_kernel, resume, grids, index),
            grid=grid,
            out_shape=[hist_shape, state_shape, sel_shape],
            in_specs=[whole(*gathered.shape), whole(*first_mat.shape), const_spec]
            + [state_spec] * resume,
            out_specs=[hist_spec, state_spec, sel_spec],
            scratch_shapes=[pltpu.VMEM((states, width), BF16)],
            compiler_params=params(8 if grids == 1 else 32),
            name="first_pass",
        )(gathered, first_mat, consts, *([state_in] if resume else []))

    def second_pass(kept, state_in, sums_in, last, extend):
        hist, own_state, sel = kept
        resume = sums_in is not None
        scratch = [
            pltpu.VMEM((states, width), BF16),
            pltpu.VMEM((rows, width), BF16),
        ]
        counts_spec, sums_spec = whole(*counts_shape.shape), whole(*sums_shape.shape)
        if last:
            out_shape = [swap_shape] * 2
            scratch += [pltpu.VMEM(counts_shape.shape, F32), pltpu.VMEM(sums_shape.shape, F32)]
        else:
            out_shape = [counts_shape, sums_shape]
        out_specs = [whole(*x.shape) for x in out_shape]
        if extend:
            out_shape, out_specs = out_shape + [state_shape], out_specs + [state_spec]
        return pl.pallas_call(
            functools.partial(second_kernel, resume, last, extend, grids),
            grid=grid,
            out_shape=out_shape,
            in_specs=[sel_spec, whole(*second_mat.shape), const_spec, hist_spec, state_spec, state_spec]
            + [counts_spec, sums_spec] * resume
            + [whole(*row_probs.shape)] * last,
            out_specs=out_specs,
            scratch_shapes=scratch,
            compiler_params=params(8 if grids == 1 else 32),
            name="second_pass",
        )(
            sel, second_mat, consts, hist, own_state, state_in,
            *(sums_in if resume else []),
            *([row_probs] if last else []),
        )

    def hand_over(state, stage):
        moves = [(stage, stage + 1), (sides - 1 - stage, sides - 2 - stage)]
        return lax.ppermute(state, "per", moves)

    if sides == 2:
        kept = [first_pass(index, None) for index in range(parts)]
        arrived = [hand_over(each[1], 0) for each in kept]
        second_mat, row_probs = prep_second(kept[-1][1])
        sums = None
        for index in range(parts):
            sums = second_pass(kept[index], arrived[index], sums, index == parts - 1, False)
        mine, other = sums
    else:
        kept = [jnp.zeros(x.shape, x.dtype) for x in (hist_shape, state_shape, sel_shape)]
        done = [jnp.zeros(x.shape, x.dtype) for x in (swap_shape, swap_shape, state_shape)]
        state = None
        second_mat, row_probs = prep_second(gathered)
        for stage in range(sides):
            active = (side == stage) | (side == sides - 1 - stage)
            if stage < sides // 2:
                kept = lax.cond(
                    active, lambda x, kept: list(first_pass(0, x)), lambda x, kept: kept, state, kept
                )
                state = kept[1]
            else:
                done = lax.cond(
                    active,
                    lambda x, done: list(second_pass(kept, x, None, True, True)),
                    lambda x, done: done,
                    state,
                    done,
                )
                state = done[2]
            if stage < sides - 1:
                state = hand_over(state, stage)
        mine, other, _ = done
        total = jnp.where(side == sides // 2, mine[-8], 0.0)
        total = lax.psum(total, "per")
        mine = mine.at[-8].set(total)
        other = other.at[-8].set(total)
    received = lax.ppermute(other, "st", swap)
    trans_grad, mean_loglik = pl.pallas_call(
        functools.partial(finish_kernel, float(states * states * periods)),
        out_shape=[shaped((steps * rows, LANES), F32), shaped((1,), F32)],
        in_specs=[vmem(), vmem()],
        out_specs=[vmem(), smem()],
        compiler_params=params(4),
        name="finish",
    )(mine, received)
    return (trans_grad.reshape(steps, rows, LANES), mean_loglik)


def solution(mesh):
    placed = (
        P(("hh", "per"), None),
        P(("hh", "per")),
        P(("hh", "per")),
        P(("hh", "per")),
        P(("grp", "per", "st"), None, None),
        P("grp"),
        P("grp"),
        P("grp"),
    )
    return jax.shard_map(
        per_device,
        mesh=mesh,
        in_specs=placed,
        out_specs=(P(("grp", "per"), "hh", "st"), P("grp")),
        check_vma=False,
    )
```

```python
import functools

import jax
import jax.numpy as jnp
from jax import lax
from jax.experimental import pallas as pl
from jax.experimental.pallas import tpu as pltpu
from jax.sharding import PartitionSpec as P

HB = 128
LANES = 128
HALF = HB // 2
SEEN = 16.0
F32 = jnp.float32
BF16 = jnp.bfloat16
LOG2E = 1.4426950408889634
LN2 = 0.6931471805599453
EXTRA = 16


def vmem():
    return pl.BlockSpec(memory_space=pltpu.VMEM)


def smem():
    return pl.BlockSpec(memory_space=pltpu.SMEM)


def hbm():
    return pl.BlockSpec(memory_space=pltpu.HBM)


def in_hbm(*arrays):
    return [pltpu.with_memory_space_constraint(x, pltpu.HBM) for x in arrays]


def params(mebibytes):
    return pltpu.CompilerParams(vmem_limit_bytes=mebibytes * 1024 * 1024)


def core_index():
    return lax.axis_index("st")


def is_forward_first():
    return 2 * lax.axis_index("per") < lax.axis_size("per")


def tiles(width):
    return [slice(q, q + LANES) for q in range(0, width, LANES)]


def fetch(pairs, sems):
    copies = [pltpu.make_async_copy(src, dst, sems.at[i]) for i, (src, dst) in enumerate(pairs)]
    for copy in copies:
        copy.start()
    for copy in copies:
        copy.wait()


def pack_kernel(count_ref, earn_any, start_any, len_any, out_ref, earn_ref, start_ref, len_ref, sems):
    fetch(((earn_any, earn_ref), (start_any, start_ref), (len_any, len_ref)), sems)
    periods, slot_rows = earn_ref.shape
    core = core_index()
    low_lane = lax.broadcasted_iota(jnp.int32, (periods // 2, HB), 1) < HALF
    time = lax.broadcasted_iota(jnp.int32, (periods, HB), 0)
    for slot in range(slot_rows // HB):
        cols = slice(slot * HB, (slot + 1) * HB)
        begin = start_ref[slot : slot + 1, :]
        seen = (time >= begin) & (time < begin + len_ref[slot : slot + 1, :])
        live = slot < count_ref[0]
        shift = jnp.where(live, jnp.where(seen, SEEN, 0.0), -SEEN)
        value = earn_ref[:, cols] + shift
        early, late = value[: periods // 2], value[periods // 2 :]
        turned = pltpu.roll(jnp.where(core == 0, late, early), HALF, 1)
        packed = jnp.where(low_lane, jnp.where(core == 0, early, turned), jnp.where(core == 0, turned, late))
        for to in range(out_ref.shape[0]):
            out_ref[to, :, cols] = packed


def put(ref, at, value):
    states = value.shape[0]
    high = value.astype(BF16)
    ref[at, :states, :states] = high
    ref[at, :states, states:] = (value - high.astype(F32)).astype(BF16)


def both_halves(mat, state):
    states = mat.shape[0]
    high = jnp.dot(mat[:, :states], state, preferred_element_type=F32)
    return high + jnp.dot(mat[:, states:], state, preferred_element_type=F32)


def fill_periods(mat, turned_pass, source, ref):
    @pl.loop(0, ref.shape[0])
    def _(i):
        at = source * ref.shape[0] + i

        @pl.when(turned_pass)
        def _():
            lifted = jnp.exp(ref[i].T.astype(F32))
            put(mat, at, lifted * (1.0 / jnp.sum(lifted, axis=0, keepdims=True)))

        @pl.when(jnp.logical_not(turned_pass))
        def _():
            lifted = jnp.exp(ref[i].astype(F32))
            put(mat, at, lifted * (1.0 / jnp.sum(lifted, axis=1, keepdims=True)))


def prep_own_kernel(
    own_any, init_any, mean_any, sd_any, mat, consts, own_ref, init_ref, mean_ref, sd_ref, sem, sems
):
    copy = pltpu.make_async_copy(own_any, own_ref, sem)
    copy.start()
    fetch(((init_any, init_ref), (mean_any, mean_ref), (sd_any, sd_ref)), sems)
    raised = jnp.exp(init_ref[...])
    rows = (
        raised / jnp.sum(raised, axis=1, keepdims=True),
        mean_ref[...],
        (-0.5 * LOG2E) * jnp.exp(-2.0 * sd_ref[...]),
        -LOG2E * sd_ref[...],
    )
    for i, row in enumerate(rows):
        consts[i] = jnp.broadcast_to(row, (LANES, own_ref.shape[1])).T
    copy.wait()
    fill_periods(mat, is_forward_first(), core_index(), own_ref)


def prep_other_kernel(other_ref, mat_in, mat):
    fill_periods(mat, is_forward_first(), 1 - core_index(), other_ref)


def prep_second_kernel(own_ref, other_ref, after_any, mat, row_probs):
    rows = row_probs.shape[1]
    here = own_rows(lax.axis_index("hh") * rows, rows)
    for source, ref in ((core_index(), own_ref), (1 - core_index(), other_ref)):
        for i in range(ref.shape[0]):
            lifted = jnp.exp(ref[i, here, :].astype(F32))
            row_probs[source * ref.shape[0] + i] = lifted * (1.0 / jnp.sum(lifted, axis=1, keepdims=True))
        fill_periods(mat, jnp.logical_not(is_forward_first()), source, ref)


def emission(sel_ref, consts, step_now, cols, less=None):
    gap = sel_ref[0, step_now, :1, cols] - consts[1]
    power = gap * gap * consts[2] + consts[3]
    return jnp.exp2(power if less is None else power - less)


def is_moving(sel_ref, step_now, cols):
    return sel_ref[1, step_now, :1, cols] > 0.5


def is_seen(sel_ref, step_now, cols):
    return sel_ref[2, step_now, :1, cols] > 0.5


def column_sum(x):
    return jnp.sum(x, axis=0, keepdims=True)


def own_rows(row_begin, rows):
    return pl.ds(pl.multiple_of(row_begin, rows), rows)


def outer_sum(weights_ref, carried):
    return lax.dot_general(weights_ref[...], carried, (((1,), (1,)), ((), ())), preferred_element_type=F32)


def run_forward(lead, mat, hist, sel_ref, consts, ab_ref, logs, second=None, fresh=False):
    steps, states, width = hist.shape
    cuts = tiles(width)
    inverse = [1.0 / column_sum(ab_ref[:, cols].astype(F32)) for cols in cuts]
    for k in range(steps):
        step_now = lead + k
        if second is None:
            hist[k] = ab_ref[...]
        else:
            weights_ref, row_begin, add_counts = second
            own_alpha = ab_ref[own_rows(row_begin, weights_ref.shape[0]), :].astype(F32)
        for q, cols in enumerate(cuts):
            begins = fresh and k == 0
            if not begins:
                moved = both_halves(mat[k], ab_ref[:, cols]) * inverse[q]
                moving = is_moving(sel_ref, step_now, cols)
            if second is not None:
                total = column_sum(moved * hist[k, :, cols].astype(F32))
                weight = jnp.where(moving, 1.0 / total, 0.0)
                weights_ref[:, cols] = (own_alpha[:, cols] * inverse[q] * weight).astype(BF16)
            emit = emission(sel_ref, consts, step_now, cols)
            joint = (consts[0] if begins else jnp.where(moving, moved, consts[0])) * emit
            scale = column_sum(joint)
            if second is None:
                seen = is_seen(sel_ref, step_now, cols)
                logs[q] = logs[q] + jnp.where(seen, jnp.log2(scale), 0.0)
            inverse[q] = 1.0 / scale
            ab_ref[:, cols] = joint.astype(BF16)
        if second is not None:
            add_counts(k, outer_sum(weights_ref, hist[k]))
    return logs


def run_backward(lead, mat, hist, sel_ref, consts, state, ub_ref, logs, leave, second=None, between=None):
    steps, states, width = hist.shape
    cuts = tiles(width)
    rest = [x[:1] for x in state]
    size = [jnp.zeros((1, LANES), F32) for _ in cuts]

    def step(k):
        step_now = lead + k
        grown = []
        for q, cols in enumerate(cuts):
            emit = emission(sel_ref, consts, step_now, cols, size[q] if second is None else None)
            carried = emit * state[q]
            ub_ref[:, cols] = carried.astype(BF16)
            whole = column_sum(carried)
            grown.append(whole)
            if second is None:
                size[q] = jnp.log2(whole)
                seen = is_seen(sel_ref, step_now, cols)
                logs[q] = logs[q] + jnp.where(seen, size[q], 0.0)
                begun = column_sum(carried * consts[0]) / whole
                rest[q] = jnp.where(seen, begun, rest[q])
        if second is None:
            hist[k] = ub_ref[...]
        else:
            weights_ref, row_begin, add_counts = second
            own_alpha = hist[k, own_rows(row_begin, weights_ref.shape[0]), :].astype(F32)
        for q, cols in enumerate(cuts):
            product = both_halves(mat[k], ub_ref[:, cols])
            moving = is_moving(sel_ref, step_now, cols)
            if second is None:
                state[q] = jnp.where(moving, product, rest[q] * grown[q])
            else:
                shrink = 1.0 / grown[q]
                product = product * shrink
                total = column_sum(product * hist[k, :, cols].astype(F32))
                weight = jnp.where(moving, 1.0 / total, 0.0)
                weights_ref[:, cols] = (own_alpha[:, cols] * weight * shrink).astype(BF16)
                state[q] = jnp.where(moving, product, rest[q])
        if second is not None:
            add_counts(k, outer_sum(weights_ref, ub_ref[...]))

    def left():
        return [x * jnp.exp2(-y) for x, y in zip(state, size)]

    for k in reversed(range(1, steps)):
        step(k)
    if second is None:
        step(0)
        leave(left())
        return
    between()

    @pl.when(lead > 0)
    def _():
        step(0)
        leave(left())

    @pl.when(lead == 0)
    def _():
        second[2](0, jnp.zeros((second[0].shape[0], states), F32))


def put_state(state_out, values, logs):
    states = state_out.shape[0] - EXTRA
    row = lax.broadcasted_iota(jnp.int32, (EXTRA, LANES), 0)
    for q, cols in enumerate(tiles(state_out.shape[1])):
        state_out[:states, cols] = values[q].astype(BF16)
        high = logs[q].astype(BF16).astype(F32)
        middle = (logs[q] - high).astype(BF16).astype(F32)
        piece = jnp.where(
            row == 0, high, jnp.where(row == 1, middle, jnp.where(row == 2, logs[q] - high - middle, 0.0))
        )
        state_out[states:, cols] = piece.astype(BF16)


def state_logs(state_ref):
    states = state_ref.shape[0] - EXTRA
    return [column_sum(state_ref[states:, cols].astype(F32)) for cols in tiles(state_ref.shape[1])]


def first_kernel(resume, grids, part, rows_ref, mat, consts, *refs):
    state_in = refs[0] if resume else None
    hist, state_out, sel_ref, ab_ref = refs[-4:]
    chunk = part * grids + (pl.program_id(0) if grids > 1 else 0)
    steps, states, width = hist.shape
    forward_first, lead = is_forward_first(), lax.axis_index("per") * steps
    cuts = tiles(width)
    group, half_periods, slot_rows = rows_ref.shape
    tops = 2 * len(cuts)

    def scan_source(d, carry):
        rank, picked = carry
        for slot in range(slot_rows // HB):
            cols = slice(slot * HB, (slot + 1) * HB)
            block = rows_ref[d, :, cols]
            live = block > -0.5 * SEEN
            picked = [jnp.where(live & (rank == chunk * tops + i), block, old) for i, old in enumerate(picked)]
            rank = rank + live.astype(jnp.int32)
        return rank, picked

    carry = (jnp.zeros((half_periods, HB), jnp.int32), [jnp.zeros((half_periods, HB), F32)] * tops)
    if group <= 8:
        for d in range(group):
            carry = scan_source(d, carry)
    else:
        carry = lax.fori_loop(0, group, scan_source, carry)
    low_lane = lax.broadcasted_iota(jnp.int32, (half_periods, HB), 1) < HALF
    for q, cols in enumerate(cuts):
        left, right = carry[1][2 * q], carry[1][2 * q + 1]
        before = jnp.zeros((1, HB), F32)
        for late in range(2):
            value = (
                jnp.where(low_lane, pltpu.roll(left, HALF, 1), right)
                if late
                else jnp.where(low_lane, left, pltpu.roll(right, HALF, 1))
            )
            seen = value > 0.5 * SEEN
            earn = jnp.where(seen, value - SEEN, value)
            seen = seen.astype(F32)
            for i in range(half_periods):
                at = late * half_periods + i
                now = seen[i : i + 1]
                sel_ref[0, at, :, cols] = jnp.broadcast_to(earn[i : i + 1], (8, HB))
                sel_ref[1, at, :, cols] = jnp.broadcast_to(now * before, (8, HB))
                sel_ref[2, at, :, cols] = jnp.broadcast_to(now, (8, HB))
                before = now
    zeros = [jnp.zeros((1, LANES), F32) for _ in cuts]

    @pl.when(forward_first)
    def _():
        if resume:
            ab_ref[...] = state_in[:states, :]
        else:
            for cols in cuts:
                ab_ref[:, cols] = consts[0].astype(BF16)
        logs = state_logs(state_in) if resume else list(zeros)
        fresh = lax.axis_size("per") == 2
        run_forward(lead, mat, hist, sel_ref, consts, ab_ref, logs, fresh=fresh)
        put_state(state_out, [ab_ref[:, cols] for cols in cuts], logs)

    @pl.when(jnp.logical_not(forward_first))
    def _():
        state = [
            state_in[:states, cols].astype(F32) if resume else jnp.ones((states, LANES), F32) for cols in cuts
        ]
        logs = state_logs(state_in) if resume else list(zeros)
        leave = lambda values: put_state(state_out, values, logs)
        run_backward(lead, mat, hist, sel_ref, consts, state, ab_ref, logs, leave)


def second_kernel(resume, last, extend, grids, *refs):
    refs = list(refs)
    sel_ref, mat, consts, hist, own_state, state_in = (refs.pop(0) for _ in range(6))
    counts_in, sums_in = (refs.pop(0), refs.pop(0)) if resume else (None, None)
    row_probs = refs.pop(0) if last else None
    mine_ref, other_ref = (refs.pop(0), refs.pop(0)) if last else (None, None)
    counts_out, sums_out = (None, None) if last else (refs.pop(0), refs.pop(0))
    state_out = refs.pop(0) if extend else None
    ab_ref, weights_ref = refs[:2]
    counts_ref, sums_ref = refs[2:] if last else (counts_out, sums_out)
    chunk = pl.program_id(0) if grids > 1 else 0
    steps, states, width = hist.shape
    core, forward_first = core_index(), is_forward_first()
    row_begin = lax.axis_index("hh") * weights_ref.shape[0]
    lead = lax.axis_index("per") * steps
    rows = weights_ref.shape[0]

    def centre(k, counts):
        probs = row_probs[k]
        weighted = probs * counts
        grad = weighted - probs * jnp.sum(weighted, axis=1, keepdims=True)
        at = slice(k * rows, (k + 1) * rows)
        left, right = grad[:, :LANES], grad[:, LANES:]
        mine_ref[at, :] = jnp.where(core == 0, left, right)
        other_ref[at, :] = jnp.where(core == 0, right, left)

    def add_counts(k, counts):
        if grids > 1:
            counts_ref[k] += counts
            return
        if resume:
            counts = counts + counts_in[k]
        if last:
            centre(k, counts)
        else:
            counts_ref[k] = counts

    second = (weights_ref, row_begin, add_counts)

    @pl.when(chunk == 0)
    def _():
        if grids > 1:
            counts_ref[...] = jnp.zeros_like(counts_ref)
        sums_ref[...] = sums_in[...] if resume else jnp.zeros_like(sums_ref)

    def add_sums(alpha_ref, other_state):
        total = jnp.zeros((1, LANES), F32)
        years = jnp.zeros((8, LANES), F32)
        for cols, here, there in zip(tiles(width), state_logs(alpha_ref), state_logs(other_state)):
            alpha = alpha_ref[:states, cols].astype(F32)
            meet = column_sum(alpha * other_state[:states, cols].astype(F32))
            total += (here + there + jnp.log2(meet / column_sum(alpha))) * LN2
            years += jnp.sum(sel_ref[2, :, :, cols], axis=0)
        total = jnp.broadcast_to(jnp.sum(total, axis=1, keepdims=True), (1, LANES))
        years = jnp.broadcast_to(jnp.sum(years[:1], axis=1, keepdims=True), (1, LANES))
        row = lax.broadcasted_iota(jnp.int32, (8, LANES), 0)
        sums_ref[...] += jnp.where(row == 0, total, jnp.where(row == 1, years, 0.0))

    zeros = [jnp.zeros((1, LANES), F32) for _ in tiles(width)]

    @pl.when(jnp.logical_not(forward_first))
    def _():
        ab_ref[...] = state_in[:states, :]
        run_forward(lead, mat, hist, sel_ref, consts, ab_ref, list(zeros), second)
        add_sums(state_in, own_state)
        if extend:
            put_state(state_out, [ab_ref[:, cols] for cols in tiles(width)], zeros)

    @pl.when(forward_first)
    def _():
        state = [state_in[:states, cols].astype(F32) for cols in tiles(width)]
        leave = lambda values: put_state(state_out, values, zeros) if extend else None
        run_backward(lead, mat, hist, sel_ref, consts, state, ab_ref, list(zeros), leave, second, lambda: add_sums(own_state, state_in))

    if last:

        @pl.when(chunk == grids - 1)
        def _():
            if grids > 1:
                for k in range(steps):
                    centre(k, counts_ref[k])
            mine_ref[steps * rows :, :] = sums_ref[...]
            other_ref[steps * rows :, :] = sums_ref[...]


def finish_kernel(scale, mine_ref, other_ref, grad_ref, mean_ref):
    count = grad_ref.shape[0]
    total = mine_ref[count : count + 1, :] + other_ref[count : count + 1, :]
    years = mine_ref[count + 1 : count + 2, :] + other_ref[count + 1 : count + 2, :]
    grad_ref[...] = (mine_ref[:count, :] + other_ref[:count, :]) * (scale / years)
    mean_ref[0] = (total / years)[0, 0]


def per_device(
    earnings, starts, lengths, block_count, trans_logits, init_logits, state_mean, log_sd
):
    slot_rows, periods = earnings.shape
    states = init_logits.shape[0]
    group = lax.axis_size(("hh", "per"))
    sides = lax.axis_size("per")
    cores = lax.axis_size("st")
    part = trans_logits.shape[0]
    steps = part * cores
    rows = states // lax.axis_size("hh")
    households = group * HB // cores
    parts = 2 if households <= 4 * HB else 1
    share = households // parts
    width = min(2 * HB, share)
    grids = share // width
    side = lax.axis_index("per")
    shaped = jax.ShapeDtypeStruct
    dma = pltpu.SemaphoreType.DMA

    swap = [(0, 1), (1, 0)]
    vec_row = pltpu.VMEM((1, states), F32)
    slots = pltpu.VMEM((slot_rows // HB, HB), jnp.int32)
    packed = pl.pallas_call(
        pack_kernel,
        out_shape=pltpu.VMEM((group, periods // 2, slot_rows), F32),
        in_specs=[smem()] + [hbm()] * 3,
        out_specs=vmem(),
        scratch_shapes=[pltpu.VMEM((periods, slot_rows), F32), slots, slots, dma((3,))],
        compiler_params=params(2),
        name="pack",
    )(block_count, *in_hbm(earnings.T, starts.reshape(-1, HB), lengths.reshape(-1, HB)))
    packed, later_logits = lax.optimization_barrier((packed, trans_logits))
    other_logits = lax.ppermute(later_logits, "st", swap)
    gathered = lax.all_to_all(
        packed, ("hh", "per", "st"), split_axis=0, concat_axis=0,
        axis_index_groups=[[n * cores + c for n in reversed(range(group))] for c in range(cores)], tiled=True,
    )
    mat_shape = shaped((steps, states, 2 * states), BF16)
    first_mat, consts = pl.pallas_call(
        prep_own_kernel,
        out_shape=[pltpu.VMEM(mat_shape.shape, BF16), pltpu.VMEM((4, states, LANES), F32)],
        in_specs=[hbm()] * 4,
        out_specs=[vmem(), vmem()],
        scratch_shapes=[pltpu.VMEM(trans_logits.shape, BF16), vec_row, vec_row, vec_row, dma, dma((3,))],
        compiler_params=params(4),
        name="prep_own",
    )(
        *in_hbm(
            trans_logits,
            init_logits.reshape(1, states), state_mean.reshape(1, states), log_sd.reshape(1, states),
        )
    )
    first_mat = pl.pallas_call(
        prep_other_kernel,
        out_shape=pltpu.VMEM(mat_shape.shape, BF16),
        in_specs=[vmem(), vmem()],
        out_specs=vmem(),
        input_output_aliases={1: 0},
        compiler_params=params(4),
        name="prep_other",
    )(other_logits, first_mat)

    def prep_second(after):
        return pl.pallas_call(
            prep_second_kernel,
            out_shape=[mat_shape, shaped((steps, rows, states), F32)],
            in_specs=[vmem(), vmem(), hbm()],
            out_specs=[vmem(), vmem()],
            compiler_params=params(4),
            name="prep_second",
        )(trans_logits, other_logits, after)

    def whole(*shape):
        if grids == 1:
            return vmem()
        return pl.BlockSpec(shape, lambda g: (0,) * len(shape))

    def lanes(*lead):
        if grids == 1:
            return vmem()
        return pl.BlockSpec(lead + (width,), lambda g: (0,) * len(lead) + (g,))

    grid = (grids,) if grids > 1 else ()
    hist_shape = shaped((steps, states, share), BF16)
    state_shape = shaped((states + EXTRA, share), BF16)
    sel_shape = shaped((3, periods, 8, share), F32)
    swap_shape = shaped((steps * rows + 8, LANES), F32)
    counts_shape = shaped((steps, rows, states), F32)
    sums_shape = shaped((8, LANES), F32)
    hist_spec, state_spec, sel_spec = lanes(steps, states), lanes(states + EXTRA), lanes(3, periods, 8)
    const_spec = whole(4, states, LANES)

    def first_pass(index, state_in):
        resume = state_in is not None
        return pl.pallas_call(
            functools.partial(first_kernel, resume, grids, index),
            grid=grid,
            out_shape=[hist_shape, state_shape, sel_shape],
            in_specs=[whole(*gathered.shape), whole(*first_mat.shape), const_spec]
            + [state_spec] * resume,
            out_specs=[hist_spec, state_spec, sel_spec],
            scratch_shapes=[pltpu.VMEM((states, width), BF16)],
            compiler_params=params(8 if grids == 1 else 32),
            name="first_pass",
        )(gathered, first_mat, consts, *([state_in] if resume else []))

    def second_pass(kept, state_in, sums_in, last, extend):
        hist, own_state, sel = kept
        resume = sums_in is not None
        scratch = [
            pltpu.VMEM((states, width), BF16),
            pltpu.VMEM((rows, width), BF16),
        ]
        counts_spec, sums_spec = whole(*counts_shape.shape), whole(*sums_shape.shape)
        if last:
            out_shape = [swap_shape] * 2
            scratch += [pltpu.VMEM(counts_shape.shape, F32), pltpu.VMEM(sums_shape.shape, F32)]
        else:
            out_shape = [counts_shape, sums_shape]
        out_specs = [whole(*x.shape) for x in out_shape]
        if extend:
            out_shape, out_specs = out_shape + [state_shape], out_specs + [state_spec]
        return pl.pallas_call(
            functools.partial(second_kernel, resume, last, extend, grids),
            grid=grid,
            out_shape=out_shape,
            in_specs=[sel_spec, whole(*second_mat.shape), const_spec, hist_spec, state_spec, state_spec]
            + [counts_spec, sums_spec] * resume
            + [whole(*row_probs.shape)] * last,
            out_specs=out_specs,
            scratch_shapes=scratch,
            compiler_params=params(8 if grids == 1 else 32),
            name="second_pass",
        )(
            sel, second_mat, consts, hist, own_state, state_in,
            *(sums_in if resume else []),
            *([row_probs] if last else []),
        )

    def hand_over(state, stage):
        moves = [(stage, stage + 1), (sides - 1 - stage, sides - 2 - stage)]
        return lax.ppermute(state, "per", moves)

    if sides == 2:
        kept = [first_pass(index, None) for index in range(parts)]
        arrived = [hand_over(each[1], 0) for each in kept]
        second_mat, row_probs = prep_second(kept[-1][1])
        sums = None
        for index in range(parts):
            sums = second_pass(kept[index], arrived[index], sums, index == parts - 1, False)
        mine, other = sums
    else:
        kept = [jnp.zeros(x.shape, x.dtype) for x in (hist_shape, state_shape, sel_shape)]
        done = [jnp.zeros(x.shape, x.dtype) for x in (swap_shape, swap_shape, state_shape)]
        state = None
        second_mat, row_probs = prep_second(gathered)
        for stage in range(sides):
            active = (side == stage) | (side == sides - 1 - stage)
            if stage < sides // 2:
                kept = lax.cond(
                    active, lambda x, kept: list(first_pass(0, x)), lambda x, kept: kept, state, kept
                )
                state = kept[1]
            else:
                done = lax.cond(
                    active,
                    lambda x, done: list(second_pass(kept, x, None, True, True)),
                    lambda x, done: done,
                    state,
                    done,
                )
                state = done[2]
            if stage < sides - 1:
                state = hand_over(state, stage)
        mine, other, _ = done
        total = jnp.where(side == sides // 2, mine[steps * rows], 0.0)
        total = lax.psum(total, "per")
        mine = mine.at[steps * rows].set(total)
        other = other.at[steps * rows].set(total)
    received = lax.ppermute(other, "st", swap)
    trans_grad, mean_loglik = pl.pallas_call(
        functools.partial(finish_kernel, float(states * states * periods)),
        out_shape=[shaped((steps * rows, LANES), F32), shaped((1,), F32)],
        in_specs=[vmem(), vmem()],
        out_specs=[vmem(), smem()],
        compiler_params=params(4),
        name="finish",
    )(mine, received)
    return (trans_grad.reshape(steps, rows, LANES), mean_loglik)


def solution(mesh):
    placed = (
        P(("hh", "per"), None),
        P(("hh", "per")),
        P(("hh", "per")),
        P(("hh", "per")),
        P(("grp", "per", "st"), None, None),
        P("grp"),
        P("grp"),
        P("grp"),
    )
    return jax.shard_map(
        per_device,
        mesh=mesh,
        in_specs=placed,
        out_specs=(P(("grp", "per"), "hh", "st"), P("grp")),
        check_vma=False,
    )
```

```python
import functools

import jax
import jax.numpy as jnp
from jax import lax
from jax.experimental import pallas as pl
from jax.experimental.pallas import tpu as pltpu
from jax.sharding import PartitionSpec as P

HB = 128
LANES = 128
HALF = HB // 2
SEEN = 16.0
F32 = jnp.float32
BF16 = jnp.bfloat16
LOG2E = 1.4426950408889634
LN2 = 0.6931471805599453
EXTRA = 16


def vmem():
    return pl.BlockSpec(memory_space=pltpu.VMEM)


def smem():
    return pl.BlockSpec(memory_space=pltpu.SMEM)


def hbm():
    return pl.BlockSpec(memory_space=pltpu.HBM)


def in_hbm(*arrays):
    return [pltpu.with_memory_space_constraint(x, pltpu.HBM) for x in arrays]


def params(mebibytes):
    return pltpu.CompilerParams(vmem_limit_bytes=mebibytes * 1024 * 1024)


def core_index():
    return lax.axis_index("st")


def is_forward_first():
    return 2 * lax.axis_index("per") < lax.axis_size("per")


def tiles(width):
    return [slice(q, q + LANES) for q in range(0, width, LANES)]


def fetch(pairs, sems):
    copies = [pltpu.make_async_copy(src, dst, sems.at[i]) for i, (src, dst) in enumerate(pairs)]
    for copy in copies:
        copy.start()
    for copy in copies:
        copy.wait()


def pack_kernel(count_ref, earn_any, start_any, len_any, out_ref, earn_ref, start_ref, len_ref, sems):
    fetch(((earn_any, earn_ref), (start_any, start_ref), (len_any, len_ref)), sems)
    periods, slot_rows = earn_ref.shape
    core = core_index()
    low_lane = lax.broadcasted_iota(jnp.int32, (periods // 2, HB), 1) < HALF
    time = lax.broadcasted_iota(jnp.int32, (periods, HB), 0)
    for slot in range(slot_rows // HB):
        cols = slice(slot * HB, (slot + 1) * HB)
        begin = start_ref[slot : slot + 1, :]
        seen = (time >= begin) & (time < begin + len_ref[slot : slot + 1, :])
        live = slot < count_ref[0]
        shift = jnp.where(live, jnp.where(seen, SEEN, 0.0), -SEEN)
        value = earn_ref[:, cols] + shift
        early, late = value[: periods // 2], value[periods // 2 :]
        turned = pltpu.roll(jnp.where(core == 0, late, early), HALF, 1)
        packed = jnp.where(low_lane, jnp.where(core == 0, early, turned), jnp.where(core == 0, turned, late))
        for to in range(out_ref.shape[0]):
            out_ref[to, :, cols] = packed


def put(ref, at, value):
    states = value.shape[0]
    high = value.astype(BF16)
    ref[at, :states, :states] = high
    ref[at, :states, states:] = (value - high.astype(F32)).astype(BF16)


def both_halves(mat, state):
    states = mat.shape[0]
    high = jnp.dot(mat[:, :states], state, preferred_element_type=F32)
    return high + jnp.dot(mat[:, states:], state, preferred_element_type=F32)


def fill_periods(mat, turned_pass, source, ref):
    @pl.loop(0, ref.shape[0])
    def _(i):
        at = source * ref.shape[0] + i

        @pl.when(turned_pass)
        def _():
            lifted = jnp.exp(ref[i].T.astype(F32))
            put(mat, at, lifted * (1.0 / jnp.sum(lifted, axis=0, keepdims=True)))

        @pl.when(jnp.logical_not(turned_pass))
        def _():
            lifted = jnp.exp(ref[i].astype(F32))
            put(mat, at, lifted * (1.0 / jnp.sum(lifted, axis=1, keepdims=True)))


def prep_own_kernel(
    own_any, init_any, mean_any, sd_any, mat, consts, own_ref, init_ref, mean_ref, sd_ref, sem, sems
):
    copy = pltpu.make_async_copy(own_any, own_ref, sem)
    copy.start()
    fetch(((init_any, init_ref), (mean_any, mean_ref), (sd_any, sd_ref)), sems)
    raised = jnp.exp(init_ref[...])
    rows = (
        raised / jnp.sum(raised, axis=1, keepdims=True),
        mean_ref[...],
        (-0.5 * LOG2E) * jnp.exp(-2.0 * sd_ref[...]),
        -LOG2E * sd_ref[...],
    )
    for i, row in enumerate(rows):
        consts[i] = jnp.broadcast_to(row, (LANES, own_ref.shape[1])).T
    copy.wait()
    fill_periods(mat, is_forward_first(), core_index(), own_ref)


def prep_other_kernel(other_ref, mat_in, mat):
    fill_periods(mat, is_forward_first(), 1 - core_index(), other_ref)


def prep_second_kernel(own_ref, other_ref, after_any, mat, row_probs):
    rows = row_probs.shape[1]
    here = own_rows(lax.axis_index("hh") * rows, rows)
    for source, ref in ((core_index(), own_ref), (1 - core_index(), other_ref)):
        for i in range(ref.shape[0]):
            lifted = jnp.exp(ref[i, here, :].astype(F32))
            row_probs[source * ref.shape[0] + i] = lifted * (1.0 / jnp.sum(lifted, axis=1, keepdims=True))
        fill_periods(mat, jnp.logical_not(is_forward_first()), source, ref)


def emission(sel_ref, consts, step_now, cols, less=None):
    gap = sel_ref[0, step_now, :1, cols] - consts[1]
    power = gap * gap * consts[2] + consts[3]
    return jnp.exp2(power if less is None else power - less)


def first_row(lead):
    return 0 if lax.axis_size("per") == 2 else lead


def is_moving(sel_ref, step_now, cols):
    return sel_ref[1, step_now, :1, cols] > 0.5


def is_seen(sel_ref, step_now, cols):
    return sel_ref[2, step_now, :1, cols] > 0.5


def column_sum(x):
    return jnp.sum(x, axis=0, keepdims=True)


def own_rows(row_begin, rows):
    return pl.ds(pl.multiple_of(row_begin, rows), rows)


def outer_sum(weights_ref, carried):
    return lax.dot_general(weights_ref[...], carried, (((1,), (1,)), ((), ())), preferred_element_type=F32)


def run_forward(lead, mat, hist, sel_ref, consts, ab_ref, logs, second=None, fresh=False):
    steps, states, width = hist.shape
    cuts = tiles(width)
    here = hist.at[0] if second is None else ab_ref
    inverse = [1.0 / column_sum(here[:, cols].astype(F32)) for cols in cuts]
    for k in range(steps):
        step_now = first_row(lead) + k
        here = there = ab_ref
        if second is None:
            here = hist.at[k]
            there = hist.at[k + 1] if k + 1 < steps else ab_ref
        else:
            weights_ref, row_begin, add_counts = second
            own_alpha = ab_ref[own_rows(row_begin, weights_ref.shape[0]), :].astype(F32)
        for q, cols in enumerate(cuts):
            begins = fresh and k == 0
            if not begins:
                moved = both_halves(mat[k], here[:, cols]) * inverse[q]
                moving = is_moving(sel_ref, step_now, cols)
            if second is not None:
                total = column_sum(moved * hist[k, :, cols].astype(F32))
                weight = jnp.where(moving, 1.0 / total, 0.0)
                weights_ref[:, cols] = (own_alpha[:, cols] * inverse[q] * weight).astype(BF16)
            emit = emission(sel_ref, consts, step_now, cols)
            joint = (consts[0] if begins else jnp.where(moving, moved, consts[0])) * emit
            scale = column_sum(joint)
            if second is None:
                seen = is_seen(sel_ref, step_now, cols)
                logs[q] = logs[q] + jnp.where(seen, jnp.log2(scale), 0.0)
            inverse[q] = 1.0 / scale
            there[:, cols] = joint.astype(BF16)
        if second is not None:
            add_counts(k, outer_sum(weights_ref, hist[k]))
    return logs


def run_backward(lead, mat, hist, sel_ref, consts, state, ub_ref, logs, leave, second=None, between=None):
    steps, states, width = hist.shape
    cuts = tiles(width)
    rest = [x[:1] for x in state]
    size = [jnp.zeros((1, LANES), F32) for _ in cuts]

    def step(k):
        step_now = first_row(lead) + k
        here = hist.at[k] if second is None else ub_ref
        grown = []
        for q, cols in enumerate(cuts):
            emit = emission(sel_ref, consts, step_now, cols, size[q] if second is None else None)
            carried = emit * state[q]
            here[:, cols] = carried.astype(BF16)
            whole = column_sum(carried)
            grown.append(whole)
            if second is None:
                size[q] = jnp.log2(whole)
                seen = is_seen(sel_ref, step_now, cols)
                logs[q] = logs[q] + jnp.where(seen, size[q], 0.0)
                begun = column_sum(carried * consts[0]) / whole
                rest[q] = jnp.where(seen, begun, rest[q])
        if second is not None:
            weights_ref, row_begin, add_counts = second
            own_alpha = hist[k, own_rows(row_begin, weights_ref.shape[0]), :].astype(F32)
        for q, cols in enumerate(cuts):
            product = both_halves(mat[k], here[:, cols])
            moving = is_moving(sel_ref, step_now, cols)
            if second is None:
                state[q] = jnp.where(moving, product, rest[q] * grown[q])
            else:
                shrink = 1.0 / grown[q]
                product = product * shrink
                total = column_sum(product * hist[k, :, cols].astype(F32))
                weight = jnp.where(moving, 1.0 / total, 0.0)
                weights_ref[:, cols] = (own_alpha[:, cols] * weight * shrink).astype(BF16)
                state[q] = jnp.where(moving, product, rest[q])
        if second is not None:
            add_counts(k, outer_sum(weights_ref, ub_ref[...]))

    def left():
        return [x * jnp.exp2(-y) for x, y in zip(state, size)]

    for k in reversed(range(1, steps)):
        step(k)
    if second is None:
        step(0)
        leave(left())
        return
    between()

    @pl.when(lead > 0)
    def _():
        step(0)
        leave(left())

    @pl.when(lead == 0)
    def _():
        second[2](0, jnp.zeros((second[0].shape[0], states), F32))


def put_state(state_out, values, logs):
    states = state_out.shape[0] - EXTRA
    row = lax.broadcasted_iota(jnp.int32, (EXTRA, LANES), 0)
    for q, cols in enumerate(tiles(state_out.shape[1])):
        state_out[:states, cols] = values[q].astype(BF16)
        high = logs[q].astype(BF16).astype(F32)
        middle = (logs[q] - high).astype(BF16).astype(F32)
        piece = jnp.where(
            row == 0, high, jnp.where(row == 1, middle, jnp.where(row == 2, logs[q] - high - middle, 0.0))
        )
        state_out[states:, cols] = piece.astype(BF16)


def state_logs(state_ref):
    states = state_ref.shape[0] - EXTRA
    return [column_sum(state_ref[states:, cols].astype(F32)) for cols in tiles(state_ref.shape[1])]


def first_kernel(resume, grids, part, rows_ref, mat, consts, *refs):
    state_in = refs[0] if resume else None
    hist, state_out, sel_ref, ab_ref = refs[-4:]
    chunk = part * grids + (pl.program_id(0) if grids > 1 else 0)
    steps, states, width = hist.shape
    forward_first, lead = is_forward_first(), lax.axis_index("per") * steps
    cuts = tiles(width)
    group, half_periods, slot_rows = rows_ref.shape
    tops = 2 * len(cuts)

    def scan_source(d, carry):
        rank, picked = carry
        for slot in range(slot_rows // HB):
            cols = slice(slot * HB, (slot + 1) * HB)
            block = rows_ref[d, :, cols]
            live = block > -0.5 * SEEN
            picked = [jnp.where(live & (rank == chunk * tops + i), block, old) for i, old in enumerate(picked)]
            rank = rank + live.astype(jnp.int32)
        return rank, picked

    carry = (jnp.zeros((half_periods, HB), jnp.int32), [jnp.zeros((half_periods, HB), F32)] * tops)
    if group <= 8:
        for d in range(group):
            carry = scan_source(d, carry)
    else:
        carry = lax.fori_loop(0, group, scan_source, carry)
    low_lane = lax.broadcasted_iota(jnp.int32, (half_periods, HB), 1) < HALF
    local = lax.axis_size("per") == 2

    def lay_out(parts):
        for q, cols in enumerate(cuts):
            left, right = carry[1][2 * q], carry[1][2 * q + 1]
            values = (
                jnp.where(low_lane, left, pltpu.roll(right, HALF, 1)),
                jnp.where(low_lane, pltpu.roll(left, HALF, 1), right),
            )
            flags = [(value > 0.5 * SEEN).astype(F32) for value in values]
            for late in parts:
                earn = jnp.where(flags[late] > 0.5, values[late] - SEEN, values[late])
                before = flags[0][half_periods - 1 :] if late else jnp.zeros((1, HB), F32)
                for i in range(half_periods):
                    at = i if local else late * half_periods + i
                    now = flags[late][i : i + 1]
                    sel_ref[0, at, :, cols] = jnp.broadcast_to(earn[i : i + 1], (8, HB))
                    sel_ref[1, at, :, cols] = jnp.broadcast_to(now * before, (8, HB))
                    sel_ref[2, at, :, cols] = jnp.broadcast_to(now, (8, HB))
                    before = now
            years = column_sum(flags[0] + flags[1])
            sel_ref[2, sel_ref.shape[1] - 1, :, cols] = jnp.broadcast_to(years, (8, HB))

    if not local:
        lay_out((0, 1))
    zeros = [jnp.zeros((1, LANES), F32) for _ in cuts]

    @pl.when(forward_first)
    def _():
        if local:
            lay_out((0,))
        if resume:
            hist[0] = state_in[:states, :]
        else:
            for cols in cuts:
                hist[0, :, cols] = consts[0].astype(BF16)
        logs = state_logs(state_in) if resume else list(zeros)
        fresh = lax.axis_size("per") == 2
        run_forward(lead, mat, hist, sel_ref, consts, ab_ref, logs, fresh=fresh)
        put_state(state_out, [ab_ref[:, cols] for cols in cuts], logs)

    @pl.when(jnp.logical_not(forward_first))
    def _():
        if local:
            lay_out((1,))
        state = [
            state_in[:states, cols].astype(F32) if resume else jnp.ones((states, LANES), F32) for cols in cuts
        ]
        logs = state_logs(state_in) if resume else list(zeros)
        leave = lambda values: put_state(state_out, values, logs)
        run_backward(lead, mat, hist, sel_ref, consts, state, ab_ref, logs, leave)


def second_kernel(resume, last, extend, grids, *refs):
    refs = list(refs)
    sel_ref, mat, consts, hist, own_state, state_in = (refs.pop(0) for _ in range(6))
    counts_in, sums_in = (refs.pop(0), refs.pop(0)) if resume else (None, None)
    row_probs = refs.pop(0) if last else None
    mine_ref, other_ref = (refs.pop(0), refs.pop(0)) if last else (None, None)
    counts_out, sums_out = (None, None) if last else (refs.pop(0), refs.pop(0))
    state_out = refs.pop(0) if extend else None
    ab_ref, weights_ref = refs[:2]
    counts_ref, sums_ref = refs[2:] if last else (counts_out, sums_out)
    chunk = pl.program_id(0) if grids > 1 else 0
    steps, states, width = hist.shape
    core, forward_first = core_index(), is_forward_first()
    row_begin = lax.axis_index("hh") * weights_ref.shape[0]
    lead = lax.axis_index("per") * steps
    rows = weights_ref.shape[0]

    def centre(k, counts):
        probs = row_probs[k]
        weighted = probs * counts
        grad = weighted - probs * jnp.sum(weighted, axis=1, keepdims=True)
        at = slice(k * rows, (k + 1) * rows)
        left, right = grad[:, :LANES], grad[:, LANES:]
        mine_ref[at, :] = jnp.where(core == 0, left, right)
        other_ref[at, :] = jnp.where(core == 0, right, left)

    def add_counts(k, counts):
        if grids > 1:
            counts_ref[k] += counts
            return
        if resume:
            counts = counts + counts_in[k]
        if last:
            centre(k, counts)
        else:
            counts_ref[k] = counts

    second = (weights_ref, row_begin, add_counts)

    @pl.when(chunk == 0)
    def _():
        if grids > 1:
            counts_ref[...] = jnp.zeros_like(counts_ref)
        sums_ref[...] = sums_in[...] if resume else jnp.zeros_like(sums_ref)

    def add_sums(alpha_ref, other_state):
        total = jnp.zeros((1, LANES), F32)
        years = jnp.zeros((8, LANES), F32)
        for cols, here, there in zip(tiles(width), state_logs(alpha_ref), state_logs(other_state)):
            alpha = alpha_ref[:states, cols].astype(F32)
            meet = column_sum(alpha * other_state[:states, cols].astype(F32))
            total += (here + there + jnp.log2(meet / column_sum(alpha))) * LN2
            years += sel_ref[2, sel_ref.shape[1] - 1, :, cols]
        total = jnp.broadcast_to(jnp.sum(total, axis=1, keepdims=True), (1, LANES))
        years = jnp.broadcast_to(jnp.sum(years[:1], axis=1, keepdims=True), (1, LANES))
        row = lax.broadcasted_iota(jnp.int32, (8, LANES), 0)
        sums_ref[...] += jnp.where(row == 0, total, jnp.where(row == 1, years, 0.0))

    zeros = [jnp.zeros((1, LANES), F32) for _ in tiles(width)]

    @pl.when(jnp.logical_not(forward_first))
    def _():
        ab_ref[...] = state_in[:states, :]
        run_forward(lead, mat, hist, sel_ref, consts, ab_ref, list(zeros), second)
        add_sums(state_in, own_state)
        if extend:
            put_state(state_out, [ab_ref[:, cols] for cols in tiles(width)], zeros)

    @pl.when(forward_first)
    def _():
        state = [state_in[:states, cols].astype(F32) for cols in tiles(width)]
        leave = lambda values: put_state(state_out, values, zeros) if extend else None
        run_backward(lead, mat, hist, sel_ref, consts, state, ab_ref, list(zeros), leave, second, lambda: add_sums(own_state, state_in))

    if last:

        @pl.when(chunk == grids - 1)
        def _():
            if grids > 1:
                for k in range(steps):
                    centre(k, counts_ref[k])
            mine_ref[steps * rows :, :] = sums_ref[...]
            other_ref[steps * rows :, :] = sums_ref[...]


def finish_kernel(scale, mine_ref, other_ref, grad_ref, mean_ref):
    count = grad_ref.shape[0]
    total = mine_ref[count : count + 1, :] + other_ref[count : count + 1, :]
    years = mine_ref[count + 1 : count + 2, :] + other_ref[count + 1 : count + 2, :]
    grad_ref[...] = (mine_ref[:count, :] + other_ref[:count, :]) * (scale / years)
    mean_ref[0] = (total / years)[0, 0]


def per_device(
    earnings, starts, lengths, block_count, trans_logits, init_logits, state_mean, log_sd
):
    slot_rows, periods = earnings.shape
    states = init_logits.shape[0]
    group = lax.axis_size(("hh", "per"))
    sides = lax.axis_size("per")
    cores = lax.axis_size("st")
    part = trans_logits.shape[0]
    steps = part * cores
    rows = states // lax.axis_size("hh")
    households = group * HB // cores
    parts = 2 if households <= 4 * HB else 1
    share = households // parts
    width = min(2 * HB, share)
    grids = share // width
    side = lax.axis_index("per")
    shaped = jax.ShapeDtypeStruct
    dma = pltpu.SemaphoreType.DMA

    swap = [(0, 1), (1, 0)]
    vec_row = pltpu.VMEM((1, states), F32)
    slots = pltpu.VMEM((slot_rows // HB, HB), jnp.int32)
    packed = pl.pallas_call(
        pack_kernel,
        out_shape=pltpu.VMEM((group, periods // 2, slot_rows), F32),
        in_specs=[smem()] + [hbm()] * 3,
        out_specs=vmem(),
        scratch_shapes=[pltpu.VMEM((periods, slot_rows), F32), slots, slots, dma((3,))],
        compiler_params=params(2),
        name="pack",
    )(block_count, *in_hbm(earnings.T, starts.reshape(-1, HB), lengths.reshape(-1, HB)))
    packed, later_logits = lax.optimization_barrier((packed, trans_logits))
    other_logits = lax.ppermute(later_logits, "st", swap)
    along = group // sides
    centre = along // 2
    outward = sorted(range(along), key=lambda z: (abs(z - centre), -z))
    listed = [z * sides + x for z in outward for x in reversed(range(sides))]
    gathered = lax.all_to_all(
        packed, ("hh", "per", "st"), split_axis=0, concat_axis=0,
        axis_index_groups=[[n * cores + c for n in listed] for c in range(cores)], tiled=True,
    )
    mat_shape = shaped((steps, states, 2 * states), BF16)
    first_mat, consts = pl.pallas_call(
        prep_own_kernel,
        out_shape=[pltpu.VMEM(mat_shape.shape, BF16), pltpu.VMEM((4, states, LANES), F32)],
        in_specs=[hbm()] * 4,
        out_specs=[vmem(), vmem()],
        scratch_shapes=[pltpu.VMEM(trans_logits.shape, BF16), vec_row, vec_row, vec_row, dma, dma((3,))],
        compiler_params=params(4),
        name="prep_own",
    )(
        *in_hbm(
            trans_logits,
            init_logits.reshape(1, states), state_mean.reshape(1, states), log_sd.reshape(1, states),
        )
    )
    first_mat = pl.pallas_call(
        prep_other_kernel,
        out_shape=pltpu.VMEM(mat_shape.shape, BF16),
        in_specs=[vmem(), vmem()],
        out_specs=vmem(),
        input_output_aliases={1: 0},
        compiler_params=params(4),
        name="prep_other",
    )(other_logits, first_mat)

    def prep_second(after):
        return pl.pallas_call(
            prep_second_kernel,
            out_shape=[mat_shape, shaped((steps, rows, states), F32)],
            in_specs=[vmem(), vmem(), hbm()],
            out_specs=[vmem(), vmem()],
            compiler_params=params(4),
            name="prep_second",
        )(trans_logits, other_logits, after)

    def whole(*shape):
        if grids == 1:
            return vmem()
        return pl.BlockSpec(shape, lambda g: (0,) * len(shape))

    def lanes(*lead):
        if grids == 1:
            return vmem()
        return pl.BlockSpec(lead + (width,), lambda g: (0,) * len(lead) + (g,))

    grid = (grids,) if grids > 1 else ()
    hist_shape = shaped((steps, states, share), BF16)
    state_shape = shaped((states + EXTRA, share), BF16)
    laid = (steps if sides == 2 else periods) + 1
    sel_shape = shaped((3, laid, 8, share), F32)
    swap_shape = shaped((steps * rows + 8, LANES), F32)
    counts_shape = shaped((steps, rows, states), F32)
    sums_shape = shaped((8, LANES), F32)
    hist_spec, state_spec, sel_spec = lanes(steps, states), lanes(states + EXTRA), lanes(3, laid, 8)
    const_spec = whole(4, states, LANES)

    def first_pass(index, state_in):
        resume = state_in is not None
        return pl.pallas_call(
            functools.partial(first_kernel, resume, grids, index),
            grid=grid,
            out_shape=[hist_shape, state_shape, sel_shape],
            in_specs=[whole(*gathered.shape), whole(*first_mat.shape), const_spec]
            + [state_spec] * resume,
            out_specs=[hist_spec, state_spec, sel_spec],
            scratch_shapes=[pltpu.VMEM((states, width), BF16)],
            compiler_params=params(8 if grids == 1 else 32),
            name="first_pass",
        )(gathered, first_mat, consts, *([state_in] if resume else []))

    def second_pass(kept, state_in, sums_in, last, extend):
        hist, own_state, sel = kept
        resume = sums_in is not None
        scratch = [
            pltpu.VMEM((states, width), BF16),
            pltpu.VMEM((rows, width), BF16),
        ]
        counts_spec, sums_spec = whole(*counts_shape.shape), whole(*sums_shape.shape)
        if last:
            out_shape = [swap_shape] * 2
            scratch += [pltpu.VMEM(counts_shape.shape, F32), pltpu.VMEM(sums_shape.shape, F32)]
        else:
            out_shape = [counts_shape, sums_shape]
        out_specs = [whole(*x.shape) for x in out_shape]
        if extend:
            out_shape, out_specs = out_shape + [state_shape], out_specs + [state_spec]
        return pl.pallas_call(
            functools.partial(second_kernel, resume, last, extend, grids),
            grid=grid,
            out_shape=out_shape,
            in_specs=[sel_spec, whole(*second_mat.shape), const_spec, hist_spec, state_spec, state_spec]
            + [counts_spec, sums_spec] * resume
            + [whole(*row_probs.shape)] * last,
            out_specs=out_specs,
            scratch_shapes=scratch,
            compiler_params=params(8 if grids == 1 else 32),
            name="second_pass",
        )(
            sel, second_mat, consts, hist, own_state, state_in,
            *(sums_in if resume else []),
            *([row_probs] if last else []),
        )

    def hand_over(state, stage):
        moves = [(stage, stage + 1), (sides - 1 - stage, sides - 2 - stage)]
        return lax.ppermute(state, "per", moves)

    if sides == 2:
        kept = [first_pass(index, None) for index in range(parts)]
        arrived = [hand_over(each[1], 0) for each in kept]
        second_mat, row_probs = prep_second(kept[-1][1])
        sums = None
        for index in range(parts):
            sums = second_pass(kept[index], arrived[index], sums, index == parts - 1, False)
        mine, other = sums
    else:
        kept = [jnp.zeros(x.shape, x.dtype) for x in (hist_shape, state_shape, sel_shape)]
        done = [jnp.zeros(x.shape, x.dtype) for x in (swap_shape, swap_shape, state_shape)]
        state = None
        second_mat, row_probs = prep_second(gathered)
        for stage in range(sides):
            active = (side == stage) | (side == sides - 1 - stage)
            if stage < sides // 2:
                kept = lax.cond(
                    active, lambda x, kept: list(first_pass(0, x)), lambda x, kept: kept, state, kept
                )
                state = kept[1]
            else:
                done = lax.cond(
                    active,
                    lambda x, done: list(second_pass(kept, x, None, True, True)),
                    lambda x, done: done,
                    state,
                    done,
                )
                state = done[2]
            if stage < sides - 1:
                state = hand_over(state, stage)
        mine, other, _ = done
        total = jnp.where(side == sides // 2, mine[steps * rows], 0.0)
        total = lax.psum(total, "per")
        mine = mine.at[steps * rows].set(total)
        other = other.at[steps * rows].set(total)
    received = lax.ppermute(other, "st", swap)
    trans_grad, mean_loglik = pl.pallas_call(
        functools.partial(finish_kernel, float(states * states * periods)),
        out_shape=[shaped((steps * rows, LANES), F32), shaped((1,), F32)],
        in_specs=[vmem(), vmem()],
        out_specs=[vmem(), smem()],
        compiler_params=params(4),
        name="finish",
    )(mine, received)
    return (trans_grad.reshape(steps, rows, LANES), mean_loglik)


def solution(mesh):
    placed = (
        P(("hh", "per"), None),
        P(("hh", "per")),
        P(("hh", "per")),
        P(("hh", "per")),
        P(("grp", "per", "st"), None, None),
        P("grp"),
        P("grp"),
        P("grp"),
    )
    return jax.shard_map(
        per_device,
        mesh=mesh,
        in_specs=placed,
        out_specs=(P(("grp", "per"), "hh", "st"), P("grp")),
        check_vma=False,
    )
```

```python
import functools

import jax
import jax.numpy as jnp
from jax import lax
from jax.experimental import pallas as pl
from jax.experimental.pallas import tpu as pltpu
from jax.sharding import PartitionSpec as P

HB = 128
LANES = 128
HALF = HB // 2
SEEN = 16.0
F32 = jnp.float32
BF16 = jnp.bfloat16
LOG2E = 1.4426950408889634
LN2 = 0.6931471805599453


def vmem():
    return pl.BlockSpec(memory_space=pltpu.VMEM)


def smem():
    return pl.BlockSpec(memory_space=pltpu.SMEM)


def hbm():
    return pl.BlockSpec(memory_space=pltpu.HBM)


def in_hbm(*arrays):
    return [pltpu.with_memory_space_constraint(x, pltpu.HBM) for x in arrays]


def params(mebibytes):
    return pltpu.CompilerParams(vmem_limit_bytes=mebibytes * 1024 * 1024)


def core_index():
    return lax.axis_index("st")


def is_forward_first():
    return 2 * lax.axis_index("per") < lax.axis_size("per")


def tiles(width):
    return [slice(q, q + LANES) for q in range(0, width, LANES)]


def fetch(pairs, sems):
    copies = [pltpu.make_async_copy(src, dst, sems.at[i]) for i, (src, dst) in enumerate(pairs)]
    for copy in copies:
        copy.start()
    for copy in copies:
        copy.wait()


def pack_kernel(count_ref, earn_any, start_any, len_any, out_ref, earn_ref, start_ref, len_ref, sems):
    fetch(((earn_any, earn_ref), (start_any, start_ref), (len_any, len_ref)), sems)
    periods, slot_rows = earn_ref.shape
    core = core_index()
    low_lane = lax.broadcasted_iota(jnp.int32, (periods // 2, HB), 1) < HALF
    time = lax.broadcasted_iota(jnp.int32, (periods, HB), 0)
    for slot in range(slot_rows // HB):
        cols = slice(slot * HB, (slot + 1) * HB)
        begin = start_ref[slot : slot + 1, :]
        seen = (time >= begin) & (time < begin + len_ref[slot : slot + 1, :])
        live = slot < count_ref[0]
        shift = jnp.where(live, jnp.where(seen, SEEN, 0.0), -SEEN)
        value = earn_ref[:, cols] + shift
        early, late = value[: periods // 2], value[periods // 2 :]
        turned = pltpu.roll(jnp.where(core == 0, late, early), HALF, 1)
        packed = jnp.where(low_lane, jnp.where(core == 0, early, turned), jnp.where(core == 0, turned, late))
        for to in range(out_ref.shape[0]):
            out_ref[to, :, cols] = packed


def put(ref, at, value):
    states = value.shape[0]
    high = value.astype(BF16)
    ref[at, :states, :states] = high
    ref[at, :states, states:] = (value - high.astype(F32)).astype(BF16)


def both_halves(mat, state):
    states = mat.shape[0]
    high = jnp.dot(mat[:, :states], state, preferred_element_type=F32)
    return high + jnp.dot(mat[:, states:], state, preferred_element_type=F32)


def fill_periods(mat, turned_pass, source, ref):
    @pl.loop(0, ref.shape[0])
    def _(i):
        at = source * ref.shape[0] + i

        @pl.when(turned_pass)
        def _():
            lifted = jnp.exp(ref[i].T.astype(F32))
            put(mat, at, lifted * (1.0 / jnp.sum(lifted, axis=0, keepdims=True)))

        @pl.when(jnp.logical_not(turned_pass))
        def _():
            lifted = jnp.exp(ref[i].astype(F32))
            put(mat, at, lifted * (1.0 / jnp.sum(lifted, axis=1, keepdims=True)))


def prep_own_kernel(
    own_any, init_any, mean_any, sd_any, mat, consts, own_ref, init_ref, mean_ref, sd_ref, sem, sems
):
    copy = pltpu.make_async_copy(own_any, own_ref, sem)
    copy.start()
    fetch(((init_any, init_ref), (mean_any, mean_ref), (sd_any, sd_ref)), sems)
    raised = jnp.exp(init_ref[...])
    rows = (
        raised / jnp.sum(raised, axis=1, keepdims=True),
        mean_ref[...],
        (-0.5 * LOG2E) * jnp.exp(-2.0 * sd_ref[...]),
        -LOG2E * sd_ref[...],
    )
    for i, row in enumerate(rows):
        consts[i] = jnp.broadcast_to(row, (LANES, own_ref.shape[1])).T
    copy.wait()
    fill_periods(mat, is_forward_first(), core_index(), own_ref)


def prep_other_kernel(other_ref, mat_in, mat):
    fill_periods(mat, is_forward_first(), 1 - core_index(), other_ref)


def prep_second_kernel(own_ref, other_ref, after_any, mat, row_probs):
    rows = row_probs.shape[1]
    here = own_rows(lax.axis_index("hh") * rows, rows)
    for source, ref in ((core_index(), own_ref), (1 - core_index(), other_ref)):
        for i in range(ref.shape[0]):
            lifted = jnp.exp(ref[i, here, :].astype(F32))
            row_probs[source * ref.shape[0] + i] = lifted * (1.0 / jnp.sum(lifted, axis=1, keepdims=True))
        fill_periods(mat, jnp.logical_not(is_forward_first()), source, ref)


def emission(sel_ref, consts, step_now, cols, less=None):
    gap = sel_ref[0, step_now, :1, cols] - consts[1]
    power = gap * gap * consts[2] + consts[3]
    return jnp.exp2(power if less is None else power - less)


def first_row(lead):
    return 0 if lax.axis_size("per") == 2 else lead


def is_moving(sel_ref, step_now, cols):
    return sel_ref[1, step_now, :1, cols] > 0.5


def is_seen(sel_ref, step_now, cols):
    return sel_ref[2, step_now, :1, cols] > 0.5


def column_sum(x):
    return jnp.sum(x, axis=0, keepdims=True)


def own_rows(row_begin, rows):
    return pl.ds(pl.multiple_of(row_begin, rows), rows)


def outer_sum(weights_ref, carried):
    return lax.dot_general(weights_ref[...], carried, (((1,), (1,)), ((), ())), preferred_element_type=F32)


def run_forward(lead, mat, hist, sel_ref, consts, ab_ref, logs, second=None, fresh=False):
    steps, states, width = hist.shape
    cuts = tiles(width)
    here = hist.at[0] if second is None else ab_ref
    last = [None] * len(cuts)
    inverse = [1.0 / column_sum(here[:, cols].astype(F32)) for cols in cuts]
    for k in range(steps):
        step_now = first_row(lead) + k
        here = there = ab_ref
        if second is None:
            here = hist.at[k]
            there = hist.at[k + 1] if k + 1 < steps else ab_ref
        else:
            weights_ref, row_begin, add_counts = second
            own_alpha = ab_ref[own_rows(row_begin, weights_ref.shape[0]), :].astype(F32)
        for q, cols in enumerate(cuts):
            begins = fresh and k == 0
            if not begins:
                moved = both_halves(mat[k], here[:, cols]) * inverse[q]
                moving = is_moving(sel_ref, step_now, cols)
            if second is not None:
                total = column_sum(moved * hist[k, :, cols].astype(F32))
                weight = jnp.where(moving, 1.0 / total, 0.0)
                weights_ref[:, cols] = (own_alpha[:, cols] * inverse[q] * weight).astype(BF16)
            emit = emission(sel_ref, consts, step_now, cols)
            joint = (consts[0] if begins else jnp.where(moving, moved, consts[0])) * emit
            scale = column_sum(joint)
            if second is None:
                seen = is_seen(sel_ref, step_now, cols)
                logs[q] = logs[q] + jnp.where(seen, jnp.log2(scale), 0.0)
            inverse[q] = 1.0 / scale
            there[:, cols] = joint.astype(BF16)
            last[q] = joint
        if second is not None:
            add_counts(k, outer_sum(weights_ref, hist[k]))
    return last


def run_backward(lead, mat, hist, sel_ref, consts, state, ub_ref, logs, leave, second=None, between=None):
    steps, states, width = hist.shape
    cuts = tiles(width)
    rest = [x[:1] for x in state]
    size = [jnp.zeros((1, LANES), F32) for _ in cuts]

    def step(k):
        step_now = first_row(lead) + k
        here = hist.at[k] if second is None else ub_ref
        grown = []
        for q, cols in enumerate(cuts):
            emit = emission(sel_ref, consts, step_now, cols, size[q] if second is None else None)
            carried = emit * state[q]
            here[:, cols] = carried.astype(BF16)
            whole = column_sum(carried)
            grown.append(whole)
            if second is None:
                size[q] = jnp.log2(whole)
                seen = is_seen(sel_ref, step_now, cols)
                logs[q] = logs[q] + jnp.where(seen, size[q], 0.0)
                begun = column_sum(carried * consts[0]) / whole
                rest[q] = jnp.where(seen, begun, rest[q])
        if second is not None:
            weights_ref, row_begin, add_counts = second
            own_alpha = hist[k, own_rows(row_begin, weights_ref.shape[0]), :].astype(F32)
        for q, cols in enumerate(cuts):
            product = both_halves(mat[k], here[:, cols])
            moving = is_moving(sel_ref, step_now, cols)
            if second is None:
                state[q] = jnp.where(moving, product, rest[q] * grown[q])
            else:
                shrink = 1.0 / grown[q]
                product = product * shrink
                total = column_sum(product * hist[k, :, cols].astype(F32))
                weight = jnp.where(moving, 1.0 / total, 0.0)
                weights_ref[:, cols] = (own_alpha[:, cols] * weight * shrink).astype(BF16)
                state[q] = jnp.where(moving, product, rest[q])
        if second is not None:
            add_counts(k, outer_sum(weights_ref, ub_ref[...]))

    def left():
        return [x * jnp.exp2(-y) for x, y in zip(state, size)]

    for k in reversed(range(1, steps)):
        step(k)
    if second is None:
        step(0)
        leave(left())
        return
    between()

    @pl.when(lead > 0)
    def _():
        step(0)
        leave(left())

    @pl.when(lead == 0)
    def _():
        second[2](0, jnp.zeros((second[0].shape[0], states), F32))


def put_state(state_out, values, logs, spread):
    for q, cols in enumerate(tiles(state_out.shape[1])):
        factor = jnp.exp2(logs[q] * (1.0 / spread)) / column_sum(values[q])
        state_out[:, cols] = (values[q] * factor).astype(BF16)


def state_sums(state_ref):
    return [column_sum(state_ref[:, cols].astype(F32)) for cols in tiles(state_ref.shape[1])]


def state_logs(sums, spread):
    return [jnp.log2(x) * spread for x in sums]


def unit_state(state_ref, sums):
    return [state_ref[:, cols].astype(F32) * (1.0 / x) for cols, x in zip(tiles(state_ref.shape[1]), sums)]


def first_kernel(resume, grids, part, rows_ref, mat, consts, *refs):
    state_in = refs[0] if resume else None
    hist, state_out, sel_ref, ab_ref = refs[-4:]
    chunk = part * grids + (pl.program_id(0) if grids > 1 else 0)
    steps, states, width = hist.shape
    forward_first, lead = is_forward_first(), lax.axis_index("per") * steps
    cuts = tiles(width)
    group, half_periods, slot_rows = rows_ref.shape
    tops = 2 * len(cuts)

    def scan_source(d, carry):
        rank, picked = carry
        for slot in range(slot_rows // HB):
            cols = slice(slot * HB, (slot + 1) * HB)
            block = rows_ref[d, :, cols]
            live = block > -0.5 * SEEN
            picked = [jnp.where(live & (rank == chunk * tops + i), block, old) for i, old in enumerate(picked)]
            rank = rank + live.astype(jnp.int32)
        return rank, picked

    carry = (jnp.zeros((half_periods, HB), jnp.int32), [jnp.zeros((half_periods, HB), F32)] * tops)
    if group <= 8:
        for d in range(group):
            carry = scan_source(d, carry)
    else:
        carry = lax.fori_loop(0, group, scan_source, carry)
    low_lane = lax.broadcasted_iota(jnp.int32, (half_periods, HB), 1) < HALF
    local = lax.axis_size("per") == 2

    def lay_out(parts):
        for q, cols in enumerate(cuts):
            left, right = carry[1][2 * q], carry[1][2 * q + 1]
            values = (
                jnp.where(low_lane, left, pltpu.roll(right, HALF, 1)),
                jnp.where(low_lane, pltpu.roll(left, HALF, 1), right),
            )
            flags = [(value > 0.5 * SEEN).astype(F32) for value in values]
            for late in parts:
                earn = jnp.where(flags[late] > 0.5, values[late] - SEEN, values[late])
                before = flags[0][half_periods - 1 :] if late else jnp.zeros((1, HB), F32)
                for i in range(half_periods):
                    at = i if local else late * half_periods + i
                    now = flags[late][i : i + 1]
                    sel_ref[0, at, :, cols] = jnp.broadcast_to(earn[i : i + 1], (8, HB))
                    sel_ref[1, at, :, cols] = jnp.broadcast_to(now * before, (8, HB))
                    sel_ref[2, at, :, cols] = jnp.broadcast_to(now, (8, HB))
                    before = now
            years = column_sum(flags[0] + flags[1])
            sel_ref[2, sel_ref.shape[1] - 1, :, cols] = jnp.broadcast_to(years, (8, HB))

    if not local:
        lay_out((0, 1))
    zeros = [jnp.zeros((1, LANES), F32) for _ in cuts]

    @pl.when(forward_first)
    def _():
        if local:
            lay_out((0,))
        if resume:
            hist[0] = state_in[...]
        else:
            for cols in cuts:
                hist[0, :, cols] = consts[0].astype(BF16)
        logs = state_logs(state_sums(state_in), half_periods) if resume else list(zeros)
        fresh = lax.axis_size("per") == 2
        last = run_forward(lead, mat, hist, sel_ref, consts, ab_ref, logs, fresh=fresh)
        put_state(state_out, last, logs, half_periods)

    @pl.when(jnp.logical_not(forward_first))
    def _():
        if local:
            lay_out((1,))
        sums = state_sums(state_in) if resume else None
        state = unit_state(state_in, sums) if resume else [jnp.ones((states, LANES), F32) for _ in cuts]
        logs = state_logs(sums, half_periods) if resume else list(zeros)

        def leave(values):
            grown = [old + jnp.log2(column_sum(x)) for old, x in zip(logs, values)]
            put_state(state_out, values, grown, half_periods)

        run_backward(lead, mat, hist, sel_ref, consts, state, ab_ref, logs, leave)


def second_kernel(resume, last, extend, grids, spread, *refs):
    refs = list(refs)
    sel_ref, mat, consts, hist, own_state, state_in = (refs.pop(0) for _ in range(6))
    counts_in, sums_in = (refs.pop(0), refs.pop(0)) if resume else (None, None)
    row_probs = refs.pop(0) if last else None
    mine_ref, other_ref = (refs.pop(0), refs.pop(0)) if last else (None, None)
    counts_out, sums_out = (None, None) if last else (refs.pop(0), refs.pop(0))
    state_out = refs.pop(0) if extend else None
    ab_ref, weights_ref = refs[:2]
    counts_ref, sums_ref = refs[2:] if last else (counts_out, sums_out)
    chunk = pl.program_id(0) if grids > 1 else 0
    steps, states, width = hist.shape
    core, forward_first = core_index(), is_forward_first()
    row_begin = lax.axis_index("hh") * weights_ref.shape[0]
    lead = lax.axis_index("per") * steps
    rows = weights_ref.shape[0]

    def centre(k, counts):
        probs = row_probs[k]
        weighted = probs * counts
        grad = weighted - probs * jnp.sum(weighted, axis=1, keepdims=True)
        at = slice(k * rows, (k + 1) * rows)
        left, right = grad[:, :LANES], grad[:, LANES:]
        mine_ref[at, :] = jnp.where(core == 0, left, right)
        other_ref[at, :] = jnp.where(core == 0, right, left)

    def add_counts(k, counts):
        if grids > 1:
            counts_ref[k] += counts
            return
        if resume:
            counts = counts + counts_in[k]
        if last:
            centre(k, counts)
        else:
            counts_ref[k] = counts

    second = (weights_ref, row_begin, add_counts)

    @pl.when(chunk == 0)
    def _():
        if grids > 1:
            counts_ref[...] = jnp.zeros_like(counts_ref)
        sums_ref[...] = sums_in[...] if resume else jnp.zeros_like(sums_ref)

    def add_sums(alpha_ref, other_state):
        total = jnp.zeros((1, LANES), F32)
        years = jnp.zeros((8, LANES), F32)
        for cols, here, there in zip(tiles(width), state_sums(alpha_ref), state_sums(other_state)):
            meet = column_sum(alpha_ref[:, cols].astype(F32) * (1.0 / here) * other_state[:, cols].astype(F32))
            scales = (jnp.log2(here) + jnp.log2(there)) * spread
            total += (scales + jnp.log2(meet / there)) * LN2
            years += sel_ref[2, sel_ref.shape[1] - 1, :, cols]
        total = jnp.broadcast_to(jnp.sum(total, axis=1, keepdims=True), (1, LANES))
        years = jnp.broadcast_to(jnp.sum(years[:1], axis=1, keepdims=True), (1, LANES))
        row = lax.broadcasted_iota(jnp.int32, (8, LANES), 0)
        sums_ref[...] += jnp.where(row == 0, total, jnp.where(row == 1, years, 0.0))

    zeros = [jnp.zeros((1, LANES), F32) for _ in tiles(width)]

    @pl.when(jnp.logical_not(forward_first))
    def _():
        ab_ref[...] = state_in[...]
        values = run_forward(lead, mat, hist, sel_ref, consts, ab_ref, list(zeros), second)
        add_sums(state_in, own_state)
        if extend:
            put_state(state_out, values, zeros, spread)

    @pl.when(forward_first)
    def _():
        state = unit_state(state_in, state_sums(state_in))
        leave = lambda values: put_state(state_out, values, zeros, spread) if extend else None
        run_backward(lead, mat, hist, sel_ref, consts, state, ab_ref, list(zeros), leave, second, lambda: add_sums(own_state, state_in))

    if last:

        @pl.when(chunk == grids - 1)
        def _():
            if grids > 1:
                for k in range(steps):
                    centre(k, counts_ref[k])
            mine_ref[steps * rows :, :] = sums_ref[...]
            other_ref[steps * rows :, :] = sums_ref[...]


def finish_kernel(scale, mine_ref, other_ref, grad_ref, mean_ref):
    count = grad_ref.shape[0]
    total = mine_ref[count : count + 1, :] + other_ref[count : count + 1, :]
    years = mine_ref[count + 1 : count + 2, :] + other_ref[count + 1 : count + 2, :]
    grad_ref[...] = (mine_ref[:count, :] + other_ref[:count, :]) * (scale / years)
    mean_ref[0] = (total / years)[0, 0]


def per_device(
    earnings, starts, lengths, block_count, trans_logits, init_logits, state_mean, log_sd
):
    slot_rows, periods = earnings.shape
    states = init_logits.shape[0]
    group = lax.axis_size(("hh", "per"))
    sides = lax.axis_size("per")
    cores = lax.axis_size("st")
    part = trans_logits.shape[0]
    steps = part * cores
    rows = states // lax.axis_size("hh")
    households = group * HB // cores
    parts = 2 if households <= 4 * HB else 1
    share = households // parts
    width = min(2 * HB, share)
    grids = share // width
    side = lax.axis_index("per")
    shaped = jax.ShapeDtypeStruct
    dma = pltpu.SemaphoreType.DMA

    swap = [(0, 1), (1, 0)]
    vec_row = pltpu.VMEM((1, states), F32)
    slots = pltpu.VMEM((slot_rows // HB, HB), jnp.int32)
    packed = pl.pallas_call(
        pack_kernel,
        out_shape=pltpu.VMEM((group, periods // 2, slot_rows), F32),
        in_specs=[smem()] + [hbm()] * 3,
        out_specs=vmem(),
        scratch_shapes=[pltpu.VMEM((periods, slot_rows), F32), slots, slots, dma((3,))],
        compiler_params=params(2),
        name="pack",
    )(block_count, *in_hbm(earnings.T, starts.reshape(-1, HB), lengths.reshape(-1, HB)))
    packed, later_logits = lax.optimization_barrier((packed, trans_logits))
    other_logits = lax.ppermute(later_logits, "st", swap)
    along = group // sides
    centre = along // 2
    outward = sorted(range(along), key=lambda z: (abs(z - centre), -z))
    listed = [z * sides + x for z in outward for x in reversed(range(sides))]
    gathered = lax.all_to_all(
        packed, ("hh", "per", "st"), split_axis=0, concat_axis=0,
        axis_index_groups=[[n * cores + c for n in listed] for c in range(cores)], tiled=True,
    )
    mat_shape = shaped((steps, states, 2 * states), BF16)
    first_mat, consts = pl.pallas_call(
        prep_own_kernel,
        out_shape=[pltpu.VMEM(mat_shape.shape, BF16), pltpu.VMEM((4, states, LANES), F32)],
        in_specs=[hbm()] * 4,
        out_specs=[vmem(), vmem()],
        scratch_shapes=[pltpu.VMEM(trans_logits.shape, BF16), vec_row, vec_row, vec_row, dma, dma((3,))],
        compiler_params=params(4),
        name="prep_own",
    )(
        *in_hbm(
            trans_logits,
            init_logits.reshape(1, states), state_mean.reshape(1, states), log_sd.reshape(1, states),
        )
    )
    first_mat = pl.pallas_call(
        prep_other_kernel,
        out_shape=pltpu.VMEM(mat_shape.shape, BF16),
        in_specs=[vmem(), vmem()],
        out_specs=vmem(),
        input_output_aliases={1: 0},
        compiler_params=params(4),
        name="prep_other",
    )(other_logits, first_mat)

    def prep_second(after):
        return pl.pallas_call(
            prep_second_kernel,
            out_shape=[mat_shape, shaped((steps, rows, states), F32)],
            in_specs=[vmem(), vmem(), hbm()],
            out_specs=[vmem(), vmem()],
            compiler_params=params(4),
            name="prep_second",
        )(trans_logits, other_logits, after)

    def whole(*shape):
        if grids == 1:
            return vmem()
        return pl.BlockSpec(shape, lambda g: (0,) * len(shape))

    def lanes(*lead):
        if grids == 1:
            return vmem()
        return pl.BlockSpec(lead + (width,), lambda g: (0,) * len(lead) + (g,))

    grid = (grids,) if grids > 1 else ()
    hist_shape = shaped((steps, states, share), BF16)
    state_shape = shaped((states, share), BF16)
    laid = (steps if sides == 2 else periods) + 1
    sel_shape = shaped((3, laid, 8, share), F32)
    swap_shape = shaped((steps * rows + 8, LANES), F32)
    counts_shape = shaped((steps, rows, states), F32)
    sums_shape = shaped((8, LANES), F32)
    hist_spec, state_spec, sel_spec = lanes(steps, states), lanes(states), lanes(3, laid, 8)
    const_spec = whole(4, states, LANES)

    def first_pass(index, state_in):
        resume = state_in is not None
        return pl.pallas_call(
            functools.partial(first_kernel, resume, grids, index),
            grid=grid,
            out_shape=[hist_shape, state_shape, sel_shape],
            in_specs=[whole(*gathered.shape), whole(*first_mat.shape), const_spec]
            + [state_spec] * resume,
            out_specs=[hist_spec, state_spec, sel_spec],
            scratch_shapes=[pltpu.VMEM((states, width), BF16)],
            compiler_params=params(8 if grids == 1 else 32),
            name="first_pass",
        )(gathered, first_mat, consts, *([state_in] if resume else []))

    def second_pass(kept, state_in, sums_in, last, extend):
        hist, own_state, sel = kept
        resume = sums_in is not None
        scratch = [
            pltpu.VMEM((states, width), BF16),
            pltpu.VMEM((rows, width), BF16),
        ]
        counts_spec, sums_spec = whole(*counts_shape.shape), whole(*sums_shape.shape)
        if last:
            out_shape = [swap_shape] * 2
            scratch += [pltpu.VMEM(counts_shape.shape, F32), pltpu.VMEM(sums_shape.shape, F32)]
        else:
            out_shape = [counts_shape, sums_shape]
        out_specs = [whole(*x.shape) for x in out_shape]
        if extend:
            out_shape, out_specs = out_shape + [state_shape], out_specs + [state_spec]
        return pl.pallas_call(
            functools.partial(second_kernel, resume, last, extend, grids, periods // 2),
            grid=grid,
            out_shape=out_shape,
            in_specs=[sel_spec, whole(*second_mat.shape), const_spec, hist_spec, state_spec, state_spec]
            + [counts_spec, sums_spec] * resume
            + [whole(*row_probs.shape)] * last,
            out_specs=out_specs,
            scratch_shapes=scratch,
            compiler_params=params(8 if grids == 1 else 32),
            name="second_pass",
        )(
            sel, second_mat, consts, hist, own_state, state_in,
            *(sums_in if resume else []),
            *([row_probs] if last else []),
        )

    def hand_over(state, stage):
        moves = [(stage, stage + 1), (sides - 1 - stage, sides - 2 - stage)]
        return lax.ppermute(state, "per", moves)

    if sides == 2:
        kept = [first_pass(index, None) for index in range(parts)]
        arrived = [hand_over(each[1], 0) for each in kept]
        second_mat, row_probs = prep_second(kept[-1][1])
        sums = None
        for index in range(parts):
            sums = second_pass(kept[index], arrived[index], sums, index == parts - 1, False)
        mine, other = sums
    else:
        kept = [jnp.zeros(x.shape, x.dtype) for x in (hist_shape, state_shape, sel_shape)]
        done = [jnp.zeros(x.shape, x.dtype) for x in (swap_shape, swap_shape, state_shape)]
        state = None
        second_mat, row_probs = prep_second(gathered)
        for stage in range(sides):
            active = (side == stage) | (side == sides - 1 - stage)
            if stage < sides // 2:
                kept = lax.cond(
                    active, lambda x, kept: list(first_pass(0, x)), lambda x, kept: kept, state, kept
                )
                state = kept[1]
            else:
                done = lax.cond(
                    active,
                    lambda x, done: list(second_pass(kept, x, None, True, True)),
                    lambda x, done: done,
                    state,
                    done,
                )
                state = done[2]
            if stage < sides - 1:
                state = hand_over(state, stage)
        mine, other, _ = done
        total = jnp.where(side == sides // 2, mine[steps * rows], 0.0)
        total = lax.psum(total, "per")
        mine = mine.at[steps * rows].set(total)
        other = other.at[steps * rows].set(total)
    received = lax.ppermute(other, "st", swap)
    trans_grad, mean_loglik = pl.pallas_call(
        functools.partial(finish_kernel, float(states * states * periods)),
        out_shape=[shaped((steps * rows, LANES), F32), shaped((1,), F32)],
        in_specs=[vmem(), vmem()],
        out_specs=[vmem(), smem()],
        compiler_params=params(4),
        name="finish",
    )(mine, received)
    return (trans_grad.reshape(steps, rows, LANES), mean_loglik)


def solution(mesh):
    placed = (
        P(("hh", "per"), None),
        P(("hh", "per")),
        P(("hh", "per")),
        P(("hh", "per")),
        P(("grp", "per", "st"), None, None),
        P("grp"),
        P("grp"),
        P("grp"),
    )
    return jax.shard_map(
        per_device,
        mesh=mesh,
        in_specs=placed,
        out_specs=(P(("grp", "per"), "hh", "st"), P("grp")),
        check_vma=False,
    )
```

```python
import functools

import jax
import jax.numpy as jnp
from jax import lax
from jax.experimental import pallas as pl
from jax.experimental.pallas import tpu as pltpu
from jax.sharding import PartitionSpec as P

HB = 128
LANES = 128
HALF = HB // 2
SEEN = 16.0
F32 = jnp.float32
BF16 = jnp.bfloat16
LOG2E = 1.4426950408889634
LN2 = 0.6931471805599453


def vmem():
    return pl.BlockSpec(memory_space=pltpu.VMEM)


def smem():
    return pl.BlockSpec(memory_space=pltpu.SMEM)


def hbm():
    return pl.BlockSpec(memory_space=pltpu.HBM)


def in_hbm(*arrays):
    return [pltpu.with_memory_space_constraint(x, pltpu.HBM) for x in arrays]


def params(mebibytes):
    return pltpu.CompilerParams(vmem_limit_bytes=mebibytes * 1024 * 1024)


def core_index():
    return lax.axis_index("st")


def is_forward_first():
    return 2 * lax.axis_index("per") < lax.axis_size("per")


def tiles(width):
    return [slice(q, q + LANES) for q in range(0, width, LANES)]


def fetch(pairs, sems):
    copies = [pltpu.make_async_copy(src, dst, sems.at[i]) for i, (src, dst) in enumerate(pairs)]
    for copy in copies:
        copy.start()
    for copy in copies:
        copy.wait()


def pack_kernel(count_ref, earn_any, start_any, len_any, out_ref, earn_ref, start_ref, len_ref, sems):
    fetch(((earn_any, earn_ref), (start_any, start_ref), (len_any, len_ref)), sems)
    periods, slot_rows = earn_ref.shape
    core = core_index()
    low_lane = lax.broadcasted_iota(jnp.int32, (periods // 2, HB), 1) < HALF
    time = lax.broadcasted_iota(jnp.int32, (periods, HB), 0)
    for slot in range(slot_rows // HB):
        cols = slice(slot * HB, (slot + 1) * HB)
        begin = start_ref[slot : slot + 1, :]
        seen = (time >= begin) & (time < begin + len_ref[slot : slot + 1, :])
        live = slot < count_ref[0]
        shift = jnp.where(live, jnp.where(seen, SEEN, 0.0), -SEEN)
        value = earn_ref[:, cols] + shift
        early, late = value[: periods // 2], value[periods // 2 :]
        turned = pltpu.roll(jnp.where(core == 0, late, early), HALF, 1)
        packed = jnp.where(low_lane, jnp.where(core == 0, early, turned), jnp.where(core == 0, turned, late))
        for to in range(out_ref.shape[0]):
            out_ref[to, :, cols] = packed


def put(ref, at, value):
    states = value.shape[0]
    high = value.astype(BF16)
    ref[at, :states, :states] = high
    ref[at, :states, states:] = (value - high.astype(F32)).astype(BF16)


def both_halves(mat, state):
    states = mat.shape[0]
    high = jnp.dot(mat[:, :states], state, preferred_element_type=F32)
    return high + jnp.dot(mat[:, states:], state, preferred_element_type=F32)


def fill_periods(mat, turned_pass, lead, ref, begin, end):
    @pl.loop(begin, end)
    def _(i):
        at = lead + i

        @pl.when(turned_pass)
        def _():
            lifted = jnp.exp(ref[i].T.astype(F32))
            put(mat, at, lifted * (1.0 / jnp.sum(lifted, axis=0, keepdims=True)))

        @pl.when(jnp.logical_not(turned_pass))
        def _():
            lifted = jnp.exp(ref[i].astype(F32))
            put(mat, at, lifted * (1.0 / jnp.sum(lifted, axis=1, keepdims=True)))


def prep_own_kernel(
    own_any, init_any, mean_any, sd_any, mat, consts, early, own_ref, init_ref, mean_ref, sd_ref, sem, sems
):
    part = own_ref.shape[0]
    copy = pltpu.make_async_copy(own_any, own_ref, sem)
    copy.start()
    fetch(((init_any, init_ref), (mean_any, mean_ref), (sd_any, sd_ref)), sems)
    raised = jnp.exp(init_ref[...])
    rows = (
        raised / jnp.sum(raised, axis=1, keepdims=True),
        mean_ref[...],
        (-0.5 * LOG2E) * jnp.exp(-2.0 * sd_ref[...]),
        -LOG2E * sd_ref[...],
    )
    for i, row in enumerate(rows):
        consts[i] = jnp.broadcast_to(row, (LANES, own_ref.shape[1])).T
    copy.wait()
    fill_periods(mat, is_forward_first(), core_index() * part, own_ref, 0, part)
    fill_periods(early, jnp.logical_not(is_forward_first()), 0, own_ref, 0, early.shape[0])


def prep_other_kernel(other_ref, mat_in, mat):
    part = other_ref.shape[0]
    fill_periods(mat, is_forward_first(), (1 - core_index()) * part, other_ref, 0, part)


def prep_second_kernel(own_ref, other_ref, early, after_any, mat, row_probs):
    rows = row_probs.shape[1]
    part = own_ref.shape[0]
    here = own_rows(lax.axis_index("hh") * rows, rows)
    turned_pass = jnp.logical_not(is_forward_first())
    own_lead = core_index() * part
    for i in range(early.shape[0]):
        mat[own_lead + i] = early[i]
    for lead, ref, begin in ((own_lead, own_ref, early.shape[0]), (part - own_lead, other_ref, 0)):
        for i in range(part):
            lifted = jnp.exp(ref[i, here, :].astype(F32))
            row_probs[lead + i] = lifted * (1.0 / jnp.sum(lifted, axis=1, keepdims=True))
        fill_periods(mat, turned_pass, lead, ref, begin, part)


def emission(sel_ref, consts, step_now, cols, less=None):
    gap = sel_ref[0, step_now, :1, cols] - consts[1]
    power = gap * gap * consts[2] + consts[3]
    return jnp.exp2(power if less is None else power - less)


def first_row(lead):
    return 0 if lax.axis_size("per") == 2 else lead


def is_moving(sel_ref, step_now, cols):
    return sel_ref[1, step_now, :1, cols] > 0.5


def is_seen(sel_ref, step_now, cols):
    return sel_ref[2, step_now, :1, cols] > 0.5


def column_sum(x):
    return jnp.sum(x, axis=0, keepdims=True)


def own_rows(row_begin, rows):
    return pl.ds(pl.multiple_of(row_begin, rows), rows)


def outer_sum(weights_ref, carried):
    return lax.dot_general(weights_ref[...], carried, (((1,), (1,)), ((), ())), preferred_element_type=F32)


def run_forward(lead, mat, hist, sel_ref, consts, ab_ref, logs, second=None, fresh=False):
    steps, states, width = hist.shape
    cuts = tiles(width)
    here = hist.at[0] if second is None else ab_ref
    last = [None] * len(cuts)
    inverse = [1.0 / column_sum(here[:, cols].astype(F32)) for cols in cuts]
    for k in range(steps):
        step_now = first_row(lead) + k
        here = there = ab_ref
        if second is None:
            here = hist.at[k]
            there = hist.at[k + 1] if k + 1 < steps else ab_ref
        else:
            weights_ref, row_begin, add_counts = second
            own_alpha = ab_ref[own_rows(row_begin, weights_ref.shape[0]), :].astype(F32)
        for q, cols in enumerate(cuts):
            begins = fresh and k == 0
            if not begins:
                moved = both_halves(mat[k], here[:, cols]) * inverse[q]
                moving = is_moving(sel_ref, step_now, cols)
            if second is not None:
                total = column_sum(moved * hist[k, :, cols].astype(F32))
                weight = jnp.where(moving, 1.0 / total, 0.0)
                weights_ref[:, cols] = (own_alpha[:, cols] * inverse[q] * weight).astype(BF16)
            emit = emission(sel_ref, consts, step_now, cols)
            joint = (consts[0] if begins else jnp.where(moving, moved, consts[0])) * emit
            scale = column_sum(joint)
            if second is None:
                seen = is_seen(sel_ref, step_now, cols)
                logs[q] = logs[q] + jnp.where(seen, jnp.log2(scale), 0.0)
            inverse[q] = 1.0 / scale
            there[:, cols] = joint.astype(BF16)
            last[q] = joint
        if second is not None:
            add_counts(k, outer_sum(weights_ref, hist[k]))
    return last


def run_backward(lead, mat, hist, sel_ref, consts, state, ub_ref, logs, leave, second=None, between=None):
    steps, states, width = hist.shape
    cuts = tiles(width)
    rest = [x[:1] for x in state]
    size = [jnp.zeros((1, LANES), F32) for _ in cuts]

    def step(k):
        step_now = first_row(lead) + k
        here = hist.at[k] if second is None else ub_ref
        grown = []
        for q, cols in enumerate(cuts):
            emit = emission(sel_ref, consts, step_now, cols, size[q] if second is None else None)
            carried = emit * state[q]
            here[:, cols] = carried.astype(BF16)
            whole = column_sum(carried)
            grown.append(whole)
            if second is None:
                size[q] = jnp.log2(whole)
                seen = is_seen(sel_ref, step_now, cols)
                logs[q] = logs[q] + jnp.where(seen, size[q], 0.0)
                begun = column_sum(carried * consts[0]) / whole
                rest[q] = jnp.where(seen, begun, rest[q])
        if second is not None:
            weights_ref, row_begin, add_counts = second
            own_alpha = hist[k, own_rows(row_begin, weights_ref.shape[0]), :].astype(F32)
        for q, cols in enumerate(cuts):
            product = both_halves(mat[k], here[:, cols])
            moving = is_moving(sel_ref, step_now, cols)
            if second is None:
                state[q] = jnp.where(moving, product, rest[q] * grown[q])
            else:
                shrink = 1.0 / grown[q]
                product = product * shrink
                total = column_sum(product * hist[k, :, cols].astype(F32))
                weight = jnp.where(moving, 1.0 / total, 0.0)
                weights_ref[:, cols] = (own_alpha[:, cols] * weight * shrink).astype(BF16)
                state[q] = jnp.where(moving, product, rest[q])
        if second is not None:
            add_counts(k, outer_sum(weights_ref, ub_ref[...]))

    def left():
        return [x * jnp.exp2(-y) for x, y in zip(state, size)]

    for k in reversed(range(1, steps)):
        step(k)
    if second is None:
        step(0)
        leave(left())
        return
    between()

    @pl.when(lead > 0)
    def _():
        step(0)
        leave(left())

    @pl.when(lead == 0)
    def _():
        second[2](0, jnp.zeros((second[0].shape[0], states), F32))


def put_state(state_out, values, logs, spread):
    for q, cols in enumerate(tiles(state_out.shape[1])):
        factor = jnp.exp2(logs[q] * (1.0 / spread)) / column_sum(values[q])
        state_out[:, cols] = (values[q] * factor).astype(BF16)


def state_sums(state_ref):
    return [column_sum(state_ref[:, cols].astype(F32)) for cols in tiles(state_ref.shape[1])]


def state_logs(sums, spread):
    return [jnp.log2(x) * spread for x in sums]


def unit_state(state_ref, sums):
    return [state_ref[:, cols].astype(F32) * (1.0 / x) for cols, x in zip(tiles(state_ref.shape[1]), sums)]


def first_kernel(resume, grids, part, rows_ref, mat, consts, *refs):
    state_in = refs[0] if resume else None
    hist, state_out, sel_ref, ab_ref = refs[-4:]
    chunk = part * grids + (pl.program_id(0) if grids > 1 else 0)
    steps, states, width = hist.shape
    forward_first, lead = is_forward_first(), lax.axis_index("per") * steps
    cuts = tiles(width)
    group, half_periods, slot_rows = rows_ref.shape
    tops = 2 * len(cuts)

    def scan_source(d, carry):
        rank, picked = carry
        for slot in range(slot_rows // HB):
            cols = slice(slot * HB, (slot + 1) * HB)
            block = rows_ref[d, :, cols]
            live = block > -0.5 * SEEN
            picked = [jnp.where(live & (rank == chunk * tops + i), block, old) for i, old in enumerate(picked)]
            rank = rank + live.astype(jnp.int32)
        return rank, picked

    carry = (jnp.zeros((half_periods, HB), jnp.int32), [jnp.zeros((half_periods, HB), F32)] * tops)
    if group <= 8:
        for d in range(group):
            carry = scan_source(d, carry)
    else:
        carry = lax.fori_loop(0, group, scan_source, carry)
    low_lane = lax.broadcasted_iota(jnp.int32, (half_periods, HB), 1) < HALF
    local = lax.axis_size("per") == 2

    def lay_out(parts):
        for q, cols in enumerate(cuts):
            left, right = carry[1][2 * q], carry[1][2 * q + 1]
            values = (
                jnp.where(low_lane, left, pltpu.roll(right, HALF, 1)),
                jnp.where(low_lane, pltpu.roll(left, HALF, 1), right),
            )
            flags = [(value > 0.5 * SEEN).astype(F32) for value in values]
            for late in parts:
                earn = jnp.where(flags[late] > 0.5, values[late] - SEEN, values[late])
                before = flags[0][half_periods - 1 :] if late else jnp.zeros((1, HB), F32)
                for i in range(half_periods):
                    at = i if local else late * half_periods + i
                    now = flags[late][i : i + 1]
                    sel_ref[0, at, :, cols] = jnp.broadcast_to(earn[i : i + 1], (8, HB))
                    sel_ref[1, at, :, cols] = jnp.broadcast_to(now * before, (8, HB))
                    sel_ref[2, at, :, cols] = jnp.broadcast_to(now, (8, HB))
                    before = now
            years = column_sum(flags[0] + flags[1])
            sel_ref[2, sel_ref.shape[1] - 1, :, cols] = jnp.broadcast_to(years, (8, HB))

    if not local:
        lay_out((0, 1))
    zeros = [jnp.zeros((1, LANES), F32) for _ in cuts]

    @pl.when(forward_first)
    def _():
        if local:
            lay_out((0,))
        if resume:
            hist[0] = state_in[...]
        else:
            for cols in cuts:
                hist[0, :, cols] = consts[0].astype(BF16)
        logs = state_logs(state_sums(state_in), half_periods) if resume else list(zeros)
        fresh = lax.axis_size("per") == 2
        last = run_forward(lead, mat, hist, sel_ref, consts, ab_ref, logs, fresh=fresh)
        put_state(state_out, last, logs, half_periods)

    @pl.when(jnp.logical_not(forward_first))
    def _():
        if local:
            lay_out((1,))
        sums = state_sums(state_in) if resume else None
        state = unit_state(state_in, sums) if resume else [jnp.ones((states, LANES), F32) for _ in cuts]
        logs = state_logs(sums, half_periods) if resume else list(zeros)

        def leave(values):
            grown = [old + jnp.log2(column_sum(x)) for old, x in zip(logs, values)]
            put_state(state_out, values, grown, half_periods)

        run_backward(lead, mat, hist, sel_ref, consts, state, ab_ref, logs, leave)


def second_kernel(resume, last, extend, grids, spread, *refs):
    refs = list(refs)
    sel_ref, mat, consts, hist, own_state, state_in = (refs.pop(0) for _ in range(6))
    counts_in, sums_in = (refs.pop(0), refs.pop(0)) if resume else (None, None)
    row_probs = refs.pop(0) if last else None
    mine_ref, other_ref = (refs.pop(0), refs.pop(0)) if last else (None, None)
    counts_out, sums_out = (None, None) if last else (refs.pop(0), refs.pop(0))
    state_out = refs.pop(0) if extend else None
    ab_ref, weights_ref = refs[:2]
    counts_ref, sums_ref = refs[2:] if last else (counts_out, sums_out)
    chunk = pl.program_id(0) if grids > 1 else 0
    steps, states, width = hist.shape
    core, forward_first = core_index(), is_forward_first()
    row_begin = lax.axis_index("hh") * weights_ref.shape[0]
    lead = lax.axis_index("per") * steps
    rows = weights_ref.shape[0]

    def centre(k, counts):
        probs = row_probs[k]
        weighted = probs * counts
        grad = weighted - probs * jnp.sum(weighted, axis=1, keepdims=True)
        at = slice(k * rows, (k + 1) * rows)
        left, right = grad[:, :LANES], grad[:, LANES:]
        mine_ref[at, :] = jnp.where(core == 0, left, right)
        other_ref[at, :] = jnp.where(core == 0, right, left)

    def add_counts(k, counts):
        if grids > 1:
            counts_ref[k] += counts
            return
        if resume:
            counts = counts + counts_in[k]
        if last:
            centre(k, counts)
        else:
            counts_ref[k] = counts

    second = (weights_ref, row_begin, add_counts)

    @pl.when(chunk == 0)
    def _():
        if grids > 1:
            counts_ref[...] = jnp.zeros_like(counts_ref)
        sums_ref[...] = sums_in[...] if resume else jnp.zeros_like(sums_ref)

    def add_sums(alpha_ref, other_state):
        total = jnp.zeros((1, LANES), F32)
        years = jnp.zeros((8, LANES), F32)
        for cols, here, there in zip(tiles(width), state_sums(alpha_ref), state_sums(other_state)):
            meet = column_sum(alpha_ref[:, cols].astype(F32) * (1.0 / here) * other_state[:, cols].astype(F32))
            scales = (jnp.log2(here) + jnp.log2(there)) * spread
            total += (scales + jnp.log2(meet / there)) * LN2
            years += sel_ref[2, sel_ref.shape[1] - 1, :, cols]
        total = jnp.broadcast_to(jnp.sum(total, axis=1, keepdims=True), (1, LANES))
        years = jnp.broadcast_to(jnp.sum(years[:1], axis=1, keepdims=True), (1, LANES))
        row = lax.broadcasted_iota(jnp.int32, (8, LANES), 0)
        sums_ref[...] += jnp.where(row == 0, total, jnp.where(row == 1, years, 0.0))

    zeros = [jnp.zeros((1, LANES), F32) for _ in tiles(width)]

    @pl.when(jnp.logical_not(forward_first))
    def _():
        ab_ref[...] = state_in[...]
        values = run_forward(lead, mat, hist, sel_ref, consts, ab_ref, list(zeros), second)
        add_sums(state_in, own_state)
        if extend:
            put_state(state_out, values, zeros, spread)

    @pl.when(forward_first)
    def _():
        state = unit_state(state_in, state_sums(state_in))
        leave = lambda values: put_state(state_out, values, zeros, spread) if extend else None
        run_backward(lead, mat, hist, sel_ref, consts, state, ab_ref, list(zeros), leave, second, lambda: add_sums(own_state, state_in))

    if last:

        @pl.when(chunk == grids - 1)
        def _():
            if grids > 1:
                for k in range(steps):
                    centre(k, counts_ref[k])
            mine_ref[steps * rows :, :] = sums_ref[...]
            other_ref[steps * rows :, :] = sums_ref[...]


def finish_kernel(scale, mine_ref, other_ref, grad_ref, mean_ref):
    count = grad_ref.shape[0]
    total = mine_ref[count : count + 1, :] + other_ref[count : count + 1, :]
    years = mine_ref[count + 1 : count + 2, :] + other_ref[count + 1 : count + 2, :]
    grad_ref[...] = (mine_ref[:count, :] + other_ref[:count, :]) * (scale / years)
    mean_ref[0] = (total / years)[0, 0]


def per_device(
    earnings, starts, lengths, block_count, trans_logits, init_logits, state_mean, log_sd
):
    slot_rows, periods = earnings.shape
    states = init_logits.shape[0]
    group = lax.axis_size(("hh", "per"))
    sides = lax.axis_size("per")
    cores = lax.axis_size("st")
    part = trans_logits.shape[0]
    steps = part * cores
    rows = states // lax.axis_size("hh")
    households = group * HB // cores
    parts = 2 if households <= 4 * HB else 1
    share = households // parts
    width = min(2 * HB, share)
    grids = share // width
    side = lax.axis_index("per")
    shaped = jax.ShapeDtypeStruct
    dma = pltpu.SemaphoreType.DMA

    swap = [(0, 1), (1, 0)]
    vec_row = pltpu.VMEM((1, states), F32)
    slots = pltpu.VMEM((slot_rows // HB, HB), jnp.int32)
    packed = pl.pallas_call(
        pack_kernel,
        out_shape=pltpu.VMEM((group, periods // 2, slot_rows), F32),
        in_specs=[smem()] + [hbm()] * 3,
        out_specs=vmem(),
        scratch_shapes=[pltpu.VMEM((periods, slot_rows), F32), slots, slots, dma((3,))],
        compiler_params=params(2),
        name="pack",
    )(block_count, *in_hbm(earnings.T, starts.reshape(-1, HB), lengths.reshape(-1, HB)))
    packed, later_logits = lax.optimization_barrier((packed, trans_logits))
    other_logits = lax.ppermute(later_logits, "st", swap)
    along = group // sides
    centre = along // 2
    outward = sorted(range(along), key=lambda z: (abs(z - centre), -z))
    listed = [z * sides + x for z in outward for x in reversed(range(sides))]
    gathered = lax.all_to_all(
        packed, ("hh", "per", "st"), split_axis=0, concat_axis=0,
        axis_index_groups=[[n * cores + c for n in listed] for c in range(cores)], tiled=True,
    )
    mat_shape = shaped((steps, states, 2 * states), BF16)
    first_mat, consts, early_mat = pl.pallas_call(
        prep_own_kernel,
        out_shape=[
            pltpu.VMEM(mat_shape.shape, BF16),
            pltpu.VMEM((4, states, LANES), F32),
            pltpu.VMEM((max(part - 1, 1),) + mat_shape.shape[1:], BF16),
        ],
        in_specs=[hbm()] * 4,
        out_specs=[vmem()] * 3,
        scratch_shapes=[pltpu.VMEM(trans_logits.shape, BF16), vec_row, vec_row, vec_row, dma, dma((3,))],
        compiler_params=params(4),
        name="prep_own",
    )(
        *in_hbm(
            trans_logits,
            init_logits.reshape(1, states), state_mean.reshape(1, states), log_sd.reshape(1, states),
        )
    )
    first_mat = pl.pallas_call(
        prep_other_kernel,
        out_shape=pltpu.VMEM(mat_shape.shape, BF16),
        in_specs=[vmem(), vmem()],
        out_specs=vmem(),
        input_output_aliases={1: 0},
        compiler_params=params(4),
        name="prep_other",
    )(other_logits, first_mat)

    def prep_second(after):
        return pl.pallas_call(
            prep_second_kernel,
            out_shape=[mat_shape, shaped((steps, rows, states), F32)],
            in_specs=[vmem(), vmem(), vmem(), hbm()],
            out_specs=[vmem(), vmem()],
            compiler_params=params(4),
            name="prep_second",
        )(trans_logits, other_logits, early_mat, after)

    def whole(*shape):
        if grids == 1:
            return vmem()
        return pl.BlockSpec(shape, lambda g: (0,) * len(shape))

    def lanes(*lead):
        if grids == 1:
            return vmem()
        return pl.BlockSpec(lead + (width,), lambda g: (0,) * len(lead) + (g,))

    grid = (grids,) if grids > 1 else ()
    hist_shape = shaped((steps, states, share), BF16)
    state_shape = shaped((states, share), BF16)
    laid = (steps if sides == 2 else periods) + 1
    sel_shape = shaped((3, laid, 8, share), F32)
    swap_shape = shaped((steps * rows + 8, LANES), F32)
    counts_shape = shaped((steps, rows, states), F32)
    sums_shape = shaped((8, LANES), F32)
    hist_spec, state_spec, sel_spec = lanes(steps, states), lanes(states), lanes(3, laid, 8)
    const_spec = whole(4, states, LANES)

    def first_pass(index, state_in):
        resume = state_in is not None
        return pl.pallas_call(
            functools.partial(first_kernel, resume, grids, index),
            grid=grid,
            out_shape=[hist_shape, state_shape, sel_shape],
            in_specs=[whole(*gathered.shape), whole(*first_mat.shape), const_spec]
            + [state_spec] * resume,
            out_specs=[hist_spec, state_spec, sel_spec],
            scratch_shapes=[pltpu.VMEM((states, width), BF16)],
            compiler_params=params(8 if grids == 1 else 32),
            name="first_pass",
        )(gathered, first_mat, consts, *([state_in] if resume else []))

    def second_pass(kept, state_in, sums_in, last, extend):
        hist, own_state, sel = kept
        resume = sums_in is not None
        scratch = [
            pltpu.VMEM((states, width), BF16),
            pltpu.VMEM((rows, width), BF16),
        ]
        counts_spec, sums_spec = whole(*counts_shape.shape), whole(*sums_shape.shape)
        if last:
            out_shape = [swap_shape] * 2
            scratch += [pltpu.VMEM(counts_shape.shape, F32), pltpu.VMEM(sums_shape.shape, F32)]
        else:
            out_shape = [counts_shape, sums_shape]
        out_specs = [whole(*x.shape) for x in out_shape]
        if extend:
            out_shape, out_specs = out_shape + [state_shape], out_specs + [state_spec]
        return pl.pallas_call(
            functools.partial(second_kernel, resume, last, extend, grids, periods // 2),
            grid=grid,
            out_shape=out_shape,
            in_specs=[sel_spec, whole(*second_mat.shape), const_spec, hist_spec, state_spec, state_spec]
            + [counts_spec, sums_spec] * resume
            + [whole(*row_probs.shape)] * last,
            out_specs=out_specs,
            scratch_shapes=scratch,
            compiler_params=params(8 if grids == 1 else 32),
            name="second_pass",
        )(
            sel, second_mat, consts, hist, own_state, state_in,
            *(sums_in if resume else []),
            *([row_probs] if last else []),
        )

    def hand_over(state, stage):
        moves = [(stage, stage + 1), (sides - 1 - stage, sides - 2 - stage)]
        return lax.ppermute(state, "per", moves)

    if sides == 2:
        kept = [first_pass(index, None) for index in range(parts)]
        arrived = [hand_over(each[1], 0) for each in kept]
        second_mat, row_probs = prep_second(kept[-1][1])
        sums = None
        for index in range(parts):
            sums = second_pass(kept[index], arrived[index], sums, index == parts - 1, False)
        mine, other = sums
    else:
        kept = [jnp.zeros(x.shape, x.dtype) for x in (hist_shape, state_shape, sel_shape)]
        done = [jnp.zeros(x.shape, x.dtype) for x in (swap_shape, swap_shape, state_shape)]
        state = None
        second_mat, row_probs = prep_second(gathered)
        for stage in range(sides):
            active = (side == stage) | (side == sides - 1 - stage)
            if stage < sides // 2:
                kept = lax.cond(
                    active, lambda x, kept: list(first_pass(0, x)), lambda x, kept: kept, state, kept
                )
                state = kept[1]
            else:
                done = lax.cond(
                    active,
                    lambda x, done: list(second_pass(kept, x, None, True, True)),
                    lambda x, done: done,
                    state,
                    done,
                )
                state = done[2]
            if stage < sides - 1:
                state = hand_over(state, stage)
        mine, other, _ = done
        total = jnp.where(side == sides // 2, mine[steps * rows], 0.0)
        total = lax.psum(total, "per")
        mine = mine.at[steps * rows].set(total)
        other = other.at[steps * rows].set(total)
    received = lax.ppermute(other, "st", swap)
    trans_grad, mean_loglik = pl.pallas_call(
        functools.partial(finish_kernel, float(states * states * periods)),
        out_shape=[shaped((steps * rows, LANES), F32), shaped((1,), F32)],
        in_specs=[vmem(), vmem()],
        out_specs=[vmem(), smem()],
        compiler_params=params(4),
        name="finish",
    )(mine, received)
    return (trans_grad.reshape(steps, rows, LANES), mean_loglik)


def solution(mesh):
    placed = (
        P(("hh", "per"), None),
        P(("hh", "per")),
        P(("hh", "per")),
        P(("hh", "per")),
        P(("grp", "per", "st"), None, None),
        P("grp"),
        P("grp"),
        P("grp"),
    )
    return jax.shard_map(
        per_device,
        mesh=mesh,
        in_specs=placed,
        out_specs=(P(("grp", "per"), "hh", "st"), P("grp")),
        check_vma=False,
    )
```

```python
import functools

import jax
import jax.numpy as jnp
from jax import lax
from jax.experimental import pallas as pl
from jax.experimental.pallas import tpu as pltpu
from jax.sharding import PartitionSpec as P

HB = 128
LANES = 128
HALF = HB // 2
SEEN = 16.0
F32 = jnp.float32
BF16 = jnp.bfloat16
LOG2E = 1.4426950408889634
LN2 = 0.6931471805599453


def vmem():
    return pl.BlockSpec(memory_space=pltpu.VMEM)


def smem():
    return pl.BlockSpec(memory_space=pltpu.SMEM)


def hbm():
    return pl.BlockSpec(memory_space=pltpu.HBM)


def in_hbm(*arrays):
    return [pltpu.with_memory_space_constraint(x, pltpu.HBM) for x in arrays]


def params(mebibytes):
    return pltpu.CompilerParams(vmem_limit_bytes=mebibytes * 1024 * 1024)


def core_index():
    return lax.axis_index("st")


def is_forward_first():
    return 2 * lax.axis_index("per") < lax.axis_size("per")


def tiles(width):
    return [slice(q, q + LANES) for q in range(0, width, LANES)]


def fetch(pairs, sems):
    copies = [pltpu.make_async_copy(src, dst, sems.at[i]) for i, (src, dst) in enumerate(pairs)]
    for copy in copies:
        copy.start()
    for copy in copies:
        copy.wait()


def pack_kernel(count_ref, earn_any, start_any, len_any, out_ref, earn_ref, start_ref, len_ref, sems):
    fetch(((earn_any, earn_ref), (start_any, start_ref), (len_any, len_ref)), sems)
    periods, slot_rows = earn_ref.shape
    core = core_index()
    low_lane = lax.broadcasted_iota(jnp.int32, (periods // 2, HB), 1) < HALF
    time = lax.broadcasted_iota(jnp.int32, (periods, HB), 0)
    for slot in range(slot_rows // HB):
        cols = slice(slot * HB, (slot + 1) * HB)
        begin = start_ref[slot : slot + 1, :]
        seen = (time >= begin) & (time < begin + len_ref[slot : slot + 1, :])
        live = slot < count_ref[0]
        shift = jnp.where(live, jnp.where(seen, SEEN, 0.0), -SEEN)
        value = earn_ref[:, cols] + shift
        early, late = value[: periods // 2], value[periods // 2 :]
        turned = pltpu.roll(jnp.where(core == 0, late, early), HALF, 1)
        packed = jnp.where(low_lane, jnp.where(core == 0, early, turned), jnp.where(core == 0, turned, late))
        for to in range(out_ref.shape[0]):
            out_ref[to, :, cols] = packed


def put(ref, at, value):
    states = value.shape[0]
    high = value.astype(BF16)
    ref[at, :states, :states] = high
    ref[at, :states, states:] = (value - high.astype(F32)).astype(BF16)


def both_halves(mat, state):
    states = mat.shape[0]
    high = jnp.dot(mat[:, :states], state, preferred_element_type=F32)
    return high + jnp.dot(mat[:, states:], state, preferred_element_type=F32)


def fill_periods(mat, turned_pass, lead, ref, begin, end):
    @pl.loop(begin, end)
    def _(i):
        at = lead + i

        @pl.when(turned_pass)
        def _():
            lifted = jnp.exp(ref[i].T.astype(F32))
            put(mat, at, lifted * (1.0 / jnp.sum(lifted, axis=0, keepdims=True)))

        @pl.when(jnp.logical_not(turned_pass))
        def _():
            lifted = jnp.exp(ref[i].astype(F32))
            put(mat, at, lifted * (1.0 / jnp.sum(lifted, axis=1, keepdims=True)))


def prep_own_kernel(
    own_any, init_any, mean_any, sd_any, mat, consts, early, own_ref, init_ref, mean_ref, sd_ref, sem, sems
):
    part = own_ref.shape[0]
    copy = pltpu.make_async_copy(own_any, own_ref, sem)
    copy.start()
    fetch(((init_any, init_ref), (mean_any, mean_ref), (sd_any, sd_ref)), sems)
    raised = jnp.exp(init_ref[...])
    rows = (
        raised / jnp.sum(raised, axis=1, keepdims=True),
        mean_ref[...],
        (-0.5 * LOG2E) * jnp.exp(-2.0 * sd_ref[...]),
        -LOG2E * sd_ref[...],
    )
    for i, row in enumerate(rows):
        consts[i] = jnp.broadcast_to(row, (LANES, own_ref.shape[1])).T
    copy.wait()
    fill_periods(mat, is_forward_first(), core_index() * part, own_ref, 0, part)
    fill_periods(early, jnp.logical_not(is_forward_first()), 0, own_ref, 0, early.shape[0])


def prep_other_kernel(other_ref, mat_in, mat):
    part = other_ref.shape[0]
    fill_periods(mat, is_forward_first(), (1 - core_index()) * part, other_ref, 0, part)


def prep_second_kernel(own_ref, other_ref, early, after_any, mat, row_probs):
    rows = row_probs.shape[1]
    part = own_ref.shape[0]
    here = own_rows(lax.axis_index("hh") * rows, rows)
    turned_pass = jnp.logical_not(is_forward_first())
    own_lead = core_index() * part
    for i in range(early.shape[0]):
        mat[own_lead + i] = early[i]
    for lead, ref, begin in ((own_lead, own_ref, early.shape[0]), (part - own_lead, other_ref, 0)):
        for i in range(part):
            lifted = jnp.exp(ref[i, here, :].astype(F32))
            row_probs[lead + i] = lifted * (1.0 / jnp.sum(lifted, axis=1, keepdims=True))
        fill_periods(mat, turned_pass, lead, ref, begin, part)


def emission(sel_ref, consts, step_now, cols, less=None):
    gap = sel_ref[0, step_now, :1, cols] - consts[1]
    power = gap * gap * consts[2] + consts[3]
    return jnp.exp2(power if less is None else power - less)


def first_row(lead):
    return 0 if lax.axis_size("per") == 2 else lead


def is_moving(sel_ref, step_now, cols):
    return sel_ref[1, step_now, :1, cols] > 0.5


def is_seen(sel_ref, step_now, cols):
    return sel_ref[2, step_now, :1, cols] > 0.5


def column_sum(x):
    return jnp.sum(x, axis=0, keepdims=True)


def own_rows(row_begin, rows):
    return pl.ds(pl.multiple_of(row_begin, rows), rows)


def outer_sum(weights_ref, carried):
    return lax.dot_general(weights_ref[...], carried, (((1,), (1,)), ((), ())), preferred_element_type=F32)


def run_forward(lead, mat, hist, sel_ref, consts, ab_ref, logs, second=None, fresh=False):
    steps, states, width = hist.shape
    cuts = tiles(width)
    here = hist.at[0] if second is None else ab_ref
    last = [None] * len(cuts)
    inverse = [1.0 / column_sum(here[:, cols].astype(F32)) for cols in cuts]
    for k in range(steps):
        step_now = first_row(lead) + k
        here = there = ab_ref
        if second is None:
            here = hist.at[k]
            there = hist.at[k + 1] if k + 1 < steps else ab_ref
        else:
            weights_ref, row_begin, add_counts = second
            own_alpha = ab_ref[own_rows(row_begin, weights_ref.shape[0]), :].astype(F32)
        for q, cols in enumerate(cuts):
            begins = fresh and k == 0
            if not begins:
                moved = both_halves(mat[k], here[:, cols]) * inverse[q]
                moving = is_moving(sel_ref, step_now, cols)
            if second is not None:
                total = column_sum(moved * hist[k, :, cols].astype(F32))
                weight = jnp.where(moving, 1.0 / total, 0.0)
                weights_ref[:, cols] = (own_alpha[:, cols] * inverse[q] * weight).astype(BF16)
            emit = emission(sel_ref, consts, step_now, cols)
            joint = (consts[0] if begins else jnp.where(moving, moved, consts[0])) * emit
            scale = column_sum(joint)
            if second is None:
                seen = is_seen(sel_ref, step_now, cols)
                logs[q] = logs[q] + jnp.where(seen, jnp.log2(scale), 0.0)
            inverse[q] = 1.0 / scale
            there[:, cols] = joint.astype(BF16)
            last[q] = joint
        if second is not None:
            add_counts(k, outer_sum(weights_ref, hist[k]))
    return last


def run_backward(lead, mat, hist, sel_ref, consts, state, ub_ref, logs, leave, second=None, between=None):
    steps, states, width = hist.shape
    cuts = tiles(width)
    rest = [x[:1] for x in state]
    size = [jnp.zeros((1, LANES), F32) for _ in cuts]

    def step(k):
        step_now = first_row(lead) + k
        here = hist.at[k] if second is None else ub_ref
        grown = []
        for q, cols in enumerate(cuts):
            emit = emission(sel_ref, consts, step_now, cols, size[q] if second is None else None)
            carried = emit * state[q]
            here[:, cols] = carried.astype(BF16)
            whole = column_sum(carried)
            grown.append(whole)
            if second is None:
                size[q] = jnp.log2(whole)
                seen = is_seen(sel_ref, step_now, cols)
                logs[q] = logs[q] + jnp.where(seen, size[q], 0.0)
                begun = column_sum(carried * consts[0]) / whole
                rest[q] = jnp.where(seen, begun, rest[q])
        if second is not None:
            weights_ref, row_begin, add_counts = second
            own_alpha = hist[k, own_rows(row_begin, weights_ref.shape[0]), :].astype(F32)
        for q, cols in enumerate(cuts):
            product = both_halves(mat[k], here[:, cols])
            moving = is_moving(sel_ref, step_now, cols)
            if second is None:
                state[q] = jnp.where(moving, product, rest[q] * grown[q])
            else:
                shrink = 1.0 / grown[q]
                product = product * shrink
                total = column_sum(product * hist[k, :, cols].astype(F32))
                weight = jnp.where(moving, 1.0 / total, 0.0)
                weights_ref[:, cols] = (own_alpha[:, cols] * weight * shrink).astype(BF16)
                state[q] = jnp.where(moving, product, rest[q])
        if second is not None:
            add_counts(k, outer_sum(weights_ref, ub_ref[...]))

    def left():
        return [x * jnp.exp2(-y) for x, y in zip(state, size)]

    for k in reversed(range(1, steps)):
        step(k)
    if second is None:
        step(0)
        leave(left())
        return
    between()

    @pl.when(lead > 0)
    def _():
        step(0)
        leave(left())

    @pl.when(lead == 0)
    def _():
        second[2](0, jnp.zeros((second[0].shape[0], states), F32))


def put_state(state_out, values, logs, spread):
    for q, cols in enumerate(tiles(state_out.shape[1])):
        factor = jnp.exp2(logs[q] * (1.0 / spread)) / column_sum(values[q])
        state_out[:, cols] = (values[q] * factor).astype(BF16)


def state_sums(state_ref):
    return [column_sum(state_ref[:, cols].astype(F32)) for cols in tiles(state_ref.shape[1])]


def state_logs(sums, spread):
    return [jnp.log2(x) * spread for x in sums]


def unit_state(state_ref, sums):
    return [state_ref[:, cols].astype(F32) * (1.0 / x) for cols, x in zip(tiles(state_ref.shape[1]), sums)]


def first_kernel(resume, grids, part, rows_ref, mat, consts, *refs):
    state_in = refs[0] if resume else None
    hist, state_out, sel_ref, ab_ref = refs[-4:]
    chunk = part * grids + (pl.program_id(0) if grids > 1 else 0)
    steps, states, width = hist.shape
    forward_first, lead = is_forward_first(), lax.axis_index("per") * steps
    cuts = tiles(width)
    group, half_periods, slot_rows = rows_ref.shape
    tops = 2 * len(cuts)

    def scan_source(d, carry):
        rank, picked = carry
        for slot in range(slot_rows // HB):
            cols = slice(slot * HB, (slot + 1) * HB)
            block = rows_ref[d, :, cols]
            live = block > -0.5 * SEEN
            picked = [jnp.where(live & (rank == chunk * tops + i), block, old) for i, old in enumerate(picked)]
            rank = rank + live.astype(jnp.int32)
        return rank, picked

    carry = (jnp.zeros((half_periods, HB), jnp.int32), [jnp.zeros((half_periods, HB), F32)] * tops)
    if group <= 8:
        for d in range(group):
            carry = scan_source(d, carry)
    else:
        carry = lax.fori_loop(0, group, scan_source, carry)
    low_lane = lax.broadcasted_iota(jnp.int32, (half_periods, HB), 1) < HALF
    local = lax.axis_size("per") == 2

    def lay_out(parts):
        for q, cols in enumerate(cuts):
            left, right = carry[1][2 * q], carry[1][2 * q + 1]
            values = (
                jnp.where(low_lane, left, pltpu.roll(right, HALF, 1)),
                jnp.where(low_lane, pltpu.roll(left, HALF, 1), right),
            )
            flags = [(value > 0.5 * SEEN).astype(F32) for value in values]
            for late in parts:
                earn = jnp.where(flags[late] > 0.5, values[late] - SEEN, values[late])
                before = flags[0][half_periods - 1 :] if late else jnp.zeros((1, HB), F32)
                for i in range(half_periods):
                    at = i if local else late * half_periods + i
                    now = flags[late][i : i + 1]
                    sel_ref[0, at, :, cols] = jnp.broadcast_to(earn[i : i + 1], (8, HB))
                    sel_ref[1, at, :, cols] = jnp.broadcast_to(now * before, (8, HB))
                    sel_ref[2, at, :, cols] = jnp.broadcast_to(now, (8, HB))
                    before = now
            years = column_sum(flags[0] + flags[1])
            sel_ref[2, sel_ref.shape[1] - 1, :, cols] = jnp.broadcast_to(years, (8, HB))

    if not local:
        lay_out((0, 1))
    zeros = [jnp.zeros((1, LANES), F32) for _ in cuts]

    @pl.when(forward_first)
    def _():
        if local:
            lay_out((0,))
        if resume:
            hist[0] = state_in[...]
        else:
            for cols in cuts:
                hist[0, :, cols] = consts[0].astype(BF16)
        logs = state_logs(state_sums(state_in), half_periods) if resume else list(zeros)
        fresh = lax.axis_size("per") == 2
        last = run_forward(lead, mat, hist, sel_ref, consts, ab_ref, logs, fresh=fresh)
        put_state(state_out, last, logs, half_periods)

    @pl.when(jnp.logical_not(forward_first))
    def _():
        if local:
            lay_out((1,))
        sums = state_sums(state_in) if resume else None
        state = unit_state(state_in, sums) if resume else [jnp.ones((states, LANES), F32) for _ in cuts]
        logs = state_logs(sums, half_periods) if resume else list(zeros)

        def leave(values):
            grown = [old + jnp.log2(column_sum(x)) for old, x in zip(logs, values)]
            put_state(state_out, values, grown, half_periods)

        run_backward(lead, mat, hist, sel_ref, consts, state, ab_ref, logs, leave)


def second_kernel(resume, last, extend, grids, spread, *refs):
    refs = list(refs)
    sel_ref, mat, consts, hist, own_state, state_in = (refs.pop(0) for _ in range(6))
    counts_in, sums_in = (refs.pop(0), refs.pop(0)) if resume else (None, None)
    row_probs = refs.pop(0) if last else None
    mine_ref, other_ref = (refs.pop(0), refs.pop(0)) if last else (None, None)
    counts_out, sums_out = (None, None) if last else (refs.pop(0), refs.pop(0))
    state_out = refs.pop(0) if extend else None
    ab_ref, weights_ref = refs[:2]
    counts_ref, sums_ref = refs[2:] if last else (counts_out, sums_out)
    chunk = pl.program_id(0) if grids > 1 else 0
    steps, states, width = hist.shape
    core, forward_first = core_index(), is_forward_first()
    row_begin = lax.axis_index("hh") * weights_ref.shape[0]
    lead = lax.axis_index("per") * steps
    rows = weights_ref.shape[0]

    def centre(k, counts):
        probs = row_probs[k]
        weighted = probs * counts
        grad = weighted - probs * jnp.sum(weighted, axis=1, keepdims=True)
        at = slice(k * rows, (k + 1) * rows)
        left, right = grad[:, :LANES], grad[:, LANES:]
        mine_ref[at, :] = jnp.where(core == 0, left, right)
        other_ref[at, :] = jnp.where(core == 0, right, left)

    def add_counts(k, counts):
        if grids > 1:
            counts_ref[k] += counts
            return
        if resume:
            counts = counts + counts_in[k]
        if last:
            centre(k, counts)
        else:
            counts_ref[k] = counts

    second = (weights_ref, row_begin, add_counts)

    @pl.when(chunk == 0)
    def _():
        if grids > 1:
            counts_ref[...] = jnp.zeros_like(counts_ref)
        sums_ref[...] = sums_in[...] if resume else jnp.zeros_like(sums_ref)

    def add_sums(alpha_ref, other_state):
        total = jnp.zeros((1, LANES), F32)
        years = jnp.zeros((8, LANES), F32)
        for cols, here, there in zip(tiles(width), state_sums(alpha_ref), state_sums(other_state)):
            meet = column_sum(alpha_ref[:, cols].astype(F32) * (1.0 / here) * other_state[:, cols].astype(F32))
            scales = (jnp.log2(here) + jnp.log2(there)) * spread
            total += (scales + jnp.log2(meet / there)) * LN2
            years += sel_ref[2, sel_ref.shape[1] - 1, :, cols]
        total = jnp.broadcast_to(jnp.sum(total, axis=1, keepdims=True), (1, LANES))
        years = jnp.broadcast_to(jnp.sum(years[:1], axis=1, keepdims=True), (1, LANES))
        row = lax.broadcasted_iota(jnp.int32, (8, LANES), 0)
        sums_ref[...] += jnp.where(row == 0, total, jnp.where(row == 1, years, 0.0))

    zeros = [jnp.zeros((1, LANES), F32) for _ in tiles(width)]

    @pl.when(jnp.logical_not(forward_first))
    def _():
        ab_ref[...] = state_in[...]
        values = run_forward(lead, mat, hist, sel_ref, consts, ab_ref, list(zeros), second)
        add_sums(state_in, own_state)
        if extend:
            put_state(state_out, values, zeros, spread)

    @pl.when(forward_first)
    def _():
        state = unit_state(state_in, state_sums(state_in))
        leave = lambda values: put_state(state_out, values, zeros, spread) if extend else None
        run_backward(lead, mat, hist, sel_ref, consts, state, ab_ref, list(zeros), leave, second, lambda: add_sums(own_state, state_in))

    if last:

        @pl.when(chunk == grids - 1)
        def _():
            if grids > 1:
                for k in range(steps):
                    centre(k, counts_ref[k])
            mine_ref[steps * rows :, :] = sums_ref[...]
            other_ref[steps * rows :, :] = sums_ref[...]


def finish_kernel(scale, mine_ref, other_ref, grad_ref, mean_ref):
    count = grad_ref.shape[0]
    total = mine_ref[count : count + 1, :] + other_ref[count : count + 1, :]
    years = mine_ref[count + 1 : count + 2, :] + other_ref[count + 1 : count + 2, :]
    grad_ref[...] = (mine_ref[:count, :] + other_ref[:count, :]) * (scale / years)
    mean_ref[0] = (total / years)[0, 0]


def per_device(
    earnings, starts, lengths, block_count, trans_logits, init_logits, state_mean, log_sd
):
    slot_rows, periods = earnings.shape
    states = init_logits.shape[0]
    group = lax.axis_size(("hh", "per"))
    sides = lax.axis_size("per")
    cores = lax.axis_size("st")
    part = trans_logits.shape[0]
    steps = part * cores
    rows = states // lax.axis_size("hh")
    households = group * HB // cores
    parts = 2 if households <= 4 * HB else 1
    share = households // parts
    width = min(2 * HB, share)
    grids = share // width
    side = lax.axis_index("per")
    shaped = jax.ShapeDtypeStruct
    dma = pltpu.SemaphoreType.DMA

    swap = [(0, 1), (1, 0)]
    vec_row = pltpu.VMEM((1, states), F32)
    slots = pltpu.VMEM((slot_rows // HB, HB), jnp.int32)
    packed = pl.pallas_call(
        pack_kernel,
        out_shape=pltpu.VMEM((group, periods // 2, slot_rows), F32),
        in_specs=[smem()] + [hbm()] * 3,
        out_specs=vmem(),
        scratch_shapes=[pltpu.VMEM((periods, slot_rows), F32), slots, slots, dma((3,))],
        compiler_params=params(2),
        name="pack",
    )(block_count, *in_hbm(earnings.T, starts.reshape(-1, HB), lengths.reshape(-1, HB)))
    packed, later_logits = lax.optimization_barrier((packed, trans_logits))
    other_logits = lax.ppermute(later_logits, "st", swap)
    along = group // sides
    centre = along // 2
    outward = sorted(range(along), key=lambda z: (abs(z - centre), -z))
    listed = [z * sides + x for z in outward for x in reversed(range(sides))]
    gathered = lax.all_to_all(
        packed, ("hh", "per", "st"), split_axis=0, concat_axis=0,
        axis_index_groups=[[n * cores + c for n in listed] for c in range(cores)], tiled=True,
    )
    mat_shape = shaped((steps, states, 2 * states), BF16)
    first_mat, consts, early_mat = pl.pallas_call(
        prep_own_kernel,
        out_shape=[
            pltpu.VMEM(mat_shape.shape, BF16),
            pltpu.VMEM((4, states, LANES), F32),
            pltpu.VMEM((max(part // 2, 1),) + mat_shape.shape[1:], BF16),
        ],
        in_specs=[hbm()] * 4,
        out_specs=[vmem()] * 3,
        scratch_shapes=[pltpu.VMEM(trans_logits.shape, BF16), vec_row, vec_row, vec_row, dma, dma((3,))],
        compiler_params=params(4),
        name="prep_own",
    )(
        *in_hbm(
            trans_logits,
            init_logits.reshape(1, states), state_mean.reshape(1, states), log_sd.reshape(1, states),
        )
    )
    first_mat = pl.pallas_call(
        prep_other_kernel,
        out_shape=pltpu.VMEM(mat_shape.shape, BF16),
        in_specs=[vmem(), vmem()],
        out_specs=vmem(),
        input_output_aliases={1: 0},
        compiler_params=params(4),
        name="prep_other",
    )(other_logits, first_mat)

    def prep_second(after):
        return pl.pallas_call(
            prep_second_kernel,
            out_shape=[mat_shape, shaped((steps, rows, states), F32)],
            in_specs=[vmem(), vmem(), vmem(), hbm()],
            out_specs=[vmem(), vmem()],
            compiler_params=params(4),
            name="prep_second",
        )(trans_logits, other_logits, early_mat, after)

    def whole(*shape):
        if grids == 1:
            return vmem()
        return pl.BlockSpec(shape, lambda g: (0,) * len(shape))

    def lanes(*lead):
        if grids == 1:
            return vmem()
        return pl.BlockSpec(lead + (width,), lambda g: (0,) * len(lead) + (g,))

    grid = (grids,) if grids > 1 else ()
    hist_shape = shaped((steps, states, share), BF16)
    state_shape = shaped((states, share), BF16)
    laid = (steps if sides == 2 else periods) + 1
    sel_shape = shaped((3, laid, 8, share), F32)
    swap_shape = shaped((steps * rows + 8, LANES), F32)
    counts_shape = shaped((steps, rows, states), F32)
    sums_shape = shaped((8, LANES), F32)
    hist_spec, state_spec, sel_spec = lanes(steps, states), lanes(states), lanes(3, laid, 8)
    const_spec = whole(4, states, LANES)

    def first_pass(index, state_in):
        resume = state_in is not None
        return pl.pallas_call(
            functools.partial(first_kernel, resume, grids, index),
            grid=grid,
            out_shape=[hist_shape, state_shape, sel_shape],
            in_specs=[whole(*gathered.shape), whole(*first_mat.shape), const_spec]
            + [state_spec] * resume,
            out_specs=[hist_spec, state_spec, sel_spec],
            scratch_shapes=[pltpu.VMEM((states, width), BF16)],
            compiler_params=params(8 if grids == 1 else 32),
            name="first_pass",
        )(gathered, first_mat, consts, *([state_in] if resume else []))

    def second_pass(kept, state_in, sums_in, last, extend):
        hist, own_state, sel = kept
        resume = sums_in is not None
        scratch = [
            pltpu.VMEM((states, width), BF16),
            pltpu.VMEM((rows, width), BF16),
        ]
        counts_spec, sums_spec = whole(*counts_shape.shape), whole(*sums_shape.shape)
        if last:
            out_shape = [swap_shape] * 2
            scratch += [pltpu.VMEM(counts_shape.shape, F32), pltpu.VMEM(sums_shape.shape, F32)]
        else:
            out_shape = [counts_shape, sums_shape]
        out_specs = [whole(*x.shape) for x in out_shape]
        if extend:
            out_shape, out_specs = out_shape + [state_shape], out_specs + [state_spec]
        return pl.pallas_call(
            functools.partial(second_kernel, resume, last, extend, grids, periods // 2),
            grid=grid,
            out_shape=out_shape,
            in_specs=[sel_spec, whole(*second_mat.shape), const_spec, hist_spec, state_spec, state_spec]
            + [counts_spec, sums_spec] * resume
            + [whole(*row_probs.shape)] * last,
            out_specs=out_specs,
            scratch_shapes=scratch,
            compiler_params=params(8 if grids == 1 else 32),
            name="second_pass",
        )(
            sel, second_mat, consts, hist, own_state, state_in,
            *(sums_in if resume else []),
            *([row_probs] if last else []),
        )

    def hand_over(state, stage):
        moves = [(stage, stage + 1), (sides - 1 - stage, sides - 2 - stage)]
        return lax.ppermute(state, "per", moves)

    if sides == 2:
        kept = [first_pass(index, None) for index in range(parts)]
        arrived = [hand_over(each[1], 0) for each in kept]
        second_mat, row_probs = prep_second(kept[-1][1])
        sums = None
        for index in range(parts):
            sums = second_pass(kept[index], arrived[index], sums, index == parts - 1, False)
        mine, other = sums
    else:
        kept = [jnp.zeros(x.shape, x.dtype) for x in (hist_shape, state_shape, sel_shape)]
        done = [jnp.zeros(x.shape, x.dtype) for x in (swap_shape, swap_shape, state_shape)]
        state = None
        second_mat, row_probs = prep_second(gathered)
        for stage in range(sides):
            active = (side == stage) | (side == sides - 1 - stage)
            if stage < sides // 2:
                kept = lax.cond(
                    active, lambda x, kept: list(first_pass(0, x)), lambda x, kept: kept, state, kept
                )
                state = kept[1]
            else:
                done = lax.cond(
                    active,
                    lambda x, done: list(second_pass(kept, x, None, True, True)),
                    lambda x, done: done,
                    state,
                    done,
                )
                state = done[2]
            if stage < sides - 1:
                state = hand_over(state, stage)
        mine, other, _ = done
        total = jnp.where(side == sides // 2, mine[steps * rows], 0.0)
        total = lax.psum(total, "per")
        mine = mine.at[steps * rows].set(total)
        other = other.at[steps * rows].set(total)
    received = lax.ppermute(other, "st", swap)
    trans_grad, mean_loglik = pl.pallas_call(
        functools.partial(finish_kernel, float(states * states * periods)),
        out_shape=[shaped((steps * rows, LANES), F32), shaped((1,), F32)],
        in_specs=[vmem(), vmem()],
        out_specs=[vmem(), smem()],
        compiler_params=params(4),
        name="finish",
    )(mine, received)
    return (trans_grad.reshape(steps, rows, LANES), mean_loglik)


def solution(mesh):
    placed = (
        P(("hh", "per"), None),
        P(("hh", "per")),
        P(("hh", "per")),
        P(("hh", "per")),
        P(("grp", "per", "st"), None, None),
        P("grp"),
        P("grp"),
        P("grp"),
    )
    return jax.shard_map(
        per_device,
        mesh=mesh,
        in_specs=placed,
        out_specs=(P(("grp", "per"), "hh", "st"), P("grp")),
        check_vma=False,
    )
```

```python
import functools

import jax
import jax.numpy as jnp
from jax import lax
from jax.experimental import pallas as pl
from jax.experimental.pallas import tpu as pltpu
from jax.sharding import PartitionSpec as P

HB = 128
LANES = 128
HALF = HB // 2
SEEN = 16.0
F32 = jnp.float32
BF16 = jnp.bfloat16
LOG2E = 1.4426950408889634
LN2 = 0.6931471805599453


def vmem():
    return pl.BlockSpec(memory_space=pltpu.VMEM)


def smem():
    return pl.BlockSpec(memory_space=pltpu.SMEM)


def hbm():
    return pl.BlockSpec(memory_space=pltpu.HBM)


def in_hbm(*arrays):
    return [pltpu.with_memory_space_constraint(x, pltpu.HBM) for x in arrays]


def params(mebibytes):
    return pltpu.CompilerParams(vmem_limit_bytes=mebibytes * 1024 * 1024)


def core_index():
    return lax.axis_index("st")


def is_forward_first():
    return 2 * lax.axis_index("per") < lax.axis_size("per")


def tiles(width):
    return [slice(q, q + LANES) for q in range(0, width, LANES)]


def fetch(pairs, sems):
    copies = [pltpu.make_async_copy(src, dst, sems.at[i]) for i, (src, dst) in enumerate(pairs)]
    for copy in copies:
        copy.start()
    for copy in copies:
        copy.wait()


def pack_kernel(count_ref, earn_any, start_any, len_any, out_ref, earn_ref, start_ref, len_ref, sems):
    fetch(((earn_any, earn_ref), (start_any, start_ref), (len_any, len_ref)), sems)
    periods, slot_rows = earn_ref.shape
    core = core_index()
    low_lane = lax.broadcasted_iota(jnp.int32, (periods // 2, HB), 1) < HALF
    time = lax.broadcasted_iota(jnp.int32, (periods, HB), 0)
    for slot in range(slot_rows // HB):
        cols = slice(slot * HB, (slot + 1) * HB)
        begin = start_ref[slot : slot + 1, :]
        seen = (time >= begin) & (time < begin + len_ref[slot : slot + 1, :])
        live = slot < count_ref[0]
        shift = jnp.where(live, jnp.where(seen, SEEN, 0.0), -SEEN)
        value = earn_ref[:, cols] + shift
        early, late = value[: periods // 2], value[periods // 2 :]
        turned = pltpu.roll(jnp.where(core == 0, late, early), HALF, 1)
        packed = jnp.where(low_lane, jnp.where(core == 0, early, turned), jnp.where(core == 0, turned, late))
        for to in range(out_ref.shape[0]):
            out_ref[to, :, cols] = packed


def put(ref, at, value):
    states = value.shape[0]
    high = value.astype(BF16)
    ref[at, :states, :states] = high
    ref[at, :states, states:] = (value - high.astype(F32)).astype(BF16)


def both_halves(mat, state):
    states = mat.shape[0]
    high = jnp.dot(mat[:, :states], state, preferred_element_type=F32)
    return high + jnp.dot(mat[:, states:], state, preferred_element_type=F32)


def fill_periods(mat, turned_pass, lead, ref, begin, end):
    @pl.loop(begin, end)
    def _(i):
        at = lead + i

        @pl.when(turned_pass)
        def _():
            lifted = jnp.exp(ref[i].T.astype(F32))
            put(mat, at, lifted * (1.0 / jnp.sum(lifted, axis=0, keepdims=True)))

        @pl.when(jnp.logical_not(turned_pass))
        def _():
            lifted = jnp.exp(ref[i].astype(F32))
            put(mat, at, lifted * (1.0 / jnp.sum(lifted, axis=1, keepdims=True)))


def prep_own_kernel(
    own_any, init_any, mean_any, sd_any, mat, consts, early, own_ref, init_ref, mean_ref, sd_ref, sem, sems
):
    part = own_ref.shape[0]
    copy = pltpu.make_async_copy(own_any, own_ref, sem)
    copy.start()
    fetch(((init_any, init_ref), (mean_any, mean_ref), (sd_any, sd_ref)), sems)
    raised = jnp.exp(init_ref[...])
    rows = (
        raised / jnp.sum(raised, axis=1, keepdims=True),
        mean_ref[...],
        (-0.5 * LOG2E) * jnp.exp(-2.0 * sd_ref[...]),
        -LOG2E * sd_ref[...],
    )
    for i, row in enumerate(rows):
        consts[i] = jnp.broadcast_to(row, (LANES, own_ref.shape[1])).T
    copy.wait()
    fill_periods(mat, is_forward_first(), core_index() * part, own_ref, 0, part)
    fill_periods(early, jnp.logical_not(is_forward_first()), 0, own_ref, 0, early.shape[0])


def prep_other_kernel(other_ref, mat_in, mat):
    part = other_ref.shape[0]
    fill_periods(mat, is_forward_first(), (1 - core_index()) * part, other_ref, 0, part)


def prep_second_kernel(own_ref, other_ref, early, after_any, mat, row_probs):
    rows = row_probs.shape[1]
    part = own_ref.shape[0]
    here = own_rows(lax.axis_index("hh") * rows, rows)
    turned_pass = jnp.logical_not(is_forward_first())
    own_lead = core_index() * part
    for i in range(early.shape[0]):
        mat[own_lead + i] = early[i]
    for lead, ref, begin in ((own_lead, own_ref, early.shape[0]), (part - own_lead, other_ref, 0)):
        for i in range(part):
            lifted = jnp.exp(ref[i, here, :].astype(F32))
            row_probs[lead + i] = lifted * (1.0 / jnp.sum(lifted, axis=1, keepdims=True))
        fill_periods(mat, turned_pass, lead, ref, begin, part)


def emission(sel_ref, consts, step_now, cols, less=None):
    gap = sel_ref[0, step_now, :1, cols] - consts[1]
    power = gap * gap * consts[2] + consts[3]
    return jnp.exp2(power if less is None else power - less)


def first_row(lead):
    return 0 if lax.axis_size("per") == 2 else lead


def is_moving(sel_ref, step_now, cols):
    return sel_ref[1, step_now, :1, cols] > 0.5


def is_seen(sel_ref, step_now, cols):
    return sel_ref[2, step_now, :1, cols] > 0.5


def column_sum(x):
    return jnp.sum(x, axis=0, keepdims=True)


def own_rows(row_begin, rows):
    return pl.ds(pl.multiple_of(row_begin, rows), rows)


def outer_sum(weights_ref, carried):
    return lax.dot_general(weights_ref[...], carried, (((1,), (1,)), ((), ())), preferred_element_type=F32)


def run_forward(lead, mat, hist, sel_ref, consts, ab_ref, logs, second=None, fresh=False, extend=True):
    steps, states, width = hist.shape
    cuts = tiles(width)
    here = hist.at[0] if second is None else ab_ref
    last = [None] * len(cuts)
    inverse = [1.0 / column_sum(here[:, cols].astype(F32)) for cols in cuts]
    for k in range(steps):
        step_now = first_row(lead) + k
        here = there = ab_ref
        if second is None:
            here = hist.at[k]
            there = hist.at[k + 1] if k + 1 < steps else ab_ref
        else:
            weights_ref, row_begin, add_counts = second
            own_alpha = ab_ref[own_rows(row_begin, weights_ref.shape[0]), :].astype(F32)
        for q, cols in enumerate(cuts):
            begins = fresh and k == 0
            if not begins:
                moved = both_halves(mat[k], here[:, cols]) * inverse[q]
                moving = is_moving(sel_ref, step_now, cols)
            if second is not None:
                total = column_sum(moved * hist[k, :, cols].astype(F32))
                weight = jnp.where(moving, 1.0 / total, 0.0)
                weights_ref[:, cols] = (own_alpha[:, cols] * inverse[q] * weight).astype(BF16)
                if k + 1 == steps and not extend:
                    continue
            emit = emission(sel_ref, consts, step_now, cols)
            joint = (consts[0] if begins else jnp.where(moving, moved, consts[0])) * emit
            scale = column_sum(joint)
            if second is None:
                seen = is_seen(sel_ref, step_now, cols)
                logs[q] = logs[q] + jnp.where(seen, jnp.log2(scale), 0.0)
            inverse[q] = 1.0 / scale
            there[:, cols] = joint.astype(BF16)
            last[q] = joint
        if second is not None:
            add_counts(k, outer_sum(weights_ref, hist[k]))
    return last


def run_backward(lead, mat, hist, sel_ref, consts, state, ub_ref, logs, leave, second=None, between=None):
    steps, states, width = hist.shape
    cuts = tiles(width)
    rest = [x[:1] for x in state]
    at_edge = lax.axis_size("per") == 2
    size = [jnp.zeros((1, LANES), F32) for _ in cuts]

    def step(k):
        step_now = first_row(lead) + k
        here = hist.at[k] if second is None else ub_ref
        grown = []
        for q, cols in enumerate(cuts):
            emit = emission(sel_ref, consts, step_now, cols, size[q] if second is None else None)
            carried = emit * state[q]
            here[:, cols] = carried.astype(BF16)
            whole = column_sum(carried)
            grown.append(whole)
            if second is None:
                size[q] = jnp.log2(whole)
                seen = is_seen(sel_ref, step_now, cols)
                logs[q] = logs[q] + jnp.where(seen, size[q], 0.0)
                begun = column_sum(carried * consts[0]) / whole
                rest[q] = jnp.where(seen, begun, rest[q])
        if second is not None:
            weights_ref, row_begin, add_counts = second
            own_alpha = hist[k, own_rows(row_begin, weights_ref.shape[0]), :].astype(F32)
        for q, cols in enumerate(cuts):
            product = both_halves(mat[k], here[:, cols])
            moving = is_moving(sel_ref, step_now, cols)
            if second is None:
                state[q] = jnp.where(moving, product, rest[q] * grown[q])
            else:
                shrink = 1.0 / grown[q]
                product = product * shrink
                total = column_sum(product * hist[k, :, cols].astype(F32))
                weight = jnp.where(moving, 1.0 / total, 0.0)
                weights_ref[:, cols] = (own_alpha[:, cols] * weight * shrink).astype(BF16)
                if k > 1 or not at_edge:
                    state[q] = jnp.where(moving, product, rest[q])
        if second is not None:
            add_counts(k, outer_sum(weights_ref, ub_ref[...]))

    def left():
        return [x * jnp.exp2(-y) for x, y in zip(state, size)]

    for k in reversed(range(1, steps)):
        step(k)
    if second is None:
        step(0)
        leave(left())
        return
    between()
    nothing = jnp.zeros((second[0].shape[0], states), F32)
    if at_edge:
        second[2](0, nothing)
        return

    @pl.when(lead > 0)
    def _():
        step(0)
        leave(left())

    @pl.when(lead == 0)
    def _():
        second[2](0, nothing)


def put_state(state_out, values, logs, spread):
    for q, cols in enumerate(tiles(state_out.shape[1])):
        factor = jnp.exp2(logs[q] * (1.0 / spread)) / column_sum(values[q])
        state_out[:, cols] = (values[q] * factor).astype(BF16)


def state_sums(state_ref):
    return [column_sum(state_ref[:, cols].astype(F32)) for cols in tiles(state_ref.shape[1])]


def state_logs(sums, spread):
    return [jnp.log2(x) * spread for x in sums]


def unit_state(state_ref, sums):
    return [state_ref[:, cols].astype(F32) * (1.0 / x) for cols, x in zip(tiles(state_ref.shape[1]), sums)]


def first_kernel(resume, grids, part, rows_ref, mat, consts, *refs):
    state_in = refs[0] if resume else None
    hist, state_out, sel_ref, ab_ref = refs[-4:]
    chunk = part * grids + (pl.program_id(0) if grids > 1 else 0)
    steps, states, width = hist.shape
    forward_first, lead = is_forward_first(), lax.axis_index("per") * steps
    cuts = tiles(width)
    group, half_periods, slot_rows = rows_ref.shape
    tops = 2 * len(cuts)

    def scan_source(d, carry):
        rank, picked = carry
        for slot in range(slot_rows // HB):
            cols = slice(slot * HB, (slot + 1) * HB)
            block = rows_ref[d, :, cols]
            live = block > -0.5 * SEEN
            picked = [jnp.where(live & (rank == chunk * tops + i), block, old) for i, old in enumerate(picked)]
            rank = rank + live.astype(jnp.int32)
        return rank, picked

    carry = (jnp.zeros((half_periods, HB), jnp.int32), [jnp.zeros((half_periods, HB), F32)] * tops)
    if group <= 8:
        for d in range(group):
            carry = scan_source(d, carry)
    else:
        carry = lax.fori_loop(0, group, scan_source, carry)
    low_lane = lax.broadcasted_iota(jnp.int32, (half_periods, HB), 1) < HALF
    local = lax.axis_size("per") == 2

    def lay_out(parts):
        for q, cols in enumerate(cuts):
            left, right = carry[1][2 * q], carry[1][2 * q + 1]
            values = (
                jnp.where(low_lane, left, pltpu.roll(right, HALF, 1)),
                jnp.where(low_lane, pltpu.roll(left, HALF, 1), right),
            )
            flags = [(value > 0.5 * SEEN).astype(F32) for value in values]
            for late in parts:
                earn = jnp.where(flags[late] > 0.5, values[late] - SEEN, values[late])
                before = flags[0][half_periods - 1 :] if late else jnp.zeros((1, HB), F32)
                for i in range(half_periods):
                    at = i if local else late * half_periods + i
                    now = flags[late][i : i + 1]
                    sel_ref[0, at, :, cols] = jnp.broadcast_to(earn[i : i + 1], (8, HB))
                    sel_ref[1, at, :, cols] = jnp.broadcast_to(now * before, (8, HB))
                    sel_ref[2, at, :, cols] = jnp.broadcast_to(now, (8, HB))
                    before = now
            years = column_sum(flags[0] + flags[1])
            sel_ref[2, sel_ref.shape[1] - 1, :, cols] = jnp.broadcast_to(years, (8, HB))

    if not local:
        lay_out((0, 1))
    zeros = [jnp.zeros((1, LANES), F32) for _ in cuts]

    @pl.when(forward_first)
    def _():
        if local:
            lay_out((0,))
        if resume:
            hist[0] = state_in[...]
        else:
            for cols in cuts:
                hist[0, :, cols] = consts[0].astype(BF16)
        logs = state_logs(state_sums(state_in), half_periods) if resume else list(zeros)
        fresh = lax.axis_size("per") == 2
        last = run_forward(lead, mat, hist, sel_ref, consts, ab_ref, logs, fresh=fresh)
        put_state(state_out, last, logs, half_periods)

    @pl.when(jnp.logical_not(forward_first))
    def _():
        if local:
            lay_out((1,))
        sums = state_sums(state_in) if resume else None
        state = unit_state(state_in, sums) if resume else [jnp.ones((states, LANES), F32) for _ in cuts]
        logs = state_logs(sums, half_periods) if resume else list(zeros)

        def leave(values):
            grown = [old + jnp.log2(column_sum(x)) for old, x in zip(logs, values)]
            put_state(state_out, values, grown, half_periods)

        run_backward(lead, mat, hist, sel_ref, consts, state, ab_ref, logs, leave)


def second_kernel(resume, last, extend, grids, spread, *refs):
    refs = list(refs)
    sel_ref, mat, consts, hist, own_state, state_in = (refs.pop(0) for _ in range(6))
    counts_in, sums_in = (refs.pop(0), refs.pop(0)) if resume else (None, None)
    row_probs = refs.pop(0) if last else None
    mine_ref, other_ref = (refs.pop(0), refs.pop(0)) if last else (None, None)
    counts_out, sums_out = (None, None) if last else (refs.pop(0), refs.pop(0))
    state_out = refs.pop(0) if extend else None
    ab_ref, weights_ref = refs[:2]
    counts_ref, sums_ref = refs[2:] if last else (counts_out, sums_out)
    chunk = pl.program_id(0) if grids > 1 else 0
    steps, states, width = hist.shape
    core, forward_first = core_index(), is_forward_first()
    row_begin = lax.axis_index("hh") * weights_ref.shape[0]
    lead = lax.axis_index("per") * steps
    rows = weights_ref.shape[0]

    def centre(k, counts):
        probs = row_probs[k]
        weighted = probs * counts
        grad = weighted - probs * jnp.sum(weighted, axis=1, keepdims=True)
        at = slice(k * rows, (k + 1) * rows)
        left, right = grad[:, :LANES], grad[:, LANES:]
        mine_ref[at, :] = jnp.where(core == 0, left, right)
        other_ref[at, :] = jnp.where(core == 0, right, left)

    def add_counts(k, counts):
        if grids > 1:
            counts_ref[k] += counts
            return
        if resume:
            counts = counts + counts_in[k]
        if last:
            centre(k, counts)
        else:
            counts_ref[k] = counts

    second = (weights_ref, row_begin, add_counts)

    @pl.when(chunk == 0)
    def _():
        if grids > 1:
            counts_ref[...] = jnp.zeros_like(counts_ref)
        sums_ref[...] = sums_in[...] if resume else jnp.zeros_like(sums_ref)

    def add_sums(alpha_ref, other_state):
        total = jnp.zeros((1, LANES), F32)
        years = jnp.zeros((8, LANES), F32)
        for cols, here, there in zip(tiles(width), state_sums(alpha_ref), state_sums(other_state)):
            meet = column_sum(alpha_ref[:, cols].astype(F32) * (1.0 / here) * other_state[:, cols].astype(F32))
            scales = (jnp.log2(here) + jnp.log2(there)) * spread
            total += (scales + jnp.log2(meet / there)) * LN2
            years += sel_ref[2, sel_ref.shape[1] - 1, :, cols]
        total = jnp.broadcast_to(jnp.sum(total, axis=1, keepdims=True), (1, LANES))
        years = jnp.broadcast_to(jnp.sum(years[:1], axis=1, keepdims=True), (1, LANES))
        row = lax.broadcasted_iota(jnp.int32, (8, LANES), 0)
        sums_ref[...] += jnp.where(row == 0, total, jnp.where(row == 1, years, 0.0))

    zeros = [jnp.zeros((1, LANES), F32) for _ in tiles(width)]

    @pl.when(jnp.logical_not(forward_first))
    def _():
        ab_ref[...] = state_in[...]
        values = run_forward(lead, mat, hist, sel_ref, consts, ab_ref, list(zeros), second, extend=extend)
        add_sums(state_in, own_state)
        if extend:
            put_state(state_out, values, zeros, spread)

    @pl.when(forward_first)
    def _():
        state = unit_state(state_in, state_sums(state_in))
        leave = lambda values: put_state(state_out, values, zeros, spread) if extend else None
        run_backward(lead, mat, hist, sel_ref, consts, state, ab_ref, list(zeros), leave, second, lambda: add_sums(own_state, state_in))

    if last:

        @pl.when(chunk == grids - 1)
        def _():
            if grids > 1:
                for k in range(steps):
                    centre(k, counts_ref[k])
            mine_ref[steps * rows :, :] = sums_ref[...]
            other_ref[steps * rows :, :] = sums_ref[...]


def finish_kernel(scale, mine_ref, other_ref, grad_ref, mean_ref):
    count = grad_ref.shape[0]
    total = mine_ref[count : count + 1, :] + other_ref[count : count + 1, :]
    years = mine_ref[count + 1 : count + 2, :] + other_ref[count + 1 : count + 2, :]
    grad_ref[...] = (mine_ref[:count, :] + other_ref[:count, :]) * (scale / years)
    mean_ref[0] = (total / years)[0, 0]


def per_device(
    earnings, starts, lengths, block_count, trans_logits, init_logits, state_mean, log_sd
):
    slot_rows, periods = earnings.shape
    states = init_logits.shape[0]
    group = lax.axis_size(("hh", "per"))
    sides = lax.axis_size("per")
    cores = lax.axis_size("st")
    part = trans_logits.shape[0]
    steps = part * cores
    rows = states // lax.axis_size("hh")
    households = group * HB // cores
    parts = 2 if households <= 4 * HB else 1
    share = households // parts
    width = min(2 * HB, share)
    grids = share // width
    side = lax.axis_index("per")
    shaped = jax.ShapeDtypeStruct
    dma = pltpu.SemaphoreType.DMA

    swap = [(0, 1), (1, 0)]
    vec_row = pltpu.VMEM((1, states), F32)
    slots = pltpu.VMEM((slot_rows // HB, HB), jnp.int32)
    packed = pl.pallas_call(
        pack_kernel,
        out_shape=pltpu.VMEM((group, periods // 2, slot_rows), F32),
        in_specs=[smem()] + [hbm()] * 3,
        out_specs=vmem(),
        scratch_shapes=[pltpu.VMEM((periods, slot_rows), F32), slots, slots, dma((3,))],
        compiler_params=params(2),
        name="pack",
    )(block_count, *in_hbm(earnings.T, starts.reshape(-1, HB), lengths.reshape(-1, HB)))
    packed, later_logits = lax.optimization_barrier((packed, trans_logits))
    other_logits = lax.ppermute(later_logits, "st", swap)
    along = group // sides
    centre = along // 2
    outward = sorted(range(along), key=lambda z: (abs(z - centre), -z))
    listed = [z * sides + x for z in outward for x in reversed(range(sides))]
    gathered = lax.all_to_all(
        packed, ("hh", "per", "st"), split_axis=0, concat_axis=0,
        axis_index_groups=[[n * cores + c for n in listed] for c in range(cores)], tiled=True,
    )
    mat_shape = shaped((steps, states, 2 * states), BF16)
    first_mat, consts, early_mat = pl.pallas_call(
        prep_own_kernel,
        out_shape=[
            pltpu.VMEM(mat_shape.shape, BF16),
            pltpu.VMEM((4, states, LANES), F32),
            pltpu.VMEM((max(part // 2, 1),) + mat_shape.shape[1:], BF16),
        ],
        in_specs=[hbm()] * 4,
        out_specs=[vmem()] * 3,
        scratch_shapes=[pltpu.VMEM(trans_logits.shape, BF16), vec_row, vec_row, vec_row, dma, dma((3,))],
        compiler_params=params(4),
        name="prep_own",
    )(
        *in_hbm(
            trans_logits,
            init_logits.reshape(1, states), state_mean.reshape(1, states), log_sd.reshape(1, states),
        )
    )
    first_mat = pl.pallas_call(
        prep_other_kernel,
        out_shape=pltpu.VMEM(mat_shape.shape, BF16),
        in_specs=[vmem(), vmem()],
        out_specs=vmem(),
        input_output_aliases={1: 0},
        compiler_params=params(4),
        name="prep_other",
    )(other_logits, first_mat)

    def prep_second(after):
        return pl.pallas_call(
            prep_second_kernel,
            out_shape=[mat_shape, shaped((steps, rows, states), F32)],
            in_specs=[vmem(), vmem(), vmem(), hbm()],
            out_specs=[vmem(), vmem()],
            compiler_params=params(4),
            name="prep_second",
        )(trans_logits, other_logits, early_mat, after)

    def whole(*shape):
        if grids == 1:
            return vmem()
        return pl.BlockSpec(shape, lambda g: (0,) * len(shape))

    def lanes(*lead):
        if grids == 1:
            return vmem()
        return pl.BlockSpec(lead + (width,), lambda g: (0,) * len(lead) + (g,))

    grid = (grids,) if grids > 1 else ()
    hist_shape = shaped((steps, states, share), BF16)
    state_shape = shaped((states, share), BF16)
    laid = (steps if sides == 2 else periods) + 1
    sel_shape = shaped((3, laid, 8, share), F32)
    swap_shape = shaped((steps * rows + 8, LANES), F32)
    counts_shape = shaped((steps, rows, states), F32)
    sums_shape = shaped((8, LANES), F32)
    hist_spec, state_spec, sel_spec = lanes(steps, states), lanes(states), lanes(3, laid, 8)
    const_spec = whole(4, states, LANES)

    def first_pass(index, state_in):
        resume = state_in is not None
        return pl.pallas_call(
            functools.partial(first_kernel, resume, grids, index),
            grid=grid,
            out_shape=[hist_shape, state_shape, sel_shape],
            in_specs=[whole(*gathered.shape), whole(*first_mat.shape), const_spec]
            + [state_spec] * resume,
            out_specs=[hist_spec, state_spec, sel_spec],
            scratch_shapes=[pltpu.VMEM((states, width), BF16)],
            compiler_params=params(8 if grids == 1 else 32),
            name="first_pass",
        )(gathered, first_mat, consts, *([state_in] if resume else []))

    def second_pass(kept, state_in, sums_in, last, extend):
        hist, own_state, sel = kept
        resume = sums_in is not None
        scratch = [
            pltpu.VMEM((states, width), BF16),
            pltpu.VMEM((rows, width), BF16),
        ]
        counts_spec, sums_spec = whole(*counts_shape.shape), whole(*sums_shape.shape)
        if last:
            out_shape = [swap_shape] * 2
            scratch += [pltpu.VMEM(counts_shape.shape, F32), pltpu.VMEM(sums_shape.shape, F32)]
        else:
            out_shape = [counts_shape, sums_shape]
        out_specs = [whole(*x.shape) for x in out_shape]
        if extend:
            out_shape, out_specs = out_shape + [state_shape], out_specs + [state_spec]
        return pl.pallas_call(
            functools.partial(second_kernel, resume, last, extend, grids, periods // 2),
            grid=grid,
            out_shape=out_shape,
            in_specs=[sel_spec, whole(*second_mat.shape), const_spec, hist_spec, state_spec, state_spec]
            + [counts_spec, sums_spec] * resume
            + [whole(*row_probs.shape)] * last,
            out_specs=out_specs,
            scratch_shapes=scratch,
            compiler_params=params(8 if grids == 1 else 32),
            name="second_pass",
        )(
            sel, second_mat, consts, hist, own_state, state_in,
            *(sums_in if resume else []),
            *([row_probs] if last else []),
        )

    def hand_over(state, stage):
        moves = [(stage, stage + 1), (sides - 1 - stage, sides - 2 - stage)]
        return lax.ppermute(state, "per", moves)

    if sides == 2:
        kept = [first_pass(index, None) for index in range(parts)]
        arrived = [hand_over(each[1], 0) for each in kept]
        second_mat, row_probs = prep_second(kept[-1][1])
        sums = None
        for index in range(parts):
            sums = second_pass(kept[index], arrived[index], sums, index == parts - 1, False)
        mine, other = sums
    else:
        kept = [jnp.zeros(x.shape, x.dtype) for x in (hist_shape, state_shape, sel_shape)]
        done = [jnp.zeros(x.shape, x.dtype) for x in (swap_shape, swap_shape, state_shape)]
        state = None
        second_mat, row_probs = prep_second(gathered)
        for stage in range(sides):
            active = (side == stage) | (side == sides - 1 - stage)
            if stage < sides // 2:
                kept = lax.cond(
                    active, lambda x, kept: list(first_pass(0, x)), lambda x, kept: kept, state, kept
                )
                state = kept[1]
            else:
                done = lax.cond(
                    active,
                    lambda x, done: list(second_pass(kept, x, None, True, True)),
                    lambda x, done: done,
                    state,
                    done,
                )
                state = done[2]
            if stage < sides - 1:
                state = hand_over(state, stage)
        mine, other, _ = done
        total = jnp.where(side == sides // 2, mine[steps * rows], 0.0)
        total = lax.psum(total, "per")
        mine = mine.at[steps * rows].set(total)
        other = other.at[steps * rows].set(total)
    received = lax.ppermute(other, "st", swap)
    trans_grad, mean_loglik = pl.pallas_call(
        functools.partial(finish_kernel, float(states * states * periods)),
        out_shape=[shaped((steps * rows, LANES), F32), shaped((1,), F32)],
        in_specs=[vmem(), vmem()],
        out_specs=[vmem(), smem()],
        compiler_params=params(4),
        name="finish",
    )(mine, received)
    return (trans_grad.reshape(steps, rows, LANES), mean_loglik)


def solution(mesh):
    placed = (
        P(("hh", "per"), None),
        P(("hh", "per")),
        P(("hh", "per")),
        P(("hh", "per")),
        P(("grp", "per", "st"), None, None),
        P("grp"),
        P("grp"),
        P("grp"),
    )
    return jax.shard_map(
        per_device,
        mesh=mesh,
        in_specs=placed,
        out_specs=(P(("grp", "per"), "hh", "st"), P("grp")),
        check_vma=False,
    )
```

```python
import functools

import jax
import jax.numpy as jnp
from jax import lax
from jax.experimental import pallas as pl
from jax.experimental.pallas import tpu as pltpu
from jax.sharding import PartitionSpec as P

HB = 128
LANES = 128
HALF = HB // 2
SEEN = 16.0
F32 = jnp.float32
BF16 = jnp.bfloat16
LOG2E = 1.4426950408889634
LN2 = 0.6931471805599453


def vmem():
    return pl.BlockSpec(memory_space=pltpu.VMEM)


def smem():
    return pl.BlockSpec(memory_space=pltpu.SMEM)


def hbm():
    return pl.BlockSpec(memory_space=pltpu.HBM)


def in_hbm(*arrays):
    return [pltpu.with_memory_space_constraint(x, pltpu.HBM) for x in arrays]


def params(mebibytes):
    return pltpu.CompilerParams(vmem_limit_bytes=mebibytes * 1024 * 1024)


def core_index():
    return lax.axis_index("st")


def is_forward_first():
    return 2 * lax.axis_index("per") < lax.axis_size("per")


def tiles(width):
    return [slice(q, q + LANES) for q in range(0, width, LANES)]


def fetch(pairs, sems):
    copies = [pltpu.make_async_copy(src, dst, sems.at[i]) for i, (src, dst) in enumerate(pairs)]
    for copy in copies:
        copy.start()
    for copy in copies:
        copy.wait()


def pack_kernel(count_ref, earn_any, start_any, len_any, out_ref, earn_ref, start_ref, len_ref, sems):
    fetch(((earn_any, earn_ref), (start_any, start_ref), (len_any, len_ref)), sems)
    periods, slot_rows = earn_ref.shape
    core = core_index()
    low_lane = lax.broadcasted_iota(jnp.int32, (periods // 2, HB), 1) < HALF
    time = lax.broadcasted_iota(jnp.int32, (periods, HB), 0)
    for slot in range(slot_rows // HB):
        cols = slice(slot * HB, (slot + 1) * HB)
        begin = start_ref[slot : slot + 1, :]
        seen = (time >= begin) & (time < begin + len_ref[slot : slot + 1, :])
        live = slot < count_ref[0]
        shift = jnp.where(live, jnp.where(seen, SEEN, 0.0), -SEEN)
        value = earn_ref[:, cols] + shift
        early, late = value[: periods // 2], value[periods // 2 :]
        turned = pltpu.roll(jnp.where(core == 0, late, early), HALF, 1)
        packed = jnp.where(low_lane, jnp.where(core == 0, early, turned), jnp.where(core == 0, turned, late))
        for to in range(out_ref.shape[0]):
            out_ref[to, :, cols] = packed


def put(ref, at, value):
    states = value.shape[0]
    high = value.astype(BF16)
    ref[at, :states, :states] = high
    ref[at, :states, states:] = (value - high.astype(F32)).astype(BF16)


def split(x):
    high = x.astype(BF16)
    return high, (x - high.astype(F32)).astype(BF16)


def both_halves(mat, state):
    states = mat.shape[0]
    high, low = split(state)
    result = jnp.dot(mat[:, states:], high, preferred_element_type=F32)
    result += jnp.dot(mat[:, :states], low, preferred_element_type=F32)
    return result + jnp.dot(mat[:, :states], high, preferred_element_type=F32)


def fill_periods(mat, turned_pass, lead, ref, begin, end):
    @pl.loop(begin, end)
    def _(i):
        at = lead + i

        @pl.when(turned_pass)
        def _():
            lifted = jnp.exp(ref[i].T.astype(F32))
            put(mat, at, lifted * (1.0 / jnp.sum(lifted, axis=0, keepdims=True)))

        @pl.when(jnp.logical_not(turned_pass))
        def _():
            lifted = jnp.exp(ref[i].astype(F32))
            put(mat, at, lifted * (1.0 / jnp.sum(lifted, axis=1, keepdims=True)))


def prep_own_kernel(
    own_any, init_any, mean_any, sd_any, mat, consts, early, own_ref, init_ref, mean_ref, sd_ref, sem, sems
):
    part = own_ref.shape[0]
    copy = pltpu.make_async_copy(own_any, own_ref, sem)
    copy.start()
    fetch(((init_any, init_ref), (mean_any, mean_ref), (sd_any, sd_ref)), sems)
    raised = jnp.exp(init_ref[...])
    rows = (
        raised / jnp.sum(raised, axis=1, keepdims=True),
        mean_ref[...],
        (-0.5 * LOG2E) * jnp.exp(-2.0 * sd_ref[...]),
        -LOG2E * sd_ref[...],
    )
    for i, row in enumerate(rows):
        consts[i] = jnp.broadcast_to(row, (LANES, own_ref.shape[1])).T
    copy.wait()
    fill_periods(mat, is_forward_first(), core_index() * part, own_ref, 0, part)
    fill_periods(early, jnp.logical_not(is_forward_first()), 0, own_ref, 0, early.shape[0])


def prep_other_kernel(other_ref, mat_in, mat):
    part = other_ref.shape[0]
    fill_periods(mat, is_forward_first(), (1 - core_index()) * part, other_ref, 0, part)


def prep_second_kernel(own_ref, other_ref, early, after_any, mat, row_probs):
    rows = row_probs.shape[1]
    part = own_ref.shape[0]
    here = own_rows(lax.axis_index("hh") * rows, rows)
    turned_pass = jnp.logical_not(is_forward_first())
    own_lead = core_index() * part
    for i in range(early.shape[0]):
        mat[own_lead + i] = early[i]
    for lead, ref, begin in ((own_lead, own_ref, early.shape[0]), (part - own_lead, other_ref, 0)):
        for i in range(part):
            lifted = jnp.exp(ref[i, here, :].astype(F32))
            row_probs[lead + i] = lifted * (1.0 / jnp.sum(lifted, axis=1, keepdims=True))
        fill_periods(mat, turned_pass, lead, ref, begin, part)


def emission(sel_ref, consts, step_now, cols, less=None):
    gap = sel_ref[0, step_now, :1, cols] - consts[1]
    power = gap * gap * consts[2] + consts[3]
    return jnp.exp2(power if less is None else power - less)


def first_row(lead):
    return 0 if lax.axis_size("per") == 2 else lead


def is_moving(sel_ref, step_now, cols):
    return sel_ref[1, step_now, :1, cols] > 0.5


def is_seen(sel_ref, step_now, cols):
    return sel_ref[2, step_now, :1, cols] > 0.5


def column_sum(x):
    return jnp.sum(x, axis=0, keepdims=True)


def own_rows(row_begin, rows):
    return pl.ds(pl.multiple_of(row_begin, rows), rows)


def outer_sum(weights_ref, carried):
    def turned(x, y):
        return lax.dot_general(x, y, (((1,), (1,)), ((), ())), preferred_element_type=F32)

    high, low = split(weights_ref[...])
    carried_high, carried_low = split(carried)
    return turned(low, carried_high) + turned(high, carried_low) + turned(high, carried_high)


def run_forward(lead, mat, hist, sel_ref, consts, ab_ref, logs, second=None, fresh=False, extend=True):
    steps, states, width = hist.shape
    cuts = tiles(width)
    here = hist.at[0] if second is None else ab_ref
    last = [None] * len(cuts)
    inverse = [1.0 / column_sum(here[:, cols].astype(F32)) for cols in cuts]
    for k in range(steps):
        step_now = first_row(lead) + k
        here = there = ab_ref
        if second is None:
            here = hist.at[k]
            there = hist.at[k + 1] if k + 1 < steps else ab_ref
        else:
            weights_ref, row_begin, add_counts = second
            own_alpha = ab_ref[own_rows(row_begin, weights_ref.shape[0]), :].astype(F32)
        for q, cols in enumerate(cuts):
            begins = fresh and k == 0
            if not begins:
                moved = both_halves(mat[k], here[:, cols]) * inverse[q]
                moving = is_moving(sel_ref, step_now, cols)
            if second is not None:
                total = column_sum(moved * hist[k, :, cols].astype(F32))
                weight = jnp.where(moving, 1.0 / total, 0.0)
                weights_ref[:, cols] = own_alpha[:, cols] * inverse[q] * weight
                if k + 1 == steps and not extend:
                    continue
            emit = emission(sel_ref, consts, step_now, cols)
            joint = (consts[0] if begins else jnp.where(moving, moved, consts[0])) * emit
            scale = column_sum(joint)
            if second is None:
                seen = is_seen(sel_ref, step_now, cols)
                logs[q] = logs[q] + jnp.where(seen, jnp.log2(scale), 0.0)
            inverse[q] = 1.0 / scale
            there[:, cols] = joint
            last[q] = joint
        if second is not None:
            add_counts(k, outer_sum(weights_ref, hist[k]))
    return last


def run_backward(lead, mat, hist, sel_ref, consts, state, ub_ref, logs, leave, second=None, between=None):
    steps, states, width = hist.shape
    cuts = tiles(width)
    rest = [x[:1] for x in state]
    at_edge = lax.axis_size("per") == 2
    size = [jnp.zeros((1, LANES), F32) for _ in cuts]

    def step(k):
        step_now = first_row(lead) + k
        here = hist.at[k] if second is None else ub_ref
        grown = []
        for q, cols in enumerate(cuts):
            emit = emission(sel_ref, consts, step_now, cols, size[q] if second is None else None)
            carried = emit * state[q]
            here[:, cols] = carried
            whole = column_sum(carried)
            grown.append(whole)
            if second is None:
                size[q] = jnp.log2(whole)
                seen = is_seen(sel_ref, step_now, cols)
                logs[q] = logs[q] + jnp.where(seen, size[q], 0.0)
                begun = column_sum(carried * consts[0]) / whole
                rest[q] = jnp.where(seen, begun, rest[q])
        if second is not None:
            weights_ref, row_begin, add_counts = second
            own_alpha = hist[k, own_rows(row_begin, weights_ref.shape[0]), :].astype(F32)
        for q, cols in enumerate(cuts):
            product = both_halves(mat[k], here[:, cols])
            moving = is_moving(sel_ref, step_now, cols)
            if second is None:
                state[q] = jnp.where(moving, product, rest[q] * grown[q])
            else:
                shrink = 1.0 / grown[q]
                product = product * shrink
                total = column_sum(product * hist[k, :, cols].astype(F32))
                weight = jnp.where(moving, 1.0 / total, 0.0)
                weights_ref[:, cols] = own_alpha[:, cols] * weight * shrink
                if k > 1 or not at_edge:
                    state[q] = jnp.where(moving, product, rest[q])
        if second is not None:
            add_counts(k, outer_sum(weights_ref, ub_ref[...]))

    def left():
        return [x * jnp.exp2(-y) for x, y in zip(state, size)]

    for k in reversed(range(1, steps)):
        step(k)
    if second is None:
        step(0)
        leave(left())
        return
    between()
    nothing = jnp.zeros((second[0].shape[0], states), F32)
    if at_edge:
        second[2](0, nothing)
        return

    @pl.when(lead > 0)
    def _():
        step(0)
        leave(left())

    @pl.when(lead == 0)
    def _():
        second[2](0, nothing)


def put_state(state_out, values, logs, spread):
    for q, cols in enumerate(tiles(state_out.shape[1])):
        factor = jnp.exp2(logs[q] * (1.0 / spread)) / column_sum(values[q])
        state_out[:, cols] = values[q] * factor


def state_sums(state_ref):
    return [column_sum(state_ref[:, cols].astype(F32)) for cols in tiles(state_ref.shape[1])]


def state_logs(sums, spread):
    return [jnp.log2(x) * spread for x in sums]


def unit_state(state_ref, sums):
    return [state_ref[:, cols].astype(F32) * (1.0 / x) for cols, x in zip(tiles(state_ref.shape[1]), sums)]


def first_kernel(resume, grids, part, rows_ref, mat, consts, *refs):
    state_in = refs[0] if resume else None
    hist, state_out, sel_ref, ab_ref = refs[-4:]
    chunk = part * grids + (pl.program_id(0) if grids > 1 else 0)
    steps, states, width = hist.shape
    forward_first, lead = is_forward_first(), lax.axis_index("per") * steps
    cuts = tiles(width)
    group, half_periods, slot_rows = rows_ref.shape
    tops = 2 * len(cuts)

    def scan_source(d, carry):
        rank, picked = carry
        for slot in range(slot_rows // HB):
            cols = slice(slot * HB, (slot + 1) * HB)
            block = rows_ref[d, :, cols]
            live = block > -0.5 * SEEN
            picked = [jnp.where(live & (rank == chunk * tops + i), block, old) for i, old in enumerate(picked)]
            rank = rank + live.astype(jnp.int32)
        return rank, picked

    carry = (jnp.zeros((half_periods, HB), jnp.int32), [jnp.zeros((half_periods, HB), F32)] * tops)
    if group <= 8:
        for d in range(group):
            carry = scan_source(d, carry)
    else:
        carry = lax.fori_loop(0, group, scan_source, carry)
    low_lane = lax.broadcasted_iota(jnp.int32, (half_periods, HB), 1) < HALF
    local = lax.axis_size("per") == 2

    def lay_out(parts):
        for q, cols in enumerate(cuts):
            left, right = carry[1][2 * q], carry[1][2 * q + 1]
            values = (
                jnp.where(low_lane, left, pltpu.roll(right, HALF, 1)),
                jnp.where(low_lane, pltpu.roll(left, HALF, 1), right),
            )
            flags = [(value > 0.5 * SEEN).astype(F32) for value in values]
            for late in parts:
                earn = jnp.where(flags[late] > 0.5, values[late] - SEEN, values[late])
                before = flags[0][half_periods - 1 :] if late else jnp.zeros((1, HB), F32)
                for i in range(half_periods):
                    at = i if local else late * half_periods + i
                    now = flags[late][i : i + 1]
                    sel_ref[0, at, :, cols] = jnp.broadcast_to(earn[i : i + 1], (8, HB))
                    sel_ref[1, at, :, cols] = jnp.broadcast_to(now * before, (8, HB))
                    sel_ref[2, at, :, cols] = jnp.broadcast_to(now, (8, HB))
                    before = now
            years = column_sum(flags[0] + flags[1])
            sel_ref[2, sel_ref.shape[1] - 1, :, cols] = jnp.broadcast_to(years, (8, HB))

    if not local:
        lay_out((0, 1))
    zeros = [jnp.zeros((1, LANES), F32) for _ in cuts]

    @pl.when(forward_first)
    def _():
        if local:
            lay_out((0,))
        if resume:
            hist[0] = state_in[...]
        else:
            for cols in cuts:
                hist[0, :, cols] = consts[0]
        logs = state_logs(state_sums(state_in), half_periods) if resume else list(zeros)
        fresh = lax.axis_size("per") == 2
        last = run_forward(lead, mat, hist, sel_ref, consts, ab_ref, logs, fresh=fresh)
        put_state(state_out, last, logs, half_periods)

    @pl.when(jnp.logical_not(forward_first))
    def _():
        if local:
            lay_out((1,))
        sums = state_sums(state_in) if resume else None
        state = unit_state(state_in, sums) if resume else [jnp.ones((states, LANES), F32) for _ in cuts]
        logs = state_logs(sums, half_periods) if resume else list(zeros)

        def leave(values):
            grown = [old + jnp.log2(column_sum(x)) for old, x in zip(logs, values)]
            put_state(state_out, values, grown, half_periods)

        run_backward(lead, mat, hist, sel_ref, consts, state, ab_ref, logs, leave)


def second_kernel(resume, last, extend, grids, spread, *refs):
    refs = list(refs)
    sel_ref, mat, consts, hist, own_state, state_in = (refs.pop(0) for _ in range(6))
    counts_in, sums_in = (refs.pop(0), refs.pop(0)) if resume else (None, None)
    row_probs = refs.pop(0) if last else None
    mine_ref, other_ref = (refs.pop(0), refs.pop(0)) if last else (None, None)
    counts_out, sums_out = (None, None) if last else (refs.pop(0), refs.pop(0))
    state_out = refs.pop(0) if extend else None
    ab_ref, weights_ref = refs[:2]
    counts_ref, sums_ref = refs[2:] if last else (counts_out, sums_out)
    chunk = pl.program_id(0) if grids > 1 else 0
    steps, states, width = hist.shape
    core, forward_first = core_index(), is_forward_first()
    row_begin = lax.axis_index("hh") * weights_ref.shape[0]
    lead = lax.axis_index("per") * steps
    rows = weights_ref.shape[0]

    def centre(k, counts):
        probs = row_probs[k]
        weighted = probs * counts
        grad = weighted - probs * jnp.sum(weighted, axis=1, keepdims=True)
        at = slice(k * rows, (k + 1) * rows)
        left, right = grad[:, :LANES], grad[:, LANES:]
        mine_ref[at, :] = jnp.where(core == 0, left, right)
        other_ref[at, :] = jnp.where(core == 0, right, left)

    def add_counts(k, counts):
        if grids > 1:
            counts_ref[k] += counts
            return
        if resume:
            counts = counts + counts_in[k]
        if last:
            centre(k, counts)
        else:
            counts_ref[k] = counts

    second = (weights_ref, row_begin, add_counts)

    @pl.when(chunk == 0)
    def _():
        if grids > 1:
            counts_ref[...] = jnp.zeros_like(counts_ref)
        sums_ref[...] = sums_in[...] if resume else jnp.zeros_like(sums_ref)

    def add_sums(alpha_ref, other_state):
        total = jnp.zeros((1, LANES), F32)
        years = jnp.zeros((8, LANES), F32)
        for cols, here, there in zip(tiles(width), state_sums(alpha_ref), state_sums(other_state)):
            meet = column_sum(alpha_ref[:, cols].astype(F32) * (1.0 / here) * other_state[:, cols].astype(F32))
            scales = (jnp.log2(here) + jnp.log2(there)) * spread
            total += (scales + jnp.log2(meet / there)) * LN2
            years += sel_ref[2, sel_ref.shape[1] - 1, :, cols]
        total = jnp.broadcast_to(jnp.sum(total, axis=1, keepdims=True), (1, LANES))
        years = jnp.broadcast_to(jnp.sum(years[:1], axis=1, keepdims=True), (1, LANES))
        row = lax.broadcasted_iota(jnp.int32, (8, LANES), 0)
        sums_ref[...] += jnp.where(row == 0, total, jnp.where(row == 1, years, 0.0))

    zeros = [jnp.zeros((1, LANES), F32) for _ in tiles(width)]

    @pl.when(jnp.logical_not(forward_first))
    def _():
        ab_ref[...] = state_in[...]
        values = run_forward(lead, mat, hist, sel_ref, consts, ab_ref, list(zeros), second, extend=extend)
        add_sums(state_in, own_state)
        if extend:
            put_state(state_out, values, zeros, spread)

    @pl.when(forward_first)
    def _():
        state = unit_state(state_in, state_sums(state_in))
        leave = lambda values: put_state(state_out, values, zeros, spread) if extend else None
        run_backward(lead, mat, hist, sel_ref, consts, state, ab_ref, list(zeros), leave, second, lambda: add_sums(own_state, state_in))

    if last:

        @pl.when(chunk == grids - 1)
        def _():
            if grids > 1:
                for k in range(steps):
                    centre(k, counts_ref[k])
            mine_ref[steps * rows :, :] = sums_ref[...]
            other_ref[steps * rows :, :] = sums_ref[...]


def finish_kernel(scale, mine_ref, other_ref, grad_ref, mean_ref):
    count = grad_ref.shape[0]
    total = mine_ref[count : count + 1, :] + other_ref[count : count + 1, :]
    years = mine_ref[count + 1 : count + 2, :] + other_ref[count + 1 : count + 2, :]
    grad_ref[...] = (mine_ref[:count, :] + other_ref[:count, :]) * (scale / years)
    mean_ref[0] = (total / years)[0, 0]


def per_device(
    earnings, starts, lengths, block_count, trans_logits, init_logits, state_mean, log_sd
):
    slot_rows, periods = earnings.shape
    states = init_logits.shape[0]
    group = lax.axis_size(("hh", "per"))
    sides = lax.axis_size("per")
    cores = lax.axis_size("st")
    part = trans_logits.shape[0]
    steps = part * cores
    rows = states // lax.axis_size("hh")
    households = group * HB // cores
    parts = 2 if households <= 4 * HB else 1
    share = households // parts
    width = min(2 * HB, share)
    grids = share // width
    side = lax.axis_index("per")
    shaped = jax.ShapeDtypeStruct
    dma = pltpu.SemaphoreType.DMA

    swap = [(0, 1), (1, 0)]
    vec_row = pltpu.VMEM((1, states), F32)
    slots = pltpu.VMEM((slot_rows // HB, HB), jnp.int32)
    packed = pl.pallas_call(
        pack_kernel,
        out_shape=pltpu.VMEM((group, periods // 2, slot_rows), F32),
        in_specs=[smem()] + [hbm()] * 3,
        out_specs=vmem(),
        scratch_shapes=[pltpu.VMEM((periods, slot_rows), F32), slots, slots, dma((3,))],
        compiler_params=params(2),
        name="pack",
    )(block_count, *in_hbm(earnings.T, starts.reshape(-1, HB), lengths.reshape(-1, HB)))
    packed, later_logits = lax.optimization_barrier((packed, trans_logits))
    other_logits = lax.ppermute(later_logits, "st", swap)
    along = group // sides
    centre = along // 2
    outward = sorted(range(along), key=lambda z: (abs(z - centre), -z))
    listed = [z * sides + x for z in outward for x in reversed(range(sides))]
    gathered = lax.all_to_all(
        packed, ("hh", "per", "st"), split_axis=0, concat_axis=0,
        axis_index_groups=[[n * cores + c for n in listed] for c in range(cores)], tiled=True,
    )
    mat_shape = shaped((steps, states, 2 * states), BF16)
    first_mat, consts, early_mat = pl.pallas_call(
        prep_own_kernel,
        out_shape=[
            pltpu.VMEM(mat_shape.shape, BF16),
            pltpu.VMEM((4, states, LANES), F32),
            pltpu.VMEM((max(part // 2, 1),) + mat_shape.shape[1:], BF16),
        ],
        in_specs=[hbm()] * 4,
        out_specs=[vmem()] * 3,
        scratch_shapes=[pltpu.VMEM(trans_logits.shape, BF16), vec_row, vec_row, vec_row, dma, dma((3,))],
        compiler_params=params(4),
        name="prep_own",
    )(
        *in_hbm(
            trans_logits,
            init_logits.reshape(1, states), state_mean.reshape(1, states), log_sd.reshape(1, states),
        )
    )
    first_mat = pl.pallas_call(
        prep_other_kernel,
        out_shape=pltpu.VMEM(mat_shape.shape, BF16),
        in_specs=[vmem(), vmem()],
        out_specs=vmem(),
        input_output_aliases={1: 0},
        compiler_params=params(4),
        name="prep_other",
    )(other_logits, first_mat)

    def prep_second(after):
        return pl.pallas_call(
            prep_second_kernel,
            out_shape=[mat_shape, shaped((steps, rows, states), F32)],
            in_specs=[vmem(), vmem(), vmem(), hbm()],
            out_specs=[vmem(), vmem()],
            compiler_params=params(4),
            name="prep_second",
        )(trans_logits, other_logits, early_mat, after)

    def whole(*shape):
        if grids == 1:
            return vmem()
        return pl.BlockSpec(shape, lambda g: (0,) * len(shape))

    def lanes(*lead):
        if grids == 1:
            return vmem()
        return pl.BlockSpec(lead + (width,), lambda g: (0,) * len(lead) + (g,))

    grid = (grids,) if grids > 1 else ()
    hist_shape = shaped((steps, states, share), F32)
    state_shape = shaped((states, share), F32)
    laid = (steps if sides == 2 else periods) + 1
    sel_shape = shaped((3, laid, 8, share), F32)
    swap_shape = shaped((steps * rows + 8, LANES), F32)
    counts_shape = shaped((steps, rows, states), F32)
    sums_shape = shaped((8, LANES), F32)
    hist_spec, state_spec, sel_spec = lanes(steps, states), lanes(states), lanes(3, laid, 8)
    const_spec = whole(4, states, LANES)

    def first_pass(index, state_in):
        resume = state_in is not None
        return pl.pallas_call(
            functools.partial(first_kernel, resume, grids, index),
            grid=grid,
            out_shape=[hist_shape, state_shape, sel_shape],
            in_specs=[whole(*gathered.shape), whole(*first_mat.shape), const_spec]
            + [state_spec] * resume,
            out_specs=[hist_spec, state_spec, sel_spec],
            scratch_shapes=[pltpu.VMEM((states, width), F32)],
            compiler_params=params(16 if grids == 1 else 40),
            name="first_pass",
        )(gathered, first_mat, consts, *([state_in] if resume else []))

    def second_pass(kept, state_in, sums_in, last, extend):
        hist, own_state, sel = kept
        resume = sums_in is not None
        scratch = [
            pltpu.VMEM((states, width), F32),
            pltpu.VMEM((rows, width), F32),
        ]
        counts_spec, sums_spec = whole(*counts_shape.shape), whole(*sums_shape.shape)
        if last:
            out_shape = [swap_shape] * 2
            scratch += [pltpu.VMEM(counts_shape.shape, F32), pltpu.VMEM(sums_shape.shape, F32)]
        else:
            out_shape = [counts_shape, sums_shape]
        out_specs = [whole(*x.shape) for x in out_shape]
        if extend:
            out_shape, out_specs = out_shape + [state_shape], out_specs + [state_spec]
        return pl.pallas_call(
            functools.partial(second_kernel, resume, last, extend, grids, periods // 2),
            grid=grid,
            out_shape=out_shape,
            in_specs=[sel_spec, whole(*second_mat.shape), const_spec, hist_spec, state_spec, state_spec]
            + [counts_spec, sums_spec] * resume
            + [whole(*row_probs.shape)] * last,
            out_specs=out_specs,
            scratch_shapes=scratch,
            compiler_params=params(16 if grids == 1 else 40),
            name="second_pass",
        )(
            sel, second_mat, consts, hist, own_state, state_in,
            *(sums_in if resume else []),
            *([row_probs] if last else []),
        )

    def hand_over(state, stage):
        moves = [(stage, stage + 1), (sides - 1 - stage, sides - 2 - stage)]
        return lax.ppermute(state, "per", moves)

    if sides == 2:
        kept = [first_pass(index, None) for index in range(parts)]
        arrived = [hand_over(each[1], 0) for each in kept]
        second_mat, row_probs = prep_second(kept[-1][1])
        sums = None
        for index in range(parts):
            sums = second_pass(kept[index], arrived[index], sums, index == parts - 1, False)
        mine, other = sums
    else:
        kept = [jnp.zeros(x.shape, x.dtype) for x in (hist_shape, state_shape, sel_shape)]
        done = [jnp.zeros(x.shape, x.dtype) for x in (swap_shape, swap_shape, state_shape)]
        state = None
        second_mat, row_probs = prep_second(gathered)
        for stage in range(sides):
            active = (side == stage) | (side == sides - 1 - stage)
            if stage < sides // 2:
                kept = lax.cond(
                    active, lambda x, kept: list(first_pass(0, x)), lambda x, kept: kept, state, kept
                )
                state = kept[1]
            else:
                done = lax.cond(
                    active,
                    lambda x, done: list(second_pass(kept, x, None, True, True)),
                    lambda x, done: done,
                    state,
                    done,
                )
                state = done[2]
            if stage < sides - 1:
                state = hand_over(state, stage)
        mine, other, _ = done
        total = jnp.where(side == sides // 2, mine[steps * rows], 0.0)
        total = lax.psum(total, "per")
        mine = mine.at[steps * rows].set(total)
        other = other.at[steps * rows].set(total)
    received = lax.ppermute(other, "st", swap)
    trans_grad, mean_loglik = pl.pallas_call(
        functools.partial(finish_kernel, float(states * states * periods)),
        out_shape=[shaped((steps * rows, LANES), F32), shaped((1,), F32)],
        in_specs=[vmem(), vmem()],
        out_specs=[vmem(), smem()],
        compiler_params=params(4),
        name="finish",
    )(mine, received)
    return (trans_grad.reshape(steps, rows, LANES), mean_loglik)


def solution(mesh):
    placed = (
        P(("hh", "per"), None),
        P(("hh", "per")),
        P(("hh", "per")),
        P(("hh", "per")),
        P(("grp", "per", "st"), None, None),
        P("grp"),
        P("grp"),
        P("grp"),
    )
    return jax.shard_map(
        per_device,
        mesh=mesh,
        in_specs=placed,
        out_specs=(P(("grp", "per"), "hh", "st"), P("grp")),
        check_vma=False,
    )
```

```python
import functools

import jax
import jax.numpy as jnp
from jax import lax
from jax.experimental import pallas as pl
from jax.experimental.pallas import tpu as pltpu
from jax.sharding import PartitionSpec as P

HB = 128
LANES = 128
HALF = HB // 2
SEEN = 16.0
F32 = jnp.float32
BF16 = jnp.bfloat16
LOG2E = 1.4426950408889634
LN2 = 0.6931471805599453


def vmem():
    return pl.BlockSpec(memory_space=pltpu.VMEM)


def smem():
    return pl.BlockSpec(memory_space=pltpu.SMEM)


def hbm():
    return pl.BlockSpec(memory_space=pltpu.HBM)


def in_hbm(*arrays):
    return [pltpu.with_memory_space_constraint(x, pltpu.HBM) for x in arrays]


def params(mebibytes):
    return pltpu.CompilerParams(vmem_limit_bytes=mebibytes * 1024 * 1024)


def core_index():
    return lax.axis_index("st")


def is_forward_first():
    return 2 * lax.axis_index("per") < lax.axis_size("per")


def tiles(width):
    return [slice(q, q + LANES) for q in range(0, width, LANES)]


def fetch(pairs, sems):
    copies = [pltpu.make_async_copy(src, dst, sems.at[i]) for i, (src, dst) in enumerate(pairs)]
    for copy in copies:
        copy.start()
    for copy in copies:
        copy.wait()


def pack_kernel(count_ref, earn_any, start_any, len_any, out_ref, earn_ref, start_ref, len_ref, sems):
    fetch(((earn_any, earn_ref), (start_any, start_ref), (len_any, len_ref)), sems)
    periods, slot_rows = earn_ref.shape
    core = core_index()
    low_lane = lax.broadcasted_iota(jnp.int32, (periods // 2, HB), 1) < HALF
    time = lax.broadcasted_iota(jnp.int32, (periods, HB), 0)
    for slot in range(slot_rows // HB):
        cols = slice(slot * HB, (slot + 1) * HB)
        begin = start_ref[slot : slot + 1, :]
        seen = (time >= begin) & (time < begin + len_ref[slot : slot + 1, :])
        live = slot < count_ref[0]
        shift = jnp.where(live, jnp.where(seen, SEEN, 0.0), -SEEN)
        value = earn_ref[:, cols] + shift
        early, late = value[: periods // 2], value[periods // 2 :]
        turned = pltpu.roll(jnp.where(core == 0, late, early), HALF, 1)
        packed = jnp.where(low_lane, jnp.where(core == 0, early, turned), jnp.where(core == 0, turned, late))
        for to in range(out_ref.shape[0]):
            out_ref[to, :, cols] = packed


def put(ref, at, value):
    states = value.shape[0]
    high = value.astype(BF16)
    ref[at, :states, :states] = high
    ref[at, :states, states:] = (value - high.astype(F32)).astype(BF16)


def split(x):
    high = x.astype(BF16)
    return high, (x - high.astype(F32)).astype(BF16)


def both_halves(mat, state):
    states = mat.shape[0]
    high, low = split(state)
    result = jnp.dot(mat[:, states:], high, preferred_element_type=F32)
    result += jnp.dot(mat[:, :states], low, preferred_element_type=F32)
    return result + jnp.dot(mat[:, :states], high, preferred_element_type=F32)


def fill_periods(mat, turned_pass, lead, ref, begin, end):
    @pl.loop(begin, end)
    def _(i):
        at = lead + i

        @pl.when(turned_pass)
        def _():
            lifted = jnp.exp(ref[i].T.astype(F32))
            put(mat, at, lifted * (1.0 / jnp.sum(lifted, axis=0, keepdims=True)))

        @pl.when(jnp.logical_not(turned_pass))
        def _():
            lifted = jnp.exp(ref[i].astype(F32))
            put(mat, at, lifted * (1.0 / jnp.sum(lifted, axis=1, keepdims=True)))


def prep_own_kernel(
    own_any, init_any, mean_any, sd_any, mat, consts, early, own_ref, init_ref, mean_ref, sd_ref, sem, sems
):
    part = own_ref.shape[0]
    copy = pltpu.make_async_copy(own_any, own_ref, sem)
    copy.start()
    fetch(((init_any, init_ref), (mean_any, mean_ref), (sd_any, sd_ref)), sems)
    raised = jnp.exp(init_ref[...])
    rows = (
        raised / jnp.sum(raised, axis=1, keepdims=True),
        mean_ref[...],
        (-0.5 * LOG2E) * jnp.exp(-2.0 * sd_ref[...]),
        -LOG2E * sd_ref[...],
    )
    for i, row in enumerate(rows):
        consts[i] = jnp.broadcast_to(row, (LANES, own_ref.shape[1])).T
    copy.wait()
    fill_periods(mat, is_forward_first(), core_index() * part, own_ref, 0, part)
    fill_periods(early, jnp.logical_not(is_forward_first()), 0, own_ref, 0, early.shape[0])


def prep_other_kernel(other_ref, mat_in, mat):
    part = other_ref.shape[0]
    fill_periods(mat, is_forward_first(), (1 - core_index()) * part, other_ref, 0, part)


def prep_second_kernel(own_ref, other_ref, early, after_any, mat, row_probs):
    rows = row_probs.shape[1]
    part = own_ref.shape[0]
    here = own_rows(lax.axis_index("hh") * rows, rows)
    turned_pass = jnp.logical_not(is_forward_first())
    own_lead = core_index() * part
    for i in range(early.shape[0]):
        mat[own_lead + i] = early[i]
    for lead, ref, begin in ((own_lead, own_ref, early.shape[0]), (part - own_lead, other_ref, 0)):
        for i in range(part):
            lifted = jnp.exp(ref[i, here, :].astype(F32))
            row_probs[lead + i] = lifted * (1.0 / jnp.sum(lifted, axis=1, keepdims=True))
        fill_periods(mat, turned_pass, lead, ref, begin, part)


def emission(sel_ref, consts, step_now, cols, less=None):
    gap = sel_ref[0, step_now, :1, cols] - consts[1]
    power = gap * gap * consts[2] + consts[3]
    return jnp.exp2(power if less is None else power - less)


def first_row(lead):
    return 0 if lax.axis_size("per") == 2 else lead


def is_moving(sel_ref, step_now, cols):
    return sel_ref[1, step_now, :1, cols] > 0.5


def is_seen(sel_ref, step_now, cols):
    return sel_ref[2, step_now, :1, cols] > 0.5


def column_sum(x):
    return jnp.sum(x, axis=0, keepdims=True)


def own_rows(row_begin, rows):
    return pl.ds(pl.multiple_of(row_begin, rows), rows)


def outer_sum(weights_ref, carried):
    def turned(x, y):
        return lax.dot_general(x, y, (((1,), (1,)), ((), ())), preferred_element_type=F32)

    high, low = split(weights_ref[...])
    carried_high, carried_low = split(carried)
    return turned(low, carried_high) + turned(high, carried_low) + turned(high, carried_high)


def run_forward(lead, mat, hist, sel_ref, consts, ab_ref, logs, second=None, fresh=False, extend=True):
    steps, states, width = hist.shape
    cuts = tiles(width)
    here = hist.at[0] if second is None else ab_ref
    last = [None] * len(cuts)
    inverse = [1.0 / column_sum(here[:, cols].astype(F32)) for cols in cuts]
    for k in range(steps):
        step_now = first_row(lead) + k
        here = there = ab_ref
        if second is None:
            here = hist.at[k]
            there = hist.at[k + 1] if k + 1 < steps else ab_ref
        else:
            weights_ref, row_begin, add_counts = second
            own_alpha = ab_ref[own_rows(row_begin, weights_ref.shape[0]), :].astype(F32)
        for q, cols in enumerate(cuts):
            begins = fresh and k == 0
            if not begins:
                moved = both_halves(mat[k], here[:, cols]) * inverse[q]
                moving = is_moving(sel_ref, step_now, cols)
            if second is not None:
                total = column_sum(moved * hist[k, :, cols].astype(F32))
                weight = jnp.where(moving, 1.0 / total, 0.0)
                weights_ref[:, cols] = own_alpha[:, cols] * inverse[q] * weight
                if k + 1 == steps and not extend:
                    continue
            emit = emission(sel_ref, consts, step_now, cols)
            joint = (consts[0] if begins else jnp.where(moving, moved, consts[0])) * emit
            scale = column_sum(joint)
            if second is None:
                seen = is_seen(sel_ref, step_now, cols)
                logs[q] = logs[q] + jnp.where(seen, jnp.log2(scale), 0.0)
            inverse[q] = 1.0 / scale
            there[:, cols] = joint
            last[q] = joint
        if second is not None:
            add_counts(k, outer_sum(weights_ref, hist[k]))
    return last


def run_backward(lead, mat, hist, sel_ref, consts, state, ub_ref, logs, leave, second=None, between=None):
    steps, states, width = hist.shape
    cuts = tiles(width)
    rest = [x[:1] for x in state]
    at_edge = lax.axis_size("per") == 2
    size = [jnp.zeros((1, LANES), F32) for _ in cuts]

    def step(k):
        step_now = first_row(lead) + k
        here = hist.at[k] if second is None else ub_ref
        grown = []
        for q, cols in enumerate(cuts):
            emit = emission(sel_ref, consts, step_now, cols, size[q] if second is None else None)
            carried = emit * state[q]
            here[:, cols] = carried
            whole = column_sum(carried)
            grown.append(whole)
            if second is None:
                size[q] = jnp.log2(whole)
                seen = is_seen(sel_ref, step_now, cols)
                logs[q] = logs[q] + jnp.where(seen, size[q], 0.0)
                begun = column_sum(carried * consts[0]) / whole
                rest[q] = jnp.where(seen, begun, rest[q])
        if second is not None:
            weights_ref, row_begin, add_counts = second
            own_alpha = hist[k, own_rows(row_begin, weights_ref.shape[0]), :].astype(F32)
        for q, cols in enumerate(cuts):
            product = both_halves(mat[k], here[:, cols])
            moving = is_moving(sel_ref, step_now, cols)
            if second is None:
                state[q] = jnp.where(moving, product, rest[q] * grown[q])
            else:
                shrink = 1.0 / grown[q]
                product = product * shrink
                total = column_sum(product * hist[k, :, cols].astype(F32))
                weight = jnp.where(moving, 1.0 / total, 0.0)
                weights_ref[:, cols] = own_alpha[:, cols] * weight * shrink
                if k > 1 or not at_edge:
                    state[q] = jnp.where(moving, product, rest[q])
        if second is not None:
            add_counts(k, outer_sum(weights_ref, ub_ref[...]))

    def left():
        return [x * jnp.exp2(-y) for x, y in zip(state, size)]

    for k in reversed(range(1, steps)):
        step(k)
    if second is None:
        step(0)
        leave(left())
        return
    between()
    nothing = jnp.zeros((second[0].shape[0], states), F32)
    if at_edge:
        second[2](0, nothing)
        return

    @pl.when(lead > 0)
    def _():
        step(0)
        leave(left())

    @pl.when(lead == 0)
    def _():
        second[2](0, nothing)


def put_state(state_out, values, logs, spread):
    for q, cols in enumerate(tiles(state_out.shape[1])):
        factor = jnp.exp2(logs[q] * (1.0 / spread)) / column_sum(values[q])
        state_out[:, cols] = (values[q] * factor).astype(BF16)


def state_sums(state_ref):
    return [column_sum(state_ref[:, cols].astype(F32)) for cols in tiles(state_ref.shape[1])]


def state_logs(sums, spread):
    return [jnp.log2(x) * spread for x in sums]


def unit_state(state_ref, sums):
    return [state_ref[:, cols].astype(F32) * (1.0 / x) for cols, x in zip(tiles(state_ref.shape[1]), sums)]


def first_kernel(resume, grids, part, rows_ref, mat, consts, *refs):
    state_in = refs[0] if resume else None
    hist, state_out, sel_ref, ab_ref = refs[-4:]
    chunk = part * grids + (pl.program_id(0) if grids > 1 else 0)
    steps, states, width = hist.shape
    forward_first, lead = is_forward_first(), lax.axis_index("per") * steps
    cuts = tiles(width)
    group, half_periods, slot_rows = rows_ref.shape
    tops = 2 * len(cuts)

    def scan_source(d, carry):
        rank, picked = carry
        for slot in range(slot_rows // HB):
            cols = slice(slot * HB, (slot + 1) * HB)
            block = rows_ref[d, :, cols]
            live = block > -0.5 * SEEN
            picked = [jnp.where(live & (rank == chunk * tops + i), block, old) for i, old in enumerate(picked)]
            rank = rank + live.astype(jnp.int32)
        return rank, picked

    carry = (jnp.zeros((half_periods, HB), jnp.int32), [jnp.zeros((half_periods, HB), F32)] * tops)
    if group <= 8:
        for d in range(group):
            carry = scan_source(d, carry)
    else:
        carry = lax.fori_loop(0, group, scan_source, carry)
    low_lane = lax.broadcasted_iota(jnp.int32, (half_periods, HB), 1) < HALF
    local = lax.axis_size("per") == 2

    def lay_out(parts):
        for q, cols in enumerate(cuts):
            left, right = carry[1][2 * q], carry[1][2 * q + 1]
            values = (
                jnp.where(low_lane, left, pltpu.roll(right, HALF, 1)),
                jnp.where(low_lane, pltpu.roll(left, HALF, 1), right),
            )
            flags = [(value > 0.5 * SEEN).astype(F32) for value in values]
            for late in parts:
                earn = jnp.where(flags[late] > 0.5, values[late] - SEEN, values[late])
                before = flags[0][half_periods - 1 :] if late else jnp.zeros((1, HB), F32)
                for i in range(half_periods):
                    at = i if local else late * half_periods + i
                    now = flags[late][i : i + 1]
                    sel_ref[0, at, :, cols] = jnp.broadcast_to(earn[i : i + 1], (8, HB))
                    sel_ref[1, at, :, cols] = jnp.broadcast_to(now * before, (8, HB))
                    sel_ref[2, at, :, cols] = jnp.broadcast_to(now, (8, HB))
                    before = now
            years = column_sum(flags[0] + flags[1])
            sel_ref[2, sel_ref.shape[1] - 1, :, cols] = jnp.broadcast_to(years, (8, HB))

    if not local:
        lay_out((0, 1))
    zeros = [jnp.zeros((1, LANES), F32) for _ in cuts]

    @pl.when(forward_first)
    def _():
        if local:
            lay_out((0,))
        if resume:
            hist[0] = state_in[...].astype(F32)
        else:
            for cols in cuts:
                hist[0, :, cols] = consts[0]
        logs = state_logs(state_sums(state_in), half_periods) if resume else list(zeros)
        fresh = lax.axis_size("per") == 2
        last = run_forward(lead, mat, hist, sel_ref, consts, ab_ref, logs, fresh=fresh)
        put_state(state_out, last, logs, half_periods)

    @pl.when(jnp.logical_not(forward_first))
    def _():
        if local:
            lay_out((1,))
        sums = state_sums(state_in) if resume else None
        state = unit_state(state_in, sums) if resume else [jnp.ones((states, LANES), F32) for _ in cuts]
        logs = state_logs(sums, half_periods) if resume else list(zeros)

        def leave(values):
            grown = [old + jnp.log2(column_sum(x)) for old, x in zip(logs, values)]
            put_state(state_out, values, grown, half_periods)

        run_backward(lead, mat, hist, sel_ref, consts, state, ab_ref, logs, leave)


def second_kernel(resume, last, extend, grids, spread, *refs):
    refs = list(refs)
    sel_ref, mat, consts, hist, own_state, state_in = (refs.pop(0) for _ in range(6))
    counts_in, sums_in = (refs.pop(0), refs.pop(0)) if resume else (None, None)
    row_probs = refs.pop(0) if last else None
    mine_ref, other_ref = (refs.pop(0), refs.pop(0)) if last else (None, None)
    counts_out, sums_out = (None, None) if last else (refs.pop(0), refs.pop(0))
    state_out = refs.pop(0) if extend else None
    ab_ref, weights_ref = refs[:2]
    counts_ref, sums_ref = refs[2:] if last else (counts_out, sums_out)
    chunk = pl.program_id(0) if grids > 1 else 0
    steps, states, width = hist.shape
    core, forward_first = core_index(), is_forward_first()
    row_begin = lax.axis_index("hh") * weights_ref.shape[0]
    lead = lax.axis_index("per") * steps
    rows = weights_ref.shape[0]

    def centre(k, counts):
        probs = row_probs[k]
        weighted = probs * counts
        grad = weighted - probs * jnp.sum(weighted, axis=1, keepdims=True)
        at = slice(k * rows, (k + 1) * rows)
        left, right = grad[:, :LANES], grad[:, LANES:]
        mine_ref[at, :] = jnp.where(core == 0, left, right)
        other_ref[at, :] = jnp.where(core == 0, right, left)

    def add_counts(k, counts):
        if grids > 1:
            counts_ref[k] += counts
            return
        if resume:
            counts = counts + counts_in[k]
        if last:
            centre(k, counts)
        else:
            counts_ref[k] = counts

    second = (weights_ref, row_begin, add_counts)

    @pl.when(chunk == 0)
    def _():
        if grids > 1:
            counts_ref[...] = jnp.zeros_like(counts_ref)
        sums_ref[...] = sums_in[...] if resume else jnp.zeros_like(sums_ref)

    def add_sums(alpha_ref, other_state):
        total = jnp.zeros((1, LANES), F32)
        years = jnp.zeros((8, LANES), F32)
        for cols, here, there in zip(tiles(width), state_sums(alpha_ref), state_sums(other_state)):
            meet = column_sum(alpha_ref[:, cols].astype(F32) * (1.0 / here) * other_state[:, cols].astype(F32))
            scales = (jnp.log2(here) + jnp.log2(there)) * spread
            total += (scales + jnp.log2(meet / there)) * LN2
            years += sel_ref[2, sel_ref.shape[1] - 1, :, cols]
        total = jnp.broadcast_to(jnp.sum(total, axis=1, keepdims=True), (1, LANES))
        years = jnp.broadcast_to(jnp.sum(years[:1], axis=1, keepdims=True), (1, LANES))
        row = lax.broadcasted_iota(jnp.int32, (8, LANES), 0)
        sums_ref[...] += jnp.where(row == 0, total, jnp.where(row == 1, years, 0.0))

    zeros = [jnp.zeros((1, LANES), F32) for _ in tiles(width)]

    @pl.when(jnp.logical_not(forward_first))
    def _():
        ab_ref[...] = state_in[...].astype(F32)
        values = run_forward(lead, mat, hist, sel_ref, consts, ab_ref, list(zeros), second, extend=extend)
        add_sums(state_in, own_state)
        if extend:
            put_state(state_out, values, zeros, spread)

    @pl.when(forward_first)
    def _():
        state = unit_state(state_in, state_sums(state_in))
        leave = lambda values: put_state(state_out, values, zeros, spread) if extend else None
        run_backward(lead, mat, hist, sel_ref, consts, state, ab_ref, list(zeros), leave, second, lambda: add_sums(own_state, state_in))

    if last:

        @pl.when(chunk == grids - 1)
        def _():
            if grids > 1:
                for k in range(steps):
                    centre(k, counts_ref[k])
            mine_ref[steps * rows :, :] = sums_ref[...]
            other_ref[steps * rows :, :] = sums_ref[...]


def finish_kernel(scale, mine_ref, other_ref, grad_ref, mean_ref):
    count = grad_ref.shape[0]
    total = mine_ref[count : count + 1, :] + other_ref[count : count + 1, :]
    years = mine_ref[count + 1 : count + 2, :] + other_ref[count + 1 : count + 2, :]
    grad_ref[...] = (mine_ref[:count, :] + other_ref[:count, :]) * (scale / years)
    mean_ref[0] = (total / years)[0, 0]


def per_device(
    earnings, starts, lengths, block_count, trans_logits, init_logits, state_mean, log_sd
):
    slot_rows, periods = earnings.shape
    states = init_logits.shape[0]
    group = lax.axis_size(("hh", "per"))
    sides = lax.axis_size("per")
    cores = lax.axis_size("st")
    part = trans_logits.shape[0]
    steps = part * cores
    rows = states // lax.axis_size("hh")
    households = group * HB // cores
    parts = 2 if households <= 4 * HB else 1
    share = households // parts
    width = min(2 * HB, share)
    grids = share // width
    side = lax.axis_index("per")
    shaped = jax.ShapeDtypeStruct
    dma = pltpu.SemaphoreType.DMA

    swap = [(0, 1), (1, 0)]
    vec_row = pltpu.VMEM((1, states), F32)
    slots = pltpu.VMEM((slot_rows // HB, HB), jnp.int32)
    packed = pl.pallas_call(
        pack_kernel,
        out_shape=pltpu.VMEM((group, periods // 2, slot_rows), F32),
        in_specs=[smem()] + [hbm()] * 3,
        out_specs=vmem(),
        scratch_shapes=[pltpu.VMEM((periods, slot_rows), F32), slots, slots, dma((3,))],
        compiler_params=params(2),
        name="pack",
    )(block_count, *in_hbm(earnings.T, starts.reshape(-1, HB), lengths.reshape(-1, HB)))
    packed, later_logits = lax.optimization_barrier((packed, trans_logits))
    other_logits = lax.ppermute(later_logits, "st", swap)
    along = group // sides
    centre = along // 2
    outward = sorted(range(along), key=lambda z: (abs(z - centre), -z))
    listed = [z * sides + x for z in outward for x in reversed(range(sides))]
    gathered = lax.all_to_all(
        packed, ("hh", "per", "st"), split_axis=0, concat_axis=0,
        axis_index_groups=[[n * cores + c for n in listed] for c in range(cores)], tiled=True,
    )
    mat_shape = shaped((steps, states, 2 * states), BF16)
    first_mat, consts, early_mat = pl.pallas_call(
        prep_own_kernel,
        out_shape=[
            pltpu.VMEM(mat_shape.shape, BF16),
            pltpu.VMEM((4, states, LANES), F32),
            pltpu.VMEM((max(part // 2, 1),) + mat_shape.shape[1:], BF16),
        ],
        in_specs=[hbm()] * 4,
        out_specs=[vmem()] * 3,
        scratch_shapes=[pltpu.VMEM(trans_logits.shape, BF16), vec_row, vec_row, vec_row, dma, dma((3,))],
        compiler_params=params(4),
        name="prep_own",
    )(
        *in_hbm(
            trans_logits,
            init_logits.reshape(1, states), state_mean.reshape(1, states), log_sd.reshape(1, states),
        )
    )
    first_mat = pl.pallas_call(
        prep_other_kernel,
        out_shape=pltpu.VMEM(mat_shape.shape, BF16),
        in_specs=[vmem(), vmem()],
        out_specs=vmem(),
        input_output_aliases={1: 0},
        compiler_params=params(4),
        name="prep_other",
    )(other_logits, first_mat)

    def prep_second(after):
        return pl.pallas_call(
            prep_second_kernel,
            out_shape=[mat_shape, shaped((steps, rows, states), F32)],
            in_specs=[vmem(), vmem(), vmem(), hbm()],
            out_specs=[vmem(), vmem()],
            compiler_params=params(4),
            name="prep_second",
        )(trans_logits, other_logits, early_mat, after)

    def whole(*shape):
        if grids == 1:
            return vmem()
        return pl.BlockSpec(shape, lambda g: (0,) * len(shape))

    def lanes(*lead):
        if grids == 1:
            return vmem()
        return pl.BlockSpec(lead + (width,), lambda g: (0,) * len(lead) + (g,))

    grid = (grids,) if grids > 1 else ()
    hist_shape = shaped((steps, states, share), F32)
    state_shape = shaped((states, share), BF16)
    laid = (steps if sides == 2 else periods) + 1
    sel_shape = shaped((3, laid, 8, share), F32)
    swap_shape = shaped((steps * rows + 8, LANES), F32)
    counts_shape = shaped((steps, rows, states), F32)
    sums_shape = shaped((8, LANES), F32)
    hist_spec, state_spec, sel_spec = lanes(steps, states), lanes(states), lanes(3, laid, 8)
    const_spec = whole(4, states, LANES)

    def first_pass(index, state_in):
        resume = state_in is not None
        return pl.pallas_call(
            functools.partial(first_kernel, resume, grids, index),
            grid=grid,
            out_shape=[hist_shape, state_shape, sel_shape],
            in_specs=[whole(*gathered.shape), whole(*first_mat.shape), const_spec]
            + [state_spec] * resume,
            out_specs=[hist_spec, state_spec, sel_spec],
            scratch_shapes=[pltpu.VMEM((states, width), F32)],
            compiler_params=params(16 if grids == 1 else 40),
            name="first_pass",
        )(gathered, first_mat, consts, *([state_in] if resume else []))

    def second_pass(kept, state_in, sums_in, last, extend):
        hist, own_state, sel = kept
        resume = sums_in is not None
        scratch = [
            pltpu.VMEM((states, width), F32),
            pltpu.VMEM((rows, width), F32),
        ]
        counts_spec, sums_spec = whole(*counts_shape.shape), whole(*sums_shape.shape)
        if last:
            out_shape = [swap_shape] * 2
            scratch += [pltpu.VMEM(counts_shape.shape, F32), pltpu.VMEM(sums_shape.shape, F32)]
        else:
            out_shape = [counts_shape, sums_shape]
        out_specs = [whole(*x.shape) for x in out_shape]
        if extend:
            out_shape, out_specs = out_shape + [state_shape], out_specs + [state_spec]
        return pl.pallas_call(
            functools.partial(second_kernel, resume, last, extend, grids, periods // 2),
            grid=grid,
            out_shape=out_shape,
            in_specs=[sel_spec, whole(*second_mat.shape), const_spec, hist_spec, state_spec, state_spec]
            + [counts_spec, sums_spec] * resume
            + [whole(*row_probs.shape)] * last,
            out_specs=out_specs,
            scratch_shapes=scratch,
            compiler_params=params(16 if grids == 1 else 40),
            name="second_pass",
        )(
            sel, second_mat, consts, hist, own_state, state_in,
            *(sums_in if resume else []),
            *([row_probs] if last else []),
        )

    def hand_over(state, stage):
        moves = [(stage, stage + 1), (sides - 1 - stage, sides - 2 - stage)]
        return lax.ppermute(state, "per", moves)

    if sides == 2:
        kept = [first_pass(index, None) for index in range(parts)]
        arrived = [hand_over(each[1], 0) for each in kept]
        second_mat, row_probs = prep_second(kept[-1][1])
        sums = None
        for index in range(parts):
            sums = second_pass(kept[index], arrived[index], sums, index == parts - 1, False)
        mine, other = sums
    else:
        kept = [jnp.zeros(x.shape, x.dtype) for x in (hist_shape, state_shape, sel_shape)]
        done = [jnp.zeros(x.shape, x.dtype) for x in (swap_shape, swap_shape, state_shape)]
        state = None
        second_mat, row_probs = prep_second(gathered)
        for stage in range(sides):
            active = (side == stage) | (side == sides - 1 - stage)
            if stage < sides // 2:
                kept = lax.cond(
                    active, lambda x, kept: list(first_pass(0, x)), lambda x, kept: kept, state, kept
                )
                state = kept[1]
            else:
                done = lax.cond(
                    active,
                    lambda x, done: list(second_pass(kept, x, None, True, True)),
                    lambda x, done: done,
                    state,
                    done,
                )
                state = done[2]
            if stage < sides - 1:
                state = hand_over(state, stage)
        mine, other, _ = done
        total = jnp.where(side == sides // 2, mine[steps * rows], 0.0)
        total = lax.psum(total, "per")
        mine = mine.at[steps * rows].set(total)
        other = other.at[steps * rows].set(total)
    received = lax.ppermute(other, "st", swap)
    trans_grad, mean_loglik = pl.pallas_call(
        functools.partial(finish_kernel, float(states * states * periods)),
        out_shape=[shaped((steps * rows, LANES), F32), shaped((1,), F32)],
        in_specs=[vmem(), vmem()],
        out_specs=[vmem(), smem()],
        compiler_params=params(4),
        name="finish",
    )(mine, received)
    return (trans_grad.reshape(steps, rows, LANES), mean_loglik)


def solution(mesh):
    placed = (
        P(("hh", "per"), None),
        P(("hh", "per")),
        P(("hh", "per")),
        P(("hh", "per")),
        P(("grp", "per", "st"), None, None),
        P("grp"),
        P("grp"),
        P("grp"),
    )
    return jax.shard_map(
        per_device,
        mesh=mesh,
        in_specs=placed,
        out_specs=(P(("grp", "per"), "hh", "st"), P("grp")),
        check_vma=False,
    )
```

```python
import functools

import jax
import jax.numpy as jnp
from jax import lax
from jax.experimental import pallas as pl
from jax.experimental.pallas import tpu as pltpu
from jax.sharding import PartitionSpec as P

HB = 128
LANES = 128
HALF = HB // 2
SEEN = 16.0
F32 = jnp.float32
BF16 = jnp.bfloat16
LOG2E = 1.4426950408889634
LN2 = 0.6931471805599453


def vmem():
    return pl.BlockSpec(memory_space=pltpu.VMEM)


def smem():
    return pl.BlockSpec(memory_space=pltpu.SMEM)


def hbm():
    return pl.BlockSpec(memory_space=pltpu.HBM)


def in_hbm(*arrays):
    return [pltpu.with_memory_space_constraint(x, pltpu.HBM) for x in arrays]


def params(mebibytes):
    return pltpu.CompilerParams(vmem_limit_bytes=mebibytes * 1024 * 1024)


def core_index():
    return lax.axis_index("st")


def is_forward_first():
    return 2 * lax.axis_index("per") < lax.axis_size("per")


def tiles(width):
    return [slice(q, q + LANES) for q in range(0, width, LANES)]


def fetch(pairs, sems):
    copies = [pltpu.make_async_copy(src, dst, sems.at[i]) for i, (src, dst) in enumerate(pairs)]
    for copy in copies:
        copy.start()
    for copy in copies:
        copy.wait()


def pack_kernel(count_ref, earn_any, start_any, len_any, out_ref, earn_ref, start_ref, len_ref, sems):
    fetch(((earn_any, earn_ref), (start_any, start_ref), (len_any, len_ref)), sems)
    periods, slot_rows = earn_ref.shape
    core = core_index()
    low_lane = lax.broadcasted_iota(jnp.int32, (periods // 2, HB), 1) < HALF
    time = lax.broadcasted_iota(jnp.int32, (periods, HB), 0)
    for slot in range(slot_rows // HB):
        cols = slice(slot * HB, (slot + 1) * HB)
        begin = start_ref[slot : slot + 1, :]
        seen = (time >= begin) & (time < begin + len_ref[slot : slot + 1, :])
        live = slot < count_ref[0]
        shift = jnp.where(live, jnp.where(seen, SEEN, 0.0), -SEEN)
        value = earn_ref[:, cols] + shift
        early, late = value[: periods // 2], value[periods // 2 :]
        turned = pltpu.roll(jnp.where(core == 0, late, early), HALF, 1)
        packed = jnp.where(low_lane, jnp.where(core == 0, early, turned), jnp.where(core == 0, turned, late))
        for to in range(out_ref.shape[0]):
            out_ref[to, :, cols] = packed


def put(ref, at, value):
    states = value.shape[0]
    high = value.astype(BF16)
    ref[at, :states, :states] = high
    ref[at, :states, states:] = (value - high.astype(F32)).astype(BF16)


def split(x):
    high = x.astype(BF16)
    return high, (x - high.astype(F32)).astype(BF16)


def both_halves(mat, state):
    states = mat.shape[0]
    high, low = split(state)
    result = jnp.dot(mat[:, states:], high, preferred_element_type=F32)
    result += jnp.dot(mat[:, :states], low, preferred_element_type=F32)
    return result + jnp.dot(mat[:, :states], high, preferred_element_type=F32)


def fill_periods(mat, turned_pass, lead, ref, begin, end):
    @pl.loop(begin, end)
    def _(i):
        at = lead + i

        @pl.when(turned_pass)
        def _():
            lifted = jnp.exp(ref[i].T.astype(F32))
            put(mat, at, lifted * (1.0 / jnp.sum(lifted, axis=0, keepdims=True)))

        @pl.when(jnp.logical_not(turned_pass))
        def _():
            lifted = jnp.exp(ref[i].astype(F32))
            put(mat, at, lifted * (1.0 / jnp.sum(lifted, axis=1, keepdims=True)))


def prep_own_kernel(
    own_any, init_any, mean_any, sd_any, mat, consts, early, own_ref, init_ref, mean_ref, sd_ref, sem, sems
):
    part = own_ref.shape[0]
    copy = pltpu.make_async_copy(own_any, own_ref, sem)
    copy.start()
    fetch(((init_any, init_ref), (mean_any, mean_ref), (sd_any, sd_ref)), sems)
    raised = jnp.exp(init_ref[...])
    rows = (
        raised / jnp.sum(raised, axis=1, keepdims=True),
        mean_ref[...],
        (-0.5 * LOG2E) * jnp.exp(-2.0 * sd_ref[...]),
        -LOG2E * sd_ref[...],
    )
    for i, row in enumerate(rows):
        consts[i] = jnp.broadcast_to(row, (LANES, own_ref.shape[1])).T
    copy.wait()
    fill_periods(mat, is_forward_first(), core_index() * part, own_ref, 0, part)
    fill_periods(early, jnp.logical_not(is_forward_first()), 0, own_ref, 0, early.shape[0])


def prep_other_kernel(other_ref, mat_in, mat):
    part = other_ref.shape[0]
    fill_periods(mat, is_forward_first(), (1 - core_index()) * part, other_ref, 0, part)


def prep_second_kernel(own_ref, other_ref, early, after_any, mat, row_probs):
    rows = row_probs.shape[1]
    part = own_ref.shape[0]
    here = own_rows(lax.axis_index("hh") * rows, rows)
    turned_pass = jnp.logical_not(is_forward_first())
    own_lead = core_index() * part
    for i in range(early.shape[0]):
        mat[own_lead + i] = early[i]
    for lead, ref, begin in ((own_lead, own_ref, early.shape[0]), (part - own_lead, other_ref, 0)):
        for i in range(part):
            lifted = jnp.exp(ref[i, here, :].astype(F32))
            row_probs[lead + i] = lifted * (1.0 / jnp.sum(lifted, axis=1, keepdims=True))
        fill_periods(mat, turned_pass, lead, ref, begin, part)


def emission(sel_ref, consts, step_now, cols, less=None):
    gap = sel_ref[0, step_now, :1, cols] - consts[1]
    power = gap * gap * consts[2] + consts[3]
    return jnp.exp2(power if less is None else power - less)


def first_row(lead):
    return 0 if lax.axis_size("per") == 2 else lead


def is_moving(sel_ref, step_now, cols):
    return sel_ref[1, step_now, :1, cols] > 0.5


def is_seen(sel_ref, step_now, cols):
    return sel_ref[2, step_now, :1, cols] > 0.5


def column_sum(x):
    return jnp.sum(x, axis=0, keepdims=True)


def own_rows(row_begin, rows):
    return pl.ds(pl.multiple_of(row_begin, rows), rows)


def outer_sum(weights_ref, carried):
    def turned(x, y):
        return lax.dot_general(x, y, (((1,), (1,)), ((), ())), preferred_element_type=F32)

    high, low = split(weights_ref[...])
    carried_high, carried_low = split(carried)
    rows = high.shape[0]
    both = turned(jnp.concatenate([high, low], axis=0), carried_high)
    return both[rows:] + turned(high, carried_low) + both[:rows]


def run_forward(lead, mat, hist, sel_ref, consts, ab_ref, logs, second=None, fresh=False, extend=True):
    steps, states, width = hist.shape
    cuts = tiles(width)
    here = hist.at[0] if second is None else ab_ref
    last = [None] * len(cuts)
    inverse = [1.0 / column_sum(here[:, cols].astype(F32)) for cols in cuts]
    for k in range(steps):
        step_now = first_row(lead) + k
        here = there = ab_ref
        if second is None:
            here = hist.at[k]
            there = hist.at[k + 1] if k + 1 < steps else ab_ref
        else:
            weights_ref, row_begin, add_counts = second
            own_alpha = ab_ref[own_rows(row_begin, weights_ref.shape[0]), :].astype(F32)
        for q, cols in enumerate(cuts):
            begins = fresh and k == 0
            if not begins:
                moved = both_halves(mat[k], here[:, cols]) * inverse[q]
                moving = is_moving(sel_ref, step_now, cols)
            if second is not None:
                total = column_sum(moved * hist[k, :, cols].astype(F32))
                weight = jnp.where(moving, 1.0 / total, 0.0)
                weights_ref[:, cols] = own_alpha[:, cols] * inverse[q] * weight
                if k + 1 == steps and not extend:
                    continue
            emit = emission(sel_ref, consts, step_now, cols)
            joint = (consts[0] if begins else jnp.where(moving, moved, consts[0])) * emit
            scale = column_sum(joint)
            if second is None:
                seen = is_seen(sel_ref, step_now, cols)
                logs[q] = logs[q] + jnp.where(seen, jnp.log2(scale), 0.0)
            inverse[q] = 1.0 / scale
            there[:, cols] = joint
            last[q] = joint
        if second is not None:
            add_counts(k, outer_sum(weights_ref, hist[k]))
    return last


def run_backward(lead, mat, hist, sel_ref, consts, state, ub_ref, logs, leave, second=None, between=None):
    steps, states, width = hist.shape
    cuts = tiles(width)
    rest = [x[:1] for x in state]
    at_edge = lax.axis_size("per") == 2
    size = [jnp.zeros((1, LANES), F32) for _ in cuts]

    def step(k):
        step_now = first_row(lead) + k
        here = hist.at[k] if second is None else ub_ref
        grown = []
        for q, cols in enumerate(cuts):
            emit = emission(sel_ref, consts, step_now, cols, size[q] if second is None else None)
            carried = emit * state[q]
            here[:, cols] = carried
            whole = column_sum(carried)
            grown.append(whole)
            if second is None:
                size[q] = jnp.log2(whole)
                seen = is_seen(sel_ref, step_now, cols)
                logs[q] = logs[q] + jnp.where(seen, size[q], 0.0)
                begun = column_sum(carried * consts[0]) / whole
                rest[q] = jnp.where(seen, begun, rest[q])
        if second is not None:
            weights_ref, row_begin, add_counts = second
            own_alpha = hist[k, own_rows(row_begin, weights_ref.shape[0]), :].astype(F32)
        for q, cols in enumerate(cuts):
            product = both_halves(mat[k], here[:, cols])
            moving = is_moving(sel_ref, step_now, cols)
            if second is None:
                state[q] = jnp.where(moving, product, rest[q] * grown[q])
            else:
                shrink = 1.0 / grown[q]
                product = product * shrink
                total = column_sum(product * hist[k, :, cols].astype(F32))
                weight = jnp.where(moving, 1.0 / total, 0.0)
                weights_ref[:, cols] = own_alpha[:, cols] * weight * shrink
                if k > 1 or not at_edge:
                    state[q] = jnp.where(moving, product, rest[q])
        if second is not None:
            add_counts(k, outer_sum(weights_ref, ub_ref[...]))

    def left():
        return [x * jnp.exp2(-y) for x, y in zip(state, size)]

    for k in reversed(range(1, steps)):
        step(k)
    if second is None:
        step(0)
        leave(left())
        return
    between()
    nothing = jnp.zeros((second[0].shape[0], states), F32)
    if at_edge:
        second[2](0, nothing)
        return

    @pl.when(lead > 0)
    def _():
        step(0)
        leave(left())

    @pl.when(lead == 0)
    def _():
        second[2](0, nothing)


def put_state(state_out, values, logs, spread):
    for q, cols in enumerate(tiles(state_out.shape[1])):
        factor = jnp.exp2(logs[q] * (1.0 / spread)) / column_sum(values[q])
        state_out[:, cols] = (values[q] * factor).astype(BF16)


def state_sums(state_ref):
    return [column_sum(state_ref[:, cols].astype(F32)) for cols in tiles(state_ref.shape[1])]


def state_logs(sums, spread):
    return [jnp.log2(x) * spread for x in sums]


def unit_state(state_ref, sums):
    return [state_ref[:, cols].astype(F32) * (1.0 / x) for cols, x in zip(tiles(state_ref.shape[1]), sums)]


def first_kernel(resume, grids, part, rows_ref, mat, consts, *refs):
    state_in = refs[0] if resume else None
    hist, state_out, sel_ref, ab_ref = refs[-4:]
    chunk = part * grids + (pl.program_id(0) if grids > 1 else 0)
    steps, states, width = hist.shape
    forward_first, lead = is_forward_first(), lax.axis_index("per") * steps
    cuts = tiles(width)
    group, half_periods, slot_rows = rows_ref.shape
    tops = 2 * len(cuts)

    def scan_source(d, carry):
        rank, picked = carry
        for slot in range(slot_rows // HB):
            cols = slice(slot * HB, (slot + 1) * HB)
            block = rows_ref[d, :, cols]
            live = block > -0.5 * SEEN
            picked = [jnp.where(live & (rank == chunk * tops + i), block, old) for i, old in enumerate(picked)]
            rank = rank + live.astype(jnp.int32)
        return rank, picked

    carry = (jnp.zeros((half_periods, HB), jnp.int32), [jnp.zeros((half_periods, HB), F32)] * tops)
    if group <= 8:
        for d in range(group):
            carry = scan_source(d, carry)
    else:
        carry = lax.fori_loop(0, group, scan_source, carry)
    low_lane = lax.broadcasted_iota(jnp.int32, (half_periods, HB), 1) < HALF
    local = lax.axis_size("per") == 2

    def lay_out(parts):
        for q, cols in enumerate(cuts):
            left, right = carry[1][2 * q], carry[1][2 * q + 1]
            values = (
                jnp.where(low_lane, left, pltpu.roll(right, HALF, 1)),
                jnp.where(low_lane, pltpu.roll(left, HALF, 1), right),
            )
            flags = [(value > 0.5 * SEEN).astype(F32) for value in values]
            for late in parts:
                earn = jnp.where(flags[late] > 0.5, values[late] - SEEN, values[late])
                before = flags[0][half_periods - 1 :] if late else jnp.zeros((1, HB), F32)
                for i in range(half_periods):
                    at = i if local else late * half_periods + i
                    now = flags[late][i : i + 1]
                    sel_ref[0, at, :, cols] = jnp.broadcast_to(earn[i : i + 1], (8, HB))
                    sel_ref[1, at, :, cols] = jnp.broadcast_to(now * before, (8, HB))
                    sel_ref[2, at, :, cols] = jnp.broadcast_to(now, (8, HB))
                    before = now
            years = column_sum(flags[0] + flags[1])
            sel_ref[2, sel_ref.shape[1] - 1, :, cols] = jnp.broadcast_to(years, (8, HB))

    if not local:
        lay_out((0, 1))
    zeros = [jnp.zeros((1, LANES), F32) for _ in cuts]

    @pl.when(forward_first)
    def _():
        if local:
            lay_out((0,))
        if resume:
            hist[0] = state_in[...].astype(F32)
        else:
            for cols in cuts:
                hist[0, :, cols] = consts[0]
        logs = state_logs(state_sums(state_in), half_periods) if resume else list(zeros)
        fresh = lax.axis_size("per") == 2
        last = run_forward(lead, mat, hist, sel_ref, consts, ab_ref, logs, fresh=fresh)
        put_state(state_out, last, logs, half_periods)

    @pl.when(jnp.logical_not(forward_first))
    def _():
        if local:
            lay_out((1,))
        sums = state_sums(state_in) if resume else None
        state = unit_state(state_in, sums) if resume else [jnp.ones((states, LANES), F32) for _ in cuts]
        logs = state_logs(sums, half_periods) if resume else list(zeros)

        def leave(values):
            grown = [old + jnp.log2(column_sum(x)) for old, x in zip(logs, values)]
            put_state(state_out, values, grown, half_periods)

        run_backward(lead, mat, hist, sel_ref, consts, state, ab_ref, logs, leave)


def second_kernel(resume, last, extend, grids, spread, *refs):
    refs = list(refs)
    sel_ref, mat, consts, hist, own_state, state_in = (refs.pop(0) for _ in range(6))
    counts_in, sums_in = (refs.pop(0), refs.pop(0)) if resume else (None, None)
    row_probs = refs.pop(0) if last else None
    mine_ref, other_ref = (refs.pop(0), refs.pop(0)) if last else (None, None)
    counts_out, sums_out = (None, None) if last else (refs.pop(0), refs.pop(0))
    state_out = refs.pop(0) if extend else None
    ab_ref, weights_ref = refs[:2]
    counts_ref, sums_ref = refs[2:] if last else (counts_out, sums_out)
    chunk = pl.program_id(0) if grids > 1 else 0
    steps, states, width = hist.shape
    core, forward_first = core_index(), is_forward_first()
    row_begin = lax.axis_index("hh") * weights_ref.shape[0]
    lead = lax.axis_index("per") * steps
    rows = weights_ref.shape[0]

    def centre(k, counts):
        probs = row_probs[k]
        weighted = probs * counts
        grad = weighted - probs * jnp.sum(weighted, axis=1, keepdims=True)
        at = slice(k * rows, (k + 1) * rows)
        left, right = grad[:, :LANES], grad[:, LANES:]
        mine_ref[at, :] = jnp.where(core == 0, left, right)
        other_ref[at, :] = jnp.where(core == 0, right, left)

    def add_counts(k, counts):
        if grids > 1:
            counts_ref[k] += counts
            return
        if resume:
            counts = counts + counts_in[k]
        if last:
            centre(k, counts)
        else:
            counts_ref[k] = counts

    second = (weights_ref, row_begin, add_counts)

    @pl.when(chunk == 0)
    def _():
        if grids > 1:
            counts_ref[...] = jnp.zeros_like(counts_ref)
        sums_ref[...] = sums_in[...] if resume else jnp.zeros_like(sums_ref)

    def add_sums(alpha_ref, other_state):
        total = jnp.zeros((1, LANES), F32)
        years = jnp.zeros((8, LANES), F32)
        for cols, here, there in zip(tiles(width), state_sums(alpha_ref), state_sums(other_state)):
            meet = column_sum(alpha_ref[:, cols].astype(F32) * (1.0 / here) * other_state[:, cols].astype(F32))
            scales = (jnp.log2(here) + jnp.log2(there)) * spread
            total += (scales + jnp.log2(meet / there)) * LN2
            years += sel_ref[2, sel_ref.shape[1] - 1, :, cols]
        total = jnp.broadcast_to(jnp.sum(total, axis=1, keepdims=True), (1, LANES))
        years = jnp.broadcast_to(jnp.sum(years[:1], axis=1, keepdims=True), (1, LANES))
        row = lax.broadcasted_iota(jnp.int32, (8, LANES), 0)
        sums_ref[...] += jnp.where(row == 0, total, jnp.where(row == 1, years, 0.0))

    zeros = [jnp.zeros((1, LANES), F32) for _ in tiles(width)]

    @pl.when(jnp.logical_not(forward_first))
    def _():
        ab_ref[...] = state_in[...].astype(F32)
        values = run_forward(lead, mat, hist, sel_ref, consts, ab_ref, list(zeros), second, extend=extend)
        add_sums(state_in, own_state)
        if extend:
            put_state(state_out, values, zeros, spread)

    @pl.when(forward_first)
    def _():
        state = unit_state(state_in, state_sums(state_in))
        leave = lambda values: put_state(state_out, values, zeros, spread) if extend else None
        run_backward(lead, mat, hist, sel_ref, consts, state, ab_ref, list(zeros), leave, second, lambda: add_sums(own_state, state_in))

    if last:

        @pl.when(chunk == grids - 1)
        def _():
            if grids > 1:
                for k in range(steps):
                    centre(k, counts_ref[k])
            mine_ref[steps * rows :, :] = sums_ref[...]
            other_ref[steps * rows :, :] = sums_ref[...]


def finish_kernel(scale, mine_ref, other_ref, grad_ref, mean_ref):
    count = grad_ref.shape[0]
    total = mine_ref[count : count + 1, :] + other_ref[count : count + 1, :]
    years = mine_ref[count + 1 : count + 2, :] + other_ref[count + 1 : count + 2, :]
    grad_ref[...] = (mine_ref[:count, :] + other_ref[:count, :]) * (scale / years)
    mean_ref[0] = (total / years)[0, 0]


def per_device(
    earnings, starts, lengths, block_count, trans_logits, init_logits, state_mean, log_sd
):
    slot_rows, periods = earnings.shape
    states = init_logits.shape[0]
    group = lax.axis_size(("hh", "per"))
    sides = lax.axis_size("per")
    cores = lax.axis_size("st")
    part = trans_logits.shape[0]
    steps = part * cores
    rows = states // lax.axis_size("hh")
    households = group * HB // cores
    parts = 2 if households <= 4 * HB else 1
    share = households // parts
    width = min(2 * HB, share)
    grids = share // width
    side = lax.axis_index("per")
    shaped = jax.ShapeDtypeStruct
    dma = pltpu.SemaphoreType.DMA

    swap = [(0, 1), (1, 0)]
    vec_row = pltpu.VMEM((1, states), F32)
    slots = pltpu.VMEM((slot_rows // HB, HB), jnp.int32)
    packed = pl.pallas_call(
        pack_kernel,
        out_shape=pltpu.VMEM((group, periods // 2, slot_rows), F32),
        in_specs=[smem()] + [hbm()] * 3,
        out_specs=vmem(),
        scratch_shapes=[pltpu.VMEM((periods, slot_rows), F32), slots, slots, dma((3,))],
        compiler_params=params(2),
        name="pack",
    )(block_count, *in_hbm(earnings.T, starts.reshape(-1, HB), lengths.reshape(-1, HB)))
    packed, later_logits = lax.optimization_barrier((packed, trans_logits))
    other_logits = lax.ppermute(later_logits, "st", swap)
    along = group // sides
    centre = along // 2
    outward = sorted(range(along), key=lambda z: (abs(z - centre), -z))
    listed = [z * sides + x for z in outward for x in reversed(range(sides))]
    gathered = lax.all_to_all(
        packed, ("hh", "per", "st"), split_axis=0, concat_axis=0,
        axis_index_groups=[[n * cores + c for n in listed] for c in range(cores)], tiled=True,
    )
    mat_shape = shaped((steps, states, 2 * states), BF16)
    first_mat, consts, early_mat = pl.pallas_call(
        prep_own_kernel,
        out_shape=[
            pltpu.VMEM(mat_shape.shape, BF16),
            pltpu.VMEM((4, states, LANES), F32),
            pltpu.VMEM((max(part // 2, 1),) + mat_shape.shape[1:], BF16),
        ],
        in_specs=[hbm()] * 4,
        out_specs=[vmem()] * 3,
        scratch_shapes=[pltpu.VMEM(trans_logits.shape, BF16), vec_row, vec_row, vec_row, dma, dma((3,))],
        compiler_params=params(4),
        name="prep_own",
    )(
        *in_hbm(
            trans_logits,
            init_logits.reshape(1, states), state_mean.reshape(1, states), log_sd.reshape(1, states),
        )
    )
    first_mat = pl.pallas_call(
        prep_other_kernel,
        out_shape=pltpu.VMEM(mat_shape.shape, BF16),
        in_specs=[vmem(), vmem()],
        out_specs=vmem(),
        input_output_aliases={1: 0},
        compiler_params=params(4),
        name="prep_other",
    )(other_logits, first_mat)

    def prep_second(after):
        return pl.pallas_call(
            prep_second_kernel,
            out_shape=[mat_shape, shaped((steps, rows, states), F32)],
            in_specs=[vmem(), vmem(), vmem(), hbm()],
            out_specs=[vmem(), vmem()],
            compiler_params=params(4),
            name="prep_second",
        )(trans_logits, other_logits, early_mat, after)

    def whole(*shape):
        if grids == 1:
            return vmem()
        return pl.BlockSpec(shape, lambda g: (0,) * len(shape))

    def lanes(*lead):
        if grids == 1:
            return vmem()
        return pl.BlockSpec(lead + (width,), lambda g: (0,) * len(lead) + (g,))

    grid = (grids,) if grids > 1 else ()
    hist_shape = shaped((steps, states, share), F32)
    state_shape = shaped((states, share), BF16)
    laid = (steps if sides == 2 else periods) + 1
    sel_shape = shaped((3, laid, 8, share), F32)
    swap_shape = shaped((steps * rows + 8, LANES), F32)
    counts_shape = shaped((steps, rows, states), F32)
    sums_shape = shaped((8, LANES), F32)
    hist_spec, state_spec, sel_spec = lanes(steps, states), lanes(states), lanes(3, laid, 8)
    const_spec = whole(4, states, LANES)

    def first_pass(index, state_in):
        resume = state_in is not None
        return pl.pallas_call(
            functools.partial(first_kernel, resume, grids, index),
            grid=grid,
            out_shape=[hist_shape, state_shape, sel_shape],
            in_specs=[whole(*gathered.shape), whole(*first_mat.shape), const_spec]
            + [state_spec] * resume,
            out_specs=[hist_spec, state_spec, sel_spec],
            scratch_shapes=[pltpu.VMEM((states, width), F32)],
            compiler_params=params(16 if grids == 1 else 40),
            name="first_pass",
        )(gathered, first_mat, consts, *([state_in] if resume else []))

    def second_pass(kept, state_in, sums_in, last, extend):
        hist, own_state, sel = kept
        resume = sums_in is not None
        scratch = [
            pltpu.VMEM((states, width), F32),
            pltpu.VMEM((rows, width), F32),
        ]
        counts_spec, sums_spec = whole(*counts_shape.shape), whole(*sums_shape.shape)
        if last:
            out_shape = [swap_shape] * 2
            scratch += [pltpu.VMEM(counts_shape.shape, F32), pltpu.VMEM(sums_shape.shape, F32)]
        else:
            out_shape = [counts_shape, sums_shape]
        out_specs = [whole(*x.shape) for x in out_shape]
        if extend:
            out_shape, out_specs = out_shape + [state_shape], out_specs + [state_spec]
        return pl.pallas_call(
            functools.partial(second_kernel, resume, last, extend, grids, periods // 2),
            grid=grid,
            out_shape=out_shape,
            in_specs=[sel_spec, whole(*second_mat.shape), const_spec, hist_spec, state_spec, state_spec]
            + [counts_spec, sums_spec] * resume
            + [whole(*row_probs.shape)] * last,
            out_specs=out_specs,
            scratch_shapes=scratch,
            compiler_params=params(16 if grids == 1 else 40),
            name="second_pass",
        )(
            sel, second_mat, consts, hist, own_state, state_in,
            *(sums_in if resume else []),
            *([row_probs] if last else []),
        )

    def hand_over(state, stage):
        moves = [(stage, stage + 1), (sides - 1 - stage, sides - 2 - stage)]
        return lax.ppermute(state, "per", moves)

    if sides == 2:
        kept = [first_pass(index, None) for index in range(parts)]
        arrived = [hand_over(each[1], 0) for each in kept]
        second_mat, row_probs = prep_second(kept[-1][1])
        sums = None
        for index in range(parts):
            sums = second_pass(kept[index], arrived[index], sums, index == parts - 1, False)
        mine, other = sums
    else:
        kept = [jnp.zeros(x.shape, x.dtype) for x in (hist_shape, state_shape, sel_shape)]
        done = [jnp.zeros(x.shape, x.dtype) for x in (swap_shape, swap_shape, state_shape)]
        state = None
        second_mat, row_probs = prep_second(gathered)
        for stage in range(sides):
            active = (side == stage) | (side == sides - 1 - stage)
            if stage < sides // 2:
                kept = lax.cond(
                    active, lambda x, kept: list(first_pass(0, x)), lambda x, kept: kept, state, kept
                )
                state = kept[1]
            else:
                done = lax.cond(
                    active,
                    lambda x, done: list(second_pass(kept, x, None, True, True)),
                    lambda x, done: done,
                    state,
                    done,
                )
                state = done[2]
            if stage < sides - 1:
                state = hand_over(state, stage)
        mine, other, _ = done
        total = jnp.where(side == sides // 2, mine[steps * rows], 0.0)
        total = lax.psum(total, "per")
        mine = mine.at[steps * rows].set(total)
        other = other.at[steps * rows].set(total)
    received = lax.ppermute(other, "st", swap)
    trans_grad, mean_loglik = pl.pallas_call(
        functools.partial(finish_kernel, float(states * states * periods)),
        out_shape=[shaped((steps * rows, LANES), F32), shaped((1,), F32)],
        in_specs=[vmem(), vmem()],
        out_specs=[vmem(), smem()],
        compiler_params=params(4),
        name="finish",
    )(mine, received)
    return (trans_grad.reshape(steps, rows, LANES), mean_loglik)


def solution(mesh):
    placed = (
        P(("hh", "per"), None),
        P(("hh", "per")),
        P(("hh", "per")),
        P(("hh", "per")),
        P(("grp", "per", "st"), None, None),
        P("grp"),
        P("grp"),
        P("grp"),
    )
    return jax.shard_map(
        per_device,
        mesh=mesh,
        in_specs=placed,
        out_specs=(P(("grp", "per"), "hh", "st"), P("grp")),
        check_vma=False,
    )
```
